32 devices in a mesh: dp: 16 (over z, y, core), tensor: 2 (over x).
Axes of the slice: x: 2, y: 2, z: 4, core: 2. Of those that a mesh axis runs over, the one named last changes fastest.
Arguments:
- tokens: bfloat16 [8192, 2048], P('dp'), may hold values from -6 to 6
- cotangent: bfloat16 [8192, 2048], P('dp'), may hold values from -6 to 6
- lengths: int32 [16], replicated, may hold values from 128 to 512, as said below
- attn_gain: float32 [2048], replicated, may hold values from 0.5 to 1.5
- query_gain: float32 [64], replicated, may hold values from 0.25 to 1.75
- key_gain: float32 [64], replicated, may hold values from 0.25 to 1.75
- w_query: bfloat16 [2048, 2048], P('dp', 'tensor'), may hold values from -0.125 to 0.125
- key_weight_matrix: bfloat16 [2048, 512], P('dp', 'tensor'), may hold values from -0.125 to 0.125
- value_weight_matrix: bfloat16 [2048, 512], P('dp', 'tensor'), may hold values from -0.125 to 0.125
- w_out: bfloat16 [2048, 2048], P(('tensor', 'dp')), may hold values from -0.5 to 0.5
- ffn_gain: float32 [2048], replicated, may hold values from 0.5 to 1.5
- w_gate: bfloat16 [2048, 8192], P('dp', 'tensor'), may hold values from -0.125 to 0.125
- w_up: bfloat16 [2048, 8192], P('dp', 'tensor'), may hold values from -0.125 to 0.125
- w_down: bfloat16 [8192, 2048], P(('tensor', 'dp')), may hold values from -0.0625 to 0.0625
Outputs:
- layer_out: bfloat16 [8192, 2048], P('dp')
- input_grad: float32 [8192, 2048], P('dp')
- attn_gain_grad: float32 [2048], replicated
- query_gain_grad: float32 [64], replicated
- key_gain_grad: float32 [64], replicated
- w_query_grad: float32 [2048, 2048], P('dp', 'tensor')
- w_key_grad: float32 [2048, 512], P('dp', 'tensor')
- w_value_grad: float32 [2048, 512], P('dp', 'tensor')
- w_out_grad: float32 [2048, 2048], P(('tensor', 'dp'))
- ffn_gain_grad: float32 [2048], replicated
- w_gate_grad: float32 [2048, 8192], P('dp', 'tensor')
- w_up_grad: float32 [2048, 8192], P('dp', 'tensor')
- w_down_grad: float32 [8192, 2048], P(('tensor', 'dp'))
The draws below stay inside these ranges and needn't reach their ends.
Inputs may be any that keep to these rules, and one draw needn't show every extreme that they name: `lengths`: valid tokens at the start of each slot of 512; the rest is padding.
All inputs are finite; a program needn't handle non-finite values.
Results may differ from the reference program's by a relative error of at most 0.014.
Values may be sent and summed in bfloat16 or wider, within the bound.
A program may use at most 256 MiB of HBM per device.

```python
import functools
import math
import jax
import jax.numpy as jnp
from jax import lax

MODEL_WIDTH = 2048
QUERY_HEADS = 32
KEY_VALUE_HEADS = 8
HEAD_SIZE = 64
FF = 8192
SLOT_TOKENS = 512
SLOT_COUNT = 16
TOKENS = 8192


def draw_lengths(key, part):
    key = jax.random.fold_in(key, 7)
    key_draw, key_full, key_short = jax.random.split(key, 3)
    drawn_lengths = jax.random.randint(key_draw, (SLOT_COUNT,), SLOT_TOKENS // 4, SLOT_TOKENS + 1)
    full_slot = jax.random.randint(key_full, (), 0, SLOT_COUNT)
    short_slot = (full_slot + 1 + jax.random.randint(key_short, (), 0, SLOT_COUNT - 1)) % SLOT_COUNT
    slot_index = jnp.arange(SLOT_COUNT, dtype=jnp.int32)
    drawn_lengths = jnp.where(slot_index == full_slot, SLOT_TOKENS, drawn_lengths)
    drawn_lengths = jnp.where(slot_index == short_slot, SLOT_TOKENS // 4, drawn_lengths)
    return drawn_lengths.astype(jnp.int32)


def shard_levels(rng, dims, cuts, least, high):
    def one(axis_at, blocks):
        heights = jax.random.uniform(jax.random.fold_in(jax.random.fold_in(rng, 6), axis_at), (blocks,), jnp.float32, least / len(cuts), high / len(cuts))
        return jnp.repeat(jnp.exp(heights), dims[axis_at] // blocks).reshape((-1,) + (1,) * (len(dims) - axis_at - 1))

    factor_of = one(*cuts[0])
    for cut in cuts[1:]:
        factor_of = factor_of * one(*cut)
    return factor_of


def bell_draw(stream_key, extent, width, most, pieces=(), kind=jnp.bfloat16):
    drawn = jax.random.normal(stream_key, extent, jnp.float32) * width
    if len(pieces) > 0:
        drawn = shard_levels(stream_key, extent, pieces, -0.22, 0.18) * drawn
    return jnp.clip(drawn, min=-most, max=most).astype(kind)


def setup_inputs(seed: int = 0) -> dict:
    arg_keys = jax.random.split(jax.random.key(seed), 15)
    return {
        "tokens": bell_draw(arg_keys[0], (TOKENS, MODEL_WIDTH), 1.0, 6.0, ((0, 16),)),
        "cotangent": bell_draw(arg_keys[1], (TOKENS, MODEL_WIDTH), 1.0, 6.0, ((0, 16),)),
        "lengths": draw_lengths(jax.random.fold_in(arg_keys[14], 71), 0),
        "attn_gain": jnp.clip(1.0 + 0.1 * jax.random.normal(arg_keys[3], (MODEL_WIDTH,), jnp.float32), 0.5, 1.5),
        "query_gain": jnp.clip(1.0 + 0.15 * jax.random.normal(arg_keys[4], (HEAD_SIZE,), jnp.float32), 0.25, 1.75),
        "key_gain": jnp.clip(1.0 + 0.15 * jax.random.normal(arg_keys[5], (HEAD_SIZE,), jnp.float32), 0.25, 1.75),
        "w_query": bell_draw(arg_keys[6], (MODEL_WIDTH, QUERY_HEADS * HEAD_SIZE), MODEL_WIDTH ** -0.5, 0.125, ((0, 16), (1, 2))),
        "key_weight_matrix": bell_draw(arg_keys[7], (MODEL_WIDTH, KEY_VALUE_HEADS * HEAD_SIZE), MODEL_WIDTH ** -0.5, 0.125, ((0, 16), (1, 2))),
        "value_weight_matrix": bell_draw(arg_keys[8], (MODEL_WIDTH, KEY_VALUE_HEADS * HEAD_SIZE), MODEL_WIDTH ** -0.5, 0.125, ((0, 16), (1, 2))),
        "w_out": bell_draw(arg_keys[9], (QUERY_HEADS * HEAD_SIZE, MODEL_WIDTH), (QUERY_HEADS * HEAD_SIZE // 16) ** -0.5, 0.5, ((0, 32),)),
        "ffn_gain": jnp.clip(1.0 + 0.1 * jax.random.normal(arg_keys[10], (MODEL_WIDTH,), jnp.float32), 0.5, 1.5),
        "w_gate": bell_draw(arg_keys[11], (MODEL_WIDTH, FF), MODEL_WIDTH ** -0.5, 0.125, ((0, 16), (1, 2))),
        "w_up": bell_draw(arg_keys[12], (MODEL_WIDTH, FF), MODEL_WIDTH ** -0.5, 0.125, ((0, 16), (1, 2))),
        "w_down": bell_draw(arg_keys[13], (FF, MODEL_WIDTH), FF ** -0.5, 0.0625, ((0, 32),)),
    }


EPS = 1e-05
ROPE_BASE = 1000000.0
MASKED = -1e+30
HIGHEST = lax.Precision.HIGHEST

@jax.custom_vjp
def lowered_forward(v):
    return lax.optimization_barrier(v.astype(jnp.bfloat16)).astype(jnp.float32)

@jax.custom_vjp
def lowered_backward(v):
    return v

def low_keep(v):
    return (lowered_forward(v), None)

def low_pass(kept, grad):
    return (grad,)

def back_keep(v):
    return (v, None)

def back_low(kept, grad):
    return (lowered_forward(grad),)
lowered_forward.defvjp(low_keep, low_pass)
lowered_backward.defvjp(back_keep, back_low)

def rms_scale(values, gain):
    return values * lax.rsqrt(lax.optimization_barrier(jnp.mean(values * values, axis=-1, keepdims=True)) + EPS) * gain

def angles(positions, head_dim):
    half_dim = head_dim // 2
    freq = jnp.exp(jnp.arange(half_dim, dtype=jnp.float32) * (-2.0 * math.log(ROPE_BASE) / head_dim))
    turned = positions.astype(jnp.float32)[:, None] * freq[None, :]
    return (jnp.cos(turned)[:, None, :], jnp.sin(turned)[:, None, :])

def rotate(values, cosine, sine_table):
    half_dim = values.shape[-1] // 2
    first_half = values[..., :half_dim]
    second_half = values[..., half_dim:]
    return jnp.concatenate([first_half * cosine - second_half * sine_table, second_half * cosine + first_half * sine_table], axis=-1)

def matrix_product(left, right):
    return jnp.dot(left, right, precision=HIGHEST)

def attend(packed):
    query_slot, k_slot, v_slot, slot_length = packed
    score_scale = 1.0 / math.sqrt(HEAD_SIZE)
    query_group = query_slot.reshape(SLOT_TOKENS, KEY_VALUE_HEADS, QUERY_HEADS // KEY_VALUE_HEADS, HEAD_SIZE)
    scores = jnp.einsum('ihgd,jhd->hgij', query_group, k_slot, precision=HIGHEST) * score_scale
    scores = lowered_backward(scores)
    here = jnp.arange(SLOT_TOKENS, dtype=jnp.int32)
    allowed = (here[None, :] <= here[:, None]) & (here[None, :] < slot_length)
    scores = jnp.where(allowed, scores, MASKED)
    probs = lowered_forward(jax.nn.softmax(scores, axis=-1))
    return jnp.einsum('hgij,jhd->ihgd', probs, v_slot, precision=HIGHEST).reshape(SLOT_TOKENS, QUERY_HEADS, HEAD_SIZE)

def forward(lengths, inputs, attn_gain, query_gain, key_gain, w_query, key_weight_matrix, value_weight_matrix, w_out, ffn_gain, w_gate, w_up, w_down):
    hidden_state = lowered_forward(rms_scale(inputs, attn_gain))
    q_proj = lowered_backward(matrix_product(hidden_state, w_query)).reshape(SLOT_COUNT, SLOT_TOKENS, QUERY_HEADS, HEAD_SIZE)
    key_projected = lowered_backward(matrix_product(hidden_state, key_weight_matrix)).reshape(SLOT_COUNT, SLOT_TOKENS, KEY_VALUE_HEADS, HEAD_SIZE)
    value_projected = lowered_forward(lowered_backward(matrix_product(hidden_state, value_weight_matrix))).reshape(SLOT_COUNT, SLOT_TOKENS, KEY_VALUE_HEADS, HEAD_SIZE)
    cosine, sine_table = angles(jnp.arange(SLOT_TOKENS, dtype=jnp.int32), HEAD_SIZE)
    q_low = lowered_forward(rotate(rms_scale(q_proj, query_gain), cosine, sine_table))
    k_low = lowered_forward(rotate(rms_scale(key_projected, key_gain), cosine, sine_table))
    attended = lax.map(jax.checkpoint(attend), (q_low, k_low, value_projected, lengths))
    o_low = lowered_forward(lowered_backward(attended.reshape(TOKENS, QUERY_HEADS * HEAD_SIZE)))
    h_one = inputs + lowered_backward(matrix_product(o_low, w_out))
    hidden_two = lowered_forward(rms_scale(h_one, ffn_gain))
    gate = lowered_backward(matrix_product(hidden_two, w_gate))
    up_proj = lowered_backward(matrix_product(hidden_two, w_up))
    act = lowered_forward(jax.nn.silu(gate) * up_proj)
    return h_one + lowered_backward(matrix_product(act, w_down))

def reference(tokens, cotangent, lengths, attn_gain, query_gain, key_gain, w_query, key_weight_matrix, value_weight_matrix, w_out, ffn_gain, w_gate, w_up, w_down):
    inputs = tokens.astype(jnp.float32)
    valid_rows = (jnp.arange(SLOT_TOKENS, dtype=jnp.int32)[None, :] < lengths[:, None]).astype(jnp.float32).reshape(TOKENS, 1)
    output, pull_back = jax.vjp(functools.partial(forward, lengths), inputs, attn_gain, query_gain, key_gain, w_query.astype(jnp.float32), key_weight_matrix.astype(jnp.float32), value_weight_matrix.astype(jnp.float32), w_out.astype(jnp.float32), ffn_gain, w_gate.astype(jnp.float32), w_up.astype(jnp.float32), w_down.astype(jnp.float32))
    g_input, g_attn, g_query, g_key, g_wq, g_wk, g_wv, g_wo, g_ffn, g_wg, g_wu, g_wd = pull_back(cotangent.astype(jnp.float32) * valid_rows)
    return (output.astype(jnp.bfloat16), g_input, g_attn, g_query, g_key, g_wq, g_wk, g_wv, g_wo, g_ffn, g_wg, g_wu, g_wd)
```

```python
import math

import jax
import jax.numpy as jnp
from jax import lax
from jax.experimental import pallas as pl
from jax.experimental.pallas import tpu as pltpu
from jax.sharding import PartitionSpec as P

EPS = 1e-05
ROPE_BASE = 1000000.0
MASKED = -1e30
LINE = 4
BF = jnp.bfloat16
F32 = jnp.float32


def rms_scale(values, gain):
    return values * lax.rsqrt(jnp.mean(values * values, axis=-1, keepdims=True) + EPS) * gain


def angles(positions, head_dim):
    half_dim = head_dim // 2
    freq = jnp.exp(
        jnp.arange(half_dim, dtype=jnp.float32) * (-2.0 * math.log(ROPE_BASE) / head_dim)
    )
    turned = positions.astype(jnp.float32)[:, None] * freq[None, :]
    return (jnp.cos(turned)[:, None, :], jnp.sin(turned)[:, None, :])


def rotate(values, cosine, sine_table):
    half_dim = values.shape[-1] // 2
    first_half = values[..., :half_dim]
    second_half = values[..., half_dim:]
    return jnp.concatenate(
        [
            first_half * cosine - second_half * sine_table,
            second_half * cosine + first_half * sine_table,
        ],
        axis=-1,
    )


def mm(left, right):
    return jnp.dot(left, right, preferred_element_type=F32)


def mm_nt(left, right):
    return lax.dot_general(left, right, (((1,), (1,)), ((), ())), preferred_element_type=F32)


def mm_tn(left, right):
    return lax.dot_general(left, right, (((0,), (0,)), ((), ())), preferred_element_type=F32)


def after(done, *values):
    held, _ = lax.optimization_barrier((values, done))
    return held if len(held) > 1 else held[0]


def slot_place(t, k):
    if k == 0:
        return t
    if k == 1:
        return jnp.where(t == 0, 1, t - 1)
    if k == 2:
        return (t + 2) % LINE
    return jnp.where(t == 3, 0, jnp.where(t == 1, 2, 3))


def coordinates():
    n = lax.axis_size("dp")
    inner = n // LINE
    here = lax.axis_index("dp")
    return here // inner, (here % inner) // 2, here % 2, lax.axis_index("tensor")


def place(blocks, spots, shape):
    listed = spots(0, 0, 0, 0)

    def kernel(*refs):
        sources = refs[: len(blocks)]
        out, held, sem, out_sem = refs[len(blocks) :]
        copies = []
        for k, (b, row, col, rows, cols, to_row, to_col) in enumerate(spots(*coordinates())):
            copies.append(
                pltpu.make_async_copy(
                    sources[b].at[pl.ds(row, rows), pl.ds(col, cols)],
                    held.at[
                        pl.ds(pl.multiple_of(to_row, rows), rows),
                        pl.ds(pl.multiple_of(to_col, cols), cols),
                    ],
                    sem.at[k],
                )
            )
        for copy in copies:
            copy.start()
        for copy in copies:
            copy.wait()
        last = pltpu.make_async_copy(held, out, out_sem)
        last.start()
        last.wait()

    item = blocks[0].dtype.itemsize
    moved = sum(2 * rows * cols * item for _, _, _, rows, cols, _, _ in listed)
    return pl.pallas_call(
        kernel,
        out_shape=jax.ShapeDtypeStruct(shape, blocks[0].dtype),
        in_specs=[pl.BlockSpec(memory_space=pl.ANY)] * len(blocks),
        out_specs=pl.BlockSpec(memory_space=pl.ANY),
        scratch_shapes=[
            pltpu.VMEM(shape, blocks[0].dtype),
            pltpu.SemaphoreType.DMA((len(listed),)),
            pltpu.SemaphoreType.DMA,
        ],
        compiler_params=pltpu.CompilerParams(vmem_limit_bytes=moved // 2 + (4 << 20)),
        cost_estimate=pl.CostEstimate(flops=0, bytes_accessed=moved, transcendentals=0),
    )(*blocks)


class Links:
    def __init__(self, n):
        self.n = n
        self.inner = n // LINE
        self.side = self.inner // 2
        self.side_bits = self.side.bit_length() - 1
        self.t, self.j, self.c, self.x = coordinates()

    def core(self, value):
        return lax.ppermute(value, "dp", [(i, i ^ 1) for i in range(self.n)])

    def over(self, value, bit):
        return lax.ppermute(value, "dp", [(i, i ^ (2 << bit)) for i in range(self.n)])

    def cross(self, value):
        return lax.ppermute(value, "tensor", [(0, 1), (1, 0)])

    def along(self, value, moves):
        pairs = [
            (a * self.inner + i, b * self.inner + i) for a, b in moves for i in range(self.inner)
        ]
        return lax.ppermute(value, "dp", pairs)

    def right(self, value, senders):
        return self.along(value, [(a, a + 1) for a in senders])

    def left(self, value, senders):
        return self.along(value, [(a, a - 1) for a in senders])

    def turn(self, value, shift):
        return self.along(value, [(a, (a + shift) % LINE) for a in range(LINE)])

    def line_gather(self, value):
        t = self.t
        r1 = self.right(value, (0, 1, 2))
        l1 = self.left(value, (1, 2, 3))
        r2 = self.right(r1, (1, 2))
        l2 = self.left(l1, (1, 2))
        r3 = self.right(r2, (2,))
        l3 = self.left(l2, (1,))
        return (
            value,
            jnp.where(t == 0, l1, r1),
            jnp.where(t < 2, l2, r2),
            jnp.where(t == 0, l3, jnp.where(t == 3, r3, l1)),
        )

    def line_scatter(self, parts):
        t = self.t
        p0, p1, p2, p3 = parts
        first = p3.astype(BF)
        r1 = self.right(first, (0,))
        l1 = self.left(first, (3,))
        second = (p2 + r1.astype(F32) + l1.astype(F32)).astype(BF)
        r2 = self.right(second, (0, 1))
        l2 = self.left(second, (2, 3))
        r3 = self.right((jnp.where(t == 0, p1, p3) + r2.astype(F32)).astype(BF), (0, 1, 2))
        l3 = self.left((p1 + l2.astype(F32)).astype(BF), (1, 2, 3))
        return p0 + r3.astype(F32) + l3.astype(F32)

    def line_send(self, parts):
        p0, p1, p2, p3 = parts
        first, second, third = p1.astype(BF), p2.astype(BF), p3.astype(BF)
        got = [
            self.left(first, (1, 2, 3)),
            self.right(first, (0,)),
            self.turn(second, 2),
            self.along(third, ((0, 3), (3, 0))),
            self.right(third, (1, 2)),
        ]
        return p0 + sum(g.astype(F32) for g in got)

    def side_all(self, value):
        blocks = [value]
        for bit in range(self.side_bits):
            blocks += [self.over(block, bit) for block in blocks]
        return blocks

    def side_sum(self, blocks):
        for bit in reversed(range(self.side_bits)):
            width = 1 << bit
            blocks = [
                a.astype(F32) + self.over(b.astype(BF), bit).astype(F32)
                for a, b in zip(blocks[:width], blocks[width:])
            ]
        return blocks[0]

    def pair_order(self, mine, other, where):
        low = jnp.where(where == 0, mine, other)
        high = jnp.where(where == 0, other, mine)
        return jnp.concatenate([low, high], 0)

    def pick(self, value, index, axis):
        return lax.dynamic_index_in_dim(value, index, axis, keepdims=False)

    def cross_sum(self, value, axis):
        kept = self.pick(value, self.x, axis)
        sent = self.pick(value, 1 - self.x, axis)
        return kept.astype(F32) + self.cross(sent.astype(BF)).astype(F32)

    def gather_rows(self, blocks):
        rows, cols = blocks[0].shape
        pieces, where = [], []
        for k, block in enumerate(blocks):
            for r, piece in enumerate(self.side_all(block)):
                pieces += [piece, self.core(piece)]
                where += [(k, r, 0), (k, r, 1)]

        def spots(t, j, c, x):
            return [
                (
                    i, 0, 0, rows, cols,
                    (((slot_place(t, k) * self.side) + (j ^ r)) * 2 + (c ^ s)) * rows, 0,
                )
                for i, (k, r, s) in enumerate(where)
            ]

        return place(pieces, spots, (self.n * rows, cols))

    def sum_rows(self, value):
        rows, cols = value.shape[0] // self.n, value.shape[1]
        parts = value.reshape(LINE, self.side, 2, rows, cols)
        kept = self.pick(parts, self.c, 2).astype(F32)
        parts = kept + self.core(self.pick(parts, 1 - self.c, 2)).astype(F32)
        parts = parts.astype(BF)
        parts = self.side_sum([self.pick(parts, self.j ^ r, 1) for r in range(self.side)])
        return self.line_scatter(
            [self.pick(parts, slot_place(self.t, k), 0).astype(F32) for k in range(LINE)]
        )

    def total(self, value):
        value = value + self.core(value)
        for bit in range(self.side_bits):
            value = value + self.over(value, bit)
        value = value + self.cross(value)
        value = value + self.along(value, ((0, 1), (1, 0), (2, 3), (3, 2)))
        return value + self.turn(value, 2)


def make_body(n):
    def body(
        tokens,
        cotangent,
        lengths,
        attn_gain,
        query_gain,
        key_gain,
        w_query,
        key_weight_matrix,
        value_weight_matrix,
        w_out,
        ffn_gain,
        w_gate,
        w_up,
        w_down,
    ):
        net = Links(n)
        t, j, c, x = net.t, net.j, net.c, net.x
        row_count, width = tokens.shape
        half = row_count // 2
        head_dim = query_gain.shape[0]
        q_cols = w_query.shape[1]
        k_cols = key_weight_matrix.shape[1]
        q_heads = q_cols // head_dim
        k_heads = k_cols // head_dim
        group_size = q_heads // k_heads
        score_scale = 1.0 / math.sqrt(head_dim)
        dp_index = lax.axis_index("dp")
        slot_length = lengths[dp_index]

        depth = w_gate.shape[0]
        piece = w_down.shape[0]
        side = net.side
        strip = side * piece
        qkv_own = jnp.concatenate([w_query, key_weight_matrix, value_weight_matrix], axis=1)
        qkv_blocks = net.line_gather(qkv_own)
        qkv_full = net.gather_rows(qkv_blocks)
        wo_blocks = net.line_gather(after(qkv_blocks, w_out))
        wo_full = net.gather_rows(wo_blocks)

        strips = []
        for weight in (w_gate, w_up):
            cols = weight.reshape(depth, LINE, side, 2, piece)
            strips.append(
                [
                    net.pick(cols, place_c, 3).transpose(1, 0, 2, 3).reshape(LINE, depth, strip)
                    for place_c in (c, 1 - c)
                ]
            )
        kept = jnp.stack([strips[0][0], strips[1][0]], 1)
        sent = jnp.stack([strips[0][1], strips[1][1]], 1)
        pairs = jnp.stack([kept, net.core(sent)], 1)
        pairs = after(qkv_blocks, pairs)
        pieces, where = [], []
        turned = []
        for shift in range(LINE):
            block = net.pick(pairs, (t + shift) % LINE, 0)
            block = block if shift == 0 else net.turn(block, shift)
            turned.append(block)
            gate_part = block[:, 0].reshape(2 * depth, strip)
            up_part = block[:, 1].reshape(2 * depth, strip)
            for kind, over_x in ((0, (gate_part, net.cross(gate_part))), (1, (up_part,))):
                for at_x, part in enumerate(over_x):
                    for r, got in enumerate(net.side_all(part)):
                        pieces.append(got)
                        where.append((kind, shift, r, at_x))
                        if kind == 1:
                            pieces.append(net.cross(got))
                            where.append((kind, shift, r, 1))

        def unit_weight(wanted):
            chosen = [(p, w) for p, w in zip(pieces, where) if w[0] == wanted]

            def spots(t, j, c, x):
                return [
                    (
                        i, s * depth, 0, depth, strip,
                        ((((t - shift) % LINE) * side + (j ^ r)) * 2 + (c ^ s)) * depth,
                        (x ^ at_x) * strip,
                    )
                    for i, (_, (_, shift, r, at_x)) in enumerate(chosen)
                    for s in range(2)
                ]

            return place([p for p, _ in chosen], spots, (width, 2 * strip))

        wg = unit_weight(0)
        wu = unit_weight(1)
        down_pieces = []
        for got in net.side_all(w_down):
            down_pieces += [got, net.cross(got)]

        def down_spots(t, j, c, x):
            return [
                (2 * r + s, 0, 0, piece, width, ((x ^ s) * side + (j ^ r)) * piece, 0)
                for r in range(side)
                for s in range(2)
            ]

        wd = place(down_pieces, down_spots, (2 * strip, width))

        positions = jnp.arange(row_count, dtype=jnp.int32)
        start = x * half
        half_positions = start + jnp.arange(half, dtype=jnp.int32)
        half_valid = (half_positions < slot_length)[:, None]
        grad_half = lax.dynamic_slice_in_dim(cotangent, start, half, 0)
        grad_half = jnp.where(half_valid, grad_half, jnp.zeros_like(grad_half))
        grad_blocks = [
            jnp.concatenate([block, net.core(block)], axis=0)
            for block in net.line_gather(after(turned, grad_half))
        ]

        allowed = (positions[None, :] <= positions[:, None]) & (positions[None, :] < slot_length)
        cosine, sine_table = angles(positions, head_dim)
        inputs = tokens.astype(F32)
        hidden_state = rms_scale(inputs, attn_gain).astype(BF)
        qkv = mm(hidden_state, qkv_full)
        q_proj = qkv[:, :q_cols]
        key_projected = qkv[:, q_cols : q_cols + k_cols]
        value_projected = qkv[:, q_cols + k_cols :]

        def prepare(q_vals, k_vals, q_gain, k_gain):
            q_norm = rms_scale(q_vals.reshape(row_count, q_heads, head_dim), q_gain)
            k_norm = rms_scale(k_vals.reshape(row_count, k_heads, head_dim), k_gain)
            return (rotate(q_norm, cosine, sine_table), rotate(k_norm, cosine, sine_table))

        (q_rot, k_rot), prep_back = jax.vjp(prepare, q_proj, key_projected, query_gain, key_gain)
        q_low = q_rot.astype(BF)
        k_low = k_rot.astype(BF)
        v_low = value_projected.astype(BF)
        q_grouped = q_low.reshape(row_count, k_heads, group_size, head_dim).transpose(1, 2, 0, 3)
        k_grouped = k_low.transpose(1, 0, 2)
        v_grouped = v_low.reshape(row_count, k_heads, head_dim).transpose(1, 0, 2)

        def scores_of(q_one, k_one):
            scores = (
                jnp.einsum("gid,jd->gij", q_one, k_one, preferred_element_type=F32) * score_scale
            )
            return jnp.where(allowed[None], scores, MASKED)

        def attend(packed):
            q_one, k_one, v_one = packed
            scores = scores_of(q_one, k_one)
            row_max = jnp.max(scores, axis=-1, keepdims=True)
            exp_scores = jnp.exp(scores - row_max)
            row_total = jnp.sum(exp_scores, axis=-1, keepdims=True)
            probs = (exp_scores / row_total).astype(BF)
            attended = jnp.einsum("gij,jd->gid", probs, v_one, preferred_element_type=F32)
            return (attended, row_max[..., 0] + jnp.log(row_total[..., 0]))

        attended, log_totals = lax.map(attend, (q_grouped, k_grouped, v_grouped))
        o_low = (
            attended.transpose(2, 0, 1, 3).reshape(row_count, q_heads * head_dim).astype(BF)
        )
        attn_part = mm(o_low, wo_full).reshape(2, half, width)
        input_half = lax.dynamic_slice_in_dim(inputs, start, half, 0)
        h_one = input_half + net.cross_sum(attn_part, 0)
        hidden_two = rms_scale(h_one, ffn_gain).astype(BF)

        hidden_blocks = [
            jnp.concatenate([block, net.core(block)], axis=0)
            for block in net.line_gather(hidden_two)
        ]

        def core_sum(value):
            low = value[half:].astype(BF)
            return value[:half] + net.core(low).astype(F32)

        out_parts, grad_parts, acts, grad_gates, grad_ups = [], [], [], [], []
        for hidden, grad in zip(hidden_blocks, grad_blocks):
            gate = mm(hidden, wg)
            up_proj = mm(hidden, wu)
            sigmoid_gate = jax.nn.sigmoid(gate)
            silu_gate = gate * sigmoid_gate
            act = (silu_gate * up_proj).astype(BF)
            out_parts.append(core_sum(mm(act, wd)))
            grad_act = mm_nt(grad, wd)
            silu_slope = sigmoid_gate * (1.0 + gate * (1.0 - sigmoid_gate))
            grad_gate = (grad_act * up_proj * silu_slope).astype(BF)
            grad_up = (grad_act * silu_gate).astype(BF)
            grad_parts.append(core_sum(mm_nt(grad_gate, wg) + mm_nt(grad_up, wu)))
            acts.append(act)
            grad_gates.append(grad_gate)
            grad_ups.append(grad_up)

        grad_hidden_two = net.line_send(grad_parts)
        out_parts = after(grad_hidden_two, *out_parts)
        layer_half = (h_one + net.line_scatter(out_parts)).astype(BF)
        layer_out = net.pair_order(layer_half, net.cross(layer_half), x)
        norm_two_back = jax.vjp(rms_scale, h_one, ffn_gain)[1]
        grad_h_part, g_ffn_part = norm_two_back(grad_hidden_two)
        grad_h_one = grad_half.astype(F32) + grad_h_part
        grad_attn_half = grad_h_one.astype(BF)
        grad_attn_low = net.pair_order(grad_attn_half, net.cross(grad_attn_half), x)

        act_all = jnp.concatenate(acts, 0)
        hidden_all = jnp.concatenate(hidden_blocks, 0)
        grad_all = jnp.concatenate(grad_blocks, 0)
        g_gate = mm_tn(hidden_all, jnp.concatenate(grad_gates, 0)).astype(BF)
        g_up = mm_tn(hidden_all, jnp.concatenate(grad_ups, 0)).astype(BF)
        g_down = mm_tn(act_all, grad_all).astype(BF)

        def home_units(value):
            rows = value.reshape(LINE, 2 * depth, strip)
            blocks = []
            for shift in range(LINE):
                block = net.pick(rows, (t + shift) % LINE, 0)
                block = block if shift == 0 else net.turn(block, shift)
                block = block.reshape(2, depth, strip)
                blocks.append(net.pick(block, c, 0))
                blocks.append(net.core(net.pick(block, 1 - c, 0)))
            if piece % 128:
                stacked = jnp.stack(blocks).reshape(LINE, 2, depth, side, piece)
                order_t = (t - jnp.arange(LINE)) % LINE
                stacked = jnp.take(stacked, order_t, axis=0)
                stacked = jnp.take(stacked, c ^ jnp.arange(2), axis=1)
                return stacked.transpose(2, 0, 3, 1, 4).reshape(depth, LINE * 2 * strip)

            def spots(t, j, c, x):
                return [
                    (
                        2 * shift + s, 0, r * piece, depth, piece, 0,
                        ((((t - shift) % LINE) * side + r) * 2 + (c ^ s)) * piece,
                    )
                    for shift in range(LINE)
                    for s in range(2)
                    for r in range(side)
                ]

            return place(blocks, spots, (depth, LINE * 2 * strip))

        def side_rows(value):
            rows = value.reshape(LINE, side, 2 * depth, value.shape[1])
            return [net.pick(rows, j ^ r, 1) for r in range(side)]

        def cross_cols(value):
            kept = lax.dynamic_slice_in_dim(value, x * strip, strip, value.ndim - 1)
            sent = lax.dynamic_slice_in_dim(value, (1 - x) * strip, strip, value.ndim - 1)
            return kept.astype(F32) + net.cross(sent.astype(BF)).astype(F32)

        gate_sum = net.side_sum(side_rows(cross_cols(g_gate).astype(BF))).astype(BF)
        up_sum = cross_cols(net.side_sum(side_rows(g_up))).astype(BF)
        g_gate_out = home_units(gate_sum).astype(F32)
        g_up_out = home_units(up_sum).astype(F32)
        down_sum = net.cross_sum(g_down.reshape(2, side, piece, width), 0).astype(BF)
        g_down_out = net.side_sum([net.pick(down_sum, j ^ r, 0) for r in range(side)])

        g_out = mm_tn(o_low, grad_attn_low).astype(BF)
        grad_o_low = mm_nt(grad_attn_low, wo_full).astype(BF)
        grad_o_grouped = grad_o_low.reshape(row_count, k_heads, group_size, head_dim).transpose(
            1, 2, 0, 3
        )

        def attend_back(packed):
            q_one, k_one, v_one, total_one, grad_one = packed
            scores = scores_of(q_one, k_one)
            probs = jnp.exp(scores - total_one[..., None])
            grad_probs = jnp.einsum("gid,jd->gij", grad_one, v_one, preferred_element_type=F32)
            grad_scores = (
                probs * (grad_probs - jnp.sum(probs * grad_probs, axis=-1, keepdims=True))
            ).astype(BF)
            grad_query = (
                jnp.einsum("gij,jd->gid", grad_scores, k_one, preferred_element_type=F32)
                * score_scale
            )
            grad_keys = (
                jnp.einsum("gij,gid->jd", grad_scores, q_one, preferred_element_type=F32)
                * score_scale
            )
            grad_values = jnp.einsum(
                "gij,gid->jd", probs.astype(BF), grad_one, preferred_element_type=F32
            )
            return (grad_query, grad_keys, grad_values)

        grad_q_grouped, grad_k_grouped, grad_v_grouped = lax.map(
            attend_back, (q_grouped, k_grouped, v_grouped, log_totals, grad_o_grouped)
        )
        grad_q_rows = grad_q_grouped.transpose(2, 0, 1, 3).reshape(row_count, q_heads, head_dim)
        grad_k_total = grad_k_grouped.transpose(1, 0, 2)
        grad_v_rows = grad_v_grouped.transpose(1, 0, 2).reshape(row_count, k_heads * head_dim)
        grad_q_proj, grad_k_proj, g_query_part, g_key_part = prep_back((grad_q_rows, grad_k_total))
        grad_qkv = jnp.concatenate(
            [grad_q_proj.astype(BF), grad_k_proj.astype(BF), grad_v_rows.astype(BF)], axis=1
        )
        g_qkv = mm_tn(hidden_state, grad_qkv).astype(BF)
        g_out_out = net.sum_rows(g_out)
        g_qkv_out = net.sum_rows(g_qkv)
        grad_hidden = mm_nt(grad_qkv, qkv_full).reshape(2, half, width)
        grad_hidden_half = net.cross_sum(grad_hidden, 0)
        norm_one_back = jax.vjp(rms_scale, input_half, attn_gain)[1]
        grad_in_half, g_attn_part = norm_one_back(grad_hidden_half)
        input_grad_half = (grad_h_one + grad_in_half).astype(BF)
        input_grad = net.pair_order(input_grad_half, net.cross(input_grad_half), x).astype(F32)
        small = jnp.concatenate([g_attn_part, g_ffn_part, g_query_part, g_key_part])
        small = net.total(small)
        return (
            layer_out,
            input_grad,
            small[:width],
            small[2 * width : 2 * width + head_dim],
            small[2 * width + head_dim :],
            g_qkv_out[:, :q_cols],
            g_qkv_out[:, q_cols : q_cols + k_cols],
            g_qkv_out[:, q_cols + k_cols :],
            g_out_out,
            small[width : 2 * width],
            g_gate_out,
            g_up_out,
            g_down_out,
        )

    return body


def solution(mesh):
    placed = (
        P("dp", None),
        P("dp", None),
        P(),
        P(),
        P(),
        P(),
        P("dp", "tensor"),
        P("dp", "tensor"),
        P("dp", "tensor"),
        P(("tensor", "dp"), None),
        P(),
        P("dp", "tensor"),
        P("dp", "tensor"),
        P(("tensor", "dp"), None),
    )
    return jax.shard_map(
        make_body(mesh.shape["dp"]),
        mesh=mesh,
        in_specs=placed,
        out_specs=(
            P("dp", None),
            P("dp", None),
            P(),
            P(),
            P(),
            P("dp", "tensor"),
            P("dp", "tensor"),
            P("dp", "tensor"),
            P(("tensor", "dp"), None),
            P(),
            P("dp", "tensor"),
            P("dp", "tensor"),
            P(("tensor", "dp"), None),
        ),
        check_vma=False,
    )
```

```python
import functools
import math

import jax
import jax.numpy as jnp
from jax import lax
from jax.experimental import pallas as pl
from jax.experimental.pallas import tpu as pltpu
from jax.sharding import PartitionSpec as P

EPS = 1e-05
ROPE_BASE = 1000000.0
MASKED = -1e30
LINE = 4
BF = jnp.bfloat16
F32 = jnp.float32


def rms_scale(values, gain):
    return values * lax.rsqrt(jnp.mean(values * values, axis=-1, keepdims=True) + EPS) * gain


def angle_tables(count, head_dim, lanes):
    half_dim = head_dim // 2
    freq = jnp.exp(
        jnp.arange(half_dim, dtype=jnp.float32) * (-2.0 * math.log(ROPE_BASE) / head_dim)
    )
    turned = jnp.arange(count, dtype=jnp.int32).astype(jnp.float32)[:, None] * freq[None, :]
    cosine, sine = jnp.cos(turned), jnp.sin(turned)
    repeats = lanes // head_dim
    return (
        jnp.tile(jnp.concatenate([cosine, cosine], 1), (1, repeats)),
        jnp.tile(jnp.concatenate([-sine, sine], 1), (1, repeats)),
    )


LANES = 128
HEAD = LANES // 2


def low_lanes(shape):
    return lax.broadcasted_iota(jnp.int32, shape, 1) < HEAD


def per_head(values):
    low = low_lanes(values.shape)
    first = jnp.sum(jnp.where(low, values, 0.0), axis=1, keepdims=True)
    second = jnp.sum(jnp.where(low, 0.0, values), axis=1, keepdims=True)
    return jnp.where(low, first, second) * (1.0 / HEAD)


def halves_swapped(values):
    lane = lax.broadcasted_iota(jnp.int32, values.shape, 1)
    return jnp.where(
        lane % HEAD < HEAD // 2,
        pltpu.roll(values, LANES - HEAD // 2, 1),
        pltpu.roll(values, HEAD // 2, 1),
    )


def head_norm(values):
    scale = lax.rsqrt(per_head(values * values) + EPS)
    return values * scale, scale


def head_turn(values, cosine, sine):
    return values * cosine + halves_swapped(values) * sine


def head_back(grad, normed, scale, gain, cosine, sine):
    grad = grad * cosine - halves_swapped(grad) * sine
    gain_grad = jnp.sum(grad * normed, axis=0, keepdims=True)
    grad = grad * gain
    return scale * (grad - normed * per_head(grad * normed)), gain_grad


def one_head(pair, second):
    low = low_lanes(pair.shape)
    return jnp.where(low == jnp.logical_not(second), pair, pltpu.roll(pair, HEAD, 1))


def two_rows(slab):
    low = low_lanes(slab.shape)
    return jnp.concatenate([jnp.where(low, slab, 0.0), jnp.where(low, 0.0, slab)], 0).astype(BF)


def allowed_mask(block, first_row, columns, length):
    row = lax.broadcasted_iota(jnp.int32, (2 * block, columns), 0) % block + first_row
    col = lax.broadcasted_iota(jnp.int32, (2 * block, columns), 1)
    return (col <= row) & (col < length)


def attend_kernel(block, scale, length, q, k, v, cosine, sine, q_gain, k_gain, out, totals):
    second = pl.program_id(0) % 2 == 1
    rows = q.shape[0]
    cos, sin = cosine[...], sine[...]
    keys = one_head(head_turn(head_norm(k[...])[0] * k_gain[...], cos, sin), second).astype(BF)
    vals = one_head(v[...], second).astype(BF)
    lane = lax.broadcasted_iota(jnp.int32, (block, LANES), 1)
    for first in range(0, rows, block):
        span = pl.ds(first, block)
        seen = first + block
        allowed = allowed_mask(block, first, seen, length[0])
        kept = jnp.zeros((block, LANES), F32)
        for slab in range(q.shape[1] // LANES):
            cols = pl.ds(slab * LANES, LANES)
            turned = head_turn(
                head_norm(q[span, cols])[0] * q_gain[...], cosine[span, :], sine[span, :]
            )
            scores = mm_nt(two_rows(turned), keys[:seen]) * scale
            scores = jnp.where(allowed, scores, MASKED)
            top = jnp.max(scores, axis=1, keepdims=True)
            probs = jnp.exp(scores - top)
            total = jnp.sum(probs, axis=1, keepdims=True)
            probs = (probs * (1.0 / total)).astype(BF)
            both = mm(probs, vals[:seen])
            out[span, cols] = jnp.where(low_lanes((block, LANES)), both[:block], both[block:]).astype(
                BF
            )
            log_total = top + jnp.log(total)
            kept = jnp.where(lane == 2 * slab, log_total[:block], kept)
            kept = jnp.where(lane == 2 * slab + 1, log_total[block:], kept)
        totals[span, :] = kept


def attend_back_kernel(
    block, scale, length, q, k, v, cosine, sine, q_gain, k_gain, totals, grad_out,
    grad_q, grad_k, grad_v, q_gain_grad, k_gain_grad, keys_sum, vals_sum,
):
    step = pl.program_id(0)
    second = step % 2 == 1
    rows = q.shape[0]
    cos, sin = cosine[...], sine[...]
    k_normed, k_scale = head_norm(k[...])
    keys = one_head(head_turn(k_normed * k_gain[...], cos, sin), second).astype(BF)
    vals = one_head(v[...], second).astype(BF)
    lane = lax.broadcasted_iota(jnp.int32, (block, LANES), 1)
    keys_sum[...] = jnp.zeros_like(keys_sum)
    vals_sum[...] = jnp.zeros_like(vals_sum)

    @pl.when(step == 0)
    def _():
        q_gain_grad[...] = jnp.zeros_like(q_gain_grad)
        k_gain_grad[...] = jnp.zeros_like(k_gain_grad)

    for first in range(0, rows, block):
        span = pl.ds(first, block)
        seen = first + block
        allowed = allowed_mask(block, first, seen, length[0])
        kept = totals[span, :]
        for slab in range(q.shape[1] // LANES):
            cols = pl.ds(slab * LANES, LANES)
            q_normed, q_scale = head_norm(q[span, cols])
            turned = two_rows(head_turn(q_normed * q_gain[...], cosine[span, :], sine[span, :]))
            log_total = jnp.concatenate(
                [
                    jnp.sum(jnp.where(lane == 2 * slab + i, kept, 0.0), axis=1, keepdims=True)
                    for i in range(2)
                ],
                0,
            )
            scores = mm_nt(turned, keys[:seen]) * scale
            probs = jnp.exp(jnp.where(allowed, scores, MASKED) - log_total)
            grad_rows = two_rows(grad_out[span, cols].astype(F32))
            grad_probs = mm_nt(grad_rows, vals[:seen])
            drop = jnp.sum(probs * grad_probs, axis=1, keepdims=True)
            grad_scores = (probs * (grad_probs - drop)).astype(BF)
            both = mm(grad_scores, keys[:seen]) * scale
            grad_turned = jnp.where(low_lanes((block, LANES)), both[:block], both[block:])
            grad_proj, gain_part = head_back(
                grad_turned, q_normed, q_scale, q_gain[...], cosine[span, :], sine[span, :]
            )
            grad_q[span, cols] = grad_proj.astype(BF)
            q_gain_grad[...] += gain_part
            keys_sum[:seen] += mm_tn(grad_scores, turned)
            vals_sum[:seen] += mm_tn(probs.astype(BF), grad_rows)

    keys_grad = keys_sum[...] * scale
    keys_grad = keys_grad + pltpu.roll(keys_grad, HEAD, 1)
    vals_grad = vals_sum[...]
    vals_grad = vals_grad + pltpu.roll(vals_grad, HEAD, 1)
    grad_proj, gain_part = head_back(
        keys_grad,
        one_head(k_normed, second),
        one_head(k_scale, second),
        k_gain[...],
        cos,
        sin,
    )
    k_gain_grad[...] += gain_part * 0.5
    keep_low = low_lanes(grad_k.shape)

    @pl.when(step % 2 == 0)
    def _():
        grad_k[...] = grad_proj.astype(BF)
        grad_v[...] = vals_grad.astype(BF)

    @pl.when(step % 2 == 1)
    def _():
        grad_k[...] = jnp.where(keep_low, grad_k[...].astype(F32), grad_proj).astype(BF)
        grad_v[...] = jnp.where(keep_low, grad_v[...].astype(F32), vals_grad).astype(BF)


def attention_specs(rows, group, k_heads, q_cols):
    wide = group * HEAD
    k_first = q_cols // LANES
    v_first = k_first + k_heads * HEAD // LANES
    return [
        pl.BlockSpec(memory_space=pltpu.SMEM),
        pl.BlockSpec((rows, wide), lambda g: (0, g)),
        pl.BlockSpec((rows, LANES), lambda g: (0, k_first + g // 2)),
        pl.BlockSpec((rows, LANES), lambda g: (0, v_first + g // 2)),
        pl.BlockSpec((rows, LANES), lambda g: (0, 0)),
        pl.BlockSpec((rows, LANES), lambda g: (0, 0)),
        pl.BlockSpec((1, LANES), lambda g: (0, 0)),
        pl.BlockSpec((1, LANES), lambda g: (0, 0)),
    ]


def attend(length, qkv, tables, gains, q_cols, k_heads):
    rows = qkv.shape[0]
    group = q_cols // HEAD // k_heads
    block = rows // 2
    return pl.pallas_call(
        functools.partial(attend_kernel, block, 1.0 / math.sqrt(HEAD)),
        grid=(k_heads,),
        in_specs=attention_specs(rows, group, k_heads, q_cols),
        out_specs=[
            pl.BlockSpec((rows, group * HEAD), lambda g: (0, g)),
            pl.BlockSpec((rows, LANES), lambda g: (0, g)),
        ],
        out_shape=[
            jax.ShapeDtypeStruct((rows, q_cols), BF),
            jax.ShapeDtypeStruct((rows, k_heads * LANES), F32),
        ],
        compiler_params=pltpu.CompilerParams(vmem_limit_bytes=40 << 20),
        cost_estimate=pl.CostEstimate(
            flops=20 * rows * rows * q_cols, bytes_accessed=8 << 20, transcendentals=rows * rows
        ),
    )(length, qkv, qkv, qkv, *tables, *gains)


def attend_back(length, qkv, tables, gains, totals, grad_out, q_cols, k_heads):
    rows = qkv.shape[0]
    group = q_cols // HEAD // k_heads
    block = rows // 2
    return pl.pallas_call(
        functools.partial(attend_back_kernel, block, 1.0 / math.sqrt(HEAD)),
        grid=(k_heads,),
        in_specs=attention_specs(rows, group, k_heads, q_cols)
        + [
            pl.BlockSpec((rows, LANES), lambda g: (0, g)),
            pl.BlockSpec((rows, group * HEAD), lambda g: (0, g)),
        ],
        out_specs=[
            pl.BlockSpec((rows, group * HEAD), lambda g: (0, g)),
            pl.BlockSpec((rows, LANES), lambda g: (0, g // 2)),
            pl.BlockSpec((rows, LANES), lambda g: (0, g // 2)),
            pl.BlockSpec((1, LANES), lambda g: (0, 0)),
            pl.BlockSpec((1, LANES), lambda g: (0, 0)),
        ],
        out_shape=[
            jax.ShapeDtypeStruct((rows, q_cols), BF),
            jax.ShapeDtypeStruct((rows, k_heads * HEAD), BF),
            jax.ShapeDtypeStruct((rows, k_heads * HEAD), BF),
            jax.ShapeDtypeStruct((1, LANES), F32),
            jax.ShapeDtypeStruct((1, LANES), F32),
        ],
        scratch_shapes=[pltpu.VMEM((rows, LANES), F32), pltpu.VMEM((rows, LANES), F32)],
        compiler_params=pltpu.CompilerParams(vmem_limit_bytes=40 << 20),
        cost_estimate=pl.CostEstimate(
            flops=50 * rows * rows * q_cols, bytes_accessed=10 << 20, transcendentals=rows * rows
        ),
    )(length, qkv, qkv, qkv, *tables, *gains, totals, grad_out)


def mm(left, right):
    return jnp.dot(left, right, preferred_element_type=F32)


def mm_nt(left, right):
    return lax.dot_general(left, right, (((1,), (1,)), ((), ())), preferred_element_type=F32)


def mm_tn(left, right):
    return lax.dot_general(left, right, (((0,), (0,)), ((), ())), preferred_element_type=F32)


def after(done, *values):
    held, _ = lax.optimization_barrier((values, done))
    return held if len(held) > 1 else held[0]


def slot_place(t, k):
    if k == 0:
        return t
    if k == 1:
        return jnp.where(t == 0, 1, t - 1)
    if k == 2:
        return (t + 2) % LINE
    return jnp.where(t == 3, 0, jnp.where(t == 1, 2, 3))


def coordinates():
    n = lax.axis_size("dp")
    inner = n // LINE
    here = lax.axis_index("dp")
    return here // inner, (here % inner) // 2, here % 2, lax.axis_index("tensor")


def place(blocks, spots, shape):
    listed = spots(0, 0, 0, 0)

    def kernel(*refs):
        sources = refs[: len(blocks)]
        out, held, sem, out_sem = refs[len(blocks) :]
        copies = []
        for k, (b, row, col, rows, cols, to_row, to_col) in enumerate(spots(*coordinates())):
            copies.append(
                pltpu.make_async_copy(
                    sources[b].at[pl.ds(row, rows), pl.ds(col, cols)],
                    held.at[
                        pl.ds(pl.multiple_of(to_row, rows), rows),
                        pl.ds(pl.multiple_of(to_col, cols), cols),
                    ],
                    sem.at[k],
                )
            )
        for copy in copies:
            copy.start()
        for copy in copies:
            copy.wait()
        last = pltpu.make_async_copy(held, out, out_sem)
        last.start()
        last.wait()

    item = blocks[0].dtype.itemsize
    moved = sum(2 * rows * cols * item for _, _, _, rows, cols, _, _ in listed)
    return pl.pallas_call(
        kernel,
        out_shape=jax.ShapeDtypeStruct(shape, blocks[0].dtype),
        in_specs=[pl.BlockSpec(memory_space=pl.ANY)] * len(blocks),
        out_specs=pl.BlockSpec(memory_space=pl.ANY),
        scratch_shapes=[
            pltpu.VMEM(shape, blocks[0].dtype),
            pltpu.SemaphoreType.DMA((len(listed),)),
            pltpu.SemaphoreType.DMA,
        ],
        compiler_params=pltpu.CompilerParams(vmem_limit_bytes=moved // 2 + (4 << 20)),
        cost_estimate=pl.CostEstimate(flops=0, bytes_accessed=moved, transcendentals=0),
    )(*blocks)


class Sends:
    def __init__(self, sems):
        self.sems = sems
        self.made = []

    def start(self, source, target, recv_sem, device, cond=None):
        sem = self.sems.at[len(self.made)]

        def copy():
            return pltpu.make_async_remote_copy(
                src_ref=source,
                dst_ref=target,
                send_sem=sem,
                recv_sem=recv_sem,
                device_id=device,
                device_id_type=pl.DeviceIdType.MESH,
            )

        self.made.append((cond, copy))
        when(cond, lambda: copy().start())

    def wait_sent(self):
        for cond, copy in self.made:
            when(cond, lambda copy=copy: copy().wait_send())


def when(cond, act):
    if cond is None:
        act()
    else:
        pl.when(cond)(act)


def both(first, second):
    if first is None:
        return second
    return first if second is None else jnp.logical_and(first, second)


def arrived(ref, recv_sem, device):
    pltpu.make_async_remote_copy(
        src_ref=ref, dst_ref=ref, send_sem=recv_sem, recv_sem=recv_sem,
        device_id=device, device_id_type=pl.DeviceIdType.MESH,
    ).wait_recv()


def greet(devices):
    barrier = pltpu.get_barrier_semaphore()
    for device in devices:
        pl.semaphore_signal(
            barrier, inc=1, device_id=device, device_id_type=pl.DeviceIdType.MESH
        )
    pl.semaphore_wait(barrier, len(devices))


def gather_kernel(side, piece, sliced, *refs):
    w_query, w_key, w_value, w_out, w_gate, w_up, w_down = refs[:7]
    outs = refs[7:11]
    qkv, out, units, down = bufs = refs[11:15]
    load_sems, send_sems, qkv_sems, out_sems, unit_sems, down_sems, store_sems = refs[15:]
    t, j, c, x = coordinates()
    bits = side.bit_length() - 1

    def at(tt, jj, cc, xx=None):
        return (((tt * side) + jj) * 2 + cc, x if xx is None else xx)

    def block(tt, jj, cc):
        return ((tt * side) + jj) * 2 + cc

    here = at(t, j, c)
    core = at(t, j, 1 - c)
    across = at(t, j, c, 1 - x)
    beside = [at(t, j ^ (1 << bit), c) for bit in range(bits)]
    others = [
        at((t + dt) % LINE, j, c ^ dc) for dt in range(LINE) for dc in range(2) if dt or dc
    ]
    mine = block(t, j, c)
    q_cols, k_cols = w_query.shape[1], w_key.shape[1]
    loads = [
        (w_query, qkv.at[mine, :, pl.ds(0, q_cols)]),
        (w_key, qkv.at[mine, :, pl.ds(q_cols, k_cols)]),
        (w_value, qkv.at[mine, :, pl.ds(q_cols + k_cols, k_cols)]),
        (w_out, out.at[mine]),
        (w_down, down.at[x * side + j]),
    ]
    depth = w_query.shape[0]

    def unit_block(which, tt, jj, cc):
        weight = (w_gate, w_up)[which]
        if sliced:
            col = pl.multiple_of(block(tt, jj, cc) * piece, piece)
            return weight.at[:, pl.ds(col, piece)]
        return weight.at[tt, cc]

    def unit_target(which, tt, jj, cc):
        if sliced:
            return units.at[which, tt * 2 + cc, :, pl.ds(jj * piece, piece)]
        return units.at[which, tt * 2 + cc]

    parts = range(side) if sliced else range(1)
    loads += [
        (unit_block(w, t, jj, c), unit_target(w, t, jj, c)) for w in range(2) for jj in parts
    ]
    loads = [
        pltpu.make_async_copy(a, b, load_sems.at[i]) for i, (a, b) in enumerate(loads)
    ]
    for load in loads:
        load.start()
    greet(others + beside + [across])
    sends = Sends(send_sems)
    for load in loads[:5]:
        load.wait()

    lines = ((qkv, qkv_sems), (out, out_sems))

    def spread(buf, sems, tt, r, cond):
        idx = block(tt, j ^ r, c)
        for bit in range(bits):
            if (1 << bit) > r:
                sends.start(buf.at[idx], buf.at[idx], sems.at[idx], beside[bit], cond)
        sends.start(buf.at[idx], buf.at[idx], sems.at[idx], core, cond)

    def pass_on(buf, sems, tt, to_right, to_left):
        idx = block(tt, j, c)
        if to_right is not False:
            sends.start(buf.at[idx], buf.at[idx], sems.at[idx], at(t + 1, j, c), to_right)
        if to_left is not False:
            sends.start(buf.at[idx], buf.at[idx], sems.at[idx], at(t - 1, j, c), to_left)

    def spread_rest(buf, sems, tt, cond):
        for r in range(1, side):
            idx = block(tt, j ^ r, c)
            when(cond, lambda idx=idx: arrived(buf.at[idx], sems.at[idx], here))
            spread(buf, sems, tt, r, cond)

    for buf, sems in lines:
        pass_on(buf, sems, t, t < LINE - 1, t > 0)
        spread(buf, sems, t, 0, None)
    own_down = x * side + j
    sends.start(down.at[own_down], down.at[own_down], down_sems.at[own_down], across)
    for bit in range(bits):
        sends.start(down.at[own_down], down.at[own_down], down_sems.at[own_down], beside[bit])
    for dt in range(LINE):
        for dc in range(2):
            if dt or dc:
                tt, cc = (t + dt) % LINE, c ^ dc
                for w in range(2):
                    for jj in parts:
                        sends.start(
                            unit_block(w, tt, jj, cc),
                            unit_target(w, t, jj, c),
                            unit_sems.at[w, t * 2 + c, jj],
                            at(tt, j, cc),
                        )
    for k in range(1, LINE):
        for buf, sems in lines:
            from_left, from_right = t >= k, t + k < LINE
            for cond, tt in ((from_left, t - k), (from_right, t + k)):
                idx = block(tt, j, c)
                when(cond, lambda idx=idx: arrived(buf.at[idx], sems.at[idx], here))
                if k < LINE - 1:
                    if tt is not None and cond is from_left:
                        pass_on(buf, sems, tt, both(cond, t < LINE - 1), False)
                    else:
                        pass_on(buf, sems, tt, False, both(cond, t > 0))
                spread(buf, sems, tt, 0, cond)
            if k == 1:
                spread_rest(buf, sems, t, None)
            else:
                spread_rest(buf, sems, t - k + 1, t >= k - 1)
                spread_rest(buf, sems, t + k - 1, t + k - 1 < LINE)
        if k == 1:
            for r in range(1, side):
                idx = x * side + (j ^ r)
                arrived(down.at[idx], down_sems.at[idx], here)
                for bit in range(bits):
                    if (1 << bit) > r:
                        sends.start(
                            down.at[idx], down.at[idx], down_sems.at[idx], beside[bit]
                        )
                sends.start(down.at[idx], down.at[idx], down_sems.at[idx], across)
    stores = []

    def store(i):
        copy = pltpu.make_async_copy(bufs[i], outs[i], store_sems.at[i])
        copy.start()
        stores.append(copy)

    for i, (buf, sems) in enumerate(lines):
        spread_rest(buf, sems, t - LINE + 1, t >= LINE - 1)
        spread_rest(buf, sems, t + LINE - 1, t < 1)
        for tt in range(LINE):
            for jj in range(side):
                idx = block(tt, jj, 1 - c)
                arrived(buf.at[idx], sems.at[idx], here)
        store(i)
    for load in loads[5:]:
        load.wait()
    for dt in range(LINE):
        for dc in range(2):
            if dt or dc:
                tt, cc = (t + dt) % LINE, c ^ dc
                for w in range(2):
                    for jj in parts:
                        arrived(
                            unit_target(w, tt, jj, cc), unit_sems.at[w, tt * 2 + cc, jj], here
                        )
    store(2)
    for jj in range(side):
        idx = (1 - x) * side + jj
        arrived(down.at[idx], down_sems.at[idx], here)
    store(3)
    sends.wait_sent()
    for copy in stores:
        copy.wait()


def gather_weights(n, w_query, w_key, w_value, w_out, w_gate, w_up, w_down):
    side = n // LINE // 2
    depth, piece, width = w_gate.shape[0], w_down.shape[0], w_down.shape[1]
    strip = side * piece
    sliced = piece % LANES == 0
    if not sliced:
        w_gate, w_up = (
            w.reshape(depth, LINE, side, 2, piece)
            .transpose(1, 3, 0, 2, 4)
            .reshape(LINE, 2, depth, strip)
            for w in (w_gate, w_up)
        )
    shapes = [
        (n, depth, w_query.shape[1] + 2 * w_key.shape[1]),
        (n,) + w_out.shape,
        (2, LINE * 2, depth, strip),
        (2 * side, piece, width),
    ]
    slots = 2 * LINE - 1
    line_sends = 2 * (LINE - 1) + slots * (2 * side - 1)
    sends = 2 * line_sends + 2 * side - 1 + 14 * side
    any_space = pl.BlockSpec(memory_space=pl.ANY)
    moved = 2 * sum(math.prod(shape) for shape in shapes)
    return pl.pallas_call(
        functools.partial(gather_kernel, side, piece, sliced),
        out_shape=[jax.ShapeDtypeStruct(shape, BF) for shape in shapes],
        in_specs=[any_space] * 7,
        out_specs=[any_space] * 4,
        scratch_shapes=[pltpu.VMEM(shape, BF) for shape in shapes]
        + [
            pltpu.SemaphoreType.DMA((5 + 2 * side,)),
            pltpu.SemaphoreType.DMA((sends,)),
            pltpu.SemaphoreType.DMA((n,)),
            pltpu.SemaphoreType.DMA((n,)),
            pltpu.SemaphoreType.DMA((2, LINE * 2, side)),
            pltpu.SemaphoreType.DMA((2 * side,)),
            pltpu.SemaphoreType.DMA((4,)),
        ],
        compiler_params=pltpu.CompilerParams(
            collective_id=0, has_side_effects=True, vmem_limit_bytes=moved + (4 << 20)
        ),
        cost_estimate=pl.CostEstimate(flops=0, bytes_accessed=40 * moved, transcendentals=0),
    )(w_query, w_key, w_value, w_out, w_gate, w_up, w_down)


class Links:
    def __init__(self, n):
        self.n = n
        self.inner = n // LINE
        self.side = self.inner // 2
        self.side_bits = self.side.bit_length() - 1
        self.t, self.j, self.c, self.x = coordinates()

    def core(self, value):
        return lax.ppermute(value, "dp", [(i, i ^ 1) for i in range(self.n)])

    def over(self, value, bit):
        return lax.ppermute(value, "dp", [(i, i ^ (2 << bit)) for i in range(self.n)])

    def cross(self, value):
        return lax.ppermute(value, "tensor", [(0, 1), (1, 0)])

    def along(self, value, moves):
        pairs = [
            (a * self.inner + i, b * self.inner + i) for a, b in moves for i in range(self.inner)
        ]
        return lax.ppermute(value, "dp", pairs)

    def right(self, value, senders):
        return self.along(value, [(a, a + 1) for a in senders])

    def left(self, value, senders):
        return self.along(value, [(a, a - 1) for a in senders])

    def turn(self, value, shift):
        return self.along(value, [(a, (a + shift) % LINE) for a in range(LINE)])

    def line_gather(self, value):
        t = self.t
        r1 = self.right(value, (0, 1, 2))
        l1 = self.left(value, (1, 2, 3))
        r2 = self.right(r1, (1, 2))
        l2 = self.left(l1, (1, 2))
        r3 = self.right(r2, (2,))
        l3 = self.left(l2, (1,))
        return (
            value,
            jnp.where(t == 0, l1, r1),
            jnp.where(t < 2, l2, r2),
            jnp.where(t == 0, l3, jnp.where(t == 3, r3, l1)),
        )

    def line_scatter(self, parts):
        t = self.t
        p0, p1, p2, p3 = parts
        first = p3.astype(BF)
        r1 = self.right(first, (0,))
        l1 = self.left(first, (3,))
        second = (p2 + r1.astype(F32) + l1.astype(F32)).astype(BF)
        r2 = self.right(second, (0, 1))
        l2 = self.left(second, (2, 3))
        r3 = self.right((jnp.where(t == 0, p1, p3) + r2.astype(F32)).astype(BF), (0, 1, 2))
        l3 = self.left((p1 + l2.astype(F32)).astype(BF), (1, 2, 3))
        return p0 + r3.astype(F32) + l3.astype(F32)

    def line_send(self, parts):
        p0, p1, p2, p3 = parts
        first, second, third = p1.astype(BF), p2.astype(BF), p3.astype(BF)
        got = [
            self.left(first, (1, 2, 3)),
            self.right(first, (0,)),
            self.turn(second, 2),
            self.along(third, ((0, 3), (3, 0))),
            self.right(third, (1, 2)),
        ]
        return p0 + sum(g.astype(F32) for g in got)

    def side_all(self, value):
        blocks = [value]
        for bit in range(self.side_bits):
            blocks += [self.over(block, bit) for block in blocks]
        return blocks

    def side_sum(self, blocks):
        for bit in reversed(range(self.side_bits)):
            width = 1 << bit
            blocks = [
                a.astype(F32) + self.over(b.astype(BF), bit).astype(F32)
                for a, b in zip(blocks[:width], blocks[width:])
            ]
        return blocks[0]

    def pair_order(self, mine, other, where):
        low = jnp.where(where == 0, mine, other)
        high = jnp.where(where == 0, other, mine)
        return jnp.concatenate([low, high], 0)

    def pick(self, value, index, axis):
        return lax.dynamic_index_in_dim(value, index, axis, keepdims=False)

    def cross_sum(self, value, axis):
        kept = self.pick(value, self.x, axis)
        sent = self.pick(value, 1 - self.x, axis)
        return kept.astype(F32) + self.cross(sent.astype(BF)).astype(F32)

    def gather_rows(self, blocks):
        rows, cols = blocks[0].shape
        pieces, where = [], []
        for k, block in enumerate(blocks):
            for r, piece in enumerate(self.side_all(block)):
                pieces += [piece, self.core(piece)]
                where += [(k, r, 0), (k, r, 1)]

        def spots(t, j, c, x):
            return [
                (
                    i, 0, 0, rows, cols,
                    (((slot_place(t, k) * self.side) + (j ^ r)) * 2 + (c ^ s)) * rows, 0,
                )
                for i, (k, r, s) in enumerate(where)
            ]

        return place(pieces, spots, (self.n * rows, cols))

    def sum_rows(self, value):
        rows, cols = value.shape[0] // self.n, value.shape[1]
        parts = value.reshape(LINE, self.side, 2, rows, cols)
        kept = self.pick(parts, self.c, 2).astype(F32)
        parts = kept + self.core(self.pick(parts, 1 - self.c, 2)).astype(F32)
        parts = parts.astype(BF)
        parts = self.side_sum([self.pick(parts, self.j ^ r, 1) for r in range(self.side)])
        return self.line_scatter(
            [self.pick(parts, slot_place(self.t, k), 0).astype(F32) for k in range(LINE)]
        )

    def total(self, value):
        value = value + self.core(value)
        for bit in range(self.side_bits):
            value = value + self.over(value, bit)
        value = value + self.cross(value)
        value = value + self.along(value, ((0, 1), (1, 0), (2, 3), (3, 2)))
        return value + self.turn(value, 2)


def make_body(n):
    def body(
        tokens,
        cotangent,
        lengths,
        attn_gain,
        query_gain,
        key_gain,
        w_query,
        key_weight_matrix,
        value_weight_matrix,
        w_out,
        ffn_gain,
        w_gate,
        w_up,
        w_down,
    ):
        net = Links(n)
        t, j, c, x = net.t, net.j, net.c, net.x
        row_count, width = tokens.shape
        half = row_count // 2
        head_dim = query_gain.shape[0]
        q_cols = w_query.shape[1]
        k_cols = key_weight_matrix.shape[1]
        k_heads = k_cols // head_dim
        dp_index = lax.axis_index("dp")
        slot_length = lengths[dp_index]

        depth = w_gate.shape[0]
        piece = w_down.shape[0]
        side = net.side
        strip = side * piece
        qkv_full, wo_full, units, wd = gather_weights(
            n, w_query, key_weight_matrix, value_weight_matrix, w_out, w_gate, w_up, w_down
        )
        qkv_full = qkv_full.reshape(width, q_cols + 2 * k_cols)
        wo_full = wo_full.reshape(q_cols, width)
        wd = wd.reshape(2 * strip, width)

        gate_own = units[0].reshape(LINE * 2 * depth, strip)
        up_own = units[1].reshape(LINE * 2 * depth, strip)
        gate_pieces, up_pieces = [], []
        for part in (gate_own, net.cross(gate_own)):
            gate_pieces.append(net.side_all(part))
        up_pieces.append(net.side_all(up_own))
        up_pieces.append([net.cross(part) for part in up_pieces[0]])

        def unit_weight(pieces):
            def spots(t, j, c, x):
                return [
                    (
                        s * side + r, tt * 2 * depth, 0, 2 * depth, strip,
                        (tt * side + (j ^ r)) * 2 * depth, (x ^ s) * strip,
                    )
                    for s in range(2)
                    for r in range(side)
                    for tt in range(LINE)
                ]

            return place(pieces[0] + pieces[1], spots, (width, 2 * strip))

        wg = unit_weight(gate_pieces)
        wu = unit_weight(up_pieces)

        start = x * half
        half_positions = start + jnp.arange(half, dtype=jnp.int32)
        half_valid = (half_positions < slot_length)[:, None]
        grad_half = lax.dynamic_slice_in_dim(cotangent, start, half, 0)
        grad_half = jnp.where(half_valid, grad_half, jnp.zeros_like(grad_half))
        grad_blocks = [
            jnp.concatenate([block, net.core(block)], axis=0)
            for block in net.line_gather(after(units, grad_half))
        ]

        tables = angle_tables(row_count, head_dim, LANES)
        gains = [jnp.tile(gain, LANES // head_dim)[None, :] for gain in (query_gain, key_gain)]
        inputs = tokens.astype(F32)
        hidden_state = rms_scale(inputs, attn_gain).astype(BF)
        qkv = mm(hidden_state, qkv_full)
        length = slot_length[None]
        o_low, log_totals = attend(length, qkv, tables, gains, q_cols, k_heads)
        attn_part = mm(o_low, wo_full).reshape(2, half, width)
        input_half = lax.dynamic_slice_in_dim(inputs, start, half, 0)
        h_one = input_half + net.cross_sum(attn_part, 0)
        hidden_two = rms_scale(h_one, ffn_gain).astype(BF)

        hidden_blocks = [
            jnp.concatenate([block, net.core(block)], axis=0)
            for block in net.line_gather(hidden_two)
        ]

        def core_sum(value):
            low = value[half:].astype(BF)
            return value[:half] + net.core(low).astype(F32)

        out_parts, grad_parts, acts, grad_gates, grad_ups = [], [], [], [], []
        for hidden, grad in zip(hidden_blocks, grad_blocks):
            gate = mm(hidden, wg)
            up_proj = mm(hidden, wu)
            sigmoid_gate = jax.nn.sigmoid(gate)
            silu_gate = gate * sigmoid_gate
            act = (silu_gate * up_proj).astype(BF)
            out_parts.append(core_sum(mm(act, wd)))
            grad_act = mm_nt(grad, wd)
            silu_slope = sigmoid_gate * (1.0 + gate * (1.0 - sigmoid_gate))
            grad_gate = (grad_act * up_proj * silu_slope).astype(BF)
            grad_up = (grad_act * silu_gate).astype(BF)
            grad_parts.append(core_sum(mm_nt(grad_gate, wg) + mm_nt(grad_up, wu)))
            acts.append(act)
            grad_gates.append(grad_gate)
            grad_ups.append(grad_up)

        grad_hidden_two = net.line_send(grad_parts)
        out_parts = after(grad_hidden_two, *out_parts)
        layer_half = (h_one + net.line_scatter(out_parts)).astype(BF)
        layer_out = net.pair_order(layer_half, net.cross(layer_half), x)
        norm_two_back = jax.vjp(rms_scale, h_one, ffn_gain)[1]
        grad_h_part, g_ffn_part = norm_two_back(grad_hidden_two)
        grad_h_one = grad_half.astype(F32) + grad_h_part
        grad_attn_half = grad_h_one.astype(BF)
        grad_attn_low = net.pair_order(grad_attn_half, net.cross(grad_attn_half), x)

        acts[0], grad_gates[0], grad_ups[0] = after(
            grad_parts, acts[0], grad_gates[0], grad_ups[0]
        )
        act_all = jnp.concatenate(acts, 0)
        hidden_all = jnp.concatenate(hidden_blocks, 0)
        grad_all = jnp.concatenate(grad_blocks, 0)
        g_gate = mm_tn(hidden_all, jnp.concatenate(grad_gates, 0)).astype(BF)
        g_up = mm_tn(hidden_all, jnp.concatenate(grad_ups, 0)).astype(BF)
        g_down = mm_tn(act_all, grad_all).astype(BF)

        def home_units(value):
            rows = value.reshape(LINE, 2 * depth, strip)
            blocks = []
            for shift in range(LINE):
                block = net.pick(rows, (t + shift) % LINE, 0)
                block = block if shift == 0 else net.turn(block, shift)
                block = block.reshape(2, depth, strip)
                blocks.append(net.pick(block, c, 0))
                blocks.append(net.core(net.pick(block, 1 - c, 0)))
            if piece % 128:
                stacked = jnp.stack(blocks).reshape(LINE, 2, depth, side, piece)
                order_t = (t - jnp.arange(LINE)) % LINE
                stacked = jnp.take(stacked, order_t, axis=0)
                stacked = jnp.take(stacked, c ^ jnp.arange(2), axis=1)
                return stacked.transpose(2, 0, 3, 1, 4).reshape(depth, LINE * 2 * strip)

            def spots(t, j, c, x):
                return [
                    (
                        2 * shift + s, 0, r * piece, depth, piece, 0,
                        ((((t - shift) % LINE) * side + r) * 2 + (c ^ s)) * piece,
                    )
                    for shift in range(LINE)
                    for s in range(2)
                    for r in range(side)
                ]

            return place(blocks, spots, (depth, LINE * 2 * strip))

        def side_rows(value):
            rows = value.reshape(LINE, side, 2 * depth, value.shape[1])
            return [net.pick(rows, j ^ r, 1) for r in range(side)]

        def cross_cols(value):
            kept = lax.dynamic_slice_in_dim(value, x * strip, strip, value.ndim - 1)
            sent = lax.dynamic_slice_in_dim(value, (1 - x) * strip, strip, value.ndim - 1)
            return kept.astype(F32) + net.cross(sent.astype(BF)).astype(F32)

        gate_sum = net.side_sum(side_rows(cross_cols(g_gate).astype(BF))).astype(BF)
        up_sum = cross_cols(net.side_sum(side_rows(g_up))).astype(BF)
        g_gate_out = home_units(gate_sum).astype(F32)
        g_up_out = home_units(up_sum).astype(F32)
        down_sum = net.cross_sum(g_down.reshape(2, side, piece, width), 0).astype(BF)
        g_down_out = net.side_sum([net.pick(down_sum, j ^ r, 0) for r in range(side)])

        g_out = mm_tn(o_low, grad_attn_low).astype(BF)
        grad_o_low = mm_nt(grad_attn_low, wo_full).astype(BF)
        grad_q, grad_k, grad_v, q_part, k_part = attend_back(
            length, qkv, tables, gains, log_totals, grad_o_low, q_cols, k_heads
        )
        g_query_part = q_part.reshape(-1, head_dim).sum(0)
        g_key_part = k_part.reshape(-1, head_dim).sum(0)
        grad_qkv = jnp.concatenate([grad_q, grad_k, grad_v], axis=1)
        g_qkv = mm_tn(hidden_state, grad_qkv).astype(BF)
        g_out_out = net.sum_rows(g_out)
        g_qkv_out = net.sum_rows(g_qkv)
        grad_hidden = mm_nt(grad_qkv, qkv_full).reshape(2, half, width)
        grad_hidden_half = net.cross_sum(grad_hidden, 0)
        norm_one_back = jax.vjp(rms_scale, input_half, attn_gain)[1]
        grad_in_half, g_attn_part = norm_one_back(grad_hidden_half)
        input_grad_half = (grad_h_one + grad_in_half).astype(BF)
        input_grad = net.pair_order(input_grad_half, net.cross(input_grad_half), x).astype(F32)
        small = jnp.concatenate([g_attn_part, g_ffn_part, g_query_part, g_key_part])
        small = net.total(small)
        return (
            layer_out,
            input_grad,
            small[:width],
            small[2 * width : 2 * width + head_dim],
            small[2 * width + head_dim :],
            g_qkv_out[:, :q_cols],
            g_qkv_out[:, q_cols : q_cols + k_cols],
            g_qkv_out[:, q_cols + k_cols :],
            g_out_out,
            small[width : 2 * width],
            g_gate_out,
            g_up_out,
            g_down_out,
        )

    return body


def solution(mesh):
    placed = (
        P("dp", None),
        P("dp", None),
        P(),
        P(),
        P(),
        P(),
        P("dp", "tensor"),
        P("dp", "tensor"),
        P("dp", "tensor"),
        P(("tensor", "dp"), None),
        P(),
        P("dp", "tensor"),
        P("dp", "tensor"),
        P(("tensor", "dp"), None),
    )
    return jax.shard_map(
        make_body(mesh.shape["dp"]),
        mesh=mesh,
        in_specs=placed,
        out_specs=(
            P("dp", None),
            P("dp", None),
            P(),
            P(),
            P(),
            P("dp", "tensor"),
            P("dp", "tensor"),
            P("dp", "tensor"),
            P(("tensor", "dp"), None),
            P(),
            P("dp", "tensor"),
            P("dp", "tensor"),
            P(("tensor", "dp"), None),
        ),
        check_vma=False,
    )
```

```python
import functools
import math

import jax
import jax.numpy as jnp
import numpy as np
from jax import lax
from jax.experimental import pallas as pl
from jax.experimental.pallas import tpu as pltpu
from jax.sharding import PartitionSpec as P

EPS = 1e-05
ROPE_BASE = 1000000.0
MASKED = -1e30
LINE = 4
BF = jnp.bfloat16
F32 = jnp.float32


def rms_scale(values, gain):
    return values * lax.rsqrt(jnp.mean(values * values, axis=-1, keepdims=True) + EPS) * gain


def angle_tables(count, head_dim, lanes):
    half_dim = head_dim // 2
    freq = ROPE_BASE ** (np.arange(half_dim) * (-2.0 / head_dim))
    turned = np.arange(count)[:, None] * freq[None, :]
    cosine, sine = np.cos(turned).astype(np.float32), np.sin(turned).astype(np.float32)
    repeats = lanes // head_dim
    return (
        jnp.asarray(np.tile(np.concatenate([cosine, cosine], 1), (1, repeats))),
        jnp.asarray(np.tile(np.concatenate([-sine, sine], 1), (1, repeats))),
    )


LANES = 128
HEAD = LANES // 2


def low_lanes(shape):
    return lax.broadcasted_iota(jnp.int32, shape, 1) < HEAD


def per_head(values):
    low = low_lanes(values.shape)
    first = jnp.sum(jnp.where(low, values, 0.0), axis=1, keepdims=True)
    second = jnp.sum(jnp.where(low, 0.0, values), axis=1, keepdims=True)
    return jnp.where(low, first, second) * (1.0 / HEAD)


def halves_swapped(values):
    lane = lax.broadcasted_iota(jnp.int32, values.shape, 1)
    return jnp.where(
        lane % HEAD < HEAD // 2,
        pltpu.roll(values, LANES - HEAD // 2, 1),
        pltpu.roll(values, HEAD // 2, 1),
    )


def head_norm(values):
    scale = lax.rsqrt(per_head(values * values) + EPS)
    return values * scale, scale


def head_turn(values, cosine, sine):
    return values * cosine + halves_swapped(values) * sine


def head_back(grad, normed, scale, gain, cosine, sine):
    grad = grad * cosine - halves_swapped(grad) * sine
    gain_grad = jnp.sum(grad * normed, axis=0, keepdims=True)
    grad = grad * gain
    return scale * (grad - normed * per_head(grad * normed)), gain_grad


def one_head(pair, second):
    low = low_lanes(pair.shape)
    return jnp.where(low == jnp.logical_not(second), pair, pltpu.roll(pair, HEAD, 1))


def two_rows(slab):
    low = low_lanes(slab.shape)
    return jnp.concatenate([jnp.where(low, slab, 0.0), jnp.where(low, 0.0, slab)], 0).astype(BF)


def allowed_mask(block, first_row, columns, length):
    row = lax.broadcasted_iota(jnp.int32, (2 * block, columns), 0) % block + first_row
    col = lax.broadcasted_iota(jnp.int32, (2 * block, columns), 1)
    return (col <= row) & (col < length)


def attend_kernel(
    block, scale, second, length, q, k, v, cosine, sine, q_gain, k_gain, out, totals
):
    rows = q.shape[0]
    cos, sin = cosine[...], sine[...]
    keys = one_head(head_turn(head_norm(k[...])[0] * k_gain[...], cos, sin), second).astype(BF)
    vals = one_head(v[...], second).astype(BF)
    lane = lax.broadcasted_iota(jnp.int32, (block, LANES), 1)
    for first in range(0, rows, block):
        span = pl.ds(first, block)
        seen = first + block
        allowed = allowed_mask(block, first, seen, length[0])
        kept = jnp.zeros((block, LANES), F32)
        for slab in range(q.shape[1] // LANES):
            cols = pl.ds(slab * LANES, LANES)
            turned = head_turn(
                head_norm(q[span, cols])[0] * q_gain[...], cosine[span, :], sine[span, :]
            )
            scores = mm_nt(two_rows(turned), keys[:seen]) * scale
            scores = jnp.where(allowed, scores, MASKED)
            top = jnp.max(scores, axis=1, keepdims=True)
            probs = jnp.exp(scores - top)
            total = jnp.sum(probs, axis=1, keepdims=True)
            probs = (probs * (1.0 / total)).astype(BF)
            both = mm(probs, vals[:seen])
            out[span, cols] = jnp.where(low_lanes((block, LANES)), both[:block], both[block:]).astype(
                BF
            )
            log_total = top + jnp.log(total)
            kept = jnp.where(lane == 2 * slab, log_total[:block], kept)
            kept = jnp.where(lane == 2 * slab + 1, log_total[block:], kept)
        totals[span, :] = kept


def attend_back_kernel(
    block, scale, length, q, k, v, cosine, sine, q_gain, k_gain, totals, grad_out,
    grad_q, grad_k, grad_v, q_gain_grad, k_gain_grad, keys_sum, vals_sum,
):
    step = pl.program_id(0)
    second = step % 2 == 1
    rows = q.shape[0]
    cos, sin = cosine[...], sine[...]
    k_normed, k_scale = head_norm(k[...])
    keys = one_head(head_turn(k_normed * k_gain[...], cos, sin), second).astype(BF)
    vals = one_head(v[...], second).astype(BF)
    lane = lax.broadcasted_iota(jnp.int32, (block, LANES), 1)
    keys_sum[...] = jnp.zeros_like(keys_sum)
    vals_sum[...] = jnp.zeros_like(vals_sum)

    @pl.when(step == 0)
    def _():
        q_gain_grad[...] = jnp.zeros_like(q_gain_grad)
        k_gain_grad[...] = jnp.zeros_like(k_gain_grad)

    for first in range(0, rows, block):
        span = pl.ds(first, block)
        seen = first + block
        allowed = allowed_mask(block, first, seen, length[0])
        kept = totals[span, :]
        for slab in range(q.shape[1] // LANES):
            cols = pl.ds(slab * LANES, LANES)
            q_normed, q_scale = head_norm(q[span, cols])
            turned = two_rows(head_turn(q_normed * q_gain[...], cosine[span, :], sine[span, :]))
            log_total = jnp.concatenate(
                [
                    jnp.sum(jnp.where(lane == 2 * slab + i, kept, 0.0), axis=1, keepdims=True)
                    for i in range(2)
                ],
                0,
            )
            scores = mm_nt(turned, keys[:seen]) * scale
            probs = jnp.exp(jnp.where(allowed, scores, MASKED) - log_total)
            grad_rows = two_rows(grad_out[span, cols].astype(F32))
            grad_probs = mm_nt(grad_rows, vals[:seen])
            drop = jnp.sum(probs * grad_probs, axis=1, keepdims=True)
            grad_scores = (probs * (grad_probs - drop)).astype(BF)
            both = mm(grad_scores, keys[:seen]) * scale
            grad_turned = jnp.where(low_lanes((block, LANES)), both[:block], both[block:])
            grad_proj, gain_part = head_back(
                grad_turned, q_normed, q_scale, q_gain[...], cosine[span, :], sine[span, :]
            )
            grad_q[span, cols] = grad_proj.astype(BF)
            q_gain_grad[...] += gain_part
            keys_sum[:seen] += mm_tn(grad_scores, turned)
            vals_sum[:seen] += mm_tn(probs.astype(BF), grad_rows)

    keys_grad = keys_sum[...] * scale
    keys_grad = keys_grad + pltpu.roll(keys_grad, HEAD, 1)
    vals_grad = vals_sum[...]
    vals_grad = vals_grad + pltpu.roll(vals_grad, HEAD, 1)
    grad_proj, gain_part = head_back(
        keys_grad,
        one_head(k_normed, second),
        one_head(k_scale, second),
        k_gain[...],
        cos,
        sin,
    )
    k_gain_grad[...] += gain_part * 0.5
    keep_low = low_lanes(grad_k.shape)

    @pl.when(step % 2 == 0)
    def _():
        grad_k[...] = grad_proj.astype(BF)
        grad_v[...] = vals_grad.astype(BF)

    @pl.when(step % 2 == 1)
    def _():
        grad_k[...] = jnp.where(keep_low, grad_k[...].astype(F32), grad_proj).astype(BF)
        grad_v[...] = jnp.where(keep_low, grad_v[...].astype(F32), vals_grad).astype(BF)


def attention_specs(rows, group, k_heads, q_cols):
    wide = group * HEAD
    k_first = q_cols // LANES
    v_first = k_first + k_heads * HEAD // LANES
    return [
        pl.BlockSpec(memory_space=pltpu.SMEM),
        pl.BlockSpec((rows, wide), lambda g: (0, g)),
        pl.BlockSpec((rows, LANES), lambda g: (0, k_first + g // 2)),
        pl.BlockSpec((rows, LANES), lambda g: (0, v_first + g // 2)),
        pl.BlockSpec((rows, LANES), lambda g: (0, 0)),
        pl.BlockSpec((rows, LANES), lambda g: (0, 0)),
        pl.BlockSpec((1, LANES), lambda g: (0, 0)),
        pl.BlockSpec((1, LANES), lambda g: (0, 0)),
    ]


def attend_back(length, qkv, tables, gains, totals, grad_out, q_cols, k_heads):
    rows = qkv.shape[0]
    group = q_cols // HEAD // k_heads
    block = rows // 2
    return pl.pallas_call(
        functools.partial(attend_back_kernel, block, 1.0 / math.sqrt(HEAD)),
        grid=(k_heads,),
        in_specs=attention_specs(rows, group, k_heads, q_cols)
        + [
            pl.BlockSpec((rows, LANES), lambda g: (0, g)),
            pl.BlockSpec((rows, group * HEAD), lambda g: (0, g)),
        ],
        out_specs=[
            pl.BlockSpec((rows, group * HEAD), lambda g: (0, g)),
            pl.BlockSpec((rows, LANES), lambda g: (0, g // 2)),
            pl.BlockSpec((rows, LANES), lambda g: (0, g // 2)),
            pl.BlockSpec((1, LANES), lambda g: (0, 0)),
            pl.BlockSpec((1, LANES), lambda g: (0, 0)),
        ],
        out_shape=[
            jax.ShapeDtypeStruct((rows, q_cols), BF),
            jax.ShapeDtypeStruct((rows, k_heads * HEAD), BF),
            jax.ShapeDtypeStruct((rows, k_heads * HEAD), BF),
            jax.ShapeDtypeStruct((1, LANES), F32),
            jax.ShapeDtypeStruct((1, LANES), F32),
        ],
        scratch_shapes=[pltpu.VMEM((rows, LANES), F32), pltpu.VMEM((rows, LANES), F32)],
        compiler_params=pltpu.CompilerParams(vmem_limit_bytes=40 << 20),
        cost_estimate=pl.CostEstimate(
            flops=50 * rows * rows * q_cols, bytes_accessed=10 << 20, transcendentals=rows * rows
        ),
    )(length, qkv, qkv, qkv, *tables, *gains, totals, grad_out)


def mm(left, right):
    return jnp.dot(left, right, preferred_element_type=F32)


def mm_nt(left, right):
    return lax.dot_general(left, right, (((1,), (1,)), ((), ())), preferred_element_type=F32)


def mm_tn(left, right):
    return lax.dot_general(left, right, (((0,), (0,)), ((), ())), preferred_element_type=F32)


def after(done, *values):
    held, _ = lax.optimization_barrier((values, done))
    return held if len(held) > 1 else held[0]


def slot_place(t, k):
    if k == 0:
        return t
    if k == 1:
        return jnp.where(t == 0, 1, t - 1)
    if k == 2:
        return (t + 2) % LINE
    return jnp.where(t == 3, 0, jnp.where(t == 1, 2, 3))


def coordinates():
    n = lax.axis_size("dp")
    inner = n // LINE
    here = lax.axis_index("dp")
    return here // inner, (here % inner) // 2, here % 2, lax.axis_index("tensor")


def place(blocks, spots, shape):
    listed = spots(0, 0, 0, 0)

    def kernel(*refs):
        sources = refs[: len(blocks)]
        out, held, sem, out_sem = refs[len(blocks) :]
        copies = []
        for k, (b, row, col, rows, cols, to_row, to_col) in enumerate(spots(*coordinates())):
            copies.append(
                pltpu.make_async_copy(
                    sources[b].at[pl.ds(row, rows), pl.ds(col, cols)],
                    held.at[
                        pl.ds(pl.multiple_of(to_row, rows), rows),
                        pl.ds(pl.multiple_of(to_col, cols), cols),
                    ],
                    sem.at[k],
                )
            )
        for copy in copies:
            copy.start()
        for copy in copies:
            copy.wait()
        last = pltpu.make_async_copy(held, out, out_sem)
        last.start()
        last.wait()

    item = blocks[0].dtype.itemsize
    moved = sum(2 * rows * cols * item for _, _, _, rows, cols, _, _ in listed)
    return pl.pallas_call(
        kernel,
        out_shape=jax.ShapeDtypeStruct(shape, blocks[0].dtype),
        in_specs=[pl.BlockSpec(memory_space=pl.ANY)] * len(blocks),
        out_specs=pl.BlockSpec(memory_space=pl.ANY),
        scratch_shapes=[
            pltpu.VMEM(shape, blocks[0].dtype),
            pltpu.SemaphoreType.DMA((len(listed),)),
            pltpu.SemaphoreType.DMA,
        ],
        compiler_params=pltpu.CompilerParams(vmem_limit_bytes=moved // 2 + (4 << 20)),
        cost_estimate=pl.CostEstimate(flops=0, bytes_accessed=moved, transcendentals=0),
    )(*blocks)


class Sends:
    def __init__(self, sems):
        self.sems = sems
        self.made = []

    def start(self, source, target, recv_sem, device, cond=None):
        sem = self.sems.at[len(self.made)]

        def copy():
            return pltpu.make_async_remote_copy(
                src_ref=source,
                dst_ref=target,
                send_sem=sem,
                recv_sem=recv_sem,
                device_id=device,
                device_id_type=pl.DeviceIdType.MESH,
            )

        self.made.append((cond, copy))
        when(cond, lambda: copy().start())

    def wait_sent(self):
        for cond, copy in self.made:
            when(cond, lambda copy=copy: copy().wait_send())


def when(cond, act):
    if cond is None:
        act()
    else:
        pl.when(cond)(act)


def both(first, second):
    if first is None:
        return second
    return first if second is None else jnp.logical_and(first, second)


def arrived(ref, recv_sem, device):
    pltpu.make_async_remote_copy(
        src_ref=ref, dst_ref=ref, send_sem=recv_sem, recv_sem=recv_sem,
        device_id=device, device_id_type=pl.DeviceIdType.MESH,
    ).wait_recv()


def greet(devices):
    barrier = pltpu.get_barrier_semaphore()
    for device in devices:
        pl.semaphore_signal(
            barrier, inc=1, device_id=device, device_id_type=pl.DeviceIdType.MESH
        )
    pl.semaphore_wait(barrier, len(devices))


def start_kernel(side, piece, sliced, scale, *refs):
    w_query, w_key, w_value, w_out, w_gate, w_up, w_down, dm_own = refs[:8]
    length, hidden, token_half, cosine, sine, q_gain, k_gain, ffn_gain = refs[8:16]
    outs = refs[16:21]
    proj, attended, totals, h_one, hidden_two = refs[21:26]
    qkv, out, units, down, dm = bufs = refs[26:31]
    part, cross_sent, cross_got = refs[31:34]
    (
        load_sems, send_sems, qkv_sems, out_sems, unit_sems, pair_sems, down_sems,
        line_sems, core_sems, cross_sem, store_sems,
    ) = refs[34:]
    t, j, c, x = coordinates()
    bits = side.bit_length() - 1
    strip = side * piece

    def at(tt, jj, cc, xx=None):
        return (((tt * side) + jj) * 2 + cc, x if xx is None else xx)

    def block(tt, jj, cc):
        return ((tt * side) + jj) * 2 + cc

    here = at(t, j, c)
    core = at(t, j, 1 - c)
    across = at(t, j, c, 1 - x)
    beside = [at(t, j ^ (1 << bit), c) for bit in range(bits)]
    others = [
        at((t + dt) % LINE, j, c ^ dc) for dt in range(LINE) for dc in range(2) if dt or dc
    ]
    mine = block(t, j, c)
    depth, q_cols = w_query.shape
    k_cols = w_key.shape[1]
    half, width = dm_own.shape

    def rows_of(buf, idx):
        count = depth if buf is qkv else w_out.shape[0]
        return buf.at[pl.ds(pl.multiple_of(idx * count, count), count)]

    own_qkv = pl.ds(pl.multiple_of(mine * depth, depth), depth)
    loads = [
        (w_query, qkv.at[own_qkv, pl.ds(0, q_cols)]),
        (w_key, qkv.at[own_qkv, pl.ds(q_cols, k_cols)]),
        (w_value, qkv.at[own_qkv, pl.ds(q_cols + k_cols, k_cols)]),
        (w_out, rows_of(out, mine)),
        (w_down, down.at[x * side + j]),
        (dm_own, dm.at[t, pl.ds(0, half)]),
    ]
    first_unit = len(loads)

    def unit_block(which, tt, jj, cc):
        weight = (w_gate, w_up)[which]
        if sliced:
            col = pl.multiple_of(block(tt, jj, cc) * piece, piece)
            return weight.at[:, pl.ds(col, piece)]
        return weight.at[tt, cc]

    def unit_target(which, tt, jj, cc):
        col = x * strip + (jj * piece if sliced else 0)
        size = piece if sliced else strip
        return units.at[
            which, tt, j, pl.ds(pl.multiple_of(cc * depth, depth), depth),
            pl.ds(pl.multiple_of(col, size), size),
        ]

    def unit_pair(which, tt, jj, xx):
        return units.at[which, tt, jj, :, pl.ds(pl.multiple_of(xx * strip, strip), strip)]

    parts = range(side) if sliced else range(1)
    loads += [
        (unit_block(w, t, jj, c), unit_target(w, t, jj, c)) for w in range(2) for jj in parts
    ]
    loads = [
        pltpu.make_async_copy(a, b, load_sems.at[i]) for i, (a, b) in enumerate(loads)
    ]
    for load in loads:
        load.start()
    greet(others + beside + [across])
    sends = Sends(send_sems)
    for load in loads[:first_unit]:
        load.wait()

    lines = ((qkv, qkv_sems), (out, out_sems))

    def spread(buf, sems, tt, r, cond):
        idx = block(tt, j ^ r, c)
        ref = rows_of(buf, idx)
        for bit in range(bits):
            if (1 << bit) > r:
                sends.start(ref, ref, sems.at[idx], beside[bit], cond)
        sends.start(ref, ref, sems.at[idx], core, cond)

    def pass_on(ref, sem, to_right, to_left):
        if to_right is not False:
            sends.start(ref, ref, sem, at(t + 1, j, c), to_right)
        if to_left is not False:
            sends.start(ref, ref, sem, at(t - 1, j, c), to_left)

    def spread_rest(buf, sems, tt, cond):
        for r in range(1, side):
            idx = block(tt, j ^ r, c)
            when(cond, lambda idx=idx: arrived(rows_of(buf, idx), sems.at[idx], here))
            spread(buf, sems, tt, r, cond)

    def line_places(k):
        return ((t >= k, t - k, True), (t + k < LINE, t + k, False))

    def forward(ref, sem, cond, rightward):
        if rightward:
            pass_on(ref, sem, both(cond, t < LINE - 1), False)
        else:
            pass_on(ref, sem, False, both(cond, t > 0))

    for buf, sems in lines:
        pass_on(rows_of(buf, mine), sems.at[mine], t < LINE - 1, t > 0)
        spread(buf, sems, t, 0, None)
    own_down = x * side + j
    sends.start(down.at[own_down], down.at[own_down], down_sems.at[own_down], across)
    for bit in range(bits):
        sends.start(down.at[own_down], down.at[own_down], down_sems.at[own_down], beside[bit])
    for k in range(1, LINE):
        for buf, sems in lines:
            for cond, tt, rightward in line_places(k):
                idx = block(tt, j, c)
                when(cond, lambda idx=idx: arrived(rows_of(buf, idx), sems.at[idx], here))
                if k < LINE - 1:
                    forward(rows_of(buf, idx), sems.at[idx], cond, rightward)
                spread(buf, sems, tt, 0, cond)
            if k == 1:
                spread_rest(buf, sems, t, None)
            else:
                spread_rest(buf, sems, t - k + 1, t >= k - 1)
                spread_rest(buf, sems, t + k - 1, t + k - 1 < LINE)
        if k == 1:
            for r in range(1, side):
                idx = x * side + (j ^ r)
                arrived(down.at[idx], down_sems.at[idx], here)
                for bit in range(bits):
                    if (1 << bit) > r:
                        sends.start(
                            down.at[idx], down.at[idx], down_sems.at[idx], beside[bit]
                        )
                sends.start(down.at[idx], down.at[idx], down_sems.at[idx], across)
        if k == LINE - 2:
            for dt in range(LINE):
                for dc in range(2):
                    if dt or dc:
                        tt, cc = (t + dt) % LINE, c ^ dc
                        for w in range(2):
                            for jj in parts:
                                sends.start(
                                    unit_block(w, tt, jj, cc),
                                    unit_target(w, t, jj, c),
                                    unit_sems.at[w, t * 2 + c, jj],
                                    at(tt, j, cc),
                                )
    stores = []

    def store(source, target):
        copy = pltpu.make_async_copy(source, target, store_sems.at[len(stores)])
        copy.start()
        stores.append(copy)

    def send_pair(w, tt, jj, xx, device):
        ref = unit_pair(w, tt, jj, xx)
        sends.start(ref, ref, pair_sems.at[w, tt, jj, xx], device)

    def pair_came(w, tt, jj, xx):
        arrived(unit_pair(w, tt, jj, xx), pair_sems.at[w, tt, jj, xx], here)

    def unit_first(tt):
        for cc in range(2):
            mine = jnp.logical_and(tt == t, cc == c)
            for w in range(2):
                for jj in parts:
                    when(
                        jnp.logical_not(mine),
                        lambda w=w, cc=cc, jj=jj: arrived(
                            unit_target(w, tt, jj, cc), unit_sems.at[w, tt * 2 + cc, jj], here
                        ),
                    )
        for w in range(2):
            for bit in range(bits):
                send_pair(w, tt, j, x, beside[bit])
            send_pair(w, tt, j, x, across)

    def unit_second(tt):
        for r in range(1, side):
            for w in (1, 0):
                pair_came(w, tt, j ^ r, x)
                for bit in range(bits):
                    if (1 << bit) > r:
                        send_pair(w, tt, j ^ r, x, beside[bit])
            send_pair(1, tt, j ^ r, x, across)
        pair_came(0, tt, j, 1 - x)
        for bit in range(bits):
            send_pair(0, tt, j, 1 - x, beside[bit])

    def unit_last(tt):
        for r in range(1, side):
            pair_came(0, tt, j ^ r, 1 - x)
            for bit in range(bits):
                if (1 << bit) > r:
                    send_pair(0, tt, j ^ r, 1 - x, beside[bit])
        for r in range(side):
            pair_came(1, tt, j ^ r, 1 - x)

    dm_rows = dm.at[t, pl.ds(0, half)]

    def dm_to_core(tt, cond):
        sends.start(
            dm.at[tt, pl.ds(0, half)], dm.at[tt, pl.ds(half, half)], core_sems.at[tt], core, cond
        )

    def dm_step(k):
        for cond, tt, rightward in line_places(k):
            ref = dm.at[tt, pl.ds(0, half)]
            when(cond, lambda ref=ref, tt=tt: arrived(ref, line_sems.at[tt], here))
            if k < LINE - 1:
                forward(ref, line_sems.at[tt], cond, rightward)
            dm_to_core(tt, cond)

    def finish_line(buf, sems):
        spread_rest(buf, sems, t - LINE + 1, t >= LINE - 1)
        spread_rest(buf, sems, t + LINE - 1, t < 1)
        for tt in range(LINE):
            for jj in range(side):
                idx = block(tt, jj, 1 - c)
                arrived(rows_of(buf, idx), sems.at[idx], here)

    finish_line(*lines[0])
    store(qkv, outs[0])
    for load in loads[first_unit:]:
        load.wait()
    unit_first(t)
    pass_on(dm_rows, line_sems.at[t], t < LINE - 1, t > 0)
    dm_to_core(t, None)

    tile = 256

    @pl.loop(0, proj.shape[1] // tile)
    def _(i):
        cols = pl.ds(pl.multiple_of(i * tile, tile), tile)
        proj[:, cols] = mm(hidden[...], qkv[:, cols])

    rows = hidden.shape[0]
    group = q_cols // k_cols * HEAD

    @pl.loop(0, k_cols // HEAD)
    def _(g):
        pair = pl.multiple_of(g // 2 * LANES, LANES)
        wide = pl.ds(pl.multiple_of(g * group, group), group)
        attend_kernel(
            rows // 2, scale, g % 2 == 1, length,
            proj.at[:, wide],
            proj.at[:, pl.ds(q_cols + pair, LANES)],
            proj.at[:, pl.ds(q_cols + k_cols + pair, LANES)],
            cosine, sine, q_gain, k_gain,
            attended.at[:, wide],
            totals.at[:, pl.ds(pl.multiple_of(g * LANES, LANES), LANES)],
        )

    finish_line(*lines[1])
    store(out, outs[1])
    wide = 512
    other_rows = pl.ds(pl.multiple_of((1 - x) * half, half), half)
    own_rows = pl.ds(pl.multiple_of(x * half, half), half)

    @pl.loop(0, width // wide)
    def _(i):
        cols = pl.ds(pl.multiple_of(i * wide, wide), wide)
        cross_sent[:, cols] = mm(attended[other_rows, :], out[:, cols]).astype(BF)

    sends.start(cross_sent, cross_got, cross_sem, across)

    @pl.loop(0, width // wide)
    def _(i):
        cols = pl.ds(pl.multiple_of(i * wide, wide), wide)
        part[:, cols] = mm(attended[own_rows, :], out[:, cols])

    for k in range(1, LINE):
        unit_first(slot_place(t, k))
    dm_step(1)
    unit_second(t)

    arrived(cross_got, cross_sem, here)
    step = half // 8

    @pl.loop(0, 8)
    def _(i):
        span = pl.ds(pl.multiple_of(i * step, step), step)
        total = token_half[span, :].astype(F32) + part[span, :] + cross_got[span, :].astype(F32)
        h_one[span, :] = total
        hidden_two[span, :] = rms_scale(total, ffn_gain[...]).astype(BF)

    unit_second(slot_place(t, 1))
    dm_step(2)
    unit_second(slot_place(t, 2))
    unit_second(slot_place(t, 3))
    dm_step(3)
    for k in range(LINE):
        unit_last(slot_place(t, k))
    store(units, outs[2])
    for jj in range(side):
        idx = (1 - x) * side + jj
        arrived(down.at[idx], down_sems.at[idx], here)
    store(down, outs[3])
    for tt in range(LINE):
        arrived(dm.at[tt, pl.ds(half, half)], core_sems.at[tt], here)
    store(dm, outs[4])
    sends.wait_sent()
    for copy in stores:
        copy.wait()


def start_layer(n, weights, dm_own, length, hidden, token_half, tables, gains, ffn_gain):
    w_query, w_key, w_value, w_out, w_gate, w_up, w_down = weights
    side = n // LINE // 2
    depth, piece, width = w_gate.shape[0], w_down.shape[0], w_down.shape[1]
    rows, half = hidden.shape[0], dm_own.shape[0]
    q_cols, k_cols = w_query.shape[1], w_key.shape[1]
    cols = q_cols + 2 * k_cols
    strip = side * piece
    sliced = piece % LANES == 0
    if not sliced:
        w_gate, w_up = (
            w.reshape(depth, LINE, side, 2, piece)
            .transpose(1, 3, 0, 2, 4)
            .reshape(LINE, 2, depth, strip)
            for w in (w_gate, w_up)
        )
    shapes = [
        (width, cols),
        (q_cols, width),
        (2, LINE, side, 2 * depth, 2 * strip),
        (2 * side, piece, width),
        (LINE, 2 * half, width),
    ]
    slots = 2 * LINE - 1
    line_sends = 2 * (LINE - 1) + slots * (2 * side - 1)
    sends = 2 * line_sends + 2 * side - 1 + 14 * side + 3 * LINE + 8 + 8 * side * LINE
    any_space = pl.BlockSpec(memory_space=pl.ANY)
    vmem = pl.BlockSpec(memory_space=pltpu.VMEM)
    return pl.pallas_call(
        functools.partial(start_kernel, side, piece, sliced, 1.0 / math.sqrt(HEAD)),
        out_shape=[jax.ShapeDtypeStruct(shape, BF) for shape in shapes]
        + [
            jax.ShapeDtypeStruct((rows, cols), F32),
            jax.ShapeDtypeStruct((rows, q_cols), BF),
            jax.ShapeDtypeStruct((rows, k_cols // HEAD * LANES), F32),
            jax.ShapeDtypeStruct((half, width), F32),
            jax.ShapeDtypeStruct((half, width), BF),
        ],
        in_specs=[any_space] * 8 + [pl.BlockSpec(memory_space=pltpu.SMEM)] + [vmem] * 7,
        out_specs=[any_space] * 5 + [vmem] * 5,
        scratch_shapes=[pltpu.VMEM(shape, BF) for shape in shapes]
        + [
            pltpu.VMEM((half, width), F32),
            pltpu.VMEM((half, width), BF),
            pltpu.VMEM((half, width), BF),
            pltpu.SemaphoreType.DMA((6 + 2 * side,)),
            pltpu.SemaphoreType.DMA((sends,)),
            pltpu.SemaphoreType.DMA((n,)),
            pltpu.SemaphoreType.DMA((n,)),
            pltpu.SemaphoreType.DMA((2, LINE * 2, side)),
            pltpu.SemaphoreType.DMA((2, LINE, side, 2)),
            pltpu.SemaphoreType.DMA((2 * side,)),
            pltpu.SemaphoreType.DMA((LINE,)),
            pltpu.SemaphoreType.DMA((LINE,)),
            pltpu.SemaphoreType.DMA,
            pltpu.SemaphoreType.DMA((5,)),
        ],
        compiler_params=pltpu.CompilerParams(
            collective_id=0, has_side_effects=True, vmem_limit_bytes=62 << 20
        ),
        cost_estimate=pl.CostEstimate(
            flops=2 * rows * width * cols, bytes_accessed=500 << 20, transcendentals=rows * rows
        ),
    )(
        w_query, w_key, w_value, w_out, w_gate, w_up, w_down, dm_own, length, hidden,
        token_half, *tables, *gains, ffn_gain[None, :],
    )


def feed_kernel(side, *refs):
    h_own, dm_all, units, down = refs[:4]
    e_out, f_out, gate_kept, gate_got, up_kept, up_got, g_down = refs[4:11]
    wg, wu, wd, h_all, dm, act, dg, du, e_stage, f_stage, f_send, f_core = refs[11:23]
    load_sems, store_sems, send_sems, line_sems, core_sems, back_sems = refs[23:29]
    done_sems, gate_sems, up_sems = refs[29:]
    t, j, c, x = coordinates()
    half, width = h_own.shape
    unit_count = wd.shape[0]
    strip = unit_count // 2
    rows = 2 * half
    bits = side.bit_length() - 1

    def at(tt, cc, jj=None, xx=None):
        jj, xx = j if jj is None else jj, x if xx is None else xx
        return ((tt * side + jj) * 2 + cc, xx)

    here, core, across = at(t, c), at(t, 1 - c), at(t, c, None, 1 - x)
    beside = at(t, c, j ^ (side // 2))
    others = [at((t + dt) % LINE, c) for dt in range(1, LINE)]
    loads = [
        (h_own, h_all.at[t, pl.ds(0, half)]),
        (units.at[0], wg), (units.at[1], wu), (dm_all, dm), (down, wd),
    ]
    loads = [pltpu.make_async_copy(a, b, load_sems.at[i]) for i, (a, b) in enumerate(loads)]
    for load in loads:
        load.start()
    greet(others + [core, across] + ([beside] if bits else []))
    sends = Sends(send_sems)

    def own_rows(tt):
        return h_all.at[tt, pl.ds(0, half)]

    def to_core(tt, cond):
        sends.start(
            own_rows(tt), h_all.at[tt, pl.ds(half, half)], core_sems.at[tt], core, cond
        )

    loads[0].wait()
    sends.start(own_rows(t), own_rows(t), line_sems.at[t], at(t + 1, c), t < LINE - 1)
    sends.start(own_rows(t), own_rows(t), line_sems.at[t], at(t - 1, c), t > 0)
    to_core(t, None)
    for load in loads[1:]:
        load.wait()

    tile = min(512, unit_count)
    wide = min(1024, width)
    e_stores, f_sent, stores = [], [], []

    def store(source, target):
        copy = pltpu.make_async_copy(source, target, store_sems.at[len(stores)])
        copy.start()
        stores.append(copy)
        return copy

    for k in range(LINE):
        tt = slot_place(t, k)
        if k:
            for cond, place_of, forward, target in (
                (t >= k, t - k, t < LINE - 1, t + 1),
                (t + k < LINE, t + k, t > 0, t - 1),
            ):
                when(
                    cond,
                    lambda p=place_of: arrived(own_rows(p), line_sems.at[p], here),
                )
                if k < LINE - 1:
                    sends.start(
                        own_rows(place_of), own_rows(place_of), line_sems.at[place_of],
                        at(target, c), jnp.logical_and(cond, forward),
                    )
                to_core(place_of, cond)
        arrived(h_all.at[tt, pl.ds(half, half)], core_sems.at[tt], here)
        if k >= 2:
            f_sent[k - 2]()

        @pl.loop(0, unit_count // tile)
        def _(i):
            cols = pl.ds(pl.multiple_of(i * tile, tile), tile)
            hidden = h_all[tt]
            gate = mm(hidden, wg[:, cols])
            up = mm(hidden, wu[:, cols])
            grad_act = mm_nt(dm[tt], wd[cols, :])
            sigma = lax.logistic(gate)
            silu = gate * sigma
            act[tt, :, cols] = (silu * up).astype(BF)
            dg[tt, :, cols] = (grad_act * up * (sigma * (1.0 + gate * (1.0 - sigma)))).astype(BF)
            du[tt, :, cols] = (grad_act * silu).astype(BF)

        slot = k % 2

        @pl.loop(0, width // wide)
        def _(i):
            span = pl.ds(pl.multiple_of(i * wide, wide), wide)
            grad = mm_nt(dg[tt], wg[span, :]) + mm_nt(du[tt], wu[span, :])
            f_stage[k, :, span] = grad[:half].astype(BF)
            f_send[slot, :, span] = grad[half:].astype(BF)

        sends.start(f_send.at[slot], f_core.at[k], back_sems.at[k], core)
        f_sent.append(lambda copy=sends.made.pop()[1]: copy().wait_send())
        sends.made.append((None, None))
        if k:
            e_stores[k - 1].wait()

        @pl.loop(0, width // wide)
        def _(i):
            span = pl.ds(pl.multiple_of(i * wide, wide), wide)
            e_stage[:, span] = mm(act[tt], wd[:, span]).astype(BF)

        e_stores.append(store(e_stage, e_out.at[tt]))
        arrived(f_core.at[k], back_sems.at[k], here)

        @pl.loop(0, 4)
        def _(i):
            part = pl.ds(pl.multiple_of(i * (half // 4), half // 4), half // 4)
            f_stage[k, part, :] = (
                f_stage[k, part, :].astype(F32) + f_core[k, part, :].astype(F32)
            ).astype(BF)

        if k == 0:
            store(f_stage.at[0], f_out.at[t])
        else:
            sends.start(f_stage.at[k], f_out.at[t], done_sems.at[t], at(tt, c))

    group = width // LINE
    far = pl.ds(pl.multiple_of((1 - x) * strip, strip), strip)
    near = pl.ds(pl.multiple_of(x * strip, strip), strip)

    def weight_grad(target, grads, tt, send):
        @pl.loop(0, 1)
        def _(i):
            span = pl.ds(tt * group, group)
            hidden = h_all[:, :, span].reshape(LINE * rows, group)
            target[span, :] = mm_tn(hidden, grads[...].reshape(LINE * rows, unit_count)).astype(BF)

        send(tt)

    block = group // side

    def send_gate(tt):
        span = pl.ds(tt * group, group)
        sends.start(wg.at[span, far], gate_got.at[span], gate_sems.at[tt], across)
        store(wg.at[span, near], gate_kept.at[span])

    def send_up(tt):
        for r in range(side):
            span = pl.ds(pl.multiple_of(tt * group + (j ^ r) * block, block), block)
            if r >= side // 2:
                k = r - side // 2
                sends.start(wu.at[span], up_got.at[k, tt], up_sems.at[k, tt], beside)
            else:
                store(wu.at[span], up_kept.at[r, tt])

    for tt in range(LINE):
        weight_grad(wg, dg, tt, send_gate)
        weight_grad(wu, du, tt, send_up)
    tile = min(256, unit_count)

    @pl.loop(0, unit_count // tile)
    def _(i):
        cols = pl.ds(pl.multiple_of(i * tile, tile), tile)
        units_part = act[:, :, cols].reshape(LINE * rows, tile)
        wd[cols, :] = mm_tn(units_part, dm[...].reshape(LINE * rows, width)).astype(BF)

    store(wd, g_down)
    for sent in f_sent[LINE - 2 :]:
        sent()
    sends.made = [item for item in sends.made if item[1] is not None]
    sends.wait_sent()
    for copy in stores:
        if all(copy is not early for early in e_stores[:-1]):
            copy.wait()
    for dt in range(1, LINE):
        p = (t + dt) % LINE
        arrived(f_out.at[p], done_sems.at[p], here)
    for tt in range(LINE):
        arrived(gate_got.at[pl.ds(tt * group, group)], gate_sems.at[tt], here)
        for k in range(side // 2):
            arrived(up_got.at[k, tt], up_sems.at[k, tt], here)


def feed_forward(side, h_own, dm_all, units, down):
    half, width = h_own.shape
    unit_count = down.shape[0]
    strip = unit_count // 2
    rows = 2 * half
    group = width // LINE
    block = group // side
    any_space = pl.BlockSpec(memory_space=pl.ANY)
    outs = [
        (LINE, rows, width),
        (LINE, half, width),
        (width, strip),
        (width, strip),
        (side // 2, LINE, block, unit_count),
        (side // 2, LINE, block, unit_count),
        (unit_count, width),
    ]
    held = [
        (width, unit_count), (width, unit_count), (unit_count, width),
        (LINE, rows, width), (LINE, rows, width),
        (LINE, rows, unit_count), (LINE, rows, unit_count), (LINE, rows, unit_count),
        (rows, width), (LINE, half, width), (2, half, width), (LINE, half, width),
    ]
    sends = 3 + 4 * (LINE - 1) + 2 * LINE + LINE + side // 2 * LINE
    return pl.pallas_call(
        functools.partial(feed_kernel, side),
        out_shape=[jax.ShapeDtypeStruct(shape, BF) for shape in outs],
        in_specs=[any_space] * 4,
        out_specs=[any_space] * 7,
        scratch_shapes=[pltpu.VMEM(shape, BF) for shape in held]
        + [
            pltpu.SemaphoreType.DMA((5,)),
            pltpu.SemaphoreType.DMA((2 * LINE + 2 + side // 2 * LINE,)),
            pltpu.SemaphoreType.DMA((sends,)),
            pltpu.SemaphoreType.DMA((LINE,)),
            pltpu.SemaphoreType.DMA((LINE,)),
            pltpu.SemaphoreType.DMA((LINE,)),
            pltpu.SemaphoreType.DMA((LINE,)),
            pltpu.SemaphoreType.DMA((LINE,)),
            pltpu.SemaphoreType.DMA((side // 2, LINE)),
        ],
        compiler_params=pltpu.CompilerParams(
            collective_id=1, has_side_effects=True, vmem_limit_bytes=63 << 20
        ),
        cost_estimate=pl.CostEstimate(
            flops=18 * LINE * rows * width * unit_count, bytes_accessed=100 << 20,
            transcendentals=LINE * rows * unit_count,
        ),
    )(h_own, dm_all, units, down)


def sum_kernel(side, piece, *refs):
    g_qkv, gate, gate_got, up, up_got, down, down_got, small = refs[:8]
    q_out, k_out, v_out, gate_out, up_out, down_out, small_out = refs[8:15]
    (
        heads, heads_core, heads_side, line_right, line_left,
        gates, gates_got, gates_side, ups, ups_got, ups_across,
        downs, downs_got, downs_across, homes, smalls,
    ) = refs[15:31]
    load_sems, send_sems, core_sems, side_sems, line_sems, gate_sems, across_sems = refs[31:38]
    home_sems, small_sems = refs[38:]
    t, j, c, x = coordinates()
    bits = side.bit_length() - 1
    depth, q_cols = q_out.shape
    k_cols = k_out.shape[1]
    strip = side * piece

    def at(tt, jj, cc, xx=None):
        return (((tt * side) + jj) * 2 + cc, x if xx is None else xx)

    def block(tt, jj, cc):
        return ((tt * side) + jj) * 2 + cc

    here, core, across = at(t, j, c), at(t, j, 1 - c), at(t, j, c, 1 - x)
    beside = [at(t, j ^ (1 << bit), c) for bit in range(bits)]
    others = [
        at((t + dt) % LINE, j, c ^ dc) for dt in range(LINE) for dc in range(2) if dt or dc
    ]
    near_col = pl.multiple_of(x * strip, strip)
    loads = [
        (g_qkv, heads),
        (gate, gates),
        (gate_got, gates_got),
        (up, ups),
        (up_got, ups_got),
        (down, downs),
        (down_got, downs_got),
        (small, smalls.at[0]),
    ]
    loads = [pltpu.make_async_copy(a, b, load_sems.at[i]) for i, (a, b) in enumerate(loads)]
    for load in loads:
        load.start()
    greet(others + beside + [across])
    sends = Sends(send_sems)

    def add(target, first, second):
        count = first.shape[0]
        step = min(64, count)

        @pl.loop(0, count // step)
        def _(i):
            part = pl.ds(pl.multiple_of(i * step, step), step)
            target[part, :] = (first[part, :].astype(F32) + second[part, :].astype(F32)).astype(
                target.dtype
            )

    loads[0].wait()
    for q in reversed(range(LINE)):
        tt = slot_place(t, q)
        for r in range(side):
            sends.start(
                heads.at[block(tt, j ^ r, 1 - c)], heads_core.at[tt, j ^ r],
                core_sems.at[tt, j ^ r], core,
            )
    loads[1].wait()
    loads[2].wait()
    for tt in range(LINE):
        for jj in range(side):
            add(gates.at[tt, jj], gates.at[tt, jj], gates_got.at[tt, jj])
    for bit in reversed(range(bits)):
        half = 1 << bit
        if bit < bits - 1:
            for r in range(half * 2):
                arrived(gates_side.at[2 * half - 1 + r], gate_sems.at[2 * half - 1 + r], here)
                for tt in range(LINE):
                    add(
                        gates.at[tt, j ^ r], gates.at[tt, j ^ r],
                        gates_side.at[2 * half - 1 + r, tt],
                    )
        for r in range(half, 2 * half):
            sends.start(
                gates.at[:, j ^ r], gates_side.at[half - 1 + r - half],
                gate_sems.at[half - 1 + r - half], beside[bit],
            )
    loads[5].wait()
    loads[6].wait()
    for xx in range(2):
        add(downs.at[xx], downs.at[xx], downs_got.at[xx])
    loads[3].wait()
    loads[4].wait()
    for tt in range(LINE):
        add(ups.at[tt], ups.at[tt], ups_got.at[tt])
    far_col = pl.multiple_of((1 - x) * strip, strip)
    sends.start(
        ups.at[:, :, pl.ds(far_col, strip)], ups_across, across_sems.at[0], across
    )
    sends.start(downs.at[1 - x], downs_across, across_sems.at[1], across)

    loads[7].wait()
    partners = [core] + beside + [across, at(t ^ 1, j, c), at(t ^ 2, j, c)]

    def small_step(i):
        if i:
            arrived(smalls.at[2 * i], small_sems.at[i - 1], here)
            smalls[2 * i - 1] = smalls[max(2 * i - 3, 0)] + smalls[2 * i]
        if i < len(partners):
            source = smalls.at[2 * i - 1] if i else smalls.at[0]
            sends.start(source, smalls.at[2 * i + 2], small_sems.at[i], partners[i])
        return i + 1

    def side_first(q):
        tt = slot_place(t, q)
        for r in reversed(range(side)):
            arrived(heads_core.at[tt, j ^ r], core_sems.at[tt, j ^ r], here)
            mine = heads.at[block(tt, j ^ r, c)]
            add(mine, mine, heads_core.at[tt, j ^ r])
            if bits and r >= side // 2:
                k = side // 2 - 1 + r - side // 2
                sends.start(mine, heads_side.at[tt, k], side_sems.at[tt, k], beside[bits - 1])

    def side_rest(q):
        tt = slot_place(t, q)
        for bit in reversed(range(bits)):
            half = 1 << bit
            for r in range(half):
                arrived(heads_side.at[tt, half - 1 + r], side_sems.at[tt, half - 1 + r], here)
                mine = heads.at[block(tt, j ^ r, c)]
                add(mine, mine, heads_side.at[tt, half - 1 + r])
                if bit and r >= half // 2:
                    k = half // 2 - 1 + r - half // 2
                    sends.start(
                        mine, heads_side.at[tt, k], side_sems.at[tt, k], beside[bit - 1]
                    )
        return heads.at[block(tt, j, c)]

    def line_came(i, way, cond, target):
        line = (line_right, line_left)[way]

        def act():
            arrived(line.at[i], line_sems.at[way, i], here)
            add(target, target, line.at[i])

        when(cond, act)

    def line_go(i, way, cond, source):
        line = (line_right, line_left)[way]
        sends.start(
            source, line.at[i], line_sems.at[way, i], at(t + 1 - 2 * way, j, c), cond
        )

    step = small_step(0)
    side_first(3)
    side_first(2)
    step = small_step(step)
    p3 = side_rest(3)
    line_go(0, 0, t == 0, p3)
    line_go(0, 1, t == 3, p3)
    side_first(1)
    step = small_step(step)
    p2 = side_rest(2)
    line_came(0, 0, t == 1, p2)
    line_came(0, 1, t == 2, p2)
    line_go(1, 0, t <= 1, p2)
    line_go(1, 1, t >= 2, p2)
    side_first(0)

    def go_home(which, rows):
        for tt in range(LINE):
            for cc in range(2):
                mine = jnp.logical_and(t == tt, c == cc)
                source = rows(tt).at[pl.ds(cc * depth, depth)]
                target = homes.at[which, t * 2 + c]
                sends.start(
                    source, target, home_sems.at[which, t * 2 + c], at(tt, j, cc),
                    jnp.logical_not(mine),
                )

                @pl.when(mine)
                def _():
                    homes[which, tt * 2 + cc] = source[...]

    if bits:
        arrived(gates_side.at[0], gate_sems.at[0], here)
        for tt in range(LINE):
            add(gates.at[tt, j], gates.at[tt, j], gates_side.at[0, tt])
    go_home(0, lambda tt: gates.at[tt, j])
    step = small_step(step)
    p1 = side_rest(1)
    line_came(1, 0, jnp.logical_and(t >= 1, t <= 2), p3)
    line_came(1, 1, jnp.logical_and(t >= 1, t <= 2), p1)
    line_go(2, 0, t == 0, p1)
    line_go(2, 0, jnp.logical_and(t >= 1, t <= 2), p3)
    line_go(2, 1, t >= 1, p1)
    arrived(ups_across, across_sems.at[0], here)
    for tt in range(LINE):
        add(ups_across.at[tt], ups.at[tt, :, pl.ds(near_col, strip)], ups_across.at[tt])
    go_home(1, lambda tt: ups_across.at[tt])
    while step <= len(partners):
        step = small_step(step)
    small_out[...] = smalls[2 * len(partners) - 1]
    arrived(downs_across, across_sems.at[1], here)
    add(down_out, downs.at[x], downs_across)
    p0 = side_rest(0)
    line_came(2, 0, t >= 1, p0)
    line_came(2, 1, t <= 2, p0)
    q_out[...] = p0[:, pl.ds(0, q_cols)].astype(F32)
    k_out[...] = p0[:, pl.ds(q_cols, k_cols)].astype(F32)
    v_out[...] = p0[:, pl.ds(q_cols + k_cols, k_cols)].astype(F32)
    for which, out in enumerate((gate_out, up_out)):
        for tt in range(LINE):
            for cc in range(2):
                mine = jnp.logical_and(t == tt, c == cc)
                source = homes.at[which, tt * 2 + cc]
                when(
                    jnp.logical_not(mine),
                    lambda w=which, k=tt * 2 + cc, ref=source: arrived(
                        ref, home_sems.at[w, k], here
                    ),
                )
                for jj in range(side):
                    out[:, pl.ds(block(tt, jj, cc) * piece, piece)] = source[
                        :, pl.ds(jj * piece, piece)
                    ].astype(F32)
    sends.wait_sent()


def sum_gradients(n, piece, q_cols, g_qkv, gate, gate_got, up, up_got, down, down_got, small):
    side = n // LINE // 2
    bits = side.bit_length() - 1
    _, depth, cols = g_qkv.shape
    k_cols = (cols - q_cols) // 2
    strip = side * piece
    width = down.shape[-1]
    any_space = pl.BlockSpec(memory_space=pl.ANY)
    steps = bits + 4
    held = [
        (n, depth, cols), (LINE, side, depth, cols), (LINE, max(side - 1, 1), depth, cols),
        (3, depth, cols), (3, depth, cols),
        (LINE, side, 2 * depth, strip), (LINE, side, 2 * depth, strip),
        (max(side - 1, 1), LINE, 2 * depth, strip),
        (LINE, 2 * depth, 2 * strip), (LINE, 2 * depth, 2 * strip), (LINE, 2 * depth, strip),
        (2, piece, width), (2, piece, width), (piece, width),
        (2, LINE * 2, depth, strip),
    ]
    sends = LINE * (2 * side - 1) + side + 2 + steps + 8 + 4 * LINE + 4
    return pl.pallas_call(
        functools.partial(sum_kernel, side, piece),
        out_shape=[
            jax.ShapeDtypeStruct((depth, q_cols), F32),
            jax.ShapeDtypeStruct((depth, k_cols), F32),
            jax.ShapeDtypeStruct((depth, k_cols), F32),
            jax.ShapeDtypeStruct((depth, LINE * 2 * strip), F32),
            jax.ShapeDtypeStruct((depth, LINE * 2 * strip), F32),
            jax.ShapeDtypeStruct((piece, width), F32),
            jax.ShapeDtypeStruct(small.shape, F32),
        ],
        in_specs=[any_space] * 8,
        scratch_shapes=[pltpu.VMEM(shape, BF) for shape in held]
        + [pltpu.VMEM((2 * steps + 1,) + small.shape, F32)]
        + [
            pltpu.SemaphoreType.DMA((8,)),
            pltpu.SemaphoreType.DMA((sends,)),
            pltpu.SemaphoreType.DMA((LINE, side)),
            pltpu.SemaphoreType.DMA((LINE, max(side - 1, 1))),
            pltpu.SemaphoreType.DMA((2, 3)),
            pltpu.SemaphoreType.DMA((max(side - 1, 1),)),
            pltpu.SemaphoreType.DMA((2,)),
            pltpu.SemaphoreType.DMA((2, LINE * 2)),
            pltpu.SemaphoreType.DMA((steps,)),
        ],
        compiler_params=pltpu.CompilerParams(
            collective_id=2, has_side_effects=True, vmem_limit_bytes=60 << 20
        ),
        cost_estimate=pl.CostEstimate(flops=0, bytes_accessed=400 << 20, transcendentals=0),
    )(g_qkv, gate, gate_got, up, up_got, down, down_got, small)


class Links:
    def __init__(self, n):
        self.n = n
        self.inner = n // LINE
        self.side = self.inner // 2
        self.side_bits = self.side.bit_length() - 1
        self.t, self.j, self.c, self.x = coordinates()

    def core(self, value):
        return lax.ppermute(value, "dp", [(i, i ^ 1) for i in range(self.n)])

    def over(self, value, bit):
        return lax.ppermute(value, "dp", [(i, i ^ (2 << bit)) for i in range(self.n)])

    def cross(self, value):
        return lax.ppermute(value, "tensor", [(0, 1), (1, 0)])

    def along(self, value, moves):
        pairs = [
            (a * self.inner + i, b * self.inner + i) for a, b in moves for i in range(self.inner)
        ]
        return lax.ppermute(value, "dp", pairs)

    def right(self, value, senders):
        return self.along(value, [(a, a + 1) for a in senders])

    def left(self, value, senders):
        return self.along(value, [(a, a - 1) for a in senders])

    def turn(self, value, shift):
        return self.along(value, [(a, (a + shift) % LINE) for a in range(LINE)])

    def line_gather(self, value):
        t = self.t
        r1 = self.right(value, (0, 1, 2))
        l1 = self.left(value, (1, 2, 3))
        r2 = self.right(r1, (1, 2))
        l2 = self.left(l1, (1, 2))
        r3 = self.right(r2, (2,))
        l3 = self.left(l2, (1,))
        return (
            value,
            jnp.where(t == 0, l1, r1),
            jnp.where(t < 2, l2, r2),
            jnp.where(t == 0, l3, jnp.where(t == 3, r3, l1)),
        )

    def lines(self):
        return [[i + k * self.inner for k in range(LINE)] for i in range(self.inner)]

    def line_all(self, value):
        return lax.all_gather(value, "dp", axis_index_groups=self.lines())

    def line_sum(self, value):
        return lax.psum_scatter(
            value, "dp", scatter_dimension=0, axis_index_groups=self.lines()
        )

    def dp_sum(self, value):
        return lax.psum_scatter(value, "dp", scatter_dimension=0, tiled=True)

    def line_scatter(self, parts):
        t = self.t
        p0, p1, p2, p3 = parts
        first = p3.astype(BF)
        r1 = self.right(first, (0,))
        l1 = self.left(first, (3,))
        second = (p2 + r1.astype(F32) + l1.astype(F32)).astype(BF)
        r2 = self.right(second, (0, 1))
        l2 = self.left(second, (2, 3))
        r3 = self.right((jnp.where(t == 0, p1, p3) + r2.astype(F32)).astype(BF), (0, 1, 2))
        l3 = self.left((p1 + l2.astype(F32)).astype(BF), (1, 2, 3))
        return p0 + r3.astype(F32) + l3.astype(F32)

    def line_send(self, parts):
        p0, p1, p2, p3 = parts
        first, second, third = p1.astype(BF), p2.astype(BF), p3.astype(BF)
        got = [
            self.left(first, (1, 2, 3)),
            self.right(first, (0,)),
            self.turn(second, 2),
            self.along(third, ((0, 3), (3, 0))),
            self.right(third, (1, 2)),
        ]
        return p0 + sum(g.astype(F32) for g in got)

    def side_all(self, value):
        blocks = [value]
        for bit in range(self.side_bits):
            blocks += [self.over(block, bit) for block in blocks]
        return blocks

    def side_sum(self, blocks):
        for bit in reversed(range(self.side_bits)):
            width = 1 << bit
            blocks = [
                a.astype(F32) + self.over(b.astype(BF), bit).astype(F32)
                for a, b in zip(blocks[:width], blocks[width:])
            ]
        return blocks[0]

    def side_start(self, blocks):
        for bit in reversed(range(1, len(blocks).bit_length() - 1)):
            half = 1 << bit
            blocks = [
                (a.astype(F32) + self.over(b, bit).astype(F32)).astype(BF)
                for a, b in zip(blocks[:half], blocks[half:])
            ]
        return blocks[0], self.over(blocks[1], 0)

    def side_end(self, kept, got):
        if kept.shape[0] == 1:
            return kept[0], got[0]
        total = (kept.astype(F32) + got.astype(F32)).astype(BF)
        return self.side_start(list(total))

    def pair_order(self, mine, other, where):
        low = jnp.where(where == 0, mine, other)
        high = jnp.where(where == 0, other, mine)
        return jnp.concatenate([low, high], 0)

    def pick(self, value, index, axis):
        return lax.dynamic_index_in_dim(value, index, axis, keepdims=False)

    def cross_sum(self, value, axis):
        kept = self.pick(value, self.x, axis)
        sent = self.pick(value, 1 - self.x, axis)
        return kept.astype(F32) + self.cross(sent.astype(BF)).astype(F32)

    def gather_rows(self, blocks):
        rows, cols = blocks[0].shape
        pieces, where = [], []
        for k, block in enumerate(blocks):
            for r, piece in enumerate(self.side_all(block)):
                pieces += [piece, self.core(piece)]
                where += [(k, r, 0), (k, r, 1)]

        def spots(t, j, c, x):
            return [
                (
                    i, 0, 0, rows, cols,
                    (((slot_place(t, k) * self.side) + (j ^ r)) * 2 + (c ^ s)) * rows, 0,
                )
                for i, (k, r, s) in enumerate(where)
            ]

        return place(pieces, spots, (self.n * rows, cols))

    def sum_rows(self, value):
        rows, cols = value.shape[0] // self.n, value.shape[1]
        parts = value.reshape(LINE, self.side, 2, rows, cols)
        kept = self.pick(parts, self.c, 2).astype(F32)
        parts = kept + self.core(self.pick(parts, 1 - self.c, 2)).astype(F32)
        parts = parts.astype(BF)
        parts = self.side_sum([self.pick(parts, self.j ^ r, 1) for r in range(self.side)])
        return self.line_scatter(
            [self.pick(parts, slot_place(self.t, k), 0).astype(F32) for k in range(LINE)]
        )

    def total(self, value):
        value = value + self.core(value)
        for bit in range(self.side_bits):
            value = value + self.over(value, bit)
        value = value + self.cross(value)
        value = value + self.along(value, ((0, 1), (1, 0), (2, 3), (3, 2)))
        return value + self.turn(value, 2)


def make_body(n):
    def body(
        tokens,
        cotangent,
        lengths,
        attn_gain,
        query_gain,
        key_gain,
        w_query,
        key_weight_matrix,
        value_weight_matrix,
        w_out,
        ffn_gain,
        w_gate,
        w_up,
        w_down,
    ):
        net = Links(n)
        t, j, c, x = net.t, net.j, net.c, net.x
        row_count, width = tokens.shape
        half = row_count // 2
        head_dim = query_gain.shape[0]
        q_cols = w_query.shape[1]
        k_cols = key_weight_matrix.shape[1]
        k_heads = k_cols // head_dim
        dp_index = lax.axis_index("dp")
        slot_length = lengths[dp_index]

        depth = w_gate.shape[0]
        piece = w_down.shape[0]
        side = net.side
        strip = side * piece
        start = x * half
        half_positions = start + jnp.arange(half, dtype=jnp.int32)
        half_valid = (half_positions < slot_length)[:, None]
        grad_half = lax.dynamic_slice_in_dim(cotangent, start, half, 0)
        grad_half = jnp.where(half_valid, grad_half, jnp.zeros_like(grad_half))
        tables = angle_tables(row_count, head_dim, LANES)
        gains = [jnp.tile(gain, LANES // head_dim)[None, :] for gain in (query_gain, key_gain)]
        inputs = tokens.astype(F32)
        input_half = lax.dynamic_slice_in_dim(tokens, start, half, 0)
        hidden_state = rms_scale(inputs, attn_gain).astype(BF)
        length = slot_length[None]
        weights = (w_query, key_weight_matrix, value_weight_matrix, w_out, w_gate, w_up, w_down)
        (
            qkv_full, wo_full, units, wd, grad_all, qkv, o_low, log_totals, h_one, hidden_two,
        ) = start_layer(
            n, weights, grad_half, length, hidden_state, input_half, tables, gains, ffn_gain
        )

        out_parts, grad_parts, gate_kept, gate_got, up_kept, up_got, g_down = feed_forward(
            side, hidden_two, grad_all, units.reshape(2, width, 2 * strip),
            wd.reshape(2 * strip, width),
        )
        grad_hidden_two = jnp.sum(grad_parts.astype(F32), axis=0)
        out_mine = out_parts[:, :half].astype(F32) + net.core(out_parts[:, half:]).astype(F32)
        out_sum = net.line_sum(out_mine.astype(BF))
        norm_two_back = jax.vjp(rms_scale, h_one, ffn_gain)[1]
        grad_h_part, g_ffn_part = norm_two_back(grad_hidden_two)
        grad_h_one = grad_half.astype(F32) + grad_h_part
        grad_attn_half = grad_h_one.astype(BF)
        grad_attn_low = net.pair_order(grad_attn_half, net.cross(grad_attn_half), x)

        near = (LINE, side, 2 * depth, strip)
        gate_kept, gate_got = gate_kept.reshape(near), gate_got.reshape(near)
        up_kept, up_got = net.side_end(up_kept, up_got)
        g_down = g_down.reshape(2, side, piece, width)
        down_kept, down_got = net.side_start([net.pick(g_down, j ^ r, 1) for r in range(side)])

        g_out = mm_tn(o_low, grad_attn_low).astype(BF)
        grad_o_low = mm_nt(grad_attn_low, wo_full).astype(BF)
        grad_q, grad_k, grad_v, q_part, k_part = attend_back(
            length, qkv, tables, gains, log_totals, grad_o_low, q_cols, k_heads
        )
        g_query_part = q_part.reshape(-1, head_dim).sum(0)
        g_key_part = k_part.reshape(-1, head_dim).sum(0)
        grad_qkv = jnp.concatenate([grad_q, grad_k, grad_v], axis=1)
        g_qkv = mm_tn(hidden_state, grad_qkv).astype(BF)
        g_out_out = net.dp_sum(g_out).astype(F32)
        layer_half = (h_one + after(g_qkv, out_sum).astype(F32)).astype(BF)
        layer_out = net.pair_order(layer_half, net.cross(layer_half), x)
        grad_hidden = mm_nt(grad_qkv, qkv_full)
        g_attn_part = jnp.sum(grad_hidden * rms_scale(inputs, 1.0), axis=0)
        low_hidden = grad_hidden.astype(BF)
        grad_hidden = low_hidden.astype(F32) + net.cross(low_hidden).astype(F32)
        small = jnp.concatenate([g_attn_part, g_ffn_part, g_query_part, g_key_part])
        small = small.reshape(-1, LANES)
        g_query_w, g_key_w, g_value_w, g_gate_out, g_up_out, g_down_out, small = sum_gradients(
            n, piece, q_cols, g_qkv.reshape(n, depth, q_cols + 2 * k_cols),
            gate_kept, gate_got, up_kept, up_got, down_kept, down_got, small,
        )
        small = small.reshape(-1)
        grad_in = jax.vjp(lambda v: rms_scale(v, attn_gain), inputs)[1](grad_hidden)[0]
        input_grad = grad_attn_low.astype(F32) + grad_in
        return (
            layer_out,
            input_grad,
            small[:width],
            small[2 * width : 2 * width + head_dim],
            small[2 * width + head_dim :],
            g_query_w,
            g_key_w,
            g_value_w,
            g_out_out,
            small[width : 2 * width],
            g_gate_out,
            g_up_out,
            g_down_out,
        )

    return body


def solution(mesh):
    placed = (
        P("dp", None),
        P("dp", None),
        P(),
        P(),
        P(),
        P(),
        P("dp", "tensor"),
        P("dp", "tensor"),
        P("dp", "tensor"),
        P(("tensor", "dp"), None),
        P(),
        P("dp", "tensor"),
        P("dp", "tensor"),
        P(("tensor", "dp"), None),
    )
    return jax.shard_map(
        make_body(mesh.shape["dp"]),
        mesh=mesh,
        in_specs=placed,
        out_specs=(
            P("dp", None),
            P("dp", None),
            P(),
            P(),
            P(),
            P("dp", "tensor"),
            P("dp", "tensor"),
            P("dp", "tensor"),
            P(("tensor", "dp"), None),
            P(),
            P("dp", "tensor"),
            P("dp", "tensor"),
            P(("tensor", "dp"), None),
        ),
        check_vma=False,
    )
```

```python
import functools
import math

import jax
import jax.numpy as jnp
import numpy as np
from jax import lax
from jax.experimental import pallas as pl
from jax.experimental.pallas import tpu as pltpu
from jax.sharding import PartitionSpec as P

EPS = 1e-05
ROPE_BASE = 1000000.0
MASKED = -1e30
LINE = 4
BF = jnp.bfloat16
F32 = jnp.float32


def rms_scale(values, gain):
    return values * lax.rsqrt(jnp.mean(values * values, axis=-1, keepdims=True) + EPS) * gain


def angle_tables(count, head_dim, lanes):
    half_dim = head_dim // 2
    freq = ROPE_BASE ** (np.arange(half_dim) * (-2.0 / head_dim))
    turned = np.arange(count)[:, None] * freq[None, :]
    cosine, sine = np.cos(turned).astype(np.float32), np.sin(turned).astype(np.float32)
    repeats = lanes // head_dim
    return (
        jnp.asarray(np.tile(np.concatenate([cosine, cosine], 1), (1, repeats))),
        jnp.asarray(np.tile(np.concatenate([-sine, sine], 1), (1, repeats))),
    )


LANES = 128
HEAD = LANES // 2


def low_lanes(shape):
    return lax.broadcasted_iota(jnp.int32, shape, 1) < HEAD


def per_head(values):
    low = low_lanes(values.shape)
    first = jnp.sum(jnp.where(low, values, 0.0), axis=1, keepdims=True)
    second = jnp.sum(jnp.where(low, 0.0, values), axis=1, keepdims=True)
    return jnp.where(low, first, second) * (1.0 / HEAD)


def halves_swapped(values):
    lane = lax.broadcasted_iota(jnp.int32, values.shape, 1)
    return jnp.where(
        lane % HEAD < HEAD // 2,
        pltpu.roll(values, LANES - HEAD // 2, 1),
        pltpu.roll(values, HEAD // 2, 1),
    )


def head_norm(values):
    scale = lax.rsqrt(per_head(values * values) + EPS)
    return values * scale, scale


def head_turn(values, cosine, sine):
    return values * cosine + halves_swapped(values) * sine


def head_back(grad, normed, scale, gain, cosine, sine):
    grad = grad * cosine - halves_swapped(grad) * sine
    gain_grad = jnp.sum(grad * normed, axis=0, keepdims=True)
    grad = grad * gain
    return scale * (grad - normed * per_head(grad * normed)), gain_grad


def one_head(pair, second):
    low = low_lanes(pair.shape)
    return jnp.where(low == jnp.logical_not(second), pair, pltpu.roll(pair, HEAD, 1))


def two_rows(slab):
    low = low_lanes(slab.shape)
    return jnp.concatenate([jnp.where(low, slab, 0.0), jnp.where(low, 0.0, slab)], 0).astype(BF)


def allowed_mask(block, first_row, columns, length):
    row = lax.broadcasted_iota(jnp.int32, (2 * block, columns), 0) % block + first_row
    col = lax.broadcasted_iota(jnp.int32, (2 * block, columns), 1)
    return (col <= row) & (col < length)


def attend_kernel(
    block, scale, second, length, q, k, v, cosine, sine, q_gain, k_gain, out, totals
):
    rows = q.shape[0]
    cos, sin = cosine[...], sine[...]
    keys = one_head(head_turn(head_norm(k[...])[0] * k_gain[...], cos, sin), second).astype(BF)
    vals = one_head(v[...], second).astype(BF)
    lane = lax.broadcasted_iota(jnp.int32, (block, LANES), 1)
    for first in range(0, rows, block):
        span = pl.ds(first, block)
        seen = first + block
        allowed = allowed_mask(block, first, seen, length[0])
        kept = jnp.zeros((block, LANES), F32)
        for slab in range(q.shape[1] // LANES):
            cols = pl.ds(slab * LANES, LANES)
            turned = head_turn(
                head_norm(q[span, cols])[0] * q_gain[...], cosine[span, :], sine[span, :]
            )
            scores = mm_nt(two_rows(turned), keys[:seen]) * scale
            scores = jnp.where(allowed, scores, MASKED)
            top = jnp.max(scores, axis=1, keepdims=True)
            probs = jnp.exp(scores - top)
            total = jnp.sum(probs, axis=1, keepdims=True)
            probs = (probs * (1.0 / total)).astype(BF)
            both = mm(probs, vals[:seen])
            out[span, cols] = jnp.where(low_lanes((block, LANES)), both[:block], both[block:]).astype(
                BF
            )
            log_total = top + jnp.log(total)
            kept = jnp.where(lane == 2 * slab, log_total[:block], kept)
            kept = jnp.where(lane == 2 * slab + 1, log_total[block:], kept)
        totals[span, :] = kept


def attend_back_kernel(
    block, scale, second, length, q, k, v, cosine, sine, q_gain, k_gain, totals, grad_out,
    grad_q, grad_k, grad_v, q_gain_grad, k_gain_grad, keys_sum, vals_sum,
):
    rows = q.shape[0]
    cos, sin = cosine[...], sine[...]
    k_normed, k_scale = head_norm(k[...])
    keys = one_head(head_turn(k_normed * k_gain[...], cos, sin), second).astype(BF)
    vals = one_head(v[...], second).astype(BF)
    lane = lax.broadcasted_iota(jnp.int32, (block, LANES), 1)
    keys_sum[...] = jnp.zeros_like(keys_sum)
    vals_sum[...] = jnp.zeros_like(vals_sum)

    for first in range(0, rows, block):
        span = pl.ds(first, block)
        seen = first + block
        allowed = allowed_mask(block, first, seen, length[0])
        kept = totals[span, :]
        for slab in range(q.shape[1] // LANES):
            cols = pl.ds(slab * LANES, LANES)
            q_normed, q_scale = head_norm(q[span, cols])
            turned = two_rows(head_turn(q_normed * q_gain[...], cosine[span, :], sine[span, :]))
            log_total = jnp.concatenate(
                [
                    jnp.sum(jnp.where(lane == 2 * slab + i, kept, 0.0), axis=1, keepdims=True)
                    for i in range(2)
                ],
                0,
            )
            scores = mm_nt(turned, keys[:seen]) * scale
            probs = jnp.exp(jnp.where(allowed, scores, MASKED) - log_total)
            grad_rows = two_rows(grad_out[span, cols].astype(F32))
            grad_probs = mm_nt(grad_rows, vals[:seen])
            drop = jnp.sum(probs * grad_probs, axis=1, keepdims=True)
            grad_scores = (probs * (grad_probs - drop)).astype(BF)
            both = mm(grad_scores, keys[:seen]) * scale
            grad_turned = jnp.where(low_lanes((block, LANES)), both[:block], both[block:])
            grad_proj, gain_part = head_back(
                grad_turned, q_normed, q_scale, q_gain[...], cosine[span, :], sine[span, :]
            )
            grad_q[span, cols] = grad_proj.astype(BF)
            q_gain_grad[...] += gain_part
            keys_sum[:seen] += mm_tn(grad_scores, turned)
            vals_sum[:seen] += mm_tn(probs.astype(BF), grad_rows)

    keys_grad = keys_sum[...] * scale
    keys_grad = keys_grad + pltpu.roll(keys_grad, HEAD, 1)
    vals_grad = vals_sum[...]
    vals_grad = vals_grad + pltpu.roll(vals_grad, HEAD, 1)
    grad_proj, gain_part = head_back(
        keys_grad,
        one_head(k_normed, second),
        one_head(k_scale, second),
        k_gain[...],
        cos,
        sin,
    )
    k_gain_grad[...] += gain_part * 0.5
    keep_low = low_lanes(grad_k.shape)

    @pl.when(jnp.logical_not(second))
    def _():
        grad_k[...] = grad_proj.astype(BF)
        grad_v[...] = vals_grad.astype(BF)

    @pl.when(second)
    def _():
        grad_k[...] = jnp.where(keep_low, grad_k[...].astype(F32), grad_proj).astype(BF)
        grad_v[...] = jnp.where(keep_low, grad_v[...].astype(F32), vals_grad).astype(BF)


def mm(left, right):
    return jnp.dot(left, right, preferred_element_type=F32)


def mm_nt(left, right):
    return lax.dot_general(left, right, (((1,), (1,)), ((), ())), preferred_element_type=F32)


def mm_tn(left, right):
    return lax.dot_general(left, right, (((0,), (0,)), ((), ())), preferred_element_type=F32)


def after(done, *values):
    held, _ = lax.optimization_barrier((values, done))
    return held if len(held) > 1 else held[0]


def slot_place(t, k):
    if k == 0:
        return t
    if k == 1:
        return jnp.where(t == 0, 1, t - 1)
    if k == 2:
        return (t + 2) % LINE
    return jnp.where(t == 3, 0, jnp.where(t == 1, 2, 3))


def coordinates():
    n = lax.axis_size("dp")
    inner = n // LINE
    here = lax.axis_index("dp")
    return here // inner, (here % inner) // 2, here % 2, lax.axis_index("tensor")


def place(blocks, spots, shape):
    listed = spots(0, 0, 0, 0)

    def kernel(*refs):
        sources = refs[: len(blocks)]
        out, held, sem, out_sem = refs[len(blocks) :]
        copies = []
        for k, (b, row, col, rows, cols, to_row, to_col) in enumerate(spots(*coordinates())):
            copies.append(
                pltpu.make_async_copy(
                    sources[b].at[pl.ds(row, rows), pl.ds(col, cols)],
                    held.at[
                        pl.ds(pl.multiple_of(to_row, rows), rows),
                        pl.ds(pl.multiple_of(to_col, cols), cols),
                    ],
                    sem.at[k],
                )
            )
        for copy in copies:
            copy.start()
        for copy in copies:
            copy.wait()
        last = pltpu.make_async_copy(held, out, out_sem)
        last.start()
        last.wait()

    item = blocks[0].dtype.itemsize
    moved = sum(2 * rows * cols * item for _, _, _, rows, cols, _, _ in listed)
    return pl.pallas_call(
        kernel,
        out_shape=jax.ShapeDtypeStruct(shape, blocks[0].dtype),
        in_specs=[pl.BlockSpec(memory_space=pl.ANY)] * len(blocks),
        out_specs=pl.BlockSpec(memory_space=pl.ANY),
        scratch_shapes=[
            pltpu.VMEM(shape, blocks[0].dtype),
            pltpu.SemaphoreType.DMA((len(listed),)),
            pltpu.SemaphoreType.DMA,
        ],
        compiler_params=pltpu.CompilerParams(vmem_limit_bytes=moved // 2 + (4 << 20)),
        cost_estimate=pl.CostEstimate(flops=0, bytes_accessed=moved, transcendentals=0),
    )(*blocks)


class Sends:
    def __init__(self, sems):
        self.sems = sems
        self.made = []

    def start(self, source, target, recv_sem, device, cond=None):
        sem = self.sems.at[len(self.made)]

        def copy():
            return pltpu.make_async_remote_copy(
                src_ref=source,
                dst_ref=target,
                send_sem=sem,
                recv_sem=recv_sem,
                device_id=device,
                device_id_type=pl.DeviceIdType.MESH,
            )

        self.made.append((cond, copy))
        when(cond, lambda: copy().start())

    def wait_sent(self):
        for cond, copy in self.made:
            when(cond, lambda copy=copy: copy().wait_send())


def when(cond, act):
    if cond is None:
        act()
    else:
        pl.when(cond)(act)


def both(first, second):
    if first is None:
        return second
    return first if second is None else jnp.logical_and(first, second)


def arrived(ref, recv_sem, device):
    pltpu.make_async_remote_copy(
        src_ref=ref, dst_ref=ref, send_sem=recv_sem, recv_sem=recv_sem,
        device_id=device, device_id_type=pl.DeviceIdType.MESH,
    ).wait_recv()


def greet(devices):
    barrier = pltpu.get_barrier_semaphore()
    for device in devices:
        pl.semaphore_signal(
            barrier, inc=1, device_id=device, device_id_type=pl.DeviceIdType.MESH
        )
    pl.semaphore_wait(barrier, len(devices))


def start_kernel(side, piece, sliced, scale, *refs):
    w_query, w_key, w_value, w_out, w_gate, w_up, w_down, dm_own = refs[:8]
    length, tokens, attn_gain, cosine, sine, q_gain, k_gain, ffn_gain = refs[8:16]
    outs = refs[16:21]
    proj, attended, totals, h_one, hidden_two, hidden = refs[21:27]
    qkv, out, units, down, dm = bufs = refs[27:32]
    part, cross_sent, cross_got = refs[32:35]
    (
        load_sems, send_sems, qkv_sems, out_sems, unit_sems, pair_sems, down_sems,
        line_sems, core_sems, cross_sem, store_sems,
    ) = refs[35:]
    t, j, c, x = coordinates()
    bits = side.bit_length() - 1
    strip = side * piece

    def at(tt, jj, cc, xx=None):
        return (((tt * side) + jj) * 2 + cc, x if xx is None else xx)

    def block(tt, jj, cc):
        return ((tt * side) + jj) * 2 + cc

    here = at(t, j, c)
    core = at(t, j, 1 - c)
    across = at(t, j, c, 1 - x)
    beside = [at(t, j ^ (1 << bit), c) for bit in range(bits)]
    others = [
        at((t + dt) % LINE, j, c ^ dc) for dt in range(LINE) for dc in range(2) if dt or dc
    ]
    mine = block(t, j, c)
    depth, q_cols = w_query.shape
    k_cols = w_key.shape[1]
    rows, width = tokens.shape
    half = rows // 2

    def rows_of(buf, idx):
        count = depth if buf is qkv else w_out.shape[0]
        return buf.at[pl.ds(pl.multiple_of(idx * count, count), count)]

    own_qkv = pl.ds(pl.multiple_of(mine * depth, depth), depth)
    loads = [
        (w_query, qkv.at[own_qkv, pl.ds(0, q_cols)]),
        (w_key, qkv.at[own_qkv, pl.ds(q_cols, k_cols)]),
        (w_value, qkv.at[own_qkv, pl.ds(q_cols + k_cols, k_cols)]),
        (w_out, rows_of(out, mine)),
        (w_down, down.at[x * side + j]),
        (dm_own.at[pl.ds(pl.multiple_of(x * half, half), half)], dm.at[t, pl.ds(0, half)]),
    ]
    first_unit = len(loads)

    def unit_block(which, tt, jj, cc):
        weight = (w_gate, w_up)[which]
        if sliced:
            col = pl.multiple_of(block(tt, jj, cc) * piece, piece)
            return weight.at[:, pl.ds(col, piece)]
        return weight.at[tt, cc]

    def unit_target(which, tt, jj, cc):
        col = x * strip + (jj * piece if sliced else 0)
        size = piece if sliced else strip
        return units.at[
            which, tt, j, pl.ds(pl.multiple_of(cc * depth, depth), depth),
            pl.ds(pl.multiple_of(col, size), size),
        ]

    def unit_pair(which, tt, jj, xx):
        return units.at[which, tt, jj, :, pl.ds(pl.multiple_of(xx * strip, strip), strip)]

    parts = range(side) if sliced else range(1)
    loads += [
        (unit_block(w, t, jj, c), unit_target(w, t, jj, c)) for w in range(2) for jj in parts
    ]
    loads = [
        pltpu.make_async_copy(a, b, load_sems.at[i]) for i, (a, b) in enumerate(loads)
    ]
    for load in loads:
        load.start()
    greet(others + beside + [across])
    sends = Sends(send_sems)
    for load in loads[:first_unit]:
        load.wait()

    lines = ((qkv, qkv_sems), (out, out_sems))

    def spread(buf, sems, tt, r, cond):
        idx = block(tt, j ^ r, c)
        ref = rows_of(buf, idx)
        for bit in range(bits):
            if (1 << bit) > r:
                sends.start(ref, ref, sems.at[idx], beside[bit], cond)
        sends.start(ref, ref, sems.at[idx], core, cond)

    def pass_on(ref, sem, to_right, to_left):
        if to_right is not False:
            sends.start(ref, ref, sem, at(t + 1, j, c), to_right)
        if to_left is not False:
            sends.start(ref, ref, sem, at(t - 1, j, c), to_left)

    def spread_rest(buf, sems, tt, cond):
        for r in range(1, side):
            idx = block(tt, j ^ r, c)
            when(cond, lambda idx=idx: arrived(rows_of(buf, idx), sems.at[idx], here))
            spread(buf, sems, tt, r, cond)

    def line_places(k):
        return ((t >= k, t - k, True), (t + k < LINE, t + k, False))

    def forward(ref, sem, cond, rightward):
        if rightward:
            pass_on(ref, sem, both(cond, t < LINE - 1), False)
        else:
            pass_on(ref, sem, False, both(cond, t > 0))

    def set_out(buf, sems):
        pass_on(rows_of(buf, mine), sems.at[mine], t < LINE - 1, t > 0)
        spread(buf, sems, t, 0, None)

    def line_step(buf, sems, k):
        for cond, tt, rightward in line_places(k):
            idx = block(tt, j, c)
            when(cond, lambda idx=idx: arrived(rows_of(buf, idx), sems.at[idx], here))
            if k < LINE - 1:
                forward(rows_of(buf, idx), sems.at[idx], cond, rightward)
            spread(buf, sems, tt, 0, cond)
        if k == 1:
            spread_rest(buf, sems, t, None)
        else:
            spread_rest(buf, sems, t - k + 1, t >= k - 1)
            spread_rest(buf, sems, t + k - 1, t + k - 1 < LINE)

    own_down = x * side + j

    def down_set_out():
        for bit in range(bits):
            sends.start(
                down.at[own_down], down.at[own_down], down_sems.at[own_down], beside[bit]
            )

    def down_rest():
        for r in range(1, side):
            idx = x * side + (j ^ r)
            arrived(down.at[idx], down_sems.at[idx], here)
            for bit in range(bits):
                if (1 << bit) > r:
                    sends.start(down.at[idx], down.at[idx], down_sems.at[idx], beside[bit])
            sends.start(down.at[idx], down.at[idx], down_sems.at[idx], across)

    def units_set_out():
        for dt in range(LINE):
            for dc in range(2):
                if dt or dc:
                    tt, cc = (t + dt) % LINE, c ^ dc
                    for w in range(2):
                        for jj in parts:
                            sends.start(
                                unit_block(w, tt, jj, cc),
                                unit_target(w, t, jj, c),
                                unit_sems.at[w, t * 2 + c, jj],
                                at(tt, j, cc),
                            )

    set_out(*lines[0])
    sends.start(down.at[own_down], down.at[own_down], down_sems.at[own_down], across)
    chunk = rows // 16

    @pl.loop(0, 16)
    def _(i):
        span = pl.ds(pl.multiple_of(i * chunk, chunk), chunk)
        hidden[span, :] = rms_scale(tokens[span, :].astype(F32), attn_gain[...]).astype(BF)

    @pl.loop(0, 8)
    def _(i):
        span = pl.ds(pl.multiple_of(i * chunk, chunk), chunk)
        row = lax.broadcasted_iota(jnp.int32, (chunk, width), 0) + i * chunk + x * half
        kept = dm[t, span, :].astype(F32)
        dm[t, span, :] = jnp.where(row < length[0], kept, 0.0).astype(BF)

    line_step(*lines[0], 1)
    line_step(*lines[0], 2)
    units_set_out()
    set_out(*lines[1])
    line_step(*lines[0], 3)
    stores = []

    def store(source, target):
        copy = pltpu.make_async_copy(source, target, store_sems.at[len(stores)])
        copy.start()
        stores.append(copy)

    def send_pair(w, tt, jj, xx, device):
        ref = unit_pair(w, tt, jj, xx)
        sends.start(ref, ref, pair_sems.at[w, tt, jj, xx], device)

    def pair_came(w, tt, jj, xx):
        arrived(unit_pair(w, tt, jj, xx), pair_sems.at[w, tt, jj, xx], here)

    def unit_first(tt):
        for cc in range(2):
            mine = jnp.logical_and(tt == t, cc == c)
            for w in range(2):
                for jj in parts:
                    when(
                        jnp.logical_not(mine),
                        lambda w=w, cc=cc, jj=jj: arrived(
                            unit_target(w, tt, jj, cc), unit_sems.at[w, tt * 2 + cc, jj], here
                        ),
                    )
        for w in range(2):
            for bit in range(bits):
                send_pair(w, tt, j, x, beside[bit])
            send_pair(w, tt, j, x, across)

    def unit_second(tt):
        for r in range(1, side):
            for w in (1, 0):
                pair_came(w, tt, j ^ r, x)
                for bit in range(bits):
                    if (1 << bit) > r:
                        send_pair(w, tt, j ^ r, x, beside[bit])
            send_pair(1, tt, j ^ r, x, across)
        pair_came(0, tt, j, 1 - x)
        for bit in range(bits):
            send_pair(0, tt, j, 1 - x, beside[bit])

    def unit_last(tt):
        for r in range(1, side):
            pair_came(0, tt, j ^ r, 1 - x)
            for bit in range(bits):
                if (1 << bit) > r:
                    send_pair(0, tt, j ^ r, 1 - x, beside[bit])
        for r in range(side):
            pair_came(1, tt, j ^ r, 1 - x)

    dm_rows = dm.at[t, pl.ds(0, half)]

    def dm_to_core(tt, cond):
        sends.start(
            dm.at[tt, pl.ds(0, half)], dm.at[tt, pl.ds(half, half)], core_sems.at[tt], core, cond
        )

    def dm_step(k):
        for cond, tt, rightward in line_places(k):
            ref = dm.at[tt, pl.ds(0, half)]
            when(cond, lambda ref=ref, tt=tt: arrived(ref, line_sems.at[tt], here))
            if k < LINE - 1:
                forward(ref, line_sems.at[tt], cond, rightward)
            dm_to_core(tt, cond)

    def finish_line(buf, sems):
        spread_rest(buf, sems, t - LINE + 1, t >= LINE - 1)
        spread_rest(buf, sems, t + LINE - 1, t < 1)
        for tt in range(LINE):
            for jj in range(side):
                idx = block(tt, jj, 1 - c)
                arrived(rows_of(buf, idx), sems.at[idx], here)

    finish_line(*lines[0])
    store(qkv, outs[0])
    down_set_out()
    for load in loads[first_unit:]:
        load.wait()
    unit_first(t)
    pass_on(dm_rows, line_sems.at[t], t < LINE - 1, t > 0)
    dm_to_core(t, None)

    tile = 256

    @pl.loop(0, proj.shape[1] // tile)
    def _(i):
        cols = pl.ds(pl.multiple_of(i * tile, tile), tile)
        proj[:, cols] = mm(hidden[...], qkv[:, cols])

    group = q_cols // k_cols * HEAD
    key_heads = k_cols // HEAD

    def attend_head(g):
        pair = pl.multiple_of(g // 2 * LANES, LANES)
        wide = pl.ds(pl.multiple_of(g * group, group), group)
        attend_kernel(
            rows // 2, scale, g % 2 == 1, length,
            proj.at[:, wide],
            proj.at[:, pl.ds(q_cols + pair, LANES)],
            proj.at[:, pl.ds(q_cols + k_cols + pair, LANES)],
            cosine, sine, q_gain, k_gain,
            attended.at[:, wide],
            totals.at[:, pl.ds(pl.multiple_of(g * LANES, LANES), LANES)],
        )

    pl.loop(0, key_heads)(attend_head)
    for k in range(1, LINE):
        unit_first(slot_place(t, k))
    down_rest()
    for k in range(1, LINE):
        line_step(*lines[1], k)

    finish_line(*lines[1])
    store(out, outs[1])
    wide = 512
    other_rows = pl.ds(pl.multiple_of((1 - x) * half, half), half)
    own_rows = pl.ds(pl.multiple_of(x * half, half), half)

    @pl.loop(0, width // wide)
    def _(i):
        cols = pl.ds(pl.multiple_of(i * wide, wide), wide)
        cross_sent[:, cols] = mm(attended[other_rows, :], out[:, cols]).astype(BF)

    sends.start(cross_sent, cross_got, cross_sem, across)

    @pl.loop(0, width // wide)
    def _(i):
        cols = pl.ds(pl.multiple_of(i * wide, wide), wide)
        part[:, cols] = mm(attended[own_rows, :], out[:, cols])

    unit_second(t)
    dm_step(1)
    for k in range(1, LINE):
        unit_second(slot_place(t, k))
    dm_step(2)

    arrived(cross_got, cross_sem, here)
    step = half // 8

    @pl.loop(0, 8)
    def _(i):
        span = pl.ds(pl.multiple_of(i * step, step), step)
        rows_here = pl.ds(pl.multiple_of(x * half + i * step, step), step)
        total = tokens[rows_here, :].astype(F32) + part[span, :] + cross_got[span, :].astype(F32)
        h_one[span, :] = total
        hidden_two[span, :] = rms_scale(total, ffn_gain[...]).astype(BF)

    dm_step(3)
    for k in range(LINE):
        unit_last(slot_place(t, k))
    store(units, outs[2])
    for jj in range(side):
        idx = (1 - x) * side + jj
        arrived(down.at[idx], down_sems.at[idx], here)
    store(down, outs[3])
    for tt in range(LINE):
        arrived(dm.at[tt, pl.ds(half, half)], core_sems.at[tt], here)
    store(dm, outs[4])
    sends.wait_sent()
    for copy in stores:
        copy.wait()


def start_layer(n, weights, cotangent, length, tokens, attn_gain, tables, gains, ffn_gain):
    w_query, w_key, w_value, w_out, w_gate, w_up, w_down = weights
    side = n // LINE // 2
    depth, piece, width = w_gate.shape[0], w_down.shape[0], w_down.shape[1]
    rows, half = tokens.shape[0], tokens.shape[0] // 2
    q_cols, k_cols = w_query.shape[1], w_key.shape[1]
    cols = q_cols + 2 * k_cols
    strip = side * piece
    sliced = piece % LANES == 0
    if not sliced:
        w_gate, w_up = (
            w.reshape(depth, LINE, side, 2, piece)
            .transpose(1, 3, 0, 2, 4)
            .reshape(LINE, 2, depth, strip)
            for w in (w_gate, w_up)
        )
    shapes = [
        (width, cols),
        (q_cols, width),
        (2, LINE, side, 2 * depth, 2 * strip),
        (2 * side, piece, width),
        (LINE, 2 * half, width),
    ]
    slots = 2 * LINE - 1
    line_sends = 2 * (LINE - 1) + slots * (2 * side - 1)
    sends = 2 * line_sends + 2 * side - 1 + 14 * side + 3 * LINE + 8 + 8 * side * LINE
    any_space = pl.BlockSpec(memory_space=pl.ANY)
    vmem = pl.BlockSpec(memory_space=pltpu.VMEM)
    return pl.pallas_call(
        functools.partial(start_kernel, side, piece, sliced, 1.0 / math.sqrt(HEAD)),
        out_shape=[jax.ShapeDtypeStruct(shape, BF) for shape in shapes]
        + [
            jax.ShapeDtypeStruct((rows, cols), F32),
            jax.ShapeDtypeStruct((rows, q_cols), BF),
            jax.ShapeDtypeStruct((rows, k_cols // HEAD * LANES), F32),
            jax.ShapeDtypeStruct((half, width), F32),
            jax.ShapeDtypeStruct((half, width), BF),
            jax.ShapeDtypeStruct((rows, width), BF),
        ],
        in_specs=[any_space] * 8 + [pl.BlockSpec(memory_space=pltpu.SMEM)] + [vmem] * 7,
        out_specs=[any_space] * 5 + [vmem] * 6,
        scratch_shapes=[pltpu.VMEM(shape, BF) for shape in shapes]
        + [
            pltpu.VMEM((half, width), F32),
            pltpu.VMEM((half, width), BF),
            pltpu.VMEM((half, width), BF),
            pltpu.SemaphoreType.DMA((6 + 2 * side,)),
            pltpu.SemaphoreType.DMA((sends,)),
            pltpu.SemaphoreType.DMA((n,)),
            pltpu.SemaphoreType.DMA((n,)),
            pltpu.SemaphoreType.DMA((2, LINE * 2, side)),
            pltpu.SemaphoreType.DMA((2, LINE, side, 2)),
            pltpu.SemaphoreType.DMA((2 * side,)),
            pltpu.SemaphoreType.DMA((LINE,)),
            pltpu.SemaphoreType.DMA((LINE,)),
            pltpu.SemaphoreType.DMA,
            pltpu.SemaphoreType.DMA((5,)),
        ],
        compiler_params=pltpu.CompilerParams(
            collective_id=0, has_side_effects=True, vmem_limit_bytes=62 << 20
        ),
        cost_estimate=pl.CostEstimate(
            flops=2 * rows * width * cols, bytes_accessed=500 << 20, transcendentals=rows * rows
        ),
    )(
        w_query, w_key, w_value, w_out, w_gate, w_up, w_down, cotangent, length, tokens,
        attn_gain[None, :], *tables, *gains, ffn_gain[None, :],
    )


def feed_kernel(side, *refs):
    h_own, dm_all, units, down, h_one, gain = refs[:6]
    out_half, dab, gain_part, e_own, e_core, e_line, f_out = refs[6:13]
    g_down, gate_mid, up_mid, gate_kept, gate_got, up_kept, up_got = refs[13:20]
    wg, wu, wd, h_all, dm, act, dg, du, e_stage, f_stage, f_send, f_core = refs[20:32]
    load_sems, store_sems, send_sems, line_sems, core_sems, back_sems = refs[32:38]
    done_sems, gate_sems, up_sems, mid_sems, last_sems, e_sems, step_sems, dab_sem, row_sems = refs[38:]
    t, j, c, x = coordinates()
    half, width = h_own.shape
    unit_count = wd.shape[0]
    strip = unit_count // 2
    rows = 2 * half
    bits = side.bit_length() - 1

    def at(tt, cc, jj=None, xx=None):
        jj, xx = j if jj is None else jj, x if xx is None else xx
        return ((tt * side + jj) * 2 + cc, xx)

    here, core, across = at(t, c), at(t, 1 - c), at(t, c, None, 1 - x)
    beside = at(t, c, j ^ (side // 2))
    others = [at((t + dt) % LINE, c) for dt in range(1, LINE)]
    loads = [
        (h_own, h_all.at[t, pl.ds(0, half)]),
        (units.at[0], wg), (units.at[1], wu), (dm_all, dm), (down, wd),
    ]
    loads = [pltpu.make_async_copy(a, b, load_sems.at[i]) for i, (a, b) in enumerate(loads)]
    for load in loads:
        load.start()
    greet(others + [core, across] + ([beside] if bits else []))
    sends, rows_sent = Sends(send_sems), Sends(row_sems)

    def own_rows(tt):
        return h_all.at[tt, pl.ds(0, half)]

    def to_core(tt, cond):
        rows_sent.start(
            own_rows(tt), h_all.at[tt, pl.ds(half, half)], core_sems.at[tt], core, cond
        )

    loads[0].wait()
    rows_sent.start(own_rows(t), own_rows(t), line_sems.at[t], at(t + 1, c), t < LINE - 1)
    rows_sent.start(own_rows(t), own_rows(t), line_sems.at[t], at(t - 1, c), t > 0)
    to_core(t, None)
    for load in loads[1:]:
        load.wait()

    tile = min(512, unit_count)
    wide = min(1024, width)
    e_waits, f_sent, stores = [], [], []

    def store(source, target):
        copy = pltpu.make_async_copy(source, target, store_sems.at[len(stores)])
        copy.start()
        stores.append(copy)
        return copy

    def f_go(k):
        sends.start(
            f_stage.at[k], f_out.at[t], done_sems.at[t], at(slot_place(t, k), c)
        )

    def kept_out(k):
        copy = pltpu.make_async_copy(
            e_stage.at[pl.ds(0, half)], e_own.at[k], mid_sems.at[2, 2 * LINE - 1]
        )
        copy.start()
        return copy.wait

    def later(source, target, sem, device):
        sends.start(source, target, sem, device)
        copy = sends.made.pop()[1]
        sends.made.append((None, None))
        return lambda: copy().wait_send()

    for k in range(LINE):
        tt = slot_place(t, k)
        if k:
            for cond, place_of, forward, target in (
                (t >= k, t - k, t < LINE - 1, t + 1),
                (t + k < LINE, t + k, t > 0, t - 1),
            ):
                when(
                    cond,
                    lambda p=place_of: arrived(own_rows(p), line_sems.at[p], here),
                )
                if k < LINE - 1:
                    rows_sent.start(
                        own_rows(place_of), own_rows(place_of), line_sems.at[place_of],
                        at(target, c), jnp.logical_and(cond, forward),
                    )
                to_core(place_of, cond)
        if k >= 2:
            f_go(k - 1)
        arrived(h_all.at[tt, pl.ds(half, half)], core_sems.at[tt], here)
        if k >= 2:
            f_sent[k - 2]()

        @pl.loop(0, unit_count // tile)
        def _(i):
            cols = pl.ds(pl.multiple_of(i * tile, tile), tile)
            hidden = h_all[tt]
            gate = mm(hidden, wg[:, cols])
            up = mm(hidden, wu[:, cols])
            grad_act = mm_nt(dm[tt], wd[cols, :])
            sigma = lax.logistic(gate)
            silu = gate * sigma
            act[tt, :, cols] = (silu * up).astype(BF)
            dg[tt, :, cols] = (grad_act * up * (sigma * (1.0 + gate * (1.0 - sigma)))).astype(BF)
            du[tt, :, cols] = (grad_act * silu).astype(BF)

        slot = k % 2

        @pl.loop(0, width // wide)
        def _(i):
            span = pl.ds(pl.multiple_of(i * wide, wide), wide)
            grad = mm_nt(dg[tt], wg[span, :]) + mm_nt(du[tt], wu[span, :])
            f_stage[k, :, span] = grad[:half].astype(BF)
            f_send[slot, :, span] = grad[half:].astype(BF)

        f_sent.append(later(f_send.at[slot], f_core.at[k], back_sems.at[k], core))
        for wait in e_waits:
            wait()

        @pl.loop(0, width // wide)
        def _(i):
            span = pl.ds(pl.multiple_of(i * wide, wide), wide)
            e_stage[:, span] = mm(act[tt], wd[:, span]).astype(BF)

        e_waits = [
            kept_out(k),
            later(e_stage.at[pl.ds(half, half)], e_core.at[k], e_sems.at[k], core),
        ]
        arrived(f_core.at[k], back_sems.at[k], here)

        @pl.loop(0, 4)
        def _(i):
            part = pl.ds(pl.multiple_of(i * (half // 4), half // 4), half // 4)
            f_stage[k, part, :] = (
                f_stage[k, part, :].astype(F32) + f_core[k, part, :].astype(F32)
            ).astype(BF)

        if k == LINE - 1:
            f_go(k)

    group = width // LINE
    far = pl.ds(pl.multiple_of((1 - x) * strip, strip), strip)
    near = pl.ds(pl.multiple_of(x * strip, strip), strip)

    def weight_grad(target, grads, tt, send):
        @pl.loop(0, 1)
        def _(i):
            span = pl.ds(tt * group, group)
            hidden = h_all[:, :, span].reshape(LINE * rows, group)
            target[span, :] = mm_tn(hidden, grads[...].reshape(LINE * rows, unit_count)).astype(BF)

        send(tt)

    block = group // side
    whole = side == 2

    def side_rows(tt, jj):
        return pl.ds(pl.multiple_of(tt * group + jj * block, block), block)

    def send_gate(tt):
        span = pl.ds(tt * group, group)
        sends.start(wg.at[span, far], gate_mid.at[span], gate_sems.at[tt], across)
        if not whole:
            store(wg.at[span, near], gate_kept.at[span])

    def send_up(tt):
        for r in range(side):
            span = side_rows(tt, j ^ r)
            if r >= side // 2:
                k = r - side // 2
                sends.start(wu.at[span], up_mid.at[k, tt], up_sems.at[k, tt], beside)
            elif not whole:
                store(wu.at[span], up_kept.at[r, tt])

    for tt in range(LINE):
        weight_grad(wg, dg, tt, send_gate)
        weight_grad(wu, du, tt, send_up)
    tile = min(256, unit_count)

    @pl.loop(0, unit_count // tile)
    def _(i):
        cols = pl.ds(pl.multiple_of(i * tile, tile), tile)
        units_part = act[:, :, cols].reshape(LINE * rows, tile)
        wd[cols, :] = mm_tn(units_part, dm[...].reshape(LINE * rows, width)).astype(BF)

    store(wd, g_down)

    def fetch(pairs):
        copies = [
            pltpu.make_async_copy(a, b, mid_sems.at[2, i]) for i, (a, b) in enumerate(pairs)
        ]
        for copy in copies:
            copy.start()
        for copy in copies:
            copy.wait()

    def add(target, other):
        count = target.shape[0]
        step = min(64, count)

        @pl.loop(0, count // step)
        def _(i):
            part = pl.ds(pl.multiple_of(i * step, step), step)
            target[part, :] = (target[part, :].astype(F32) + other[part, :].astype(F32)).astype(BF)

    upper, lower = pl.ds(0, half), pl.ds(half, half)
    for wait in e_waits:
        wait()
    rows_sent.wait_sent()
    for k in range(LINE):
        arrived(e_core.at[k], e_sems.at[k], here)
    fetch(
        [(e_own.at[k], h_all.at[k, upper]) for k in range(LINE)]
        + [(e_core.at[k], h_all.at[k, lower]) for k in range(LINE)]
    )
    for k in reversed(range(LINE)):
        add(h_all.at[k, upper], h_all.at[k, lower])

    def line_came(i, way, cond, k):
        def act_on():
            arrived(e_line.at[way, i], step_sems.at[way, i], here)
            fetch([(e_line.at[way, i], h_all.at[way, lower])])
            add(h_all.at[k, upper], h_all.at[way, lower])

        when(cond, act_on)

    def line_go(i, way, cond, k):
        sends.start(
            h_all.at[k, upper], e_line.at[way, i], step_sems.at[way, i], at(t + 1 - 2 * way, c),
            cond,
        )

    inner = jnp.logical_and(t >= 1, t <= 2)
    line_go(0, 0, t == 0, 3)
    line_go(0, 1, t == 3, 3)

    for dt in range(1, LINE):
        p = (t + dt) % LINE
        arrived(f_out.at[p], done_sems.at[p], here)
    fetch([(f_out.at[(t + dt) % LINE], f_core.at[dt]) for dt in range(1, LINE)])
    gain_part[...] = jnp.zeros_like(gain_part)
    step = half // 16

    @pl.loop(0, 16)
    def _(i):
        part = pl.ds(pl.multiple_of(i * step, step), step)
        grad = f_stage[0, part, :].astype(F32)
        for dt in range(1, LINE):
            grad = grad + f_core[dt, part, :].astype(F32)
        values = h_one[part, :]
        scale = lax.rsqrt(jnp.mean(values * values, axis=1, keepdims=True) + EPS)
        gain_part[...] += jnp.sum(grad * values * scale, axis=0, keepdims=True)
        grad = grad * gain[...]
        back = jnp.mean(grad * values, axis=1, keepdims=True) * scale * scale
        grad = dm[t, part, :].astype(F32) + scale * (grad - values * back)
        e_stage[part, :] = grad.astype(BF)

    own_rows_out = dab.at[pl.ds(pl.multiple_of(x * half, half), half)]
    store(e_stage.at[upper], own_rows_out)
    sends.start(e_stage.at[upper], own_rows_out, dab_sem, across)
    line_came(0, 0, t == 1, 2)
    line_came(0, 1, t == 2, 2)
    line_go(1, 0, t <= 1, 2)
    line_go(1, 1, t >= 2, 2)
    if whole:
        copies = []
        for tt in range(LINE):
            span = pl.ds(tt * group, group)
            arrived(gate_mid.at[span], gate_sems.at[tt], here)
            arrived(up_mid.at[0, tt], up_sems.at[0, tt], here)
            for i, (source, target) in enumerate(
                (
                    (gate_mid.at[span], dg.at[tt, :, pl.ds(0, strip)]),
                    (up_mid.at[0, tt], du.at[tt, pl.ds(0, block)]),
                )
            ):
                copies.append(pltpu.make_async_copy(source, target, mid_sems.at[i, tt]))
                copies[-1].start()
        for tt in range(LINE):
            mine = side_rows(tt, j)
            copies[2 * tt].wait()
            for jj in range(side):
                span = pl.ds(tt * group + jj * block, block)
                wg[span, near] = (
                    wg[span, near].astype(F32)
                    + dg[tt, pl.ds(jj * block, block), pl.ds(0, strip)].astype(F32)
                ).astype(BF)
            sends.start(
                wg.at[side_rows(tt, 1 - j), near], gate_got.at[tt], last_sems.at[0, tt], beside
            )
            store(wg.at[mine, near], gate_kept.at[tt])
            copies[2 * tt + 1].wait()
            wu[mine, :] = (
                wu[mine, :].astype(F32) + du[tt, pl.ds(0, block), :].astype(F32)
            ).astype(BF)
            sends.start(wu.at[mine, far], up_got.at[tt], last_sems.at[1, tt], across)
            store(wu.at[mine, near], up_kept.at[tt])
    line_came(1, 0, inner, 3)
    line_came(1, 1, inner, 1)
    line_go(2, 0, t == 0, 1)
    line_go(2, 0, inner, 3)
    line_go(2, 1, t >= 1, 1)
    for sent in f_sent[LINE - 2 :]:
        sent()
    sends.made = [item for item in sends.made if item[1] is not None]
    for tt in range(LINE):
        if whole:
            arrived(gate_got.at[tt], last_sems.at[0, tt], here)
            arrived(up_got.at[tt], last_sems.at[1, tt], here)
        else:
            arrived(gate_mid.at[pl.ds(tt * group, group)], gate_sems.at[tt], here)
            for k in range(side // 2):
                arrived(up_mid.at[k, tt], up_sems.at[k, tt], here)
    arrived(dab.at[pl.ds(pl.multiple_of((1 - x) * half, half), half)], dab_sem, here)
    line_came(2, 0, t >= 1, 0)
    line_came(2, 1, t <= 2, 0)

    @pl.loop(0, 16)
    def _(i):
        part = pl.ds(pl.multiple_of(i * step, step), step)
        out_half[part, :] = (h_one[part, :] + h_all[0, part, :].astype(F32)).astype(BF)

    sends.wait_sent()
    for copy in stores:
        copy.wait()


def feed_forward(side, h_own, dm_all, units, down, h_one, ffn_gain):
    half, width = h_own.shape
    unit_count = down.shape[0]
    strip = unit_count // 2
    rows = 2 * half
    group = width // LINE
    block = group // side
    any_space = pl.BlockSpec(memory_space=pl.ANY)
    vmem = pl.BlockSpec(memory_space=pltpu.VMEM)
    mids = [(width, strip), (side // 2, LINE, block, unit_count)]
    last = (LINE, block, strip)
    blocks = (LINE, half, width)
    outs = [blocks, blocks, (2, 3, half, width), blocks, (unit_count, width)] + mids
    outs += [last] * 4 if side == 2 else [mids[0], (1, LANES), mids[1], (1, LANES)]
    held = [
        (width, unit_count), (width, unit_count), (unit_count, width),
        (LINE, rows, width), (LINE, rows, width),
        (LINE, rows, unit_count), (LINE, rows, unit_count), (LINE, rows, unit_count),
        (rows, width), (LINE, half, width), (2, half, width), (LINE, half, width),
    ]
    sends = 3 + 4 * (LINE - 1) + 3 * LINE + 3 * LINE + side // 2 * LINE + 8
    return pl.pallas_call(
        functools.partial(feed_kernel, side),
        out_shape=[
            jax.ShapeDtypeStruct((half, width), BF),
            jax.ShapeDtypeStruct((rows, width), BF),
            jax.ShapeDtypeStruct((1, width), F32),
        ]
        + [jax.ShapeDtypeStruct(shape, BF) for shape in outs],
        in_specs=[any_space] * 4 + [vmem] * 2,
        out_specs=[vmem, any_space, vmem] + [any_space] * len(outs),
        scratch_shapes=[pltpu.VMEM(shape, BF) for shape in held]
        + [
            pltpu.SemaphoreType.DMA((5,)),
            pltpu.SemaphoreType.DMA((3 * LINE + 2 + side // 2 * LINE,)),
            pltpu.SemaphoreType.DMA((sends,)),
            pltpu.SemaphoreType.DMA((LINE,)),
            pltpu.SemaphoreType.DMA((LINE,)),
            pltpu.SemaphoreType.DMA((LINE,)),
            pltpu.SemaphoreType.DMA((LINE,)),
            pltpu.SemaphoreType.DMA((LINE,)),
            pltpu.SemaphoreType.DMA((side // 2, LINE)),
            pltpu.SemaphoreType.DMA((3, 2 * LINE)),
            pltpu.SemaphoreType.DMA((2, LINE)),
            pltpu.SemaphoreType.DMA((LINE,)),
            pltpu.SemaphoreType.DMA((2, 3)),
            pltpu.SemaphoreType.DMA,
            pltpu.SemaphoreType.DMA((3 + 4 * (LINE - 1),)),
        ],
        compiler_params=pltpu.CompilerParams(
            collective_id=1, has_side_effects=True, vmem_limit_bytes=63 << 20
        ),
        cost_estimate=pl.CostEstimate(
            flops=18 * LINE * rows * width * unit_count, bytes_accessed=100 << 20,
            transcendentals=LINE * rows * unit_count,
        ),
    )(h_own, dm_all, units, down, h_one, ffn_gain[None, :])


def end_kernel(side, piece, scale, *refs):
    gate, gate_got, up, up_got, down, down_got, w_qkv, length = refs[:8]
    hidden, proj, totals, grad_o, cosine, sine, q_gain, k_gain, attn_gain, ffn_part = refs[8:18]
    q_out, k_out, v_out, gate_out, up_out, down_out, small_out, low_out, low_got_out = refs[18:27]
    (
        heads, heads_core, heads_side, line_right, line_left,
        gates, gates_got, ups, ups_got, downs, downs_got, downs_across, homes,
        grads, weights, low, low_got, wide_out, keys_sum, vals_sum, q_sum, k_sum, smalls,
    ) = refs[27:50]
    load_sems, send_sems, core_sems, side_sems, line_sems, across_sems = refs[50:56]
    home_sems, small_sems, store_sems = refs[56:]
    t, j, c, x = coordinates()
    bits = side.bit_length() - 1
    depth, q_cols = q_out.shape
    k_cols = k_out.shape[1]
    strip = side * piece

    def at(tt, jj, cc, xx=None):
        return (((tt * side) + jj) * 2 + cc, x if xx is None else xx)

    def block(tt, jj, cc):
        return ((tt * side) + jj) * 2 + cc

    here, core, across = at(t, j, c), at(t, j, 1 - c), at(t, j, c, 1 - x)
    beside = [at(t, j ^ (1 << bit), c) for bit in range(bits)]
    others = [
        at((t + dt) % LINE, j, c ^ dc) for dt in range(LINE) for dc in range(2) if dt or dc
    ]
    loads = [
        (gate, gates), (gate_got, gates_got), (up, ups), (up_got, ups_got),
        (down.at[:, j], downs) if side == 2 else (down, downs),
        (w_qkv, weights),
    ]
    if side != 2:
        loads.append((down_got, downs_got))
    loads = [pltpu.make_async_copy(a, b, load_sems.at[i]) for i, (a, b) in enumerate(loads)]
    for load in loads:
        load.start()
    greet(others + beside + [across])
    sends = Sends(send_sems)

    def add(target, first, second):
        count = first.shape[0]
        step = min(64, count)

        @pl.loop(0, count // step)
        def _(i):
            part = pl.ds(pl.multiple_of(i * step, step), step)
            target[part, :] = (first[part, :].astype(F32) + second[part, :].astype(F32)).astype(
                target.dtype
            )

    def go_home(which, rows):
        for tt in range(LINE):
            for cc in range(2):
                mine = jnp.logical_and(t == tt, c == cc)
                source = rows.at[tt, pl.ds(cc * depth, depth)]
                target = homes.at[which, t * 2 + c]
                sends.start(
                    source, target, home_sems.at[which, t * 2 + c], at(tt, j, cc),
                    jnp.logical_not(mine),
                )

                @pl.when(mine)
                def _():
                    homes[which, tt * 2 + cc] = source[...]

    if side == 2:
        sends.start(down.at[:, 1 - j], downs_got, across_sems.at[2], beside[0])
    for which, (mine, got) in enumerate(((gates, gates_got), (ups, ups_got))):
        loads[2 * which].wait()
        loads[2 * which + 1].wait()
        for tt in range(LINE):
            add(mine.at[tt], mine.at[tt], got.at[tt])
        go_home(which, mine)

    def down_second():
        loads[4].wait()
        if side == 2:
            arrived(downs_got, across_sems.at[2], here)
        else:
            loads[6].wait()
        for xx in range(2):
            add(downs.at[xx], downs.at[xx], downs_got.at[xx])
        sends.start(downs.at[1 - x], downs_across, across_sems.at[0], across)

    q_sum[...] = jnp.zeros_like(q_sum)
    k_sum[...] = jnp.zeros_like(k_sum)
    rows = hidden.shape[0]
    group = q_cols // k_cols * HEAD

    @pl.loop(0, k_cols // HEAD)
    def _(g):
        pair = pl.multiple_of(g // 2 * LANES, LANES)
        wide = pl.ds(pl.multiple_of(g * group, group), group)
        k_pair = pl.ds(q_cols + pair, LANES)
        v_pair = pl.ds(q_cols + k_cols + pair, LANES)
        attend_back_kernel(
            rows // 2, scale, g % 2 == 1, length,
            proj.at[:, wide], proj.at[:, k_pair], proj.at[:, v_pair],
            cosine, sine, q_gain, k_gain,
            totals.at[:, pl.ds(pl.multiple_of(g * LANES, LANES), LANES)],
            grad_o.at[:, wide],
            grads.at[:, wide], grads.at[:, k_pair], grads.at[:, v_pair],
            q_sum, k_sum, keys_sum, vals_sum,
        )

    width = hidden.shape[1]
    place_rows = width // LINE
    tile = min(256, place_rows)
    for q in reversed(range(LINE)):
        tt = slot_place(t, q)

        @pl.loop(0, place_rows // tile)
        def _(i):
            span = pl.ds(pl.multiple_of(tt * place_rows + i * tile, tile), tile)
            grad = mm_tn(hidden[:, span], grads[...]).astype(BF)
            first = tt * (2 * side) + i * (tile // depth)
            heads[pl.ds(first, tile // depth)] = grad.reshape(tile // depth, depth, -1)

        for r in range(side):
            sends.start(
                heads.at[block(tt, j ^ r, 1 - c)], heads_core.at[tt, j ^ r],
                core_sems.at[tt, j ^ r], core,
            )

    loads[5].wait()
    wide = min(512, width)
    for i in range(width // wide):
        cols = pl.ds(i * wide, wide)
        grad = mm_nt(grads[...], weights[cols, :])
        low[:, cols] = grad.astype(BF)
        part = jnp.sum(grad * hidden[:, cols].astype(F32), axis=0, keepdims=True)
        part = part / attn_gain[:, cols]
        for k in range(wide // LANES):
            smalls[0, pl.ds(i * (wide // LANES) + k, 1), :] = part[:, k * LANES : (k + 1) * LANES]
    sends.start(low, low_got, across_sems.at[1], across)
    down_second()
    count = width // LANES
    smalls[0, pl.ds(count, count), :] = ffn_part[...]
    q_part, k_part = q_sum[...], k_sum[...]
    q_part = q_part + pltpu.roll(q_part, HEAD, 1)
    k_part = k_part + pltpu.roll(k_part, HEAD, 1)
    smalls[0, pl.ds(2 * count, 1), :] = jnp.where(low_lanes(q_part.shape), q_part, k_part)

    partners = [core] + beside + [across, at(t ^ 1, j, c), at(t ^ 2, j, c)]

    def small_step(i):
        if i:
            arrived(smalls.at[2 * i], small_sems.at[i - 1], here)
            smalls[2 * i - 1] = smalls[max(2 * i - 3, 0)] + smalls[2 * i]
        if i < len(partners):
            source = smalls.at[2 * i - 1] if i else smalls.at[0]
            sends.start(source, smalls.at[2 * i + 2], small_sems.at[i], partners[i])
        return i + 1

    def side_first(q):
        tt = slot_place(t, q)
        for r in reversed(range(side)):
            arrived(heads_core.at[tt, j ^ r], core_sems.at[tt, j ^ r], here)
            mine = heads.at[block(tt, j ^ r, c)]
            add(mine, mine, heads_core.at[tt, j ^ r])
            if bits and r >= side // 2:
                k = side // 2 - 1 + r - side // 2
                sends.start(mine, heads_side.at[tt, k], side_sems.at[tt, k], beside[bits - 1])

    def side_rest(q):
        tt = slot_place(t, q)
        for bit in reversed(range(bits)):
            half = 1 << bit
            for r in range(half):
                arrived(heads_side.at[tt, half - 1 + r], side_sems.at[tt, half - 1 + r], here)
                mine = heads.at[block(tt, j ^ r, c)]
                add(mine, mine, heads_side.at[tt, half - 1 + r])
                if bit and r >= half // 2:
                    k = half // 2 - 1 + r - half // 2
                    sends.start(
                        mine, heads_side.at[tt, k], side_sems.at[tt, k], beside[bit - 1]
                    )
        return heads.at[block(tt, j, c)]

    def line_came(i, way, cond, target):
        line = (line_right, line_left)[way]

        def act():
            arrived(line.at[i], line_sems.at[way, i], here)
            add(target, target, line.at[i])

        when(cond, act)

    def line_go(i, way, cond, source):
        line = (line_right, line_left)[way]
        sends.start(
            source, line.at[i], line_sems.at[way, i], at(t + 1 - 2 * way, j, c), cond
        )

    step = small_step(0)
    side_first(3)
    side_first(2)
    step = small_step(step)
    p3 = side_rest(3)
    line_go(0, 0, t == 0, p3)
    line_go(0, 1, t == 3, p3)
    side_first(1)
    step = small_step(step)
    p2 = side_rest(2)
    line_came(0, 0, t == 1, p2)
    line_came(0, 1, t == 2, p2)
    line_go(1, 0, t <= 1, p2)
    line_go(1, 1, t >= 2, p2)
    side_first(0)

    step = small_step(step)
    p1 = side_rest(1)
    line_came(1, 0, jnp.logical_and(t >= 1, t <= 2), p3)
    line_came(1, 1, jnp.logical_and(t >= 1, t <= 2), p1)
    line_go(2, 0, t == 0, p1)
    line_go(2, 0, jnp.logical_and(t >= 1, t <= 2), p3)
    line_go(2, 1, t >= 1, p1)
    while step <= len(partners):
        step = small_step(step)
    small_out[...] = smalls[2 * len(partners) - 1]
    arrived(downs_across, across_sems.at[0], here)
    add(down_out, downs.at[x], downs_across)
    p0 = side_rest(0)
    line_came(2, 0, t >= 1, p0)
    line_came(2, 1, t <= 2, p0)
    q_out[...] = p0[:, pl.ds(0, q_cols)].astype(F32)
    k_out[...] = p0[:, pl.ds(q_cols, k_cols)].astype(F32)
    v_out[...] = p0[:, pl.ds(q_cols + k_cols, k_cols)].astype(F32)
    stores = []

    def store(source, target):
        copy = pltpu.make_async_copy(source, target, store_sems.at[len(stores)])
        copy.start()
        stores.append(copy)

    for which, out in enumerate((gate_out, up_out)):
        if which:
            stores[0].wait()
        for tt in range(LINE):
            for cc in range(2):
                mine = jnp.logical_and(t == tt, c == cc)
                source = homes.at[which, tt * 2 + cc]
                when(
                    jnp.logical_not(mine),
                    lambda w=which, k=tt * 2 + cc, ref=source: arrived(
                        ref, home_sems.at[w, k], here
                    ),
                )
                for jj in range(side):
                    wide_out[:, pl.ds(block(tt, jj, cc) * piece, piece)] = source[
                        :, pl.ds(jj * piece, piece)
                    ].astype(F32)
        store(wide_out, out)
    arrived(low_got, across_sems.at[1], here)
    store(low, low_out)
    store(low_got, low_got_out)
    sends.wait_sent()
    for copy in stores[1:]:
        copy.wait()


def end_layer(n, piece, pairs, down, w_qkv, length, hidden, proj, totals, grad_o, tables, gains,
              attn_gain, ffn_part):
    side = n // LINE // 2
    bits = side.bit_length() - 1
    rows, width = hidden.shape
    cols = w_qkv.shape[1]
    q_cols = grad_o.shape[1]
    depth = width // n
    k_cols = (cols - q_cols) // 2
    strip = side * piece
    any_space = pl.BlockSpec(memory_space=pl.ANY)
    vmem = pl.BlockSpec(memory_space=pltpu.VMEM)
    steps = bits + 4
    sides = max(side - 1, 1)
    home = (LINE, 2 * depth, strip)
    held = [
        (n, depth, cols), (LINE, side, depth, cols), (LINE, sides, depth, cols),
        (3, depth, cols), (3, depth, cols),
        home, home, home, home,
        (2, piece, width), (2, piece, width), (piece, width),
        (2, LINE * 2, depth, strip),
        (rows, cols), (width, cols), (rows, width), (rows, width),
    ]
    small = (2 * (width // LANES) + 1, LANES)
    floats = [
        (depth, LINE * 2 * strip), (rows, LANES), (rows, LANES), (1, LANES), (1, LANES),
        (2 * steps + 1,) + small,
    ]
    sends = LINE * (2 * side - 1) + 3 + steps + 8 + 4 * LINE + 4
    return pl.pallas_call(
        functools.partial(end_kernel, side, piece, 1.0 / math.sqrt(HEAD)),
        out_shape=[
            jax.ShapeDtypeStruct((depth, q_cols), F32),
            jax.ShapeDtypeStruct((depth, k_cols), F32),
            jax.ShapeDtypeStruct((depth, k_cols), F32),
            jax.ShapeDtypeStruct((depth, LINE * 2 * strip), F32),
            jax.ShapeDtypeStruct((depth, LINE * 2 * strip), F32),
            jax.ShapeDtypeStruct((piece, width), F32),
            jax.ShapeDtypeStruct(small, F32),
            jax.ShapeDtypeStruct((rows, width), BF),
            jax.ShapeDtypeStruct((rows, width), BF),
        ],
        in_specs=[any_space] * 7 + [pl.BlockSpec(memory_space=pltpu.SMEM)] + [vmem] * 10,
        out_specs=[vmem] * 3 + [any_space] * 2 + [vmem] * 2 + [any_space] * 2,
        scratch_shapes=[pltpu.VMEM(shape, BF) for shape in held]
        + [pltpu.VMEM(shape, F32) for shape in floats]
        + [
            pltpu.SemaphoreType.DMA((7,)),
            pltpu.SemaphoreType.DMA((sends,)),
            pltpu.SemaphoreType.DMA((LINE, side)),
            pltpu.SemaphoreType.DMA((LINE, sides)),
            pltpu.SemaphoreType.DMA((2, 3)),
            pltpu.SemaphoreType.DMA((3,)),
            pltpu.SemaphoreType.DMA((2, LINE * 2)),
            pltpu.SemaphoreType.DMA((steps,)),
            pltpu.SemaphoreType.DMA((4,)),
        ],
        compiler_params=pltpu.CompilerParams(
            collective_id=2, has_side_effects=True, vmem_limit_bytes=62 << 20
        ),
        cost_estimate=pl.CostEstimate(
            flops=8 * rows * width * cols, bytes_accessed=300 << 20, transcendentals=rows * rows
        ),
    )(
        *pairs, *down, w_qkv, length, hidden, proj, totals, grad_o, *tables, *gains,
        attn_gain[None, :], ffn_part,
    )


class Links:
    def __init__(self, n):
        self.n = n
        self.inner = n // LINE
        self.side = self.inner // 2
        self.side_bits = self.side.bit_length() - 1
        self.t, self.j, self.c, self.x = coordinates()

    def core(self, value):
        return lax.ppermute(value, "dp", [(i, i ^ 1) for i in range(self.n)])

    def over(self, value, bit):
        return lax.ppermute(value, "dp", [(i, i ^ (2 << bit)) for i in range(self.n)])

    def cross(self, value):
        return lax.ppermute(value, "tensor", [(0, 1), (1, 0)])

    def along(self, value, moves):
        pairs = [
            (a * self.inner + i, b * self.inner + i) for a, b in moves for i in range(self.inner)
        ]
        return lax.ppermute(value, "dp", pairs)

    def right(self, value, senders):
        return self.along(value, [(a, a + 1) for a in senders])

    def left(self, value, senders):
        return self.along(value, [(a, a - 1) for a in senders])

    def turn(self, value, shift):
        return self.along(value, [(a, (a + shift) % LINE) for a in range(LINE)])

    def line_gather(self, value):
        t = self.t
        r1 = self.right(value, (0, 1, 2))
        l1 = self.left(value, (1, 2, 3))
        r2 = self.right(r1, (1, 2))
        l2 = self.left(l1, (1, 2))
        r3 = self.right(r2, (2,))
        l3 = self.left(l2, (1,))
        return (
            value,
            jnp.where(t == 0, l1, r1),
            jnp.where(t < 2, l2, r2),
            jnp.where(t == 0, l3, jnp.where(t == 3, r3, l1)),
        )

    def lines(self):
        return [[i + k * self.inner for k in range(LINE)] for i in range(self.inner)]

    def line_all(self, value):
        return lax.all_gather(value, "dp", axis_index_groups=self.lines())

    def line_sum(self, value):
        return lax.psum_scatter(
            value, "dp", scatter_dimension=0, axis_index_groups=self.lines()
        )

    def dp_sum(self, value):
        return lax.psum_scatter(value, "dp", scatter_dimension=0, tiled=True)

    def line_scatter(self, parts):
        t = self.t
        p0, p1, p2, p3 = parts
        first = p3.astype(BF)
        r1 = self.right(first, (0,))
        l1 = self.left(first, (3,))
        second = (p2 + r1.astype(F32) + l1.astype(F32)).astype(BF)
        r2 = self.right(second, (0, 1))
        l2 = self.left(second, (2, 3))
        r3 = self.right((jnp.where(t == 0, p1, p3) + r2.astype(F32)).astype(BF), (0, 1, 2))
        l3 = self.left((p1 + l2.astype(F32)).astype(BF), (1, 2, 3))
        return p0 + r3.astype(F32) + l3.astype(F32)

    def line_send(self, parts):
        p0, p1, p2, p3 = parts
        first, second, third = p1.astype(BF), p2.astype(BF), p3.astype(BF)
        got = [
            self.left(first, (1, 2, 3)),
            self.right(first, (0,)),
            self.turn(second, 2),
            self.along(third, ((0, 3), (3, 0))),
            self.right(third, (1, 2)),
        ]
        return p0 + sum(g.astype(F32) for g in got)

    def side_all(self, value):
        blocks = [value]
        for bit in range(self.side_bits):
            blocks += [self.over(block, bit) for block in blocks]
        return blocks

    def side_sum(self, blocks):
        for bit in reversed(range(self.side_bits)):
            width = 1 << bit
            blocks = [
                a.astype(F32) + self.over(b.astype(BF), bit).astype(F32)
                for a, b in zip(blocks[:width], blocks[width:])
            ]
        return blocks[0]

    def side_start(self, blocks):
        for bit in reversed(range(1, len(blocks).bit_length() - 1)):
            half = 1 << bit
            blocks = [
                (a.astype(F32) + self.over(b, bit).astype(F32)).astype(BF)
                for a, b in zip(blocks[:half], blocks[half:])
            ]
        return blocks[0], self.over(blocks[1], 0)

    def side_end(self, kept, got):
        if kept.shape[0] == 1:
            return kept[0], got[0]
        total = (kept.astype(F32) + got.astype(F32)).astype(BF)
        return self.side_start(list(total))

    def pair_order(self, mine, other, where):
        low = jnp.where(where == 0, mine, other)
        high = jnp.where(where == 0, other, mine)
        return jnp.concatenate([low, high], 0)

    def pick(self, value, index, axis):
        return lax.dynamic_index_in_dim(value, index, axis, keepdims=False)

    def cross_sum(self, value, axis):
        kept = self.pick(value, self.x, axis)
        sent = self.pick(value, 1 - self.x, axis)
        return kept.astype(F32) + self.cross(sent.astype(BF)).astype(F32)

    def gather_rows(self, blocks):
        rows, cols = blocks[0].shape
        pieces, where = [], []
        for k, block in enumerate(blocks):
            for r, piece in enumerate(self.side_all(block)):
                pieces += [piece, self.core(piece)]
                where += [(k, r, 0), (k, r, 1)]

        def spots(t, j, c, x):
            return [
                (
                    i, 0, 0, rows, cols,
                    (((slot_place(t, k) * self.side) + (j ^ r)) * 2 + (c ^ s)) * rows, 0,
                )
                for i, (k, r, s) in enumerate(where)
            ]

        return place(pieces, spots, (self.n * rows, cols))

    def sum_rows(self, value):
        rows, cols = value.shape[0] // self.n, value.shape[1]
        parts = value.reshape(LINE, self.side, 2, rows, cols)
        kept = self.pick(parts, self.c, 2).astype(F32)
        parts = kept + self.core(self.pick(parts, 1 - self.c, 2)).astype(F32)
        parts = parts.astype(BF)
        parts = self.side_sum([self.pick(parts, self.j ^ r, 1) for r in range(self.side)])
        return self.line_scatter(
            [self.pick(parts, slot_place(self.t, k), 0).astype(F32) for k in range(LINE)]
        )

    def total(self, value):
        value = value + self.core(value)
        for bit in range(self.side_bits):
            value = value + self.over(value, bit)
        value = value + self.cross(value)
        value = value + self.along(value, ((0, 1), (1, 0), (2, 3), (3, 2)))
        return value + self.turn(value, 2)


def make_body(n):
    def body(
        tokens,
        cotangent,
        lengths,
        attn_gain,
        query_gain,
        key_gain,
        w_query,
        key_weight_matrix,
        value_weight_matrix,
        w_out,
        ffn_gain,
        w_gate,
        w_up,
        w_down,
    ):
        net = Links(n)
        t, j, c, x = net.t, net.j, net.c, net.x
        row_count, width = tokens.shape
        half = row_count // 2
        head_dim = query_gain.shape[0]
        q_cols = w_query.shape[1]
        k_cols = key_weight_matrix.shape[1]
        k_heads = k_cols // head_dim
        dp_index = lax.axis_index("dp")
        slot_length = lengths[dp_index]

        depth = w_gate.shape[0]
        piece = w_down.shape[0]
        side = net.side
        strip = side * piece
        tables = angle_tables(row_count, head_dim, LANES)
        gains = [jnp.tile(gain, LANES // head_dim)[None, :] for gain in (query_gain, key_gain)]
        inputs = tokens.astype(F32)
        length = slot_length[None]
        weights = (w_query, key_weight_matrix, value_weight_matrix, w_out, w_gate, w_up, w_down)
        (
            qkv_full, wo_full, units, wd, grad_all, qkv, o_low, log_totals, h_one, hidden_two,
            hidden_state,
        ) = start_layer(
            n, weights, cotangent, length, tokens, attn_gain, tables, gains, ffn_gain
        )

        (
            layer_half, grad_attn_low, g_ffn_part, _, _, _, _,
            g_down, gate_mid, up_mid, gate_kept, gate_got, up_kept, up_got,
        ) = feed_forward(
            side, hidden_two, grad_all, units.reshape(2, width, 2 * strip),
            wd.reshape(2 * strip, width), h_one, ffn_gain,
        )
        layer_out = net.pair_order(layer_half, net.cross(layer_half), x)

        if side != 2:
            gate_sum = (gate_kept.astype(F32) + gate_mid.astype(F32)).astype(BF)
            gate_sum = gate_sum.reshape(LINE, side, 2 * depth, strip)
            gate_kept, gate_got = net.side_start([net.pick(gate_sum, j ^ r, 1) for r in range(side)])
            up_kept, up_got = net.side_end(up_kept, up_mid)
            up_sum = (up_kept.astype(F32) + up_got.astype(F32)).astype(BF)
            up_kept = lax.dynamic_slice_in_dim(up_sum, x * strip, strip, 2)
            up_got = net.cross(lax.dynamic_slice_in_dim(up_sum, (1 - x) * strip, strip, 2))
        g_down = g_down.reshape(2, side, piece, width)
        down_pair = (g_down, g_down)
        if side != 2:
            down_pair = net.side_start([net.pick(g_down, j ^ r, 1) for r in range(side)])

        g_out = mm_tn(o_low, grad_attn_low).astype(BF)
        grad_o_low = mm_nt(grad_attn_low, wo_full).astype(BF)
        g_out_out = net.dp_sum(g_out).astype(F32)
        (
            g_query_w, g_key_w, g_value_w, g_gate_out, g_up_out, g_down_out, small, low, low_got,
        ) = end_layer(
            n, piece, (gate_kept, gate_got, up_kept, up_got), down_pair, qkv_full, length,
            hidden_state, qkv, log_totals, grad_o_low, tables, gains, attn_gain,
            g_ffn_part.reshape(-1, LANES),
        )
        grad_hidden = low.astype(F32) + low_got.astype(F32)
        small = small.reshape(-1)
        grad_in = jax.vjp(lambda v: rms_scale(v, attn_gain), inputs)[1](grad_hidden)[0]
        input_grad = grad_attn_low.astype(F32) + grad_in
        return (
            layer_out,
            input_grad,
            small[:width],
            small[2 * width : 2 * width + head_dim],
            small[2 * width + head_dim :],
            g_query_w,
            g_key_w,
            g_value_w,
            g_out_out,
            small[width : 2 * width],
            g_gate_out,
            g_up_out,
            g_down_out,
        )

    return body


def solution(mesh):
    placed = (
        P("dp", None),
        P("dp", None),
        P(),
        P(),
        P(),
        P(),
        P("dp", "tensor"),
        P("dp", "tensor"),
        P("dp", "tensor"),
        P(("tensor", "dp"), None),
        P(),
        P("dp", "tensor"),
        P("dp", "tensor"),
        P(("tensor", "dp"), None),
    )
    return jax.shard_map(
        make_body(mesh.shape["dp"]),
        mesh=mesh,
        in_specs=placed,
        out_specs=(
            P("dp", None),
            P("dp", None),
            P(),
            P(),
            P(),
            P("dp", "tensor"),
            P("dp", "tensor"),
            P("dp", "tensor"),
            P(("tensor", "dp"), None),
            P(),
            P("dp", "tensor"),
            P("dp", "tensor"),
            P(("tensor", "dp"), None),
        ),
        check_vma=False,
    )
```

```python
import functools
import math

import jax
import jax.numpy as jnp
import numpy as np
from jax import lax
from jax.experimental import pallas as pl
from jax.experimental.pallas import tpu as pltpu
from jax.sharding import PartitionSpec as P

EPS = 1e-05
ROPE_BASE = 1000000.0
MASKED = -1e30
LINE = 4
BF = jnp.bfloat16
F32 = jnp.float32


def rms_scale(values, gain):
    return values * lax.rsqrt(jnp.mean(values * values, axis=-1, keepdims=True) + EPS) * gain


def angle_tables(count, head_dim, lanes):
    half_dim = head_dim // 2
    freq = ROPE_BASE ** (np.arange(half_dim) * (-2.0 / head_dim))
    turned = np.arange(count)[:, None] * freq[None, :]
    cosine, sine = np.cos(turned).astype(np.float32), np.sin(turned).astype(np.float32)
    repeats = lanes // head_dim
    return (
        jnp.asarray(np.tile(np.concatenate([cosine, cosine], 1), (1, repeats))),
        jnp.asarray(np.tile(np.concatenate([-sine, sine], 1), (1, repeats))),
    )


LANES = 128
HEAD = LANES // 2


def low_lanes(shape):
    return lax.broadcasted_iota(jnp.int32, shape, 1) < HEAD


def per_head(values):
    low = low_lanes(values.shape)
    first = jnp.sum(jnp.where(low, values, 0.0), axis=1, keepdims=True)
    second = jnp.sum(jnp.where(low, 0.0, values), axis=1, keepdims=True)
    return jnp.where(low, first, second) * (1.0 / HEAD)


def halves_swapped(values):
    lane = lax.broadcasted_iota(jnp.int32, values.shape, 1)
    return jnp.where(
        lane % HEAD < HEAD // 2,
        pltpu.roll(values, LANES - HEAD // 2, 1),
        pltpu.roll(values, HEAD // 2, 1),
    )


def head_norm(values):
    scale = lax.rsqrt(per_head(values * values) + EPS)
    return values * scale, scale


def head_turn(values, cosine, sine):
    return values * cosine + halves_swapped(values) * sine


def head_back(grad, normed, scale, gain, cosine, sine):
    grad = grad * cosine - halves_swapped(grad) * sine
    gain_grad = jnp.sum(grad * normed, axis=0, keepdims=True)
    grad = grad * gain
    return scale * (grad - normed * per_head(grad * normed)), gain_grad


def one_head(pair, second):
    low = low_lanes(pair.shape)
    return jnp.where(low == jnp.logical_not(second), pair, pltpu.roll(pair, HEAD, 1))


def two_rows(slab):
    low = low_lanes(slab.shape)
    return jnp.concatenate([jnp.where(low, slab, 0.0), jnp.where(low, 0.0, slab)], 0).astype(BF)


def allowed_mask(block, first_row, columns, length):
    row = lax.broadcasted_iota(jnp.int32, (2 * block, columns), 0) % block + first_row
    col = lax.broadcasted_iota(jnp.int32, (2 * block, columns), 1)
    return (col <= row) & (col < length)


def attend_kernel(
    block, scale, second, length, q, k, v, cosine, sine, q_gain, k_gain, out, totals
):
    rows = q.shape[0]
    cos, sin = cosine[...], sine[...]
    keys = one_head(head_turn(head_norm(k[...])[0] * k_gain[...], cos, sin), second).astype(BF)
    vals = one_head(v[...], second).astype(BF)
    lane = lax.broadcasted_iota(jnp.int32, (block, LANES), 1)
    for first in range(0, rows, block):
        span = pl.ds(first, block)
        seen = first + block
        allowed = allowed_mask(block, first, seen, length[0])
        kept = jnp.zeros((block, LANES), F32)
        for slab in range(q.shape[1] // LANES):
            cols = pl.ds(slab * LANES, LANES)
            turned = head_turn(
                head_norm(q[span, cols])[0] * q_gain[...], cosine[span, :], sine[span, :]
            )
            scores = mm_nt(two_rows(turned), keys[:seen]) * scale
            scores = jnp.where(allowed, scores, MASKED)
            top = jnp.max(scores, axis=1, keepdims=True)
            probs = jnp.exp(scores - top)
            total = jnp.sum(probs, axis=1, keepdims=True)
            probs = (probs * (1.0 / total)).astype(BF)
            both = mm(probs, vals[:seen])
            out[span, cols] = jnp.where(low_lanes((block, LANES)), both[:block], both[block:]).astype(
                BF
            )
            log_total = top + jnp.log(total)
            kept = jnp.where(lane == 2 * slab, log_total[:block], kept)
            kept = jnp.where(lane == 2 * slab + 1, log_total[block:], kept)
        totals[span, :] = kept


def attend_back_kernel(
    block, scale, second, length, q, k, v, cosine, sine, q_gain, k_gain, totals, grad_out,
    grad_q, grad_k, grad_v, q_gain_grad, k_gain_grad, keys_sum, vals_sum,
):
    rows = q.shape[0]
    cos, sin = cosine[...], sine[...]
    k_normed, k_scale = head_norm(k[...])
    keys = one_head(head_turn(k_normed * k_gain[...], cos, sin), second).astype(BF)
    vals = one_head(v[...], second).astype(BF)
    lane = lax.broadcasted_iota(jnp.int32, (block, LANES), 1)
    keys_sum[...] = jnp.zeros_like(keys_sum)
    vals_sum[...] = jnp.zeros_like(vals_sum)

    for first in range(0, rows, block):
        span = pl.ds(first, block)
        seen = first + block
        allowed = allowed_mask(block, first, seen, length[0])
        kept = totals[span, :]
        for slab in range(q.shape[1] // LANES):
            cols = pl.ds(slab * LANES, LANES)
            q_normed, q_scale = head_norm(q[span, cols])
            turned = two_rows(head_turn(q_normed * q_gain[...], cosine[span, :], sine[span, :]))
            log_total = jnp.concatenate(
                [
                    jnp.sum(jnp.where(lane == 2 * slab + i, kept, 0.0), axis=1, keepdims=True)
                    for i in range(2)
                ],
                0,
            )
            scores = mm_nt(turned, keys[:seen]) * scale
            probs = jnp.exp(jnp.where(allowed, scores, MASKED) - log_total)
            grad_rows = two_rows(grad_out[span, cols].astype(F32))
            grad_probs = mm_nt(grad_rows, vals[:seen])
            drop = jnp.sum(probs * grad_probs, axis=1, keepdims=True)
            grad_scores = (probs * (grad_probs - drop)).astype(BF)
            both = mm(grad_scores, keys[:seen]) * scale
            grad_turned = jnp.where(low_lanes((block, LANES)), both[:block], both[block:])
            grad_proj, gain_part = head_back(
                grad_turned, q_normed, q_scale, q_gain[...], cosine[span, :], sine[span, :]
            )
            grad_q[span, cols] = grad_proj.astype(BF)
            q_gain_grad[...] += gain_part
            keys_sum[:seen] += mm_tn(grad_scores, turned)
            vals_sum[:seen] += mm_tn(probs.astype(BF), grad_rows)

    keys_grad = keys_sum[...] * scale
    keys_grad = keys_grad + pltpu.roll(keys_grad, HEAD, 1)
    vals_grad = vals_sum[...]
    vals_grad = vals_grad + pltpu.roll(vals_grad, HEAD, 1)
    grad_proj, gain_part = head_back(
        keys_grad,
        one_head(k_normed, second),
        one_head(k_scale, second),
        k_gain[...],
        cos,
        sin,
    )
    k_gain_grad[...] += gain_part * 0.5
    keep_low = low_lanes(grad_k.shape)

    @pl.when(jnp.logical_not(second))
    def _():
        grad_k[...] = grad_proj.astype(BF)
        grad_v[...] = vals_grad.astype(BF)

    @pl.when(second)
    def _():
        grad_k[...] = jnp.where(keep_low, grad_k[...].astype(F32), grad_proj).astype(BF)
        grad_v[...] = jnp.where(keep_low, grad_v[...].astype(F32), vals_grad).astype(BF)


def mm(left, right):
    return jnp.dot(left, right, preferred_element_type=F32)


def mm_nt(left, right):
    return lax.dot_general(left, right, (((1,), (1,)), ((), ())), preferred_element_type=F32)


def mm_tn(left, right):
    return lax.dot_general(left, right, (((0,), (0,)), ((), ())), preferred_element_type=F32)


def after(done, *values):
    held, _ = lax.optimization_barrier((values, done))
    return held if len(held) > 1 else held[0]


def slot_place(t, k):
    if k == 0:
        return t
    if k == 1:
        return jnp.where(t == 0, 1, t - 1)
    if k == 2:
        return (t + 2) % LINE
    return jnp.where(t == 3, 0, jnp.where(t == 1, 2, 3))


def coordinates():
    n = lax.axis_size("dp")
    inner = n // LINE
    here = lax.axis_index("dp")
    return here // inner, (here % inner) // 2, here % 2, lax.axis_index("tensor")


def place(blocks, spots, shape):
    listed = spots(0, 0, 0, 0)

    def kernel(*refs):
        sources = refs[: len(blocks)]
        out, held, sem, out_sem = refs[len(blocks) :]
        copies = []
        for k, (b, row, col, rows, cols, to_row, to_col) in enumerate(spots(*coordinates())):
            copies.append(
                pltpu.make_async_copy(
                    sources[b].at[pl.ds(row, rows), pl.ds(col, cols)],
                    held.at[
                        pl.ds(pl.multiple_of(to_row, rows), rows),
                        pl.ds(pl.multiple_of(to_col, cols), cols),
                    ],
                    sem.at[k],
                )
            )
        for copy in copies:
            copy.start()
        for copy in copies:
            copy.wait()
        last = pltpu.make_async_copy(held, out, out_sem)
        last.start()
        last.wait()

    item = blocks[0].dtype.itemsize
    moved = sum(2 * rows * cols * item for _, _, _, rows, cols, _, _ in listed)
    return pl.pallas_call(
        kernel,
        out_shape=jax.ShapeDtypeStruct(shape, blocks[0].dtype),
        in_specs=[pl.BlockSpec(memory_space=pl.ANY)] * len(blocks),
        out_specs=pl.BlockSpec(memory_space=pl.ANY),
        scratch_shapes=[
            pltpu.VMEM(shape, blocks[0].dtype),
            pltpu.SemaphoreType.DMA((len(listed),)),
            pltpu.SemaphoreType.DMA,
        ],
        compiler_params=pltpu.CompilerParams(vmem_limit_bytes=moved // 2 + (4 << 20)),
        cost_estimate=pl.CostEstimate(flops=0, bytes_accessed=moved, transcendentals=0),
    )(*blocks)


class Sends:
    def __init__(self, sems):
        self.sems = sems
        self.made = []

    def start(self, source, target, recv_sem, device, cond=None):
        sem = self.sems.at[len(self.made)]

        def copy():
            return pltpu.make_async_remote_copy(
                src_ref=source,
                dst_ref=target,
                send_sem=sem,
                recv_sem=recv_sem,
                device_id=device,
                device_id_type=pl.DeviceIdType.MESH,
            )

        self.made.append((cond, copy))
        when(cond, lambda: copy().start())

    def wait_sent(self):
        for cond, copy in self.made:
            when(cond, lambda copy=copy: copy().wait_send())


def when(cond, act):
    if cond is None:
        act()
    else:
        pl.when(cond)(act)


def both(first, second):
    if first is None:
        return second
    return first if second is None else jnp.logical_and(first, second)


def arrived(ref, recv_sem, device):
    pltpu.make_async_remote_copy(
        src_ref=ref, dst_ref=ref, send_sem=recv_sem, recv_sem=recv_sem,
        device_id=device, device_id_type=pl.DeviceIdType.MESH,
    ).wait_recv()


def greet(devices):
    barrier = pltpu.get_barrier_semaphore()
    for device in devices:
        pl.semaphore_signal(
            barrier, inc=1, device_id=device, device_id_type=pl.DeviceIdType.MESH
        )
    pl.semaphore_wait(barrier, len(devices))


def start_kernel(side, piece, sliced, scale, *refs):
    w_query, w_key, w_value, w_out, w_gate, w_up, w_down, dm_own = refs[:8]
    length, tokens, attn_gain, cosine, sine, q_gain, k_gain, ffn_gain = refs[8:16]
    outs = refs[16:21]
    proj, attended, totals, h_one, hidden_two, hidden = refs[21:27]
    qkv, out, units, down, dm = bufs = refs[27:32]
    part, cross_sent, cross_got = refs[32:35]
    (
        load_sems, send_sems, qkv_sems, out_sems, unit_sems, pair_sems, down_sems,
        line_sems, core_sems, cross_sem, store_sems,
    ) = refs[35:]
    t, j, c, x = coordinates()
    bits = side.bit_length() - 1
    strip = side * piece

    def at(tt, jj, cc, xx=None):
        return (((tt * side) + jj) * 2 + cc, x if xx is None else xx)

    def block(tt, jj, cc):
        return ((tt * side) + jj) * 2 + cc

    here = at(t, j, c)
    core = at(t, j, 1 - c)
    across = at(t, j, c, 1 - x)
    beside = [at(t, j ^ (1 << bit), c) for bit in range(bits)]
    others = [
        at((t + dt) % LINE, j, c ^ dc) for dt in range(LINE) for dc in range(2) if dt or dc
    ]
    mine = block(t, j, c)
    depth, q_cols = w_query.shape
    k_cols = w_key.shape[1]
    rows, width = tokens.shape
    half = rows // 2

    def rows_of(buf, idx):
        count = depth if buf is qkv else w_out.shape[0]
        return buf.at[pl.ds(pl.multiple_of(idx * count, count), count)]

    own_qkv = pl.ds(pl.multiple_of(mine * depth, depth), depth)
    loads = [
        (w_query, qkv.at[own_qkv, pl.ds(0, q_cols)]),
        (w_key, qkv.at[own_qkv, pl.ds(q_cols, k_cols)]),
        (w_value, qkv.at[own_qkv, pl.ds(q_cols + k_cols, k_cols)]),
        (w_out, rows_of(out, mine)),
        (w_down, down.at[x * side + j]),
        (dm_own.at[pl.ds(pl.multiple_of(x * half, half), half)], dm.at[t, pl.ds(0, half)]),
    ]
    first_unit = len(loads)

    def unit_block(which, tt, jj, cc):
        weight = (w_gate, w_up)[which]
        if sliced:
            col = pl.multiple_of(block(tt, jj, cc) * piece, piece)
            return weight.at[:, pl.ds(col, piece)]
        return weight.at[tt, cc]

    def unit_target(which, tt, jj, cc):
        col = x * strip + (jj * piece if sliced else 0)
        size = piece if sliced else strip
        return units.at[
            which, tt, j, pl.ds(pl.multiple_of(cc * depth, depth), depth),
            pl.ds(pl.multiple_of(col, size), size),
        ]

    def unit_pair(which, tt, jj, xx):
        return units.at[which, tt, jj, :, pl.ds(pl.multiple_of(xx * strip, strip), strip)]

    parts = range(side) if sliced else range(1)
    loads += [
        (unit_block(w, t, jj, c), unit_target(w, t, jj, c)) for w in range(2) for jj in parts
    ]
    loads = [
        pltpu.make_async_copy(a, b, load_sems.at[i]) for i, (a, b) in enumerate(loads)
    ]
    for load in loads:
        load.start()
    greet(others + beside + [across])
    sends = Sends(send_sems)
    for load in loads[:first_unit]:
        load.wait()

    lines = ((qkv, qkv_sems), (out, out_sems))

    def spread(buf, sems, tt, r, cond):
        idx = block(tt, j ^ r, c)
        ref = rows_of(buf, idx)
        for bit in range(bits):
            if (1 << bit) > r:
                sends.start(ref, ref, sems.at[idx], beside[bit], cond)
        sends.start(ref, ref, sems.at[idx], core, cond)

    def pass_on(ref, sem, to_right, to_left):
        if to_right is not False:
            sends.start(ref, ref, sem, at(t + 1, j, c), to_right)
        if to_left is not False:
            sends.start(ref, ref, sem, at(t - 1, j, c), to_left)

    def spread_rest(buf, sems, tt, cond):
        for r in range(1, side):
            idx = block(tt, j ^ r, c)
            when(cond, lambda idx=idx: arrived(rows_of(buf, idx), sems.at[idx], here))
            spread(buf, sems, tt, r, cond)

    def line_places(k):
        return ((t >= k, t - k, True), (t + k < LINE, t + k, False))

    def forward(ref, sem, cond, rightward):
        if rightward:
            pass_on(ref, sem, both(cond, t < LINE - 1), False)
        else:
            pass_on(ref, sem, False, both(cond, t > 0))

    def set_out(buf, sems):
        pass_on(rows_of(buf, mine), sems.at[mine], t < LINE - 1, t > 0)
        spread(buf, sems, t, 0, None)

    def line_step(buf, sems, k):
        for cond, tt, rightward in line_places(k):
            idx = block(tt, j, c)
            when(cond, lambda idx=idx: arrived(rows_of(buf, idx), sems.at[idx], here))
            if k < LINE - 1:
                forward(rows_of(buf, idx), sems.at[idx], cond, rightward)
            spread(buf, sems, tt, 0, cond)
        if k == 1:
            spread_rest(buf, sems, t, None)
        else:
            spread_rest(buf, sems, t - k + 1, t >= k - 1)
            spread_rest(buf, sems, t + k - 1, t + k - 1 < LINE)

    own_down = x * side + j

    def down_set_out():
        for bit in range(bits):
            sends.start(
                down.at[own_down], down.at[own_down], down_sems.at[own_down], beside[bit]
            )

    def down_rest():
        for r in range(1, side):
            idx = x * side + (j ^ r)
            arrived(down.at[idx], down_sems.at[idx], here)
            for bit in range(bits):
                if (1 << bit) > r:
                    sends.start(down.at[idx], down.at[idx], down_sems.at[idx], beside[bit])
            sends.start(down.at[idx], down.at[idx], down_sems.at[idx], across)

    def units_set_out():
        for dt in range(LINE):
            for dc in range(2):
                if dt or dc:
                    tt, cc = (t + dt) % LINE, c ^ dc
                    for w in range(2):
                        for jj in parts:
                            sends.start(
                                unit_block(w, tt, jj, cc),
                                unit_target(w, t, jj, c),
                                unit_sems.at[w, t * 2 + c, jj],
                                at(tt, j, cc),
                            )

    set_out(*lines[0])
    set_out(*lines[1])
    sends.start(down.at[own_down], down.at[own_down], down_sems.at[own_down], across)
    chunk = rows // 16

    @pl.loop(0, 16)
    def _(i):
        span = pl.ds(pl.multiple_of(i * chunk, chunk), chunk)
        hidden[span, :] = rms_scale(tokens[span, :].astype(F32), attn_gain[...]).astype(BF)

    @pl.loop(0, 8)
    def _(i):
        span = pl.ds(pl.multiple_of(i * chunk, chunk), chunk)
        row = lax.broadcasted_iota(jnp.int32, (chunk, width), 0) + i * chunk + x * half
        kept = dm[t, span, :].astype(F32)
        dm[t, span, :] = jnp.where(row < length[0], kept, 0.0).astype(BF)

    for k in range(1, LINE):
        line_step(*lines[0], k)
        line_step(*lines[1], k)
        if k == LINE - 2:
            units_set_out()
    down_set_out()
    stores = []

    def store(source, target):
        copy = pltpu.make_async_copy(source, target, store_sems.at[len(stores)])
        copy.start()
        stores.append(copy)

    def send_pair(w, tt, jj, xx, device):
        ref = unit_pair(w, tt, jj, xx)
        sends.start(ref, ref, pair_sems.at[w, tt, jj, xx], device)

    def pair_came(w, tt, jj, xx):
        arrived(unit_pair(w, tt, jj, xx), pair_sems.at[w, tt, jj, xx], here)

    def unit_first(tt):
        for cc in range(2):
            mine = jnp.logical_and(tt == t, cc == c)
            for w in range(2):
                for jj in parts:
                    when(
                        jnp.logical_not(mine),
                        lambda w=w, cc=cc, jj=jj: arrived(
                            unit_target(w, tt, jj, cc), unit_sems.at[w, tt * 2 + cc, jj], here
                        ),
                    )
        for w in range(2):
            for bit in range(bits):
                send_pair(w, tt, j, x, beside[bit])
            send_pair(w, tt, j, x, across)

    def unit_second(tt, by_side):
        for r in range(1, side):
            for w in range(2):
                pair_came(w, tt, j ^ r, x)
                for bit in range(bits):
                    if (1 << bit) > r:
                        send_pair(w, tt, j ^ r, x, beside[bit])
                if w not in by_side:
                    send_pair(w, tt, j ^ r, x, across)
        for w in by_side:
            pair_came(w, tt, j, 1 - x)
            for bit in range(bits):
                send_pair(w, tt, j, 1 - x, beside[bit])

    def unit_last(tt, by_side):
        for w in range(2):
            for r in range(1 if w in by_side else 0, side):
                pair_came(w, tt, j ^ r, 1 - x)
                for bit in range(bits):
                    if w in by_side and (1 << bit) > r:
                        send_pair(w, tt, j ^ r, 1 - x, beside[bit])

    dm_rows = dm.at[t, pl.ds(0, half)]

    def dm_to_core(tt, cond):
        sends.start(
            dm.at[tt, pl.ds(0, half)], dm.at[tt, pl.ds(half, half)], core_sems.at[tt], core, cond
        )

    def dm_step(k):
        for cond, tt, rightward in line_places(k):
            ref = dm.at[tt, pl.ds(0, half)]
            when(cond, lambda ref=ref, tt=tt: arrived(ref, line_sems.at[tt], here))
            if k < LINE - 1:
                forward(ref, line_sems.at[tt], cond, rightward)
            dm_to_core(tt, cond)

    def finish_line(buf, sems):
        spread_rest(buf, sems, t - LINE + 1, t >= LINE - 1)
        spread_rest(buf, sems, t + LINE - 1, t < 1)
        for tt in range(LINE):
            for jj in range(side):
                idx = block(tt, jj, 1 - c)
                arrived(rows_of(buf, idx), sems.at[idx], here)

    finish_line(*lines[0])
    store(qkv, outs[0])
    for load in loads[first_unit:]:
        load.wait()
    unit_first(t)
    pass_on(dm_rows, line_sems.at[t], t < LINE - 1, t > 0)
    dm_to_core(t, None)

    tile = 256

    @pl.loop(0, proj.shape[1] // tile)
    def _(i):
        cols = pl.ds(pl.multiple_of(i * tile, tile), tile)
        proj[:, cols] = mm(hidden[...], qkv[:, cols])

    group = q_cols // k_cols * HEAD
    key_heads = k_cols // HEAD

    def attend_head(g):
        pair = pl.multiple_of(g // 2 * LANES, LANES)
        wide = pl.ds(pl.multiple_of(g * group, group), group)
        attend_kernel(
            rows // 2, scale, g % 2 == 1, length,
            proj.at[:, wide],
            proj.at[:, pl.ds(q_cols + pair, LANES)],
            proj.at[:, pl.ds(q_cols + k_cols + pair, LANES)],
            cosine, sine, q_gain, k_gain,
            attended.at[:, wide],
            totals.at[:, pl.ds(pl.multiple_of(g * LANES, LANES), LANES)],
        )

    pl.loop(0, key_heads)(attend_head)

    finish_line(*lines[1])
    store(out, outs[1])
    wide = 512
    other_rows = pl.ds(pl.multiple_of((1 - x) * half, half), half)
    own_rows = pl.ds(pl.multiple_of(x * half, half), half)

    @pl.loop(0, width // wide)
    def _(i):
        cols = pl.ds(pl.multiple_of(i * wide, wide), wide)
        cross_sent[:, cols] = mm(attended[other_rows, :], out[:, cols]).astype(BF)

    sends.start(cross_sent, cross_got, cross_sem, across)

    @pl.loop(0, width // wide)
    def _(i):
        cols = pl.ds(pl.multiple_of(i * wide, wide), wide)
        part[:, cols] = mm(attended[own_rows, :], out[:, cols])

    for k in range(1, LINE):
        unit_first(slot_place(t, k))
    down_rest()
    unit_second(t, (0,))
    dm_step(1)
    for k in range(1, LINE):
        unit_second(slot_place(t, k), (0, 1))
    dm_step(2)

    arrived(cross_got, cross_sem, here)
    step = half // 8

    @pl.loop(0, 8)
    def _(i):
        span = pl.ds(pl.multiple_of(i * step, step), step)
        rows_here = pl.ds(pl.multiple_of(x * half + i * step, step), step)
        total = tokens[rows_here, :].astype(F32) + part[span, :] + cross_got[span, :].astype(F32)
        h_one[span, :] = total
        hidden_two[span, :] = rms_scale(total, ffn_gain[...]).astype(BF)

    dm_step(3)
    for k in range(LINE):
        unit_last(slot_place(t, k), (0, 1) if k else (0,))
    store(units, outs[2])
    for jj in range(side):
        idx = (1 - x) * side + jj
        arrived(down.at[idx], down_sems.at[idx], here)
    store(down, outs[3])
    for tt in range(LINE):
        arrived(dm.at[tt, pl.ds(half, half)], core_sems.at[tt], here)
    store(dm, outs[4])
    sends.wait_sent()
    for copy in stores:
        copy.wait()


def start_layer(n, weights, cotangent, length, tokens, attn_gain, tables, gains, ffn_gain):
    w_query, w_key, w_value, w_out, w_gate, w_up, w_down = weights
    side = n // LINE // 2
    depth, piece, width = w_gate.shape[0], w_down.shape[0], w_down.shape[1]
    rows, half = tokens.shape[0], tokens.shape[0] // 2
    q_cols, k_cols = w_query.shape[1], w_key.shape[1]
    cols = q_cols + 2 * k_cols
    strip = side * piece
    sliced = piece % LANES == 0
    if not sliced:
        w_gate, w_up = (
            w.reshape(depth, LINE, side, 2, piece)
            .transpose(1, 3, 0, 2, 4)
            .reshape(LINE, 2, depth, strip)
            for w in (w_gate, w_up)
        )
    shapes = [
        (width, cols),
        (q_cols, width),
        (2, LINE, side, 2 * depth, 2 * strip),
        (2 * side, piece, width),
        (LINE, 2 * half, width),
    ]
    slots = 2 * LINE - 1
    line_sends = 2 * (LINE - 1) + slots * (2 * side - 1)
    sends = 2 * line_sends + 2 * side - 1 + 14 * side + 3 * LINE + 8 + 8 * side * LINE
    any_space = pl.BlockSpec(memory_space=pl.ANY)
    vmem = pl.BlockSpec(memory_space=pltpu.VMEM)
    return pl.pallas_call(
        functools.partial(start_kernel, side, piece, sliced, 1.0 / math.sqrt(HEAD)),
        out_shape=[jax.ShapeDtypeStruct(shape, BF) for shape in shapes]
        + [
            jax.ShapeDtypeStruct((rows, cols), F32),
            jax.ShapeDtypeStruct((rows, q_cols), BF),
            jax.ShapeDtypeStruct((rows, k_cols // HEAD * LANES), F32),
            jax.ShapeDtypeStruct((half, width), F32),
            jax.ShapeDtypeStruct((half, width), BF),
            jax.ShapeDtypeStruct((rows, width), BF),
        ],
        in_specs=[any_space] * 8 + [pl.BlockSpec(memory_space=pltpu.SMEM)] + [vmem] * 7,
        out_specs=[any_space] * 5 + [vmem] * 6,
        scratch_shapes=[pltpu.VMEM(shape, BF) for shape in shapes]
        + [
            pltpu.VMEM((half, width), F32),
            pltpu.VMEM((half, width), BF),
            pltpu.VMEM((half, width), BF),
            pltpu.SemaphoreType.DMA((6 + 2 * side,)),
            pltpu.SemaphoreType.DMA((sends,)),
            pltpu.SemaphoreType.DMA((n,)),
            pltpu.SemaphoreType.DMA((n,)),
            pltpu.SemaphoreType.DMA((2, LINE * 2, side)),
            pltpu.SemaphoreType.DMA((2, LINE, side, 2)),
            pltpu.SemaphoreType.DMA((2 * side,)),
            pltpu.SemaphoreType.DMA((LINE,)),
            pltpu.SemaphoreType.DMA((LINE,)),
            pltpu.SemaphoreType.DMA,
            pltpu.SemaphoreType.DMA((5,)),
        ],
        compiler_params=pltpu.CompilerParams(
            collective_id=0, has_side_effects=True, vmem_limit_bytes=62 << 20
        ),
        cost_estimate=pl.CostEstimate(
            flops=2 * rows * width * cols, bytes_accessed=500 << 20, transcendentals=rows * rows
        ),
    )(
        w_query, w_key, w_value, w_out, w_gate, w_up, w_down, cotangent, length, tokens,
        attn_gain[None, :], *tables, *gains, ffn_gain[None, :],
    )


def feed_kernel(side, *refs):
    h_own, dm_all, units, down, h_one, gain = refs[:6]
    out_half, dab, gain_part, e_own, e_core, e_line, f_out = refs[6:13]
    g_down, gate_mid, up_mid, gate_kept, gate_got, up_kept, up_got = refs[13:20]
    wg, wu, wd, h_all, dm, act, dg, du, e_stage, f_stage, f_send, f_core = refs[20:32]
    load_sems, store_sems, send_sems, line_sems, core_sems, back_sems = refs[32:38]
    done_sems, gate_sems, up_sems, mid_sems, last_sems, e_sems, step_sems, dab_sem, row_sems = refs[38:]
    t, j, c, x = coordinates()
    half, width = h_own.shape
    unit_count = wd.shape[0]
    strip = unit_count // 2
    rows = 2 * half
    bits = side.bit_length() - 1

    def at(tt, cc, jj=None, xx=None):
        jj, xx = j if jj is None else jj, x if xx is None else xx
        return ((tt * side + jj) * 2 + cc, xx)

    here, core, across = at(t, c), at(t, 1 - c), at(t, c, None, 1 - x)
    beside = at(t, c, j ^ (side // 2))
    others = [at((t + dt) % LINE, c) for dt in range(1, LINE)]
    loads = [
        (h_own, h_all.at[t, pl.ds(0, half)]),
        (units.at[0], wg), (units.at[1], wu), (dm_all, dm), (down, wd),
    ]
    loads = [pltpu.make_async_copy(a, b, load_sems.at[i]) for i, (a, b) in enumerate(loads)]
    for load in loads:
        load.start()
    greet(others + [core, across] + ([beside] if bits else []))
    sends, rows_sent = Sends(send_sems), Sends(row_sems)

    def own_rows(tt):
        return h_all.at[tt, pl.ds(0, half)]

    def to_core(tt, cond):
        rows_sent.start(
            own_rows(tt), h_all.at[tt, pl.ds(half, half)], core_sems.at[tt], core, cond
        )

    loads[0].wait()
    rows_sent.start(own_rows(t), own_rows(t), line_sems.at[t], at(t + 1, c), t < LINE - 1)
    rows_sent.start(own_rows(t), own_rows(t), line_sems.at[t], at(t - 1, c), t > 0)
    to_core(t, None)
    for load in loads[1:]:
        load.wait()

    tile = min(512, unit_count)
    wide = min(1024, width)
    e_waits, f_sent, stores = [], [], []

    def store(source, target):
        copy = pltpu.make_async_copy(source, target, store_sems.at[len(stores)])
        copy.start()
        stores.append(copy)
        return copy

    def f_go(k):
        sends.start(
            f_stage.at[k], f_out.at[t], done_sems.at[t], at(slot_place(t, k), c)
        )

    def kept_out(k):
        copy = pltpu.make_async_copy(
            e_stage.at[pl.ds(0, half)], e_own.at[k], mid_sems.at[2, 2 * LINE - 1]
        )
        copy.start()
        return copy.wait

    def later(source, target, sem, device):
        sends.start(source, target, sem, device)
        copy = sends.made.pop()[1]
        sends.made.append((None, None))
        return lambda: copy().wait_send()

    for k in range(LINE):
        tt = slot_place(t, k)
        if k:
            for cond, place_of, forward, target in (
                (t >= k, t - k, t < LINE - 1, t + 1),
                (t + k < LINE, t + k, t > 0, t - 1),
            ):
                when(
                    cond,
                    lambda p=place_of: arrived(own_rows(p), line_sems.at[p], here),
                )
                if k < LINE - 1:
                    rows_sent.start(
                        own_rows(place_of), own_rows(place_of), line_sems.at[place_of],
                        at(target, c), jnp.logical_and(cond, forward),
                    )
                to_core(place_of, cond)
        if k >= 2:
            f_go(k - 1)
        arrived(h_all.at[tt, pl.ds(half, half)], core_sems.at[tt], here)
        if k >= 2:
            f_sent[k - 2]()

        @pl.loop(0, unit_count // tile)
        def _(i):
            cols = pl.ds(pl.multiple_of(i * tile, tile), tile)
            hidden = h_all[tt]
            gate = mm(hidden, wg[:, cols])
            up = mm(hidden, wu[:, cols])
            grad_act = mm_nt(dm[tt], wd[cols, :])
            sigma = lax.logistic(gate)
            silu = gate * sigma
            act[tt, :, cols] = (silu * up).astype(BF)
            dg[tt, :, cols] = (grad_act * up * (sigma * (1.0 + gate * (1.0 - sigma)))).astype(BF)
            du[tt, :, cols] = (grad_act * silu).astype(BF)

        slot = k % 2

        @pl.loop(0, width // wide)
        def _(i):
            span = pl.ds(pl.multiple_of(i * wide, wide), wide)
            grad = mm_nt(dg[tt], wg[span, :]) + mm_nt(du[tt], wu[span, :])
            f_stage[k, :, span] = grad[:half].astype(BF)
            f_send[slot, :, span] = grad[half:].astype(BF)

        f_sent.append(later(f_send.at[slot], f_core.at[k], back_sems.at[k], core))
        for wait in e_waits:
            wait()

        @pl.loop(0, width // wide)
        def _(i):
            span = pl.ds(pl.multiple_of(i * wide, wide), wide)
            e_stage[:, span] = mm(act[tt], wd[:, span]).astype(BF)

        e_waits = [
            kept_out(k),
            later(e_stage.at[pl.ds(half, half)], e_core.at[k], e_sems.at[k], core),
        ]
        arrived(f_core.at[k], back_sems.at[k], here)

        @pl.loop(0, 4)
        def _(i):
            part = pl.ds(pl.multiple_of(i * (half // 4), half // 4), half // 4)
            f_stage[k, part, :] = (
                f_stage[k, part, :].astype(F32) + f_core[k, part, :].astype(F32)
            ).astype(BF)

        if k == LINE - 1:
            f_go(k)

    group = width // LINE
    far = pl.ds(pl.multiple_of((1 - x) * strip, strip), strip)
    near = pl.ds(pl.multiple_of(x * strip, strip), strip)

    def weight_grad(target, grads, tt, send):
        @pl.loop(0, 1)
        def _(i):
            span = pl.ds(tt * group, group)
            hidden = h_all[:, :, span].reshape(LINE * rows, group)
            target[span, :] = mm_tn(hidden, grads[...].reshape(LINE * rows, unit_count)).astype(BF)

        send(tt)

    block = group // side
    whole = side == 2

    def side_rows(tt, jj):
        return pl.ds(pl.multiple_of(tt * group + jj * block, block), block)

    def send_gate(tt):
        span = pl.ds(tt * group, group)
        sends.start(wg.at[span, far], gate_mid.at[span], gate_sems.at[tt], across)
        if not whole:
            store(wg.at[span, near], gate_kept.at[span])

    def send_up(tt):
        for r in range(side):
            span = side_rows(tt, j ^ r)
            if r >= side // 2:
                k = r - side // 2
                sends.start(wu.at[span], up_mid.at[k, tt], up_sems.at[k, tt], beside)
            elif not whole:
                store(wu.at[span], up_kept.at[r, tt])

    for tt in range(LINE):
        weight_grad(wg, dg, tt, send_gate)
        weight_grad(wu, du, tt, send_up)
    tile = min(256, unit_count)

    @pl.loop(0, unit_count // tile)
    def _(i):
        cols = pl.ds(pl.multiple_of(i * tile, tile), tile)
        units_part = act[:, :, cols].reshape(LINE * rows, tile)
        wd[cols, :] = mm_tn(units_part, dm[...].reshape(LINE * rows, width)).astype(BF)

    store(wd, g_down)

    def fetch(pairs):
        copies = [
            pltpu.make_async_copy(a, b, mid_sems.at[2, i]) for i, (a, b) in enumerate(pairs)
        ]
        for copy in copies:
            copy.start()
        for copy in copies:
            copy.wait()

    def add(target, other):
        count = target.shape[0]
        step = min(64, count)

        @pl.loop(0, count // step)
        def _(i):
            part = pl.ds(pl.multiple_of(i * step, step), step)
            target[part, :] = (target[part, :].astype(F32) + other[part, :].astype(F32)).astype(BF)

    upper, lower = pl.ds(0, half), pl.ds(half, half)
    for wait in e_waits:
        wait()
    rows_sent.wait_sent()
    for k in range(LINE):
        arrived(e_core.at[k], e_sems.at[k], here)
    fetch(
        [(e_own.at[k], h_all.at[k, upper]) for k in range(LINE)]
        + [(e_core.at[k], h_all.at[k, lower]) for k in range(LINE)]
    )
    for k in reversed(range(LINE)):
        add(h_all.at[k, upper], h_all.at[k, lower])

    def line_came(i, way, cond, k):
        def act_on():
            arrived(e_line.at[way, i], step_sems.at[way, i], here)
            fetch([(e_line.at[way, i], h_all.at[way, lower])])
            add(h_all.at[k, upper], h_all.at[way, lower])

        when(cond, act_on)

    def line_go(i, way, cond, k):
        sends.start(
            h_all.at[k, upper], e_line.at[way, i], step_sems.at[way, i], at(t + 1 - 2 * way, c),
            cond,
        )

    inner = jnp.logical_and(t >= 1, t <= 2)
    line_go(0, 0, t == 0, 3)
    line_go(0, 1, t == 3, 3)

    for dt in range(1, LINE):
        p = (t + dt) % LINE
        arrived(f_out.at[p], done_sems.at[p], here)
    fetch([(f_out.at[(t + dt) % LINE], f_core.at[dt]) for dt in range(1, LINE)])
    gain_part[...] = jnp.zeros_like(gain_part)
    step = half // 16

    @pl.loop(0, 16)
    def _(i):
        part = pl.ds(pl.multiple_of(i * step, step), step)
        grad = f_stage[0, part, :].astype(F32)
        for dt in range(1, LINE):
            grad = grad + f_core[dt, part, :].astype(F32)
        values = h_one[part, :]
        scale = lax.rsqrt(jnp.mean(values * values, axis=1, keepdims=True) + EPS)
        gain_part[...] += jnp.sum(grad * values * scale, axis=0, keepdims=True)
        grad = grad * gain[...]
        back = jnp.mean(grad * values, axis=1, keepdims=True) * scale * scale
        grad = dm[t, part, :].astype(F32) + scale * (grad - values * back)
        e_stage[part, :] = grad.astype(BF)

    own_rows_out = dab.at[pl.ds(pl.multiple_of(x * half, half), half)]
    store(e_stage.at[upper], own_rows_out)
    sends.start(e_stage.at[upper], own_rows_out, dab_sem, across)
    line_came(0, 0, t == 1, 2)
    line_came(0, 1, t == 2, 2)
    line_go(1, 0, t <= 1, 2)
    line_go(1, 1, t >= 2, 2)
    if whole:
        copies = []
        for tt in range(LINE):
            span = pl.ds(tt * group, group)
            arrived(gate_mid.at[span], gate_sems.at[tt], here)
            arrived(up_mid.at[0, tt], up_sems.at[0, tt], here)
            for i, (source, target) in enumerate(
                (
                    (gate_mid.at[span], dg.at[tt, :, pl.ds(0, strip)]),
                    (up_mid.at[0, tt], du.at[tt, pl.ds(0, block)]),
                )
            ):
                copies.append(pltpu.make_async_copy(source, target, mid_sems.at[i, tt]))
                copies[-1].start()
        for tt in range(LINE):
            mine = side_rows(tt, j)
            copies[2 * tt].wait()
            for jj in range(side):
                span = pl.ds(tt * group + jj * block, block)
                wg[span, near] = (
                    wg[span, near].astype(F32)
                    + dg[tt, pl.ds(jj * block, block), pl.ds(0, strip)].astype(F32)
                ).astype(BF)
            sends.start(
                wg.at[side_rows(tt, 1 - j), near], gate_got.at[tt], last_sems.at[0, tt], beside
            )
            store(wg.at[mine, near], gate_kept.at[tt])
            copies[2 * tt + 1].wait()
            wu[mine, :] = (
                wu[mine, :].astype(F32) + du[tt, pl.ds(0, block), :].astype(F32)
            ).astype(BF)
            sends.start(wu.at[mine, far], up_got.at[tt], last_sems.at[1, tt], across)
            store(wu.at[mine, near], up_kept.at[tt])
    line_came(1, 0, inner, 3)
    line_came(1, 1, inner, 1)
    line_go(2, 0, t == 0, 1)
    line_go(2, 0, inner, 3)
    line_go(2, 1, t >= 1, 1)
    for sent in f_sent[LINE - 2 :]:
        sent()
    sends.made = [item for item in sends.made if item[1] is not None]
    for tt in range(LINE):
        if whole:
            arrived(gate_got.at[tt], last_sems.at[0, tt], here)
            arrived(up_got.at[tt], last_sems.at[1, tt], here)
        else:
            arrived(gate_mid.at[pl.ds(tt * group, group)], gate_sems.at[tt], here)
            for k in range(side // 2):
                arrived(up_mid.at[k, tt], up_sems.at[k, tt], here)
    arrived(dab.at[pl.ds(pl.multiple_of((1 - x) * half, half), half)], dab_sem, here)
    line_came(2, 0, t >= 1, 0)
    line_came(2, 1, t <= 2, 0)

    @pl.loop(0, 16)
    def _(i):
        part = pl.ds(pl.multiple_of(i * step, step), step)
        out_half[part, :] = (h_one[part, :] + h_all[0, part, :].astype(F32)).astype(BF)

    sends.wait_sent()
    for copy in stores:
        copy.wait()


def feed_forward(side, h_own, dm_all, units, down, h_one, ffn_gain):
    half, width = h_own.shape
    unit_count = down.shape[0]
    strip = unit_count // 2
    rows = 2 * half
    group = width // LINE
    block = group // side
    any_space = pl.BlockSpec(memory_space=pl.ANY)
    vmem = pl.BlockSpec(memory_space=pltpu.VMEM)
    mids = [(width, strip), (side // 2, LINE, block, unit_count)]
    last = (LINE, block, strip)
    blocks = (LINE, half, width)
    outs = [blocks, blocks, (2, 3, half, width), blocks, (unit_count, width)] + mids
    outs += [last] * 4 if side == 2 else [mids[0], (1, LANES), mids[1], (1, LANES)]
    held = [
        (width, unit_count), (width, unit_count), (unit_count, width),
        (LINE, rows, width), (LINE, rows, width),
        (LINE, rows, unit_count), (LINE, rows, unit_count), (LINE, rows, unit_count),
        (rows, width), (LINE, half, width), (2, half, width), (LINE, half, width),
    ]
    sends = 3 + 4 * (LINE - 1) + 3 * LINE + 3 * LINE + side // 2 * LINE + 8
    return pl.pallas_call(
        functools.partial(feed_kernel, side),
        out_shape=[
            jax.ShapeDtypeStruct((half, width), BF),
            jax.ShapeDtypeStruct((rows, width), BF),
            jax.ShapeDtypeStruct((1, width), F32),
        ]
        + [jax.ShapeDtypeStruct(shape, BF) for shape in outs],
        in_specs=[any_space] * 4 + [vmem] * 2,
        out_specs=[vmem, any_space, vmem] + [any_space] * len(outs),
        scratch_shapes=[pltpu.VMEM(shape, BF) for shape in held]
        + [
            pltpu.SemaphoreType.DMA((5,)),
            pltpu.SemaphoreType.DMA((3 * LINE + 2 + side // 2 * LINE,)),
            pltpu.SemaphoreType.DMA((sends,)),
            pltpu.SemaphoreType.DMA((LINE,)),
            pltpu.SemaphoreType.DMA((LINE,)),
            pltpu.SemaphoreType.DMA((LINE,)),
            pltpu.SemaphoreType.DMA((LINE,)),
            pltpu.SemaphoreType.DMA((LINE,)),
            pltpu.SemaphoreType.DMA((side // 2, LINE)),
            pltpu.SemaphoreType.DMA((3, 2 * LINE)),
            pltpu.SemaphoreType.DMA((2, LINE)),
            pltpu.SemaphoreType.DMA((LINE,)),
            pltpu.SemaphoreType.DMA((2, 3)),
            pltpu.SemaphoreType.DMA,
            pltpu.SemaphoreType.DMA((3 + 4 * (LINE - 1),)),
        ],
        compiler_params=pltpu.CompilerParams(
            collective_id=1, has_side_effects=True, vmem_limit_bytes=63 << 20
        ),
        cost_estimate=pl.CostEstimate(
            flops=18 * LINE * rows * width * unit_count, bytes_accessed=100 << 20,
            transcendentals=LINE * rows * unit_count,
        ),
    )(h_own, dm_all, units, down, h_one, ffn_gain[None, :])


def end_kernel(side, piece, scale, *refs):
    gate, gate_got, up, up_got, down, down_got, w_qkv, length = refs[:8]
    hidden, proj, totals, grad_o, cosine, sine, q_gain, k_gain, attn_gain, ffn_part = refs[8:18]
    q_out, k_out, v_out, homes_out, down_out, small_out, low_out, low_got_out = refs[18:26]
    (
        heads, heads_core, heads_side, line_right, line_left,
        gates, gates_got, ups, ups_got, downs, downs_got, downs_across, homes,
        grads, weights, low, low_got, keys_sum, vals_sum, q_sum, k_sum, smalls,
    ) = refs[26:48]
    load_sems, send_sems, core_sems, side_sems, line_sems, across_sems = refs[48:54]
    home_sems, small_sems, store_sems = refs[54:]
    t, j, c, x = coordinates()
    bits = side.bit_length() - 1
    depth, q_cols = q_out.shape
    k_cols = k_out.shape[1]
    strip = side * piece

    def at(tt, jj, cc, xx=None):
        return (((tt * side) + jj) * 2 + cc, x if xx is None else xx)

    def block(tt, jj, cc):
        return ((tt * side) + jj) * 2 + cc

    here, core, across = at(t, j, c), at(t, j, 1 - c), at(t, j, c, 1 - x)
    beside = [at(t, j ^ (1 << bit), c) for bit in range(bits)]
    others = [
        at((t + dt) % LINE, j, c ^ dc) for dt in range(LINE) for dc in range(2) if dt or dc
    ]
    loads = [
        (gate, gates), (gate_got, gates_got), (up, ups), (up_got, ups_got),
        (down.at[x], downs) if side == 2 else (down, downs),
        (w_qkv, weights),
    ]
    if side != 2:
        loads.append((down_got, downs_got))
    loads = [pltpu.make_async_copy(a, b, load_sems.at[i]) for i, (a, b) in enumerate(loads)]
    for load in loads:
        load.start()
    greet(others + beside + [across])
    sends = Sends(send_sems)

    def add(target, first, second):
        count = first.shape[0]
        step = min(64, count)

        @pl.loop(0, count // step)
        def _(i):
            part = pl.ds(pl.multiple_of(i * step, step), step)
            target[part, :] = (first[part, :].astype(F32) + second[part, :].astype(F32)).astype(
                target.dtype
            )

    def go_home(which, rows):
        for tt in range(LINE):
            for cc in range(2):
                mine = jnp.logical_and(t == tt, c == cc)
                source = rows.at[tt, pl.ds(cc * depth, depth)]
                target = homes.at[which, t * 2 + c]
                sends.start(
                    source, target, home_sems.at[which, t * 2 + c], at(tt, j, cc),
                    jnp.logical_not(mine),
                )

                @pl.when(mine)
                def _():
                    homes[which, tt * 2 + cc] = source[...]

    if side == 2:
        sends.start(down.at[1 - x], downs_got, across_sems.at[2], across)
    for which, (mine, got) in enumerate(((gates, gates_got), (ups, ups_got))):
        loads[2 * which].wait()
        loads[2 * which + 1].wait()
        for tt in range(LINE):
            add(mine.at[tt], mine.at[tt], got.at[tt])
        go_home(which, mine)

    def down_second():
        loads[4].wait()
        if side == 2:
            arrived(downs_got, across_sems.at[2], here)
        else:
            loads[6].wait()
        for xx in range(2):
            add(downs.at[xx], downs.at[xx], downs_got.at[xx])
        if side == 2:
            sends.start(downs.at[1 - j], downs_across, across_sems.at[0], beside[0])
        else:
            sends.start(downs.at[1 - x], downs_across, across_sems.at[0], across)

    q_sum[...] = jnp.zeros_like(q_sum)
    k_sum[...] = jnp.zeros_like(k_sum)
    rows = hidden.shape[0]
    group = q_cols // k_cols * HEAD

    @pl.loop(0, k_cols // HEAD)
    def _(g):
        pair = pl.multiple_of(g // 2 * LANES, LANES)
        wide = pl.ds(pl.multiple_of(g * group, group), group)
        k_pair = pl.ds(q_cols + pair, LANES)
        v_pair = pl.ds(q_cols + k_cols + pair, LANES)
        attend_back_kernel(
            rows // 2, scale, g % 2 == 1, length,
            proj.at[:, wide], proj.at[:, k_pair], proj.at[:, v_pair],
            cosine, sine, q_gain, k_gain,
            totals.at[:, pl.ds(pl.multiple_of(g * LANES, LANES), LANES)],
            grad_o.at[:, wide],
            grads.at[:, wide], grads.at[:, k_pair], grads.at[:, v_pair],
            q_sum, k_sum, keys_sum, vals_sum,
        )

    width = hidden.shape[1]
    place_rows = width // LINE
    tile = min(256, place_rows)
    for q in reversed(range(LINE)):
        tt = slot_place(t, q)

        @pl.loop(0, place_rows // tile)
        def _(i):
            span = pl.ds(pl.multiple_of(tt * place_rows + i * tile, tile), tile)
            grad = mm_tn(hidden[:, span], grads[...]).astype(BF)
            first = tt * (2 * side) + i * (tile // depth)
            heads[pl.ds(first, tile // depth)] = grad.reshape(tile // depth, depth, -1)

        for r in range(side):
            sends.start(
                heads.at[block(tt, j ^ r, 1 - c)], heads_core.at[tt, j ^ r],
                core_sems.at[tt, j ^ r], core,
            )

    loads[5].wait()
    wide = min(512, width)
    for i in range(width // wide):
        cols = pl.ds(i * wide, wide)
        grad = mm_nt(grads[...], weights[cols, :])
        low[:, cols] = grad.astype(BF)
        part = jnp.sum(grad * hidden[:, cols].astype(F32), axis=0, keepdims=True)
        part = part / attn_gain[:, cols]
        for k in range(wide // LANES):
            smalls[0, pl.ds(i * (wide // LANES) + k, 1), :] = part[:, k * LANES : (k + 1) * LANES]
    sends.start(low, low_got, across_sems.at[1], across)
    count = width // LANES
    smalls[0, pl.ds(count, count), :] = ffn_part[...]
    q_part, k_part = q_sum[...], k_sum[...]
    q_part = q_part + pltpu.roll(q_part, HEAD, 1)
    k_part = k_part + pltpu.roll(k_part, HEAD, 1)
    smalls[0, pl.ds(2 * count, 1), :] = jnp.where(low_lanes(q_part.shape), q_part, k_part)

    partners = [core] + beside + [across, at(t ^ 1, j, c), at(t ^ 2, j, c)]

    def small_step(i):
        if i:
            arrived(smalls.at[2 * i], small_sems.at[i - 1], here)
            smalls[2 * i - 1] = smalls[max(2 * i - 3, 0)] + smalls[2 * i]
        if i < len(partners):
            source = smalls.at[2 * i - 1] if i else smalls.at[0]
            sends.start(source, smalls.at[2 * i + 2], small_sems.at[i], partners[i])
        return i + 1

    def side_first(q):
        tt = slot_place(t, q)
        for r in reversed(range(side)):
            arrived(heads_core.at[tt, j ^ r], core_sems.at[tt, j ^ r], here)
            mine = heads.at[block(tt, j ^ r, c)]
            add(mine, mine, heads_core.at[tt, j ^ r])
            if bits and r >= side // 2:
                k = side // 2 - 1 + r - side // 2
                sends.start(mine, heads_side.at[tt, k], side_sems.at[tt, k], beside[bits - 1])

    def side_rest(q):
        tt = slot_place(t, q)
        for bit in reversed(range(bits)):
            half = 1 << bit
            for r in range(half):
                arrived(heads_side.at[tt, half - 1 + r], side_sems.at[tt, half - 1 + r], here)
                mine = heads.at[block(tt, j ^ r, c)]
                add(mine, mine, heads_side.at[tt, half - 1 + r])
                if bit and r >= half // 2:
                    k = half // 2 - 1 + r - half // 2
                    sends.start(
                        mine, heads_side.at[tt, k], side_sems.at[tt, k], beside[bit - 1]
                    )
        return heads.at[block(tt, j, c)]

    def line_came(i, way, cond, target):
        line = (line_right, line_left)[way]

        def act():
            arrived(line.at[i], line_sems.at[way, i], here)
            add(target, target, line.at[i])

        when(cond, act)

    def line_go(i, way, cond, source):
        line = (line_right, line_left)[way]
        sends.start(
            source, line.at[i], line_sems.at[way, i], at(t + 1 - 2 * way, j, c), cond
        )

    step = small_step(0)
    side_first(3)
    side_first(2)
    step = small_step(step)
    p3 = side_rest(3)
    line_go(0, 0, t == 0, p3)
    line_go(0, 1, t == 3, p3)
    side_first(1)
    step = small_step(step)
    p2 = side_rest(2)
    line_came(0, 0, t == 1, p2)
    line_came(0, 1, t == 2, p2)
    line_go(1, 0, t <= 1, p2)
    line_go(1, 1, t >= 2, p2)
    side_first(0)
    down_second()

    step = small_step(step)
    p1 = side_rest(1)
    line_came(1, 0, jnp.logical_and(t >= 1, t <= 2), p3)
    line_came(1, 1, jnp.logical_and(t >= 1, t <= 2), p1)
    line_go(2, 0, t == 0, p1)
    line_go(2, 0, jnp.logical_and(t >= 1, t <= 2), p3)
    line_go(2, 1, t >= 1, p1)
    while step <= len(partners):
        step = small_step(step)
    small_out[...] = smalls[2 * len(partners) - 1]
    arrived(downs_across, across_sems.at[0], here)
    add(down_out, downs.at[j if side == 2 else x], downs_across)
    p0 = side_rest(0)
    line_came(2, 0, t >= 1, p0)
    line_came(2, 1, t <= 2, p0)
    q_out[...] = p0[:, pl.ds(0, q_cols)].astype(F32)
    k_out[...] = p0[:, pl.ds(q_cols, k_cols)].astype(F32)
    v_out[...] = p0[:, pl.ds(q_cols + k_cols, k_cols)].astype(F32)
    stores = []

    def store(source, target):
        copy = pltpu.make_async_copy(source, target, store_sems.at[len(stores)])
        copy.start()
        stores.append(copy)

    for which in range(2):
        for tt in range(LINE):
            for cc in range(2):
                when(
                    jnp.logical_not(jnp.logical_and(t == tt, c == cc)),
                    lambda w=which, k=tt * 2 + cc: arrived(
                        homes.at[w, k], home_sems.at[w, k], here
                    ),
                )
    store(homes, homes_out)
    arrived(low_got, across_sems.at[1], here)
    store(low, low_out)
    store(low_got, low_got_out)
    sends.wait_sent()
    for copy in stores:
        copy.wait()


def end_layer(n, piece, pairs, down, w_qkv, length, hidden, proj, totals, grad_o, tables, gains,
              attn_gain, ffn_part):
    side = n // LINE // 2
    bits = side.bit_length() - 1
    rows, width = hidden.shape
    cols = w_qkv.shape[1]
    q_cols = grad_o.shape[1]
    depth = width // n
    k_cols = (cols - q_cols) // 2
    strip = side * piece
    any_space = pl.BlockSpec(memory_space=pl.ANY)
    vmem = pl.BlockSpec(memory_space=pltpu.VMEM)
    steps = bits + 4
    sides = max(side - 1, 1)
    home = (LINE, 2 * depth, strip)
    held = [
        (n, depth, cols), (LINE, side, depth, cols), (LINE, sides, depth, cols),
        (3, depth, cols), (3, depth, cols),
        home, home, home, home,
        (2, piece, width), (2, piece, width), (piece, width),
        (2, LINE * 2, depth, strip),
        (rows, cols), (width, cols), (rows, width), (rows, width),
    ]
    small = (2 * (width // LANES) + 1, LANES)
    floats = [
        (rows, LANES), (rows, LANES), (1, LANES), (1, LANES),
        (2 * steps + 1,) + small,
    ]
    sends = LINE * (2 * side - 1) + 3 + steps + 8 + 4 * LINE + 4
    return pl.pallas_call(
        functools.partial(end_kernel, side, piece, 1.0 / math.sqrt(HEAD)),
        out_shape=[
            jax.ShapeDtypeStruct((depth, q_cols), F32),
            jax.ShapeDtypeStruct((depth, k_cols), F32),
            jax.ShapeDtypeStruct((depth, k_cols), F32),
            jax.ShapeDtypeStruct((2, LINE * 2, depth, strip), BF),
            jax.ShapeDtypeStruct((piece, width), F32),
            jax.ShapeDtypeStruct(small, F32),
            jax.ShapeDtypeStruct((rows, width), BF),
            jax.ShapeDtypeStruct((rows, width), BF),
        ],
        in_specs=[any_space] * 7 + [pl.BlockSpec(memory_space=pltpu.SMEM)] + [vmem] * 10,
        out_specs=[vmem] * 3 + [any_space] + [vmem] * 2 + [any_space] * 2,
        scratch_shapes=[pltpu.VMEM(shape, BF) for shape in held]
        + [pltpu.VMEM(shape, F32) for shape in floats]
        + [
            pltpu.SemaphoreType.DMA((7,)),
            pltpu.SemaphoreType.DMA((sends,)),
            pltpu.SemaphoreType.DMA((LINE, side)),
            pltpu.SemaphoreType.DMA((LINE, sides)),
            pltpu.SemaphoreType.DMA((2, 3)),
            pltpu.SemaphoreType.DMA((3,)),
            pltpu.SemaphoreType.DMA((2, LINE * 2)),
            pltpu.SemaphoreType.DMA((steps,)),
            pltpu.SemaphoreType.DMA((4,)),
        ],
        compiler_params=pltpu.CompilerParams(
            collective_id=2, has_side_effects=True, vmem_limit_bytes=62 << 20
        ),
        cost_estimate=pl.CostEstimate(
            flops=8 * rows * width * cols, bytes_accessed=300 << 20, transcendentals=rows * rows
        ),
    )(
        *pairs, *down, w_qkv, length, hidden, proj, totals, grad_o, *tables, *gains,
        attn_gain[None, :], ffn_part,
    )


def finish_kernel(side, piece, homes, low, low_got, tokens, dab, gain, gate, up, grad):
    count = gate.shape[0]
    for which, out in enumerate((gate, up)):
        for tt in range(LINE):
            for jj in range(side):
                for cc in range(2):
                    col = ((tt * side + jj) * 2 + cc) * piece
                    out[:, pl.ds(col, piece)] = homes[
                        which, tt * 2 + cc, pl.ds(0, count), pl.ds(jj * piece, piece)
                    ].astype(F32)
    values = tokens[...].astype(F32)
    scale = lax.rsqrt(jnp.mean(values * values, axis=1, keepdims=True) + EPS)
    part = (low[...].astype(F32) + low_got[...].astype(F32)) * gain[...]
    back = jnp.mean(part * values, axis=1, keepdims=True) * scale * scale
    grad[...] = dab[...].astype(F32) + scale * (part - values * back)


def finish(side, piece, homes, low, low_got, tokens, dab, gain):
    rows, width = tokens.shape
    depth, strip = homes.shape[2], homes.shape[3]
    steps = 8 if depth % 128 == 0 else 2
    columns = LINE * 2 * strip
    block = pl.BlockSpec((rows // steps, width), lambda i: (i, 0))
    wide = pl.BlockSpec((depth // steps, columns), lambda i: (i, 0))
    return pl.pallas_call(
        functools.partial(finish_kernel, side, piece),
        grid=(steps,),
        in_specs=[
            pl.BlockSpec((2, LINE * 2, depth // steps, strip), lambda i: (0, 0, i, 0)),
            block, block, block, block,
            pl.BlockSpec((1, width), lambda i: (0, 0)),
        ],
        out_specs=[wide, wide, block],
        out_shape=[
            jax.ShapeDtypeStruct((depth, columns), F32),
            jax.ShapeDtypeStruct((depth, columns), F32),
            jax.ShapeDtypeStruct((rows, width), F32),
        ],
        compiler_params=pltpu.CompilerParams(vmem_limit_bytes=62 << 20),
        cost_estimate=pl.CostEstimate(
            flops=20 * rows * width, bytes_accessed=20 << 20, transcendentals=0
        ),
    )(homes, low, low_got, tokens, dab, gain[None, :])


class Links:
    def __init__(self, n):
        self.n = n
        self.inner = n // LINE
        self.side = self.inner // 2
        self.side_bits = self.side.bit_length() - 1
        self.t, self.j, self.c, self.x = coordinates()

    def core(self, value):
        return lax.ppermute(value, "dp", [(i, i ^ 1) for i in range(self.n)])

    def over(self, value, bit):
        return lax.ppermute(value, "dp", [(i, i ^ (2 << bit)) for i in range(self.n)])

    def cross(self, value):
        return lax.ppermute(value, "tensor", [(0, 1), (1, 0)])

    def along(self, value, moves):
        pairs = [
            (a * self.inner + i, b * self.inner + i) for a, b in moves for i in range(self.inner)
        ]
        return lax.ppermute(value, "dp", pairs)

    def right(self, value, senders):
        return self.along(value, [(a, a + 1) for a in senders])

    def left(self, value, senders):
        return self.along(value, [(a, a - 1) for a in senders])

    def turn(self, value, shift):
        return self.along(value, [(a, (a + shift) % LINE) for a in range(LINE)])

    def line_gather(self, value):
        t = self.t
        r1 = self.right(value, (0, 1, 2))
        l1 = self.left(value, (1, 2, 3))
        r2 = self.right(r1, (1, 2))
        l2 = self.left(l1, (1, 2))
        r3 = self.right(r2, (2,))
        l3 = self.left(l2, (1,))
        return (
            value,
            jnp.where(t == 0, l1, r1),
            jnp.where(t < 2, l2, r2),
            jnp.where(t == 0, l3, jnp.where(t == 3, r3, l1)),
        )

    def lines(self):
        return [[i + k * self.inner for k in range(LINE)] for i in range(self.inner)]

    def line_all(self, value):
        return lax.all_gather(value, "dp", axis_index_groups=self.lines())

    def line_sum(self, value):
        return lax.psum_scatter(
            value, "dp", scatter_dimension=0, axis_index_groups=self.lines()
        )

    def dp_sum(self, value):
        return lax.psum_scatter(value, "dp", scatter_dimension=0, tiled=True)

    def line_scatter(self, parts):
        t = self.t
        p0, p1, p2, p3 = parts
        first = p3.astype(BF)
        r1 = self.right(first, (0,))
        l1 = self.left(first, (3,))
        second = (p2 + r1.astype(F32) + l1.astype(F32)).astype(BF)
        r2 = self.right(second, (0, 1))
        l2 = self.left(second, (2, 3))
        r3 = self.right((jnp.where(t == 0, p1, p3) + r2.astype(F32)).astype(BF), (0, 1, 2))
        l3 = self.left((p1 + l2.astype(F32)).astype(BF), (1, 2, 3))
        return p0 + r3.astype(F32) + l3.astype(F32)

    def line_send(self, parts):
        p0, p1, p2, p3 = parts
        first, second, third = p1.astype(BF), p2.astype(BF), p3.astype(BF)
        got = [
            self.left(first, (1, 2, 3)),
            self.right(first, (0,)),
            self.turn(second, 2),
            self.along(third, ((0, 3), (3, 0))),
            self.right(third, (1, 2)),
        ]
        return p0 + sum(g.astype(F32) for g in got)

    def side_all(self, value):
        blocks = [value]
        for bit in range(self.side_bits):
            blocks += [self.over(block, bit) for block in blocks]
        return blocks

    def side_sum(self, blocks):
        for bit in reversed(range(self.side_bits)):
            width = 1 << bit
            blocks = [
                a.astype(F32) + self.over(b.astype(BF), bit).astype(F32)
                for a, b in zip(blocks[:width], blocks[width:])
            ]
        return blocks[0]

    def side_start(self, blocks):
        for bit in reversed(range(1, len(blocks).bit_length() - 1)):
            half = 1 << bit
            blocks = [
                (a.astype(F32) + self.over(b, bit).astype(F32)).astype(BF)
                for a, b in zip(blocks[:half], blocks[half:])
            ]
        return blocks[0], self.over(blocks[1], 0)

    def side_end(self, kept, got):
        if kept.shape[0] == 1:
            return kept[0], got[0]
        total = (kept.astype(F32) + got.astype(F32)).astype(BF)
        return self.side_start(list(total))

    def pair_order(self, mine, other, where):
        low = jnp.where(where == 0, mine, other)
        high = jnp.where(where == 0, other, mine)
        return jnp.concatenate([low, high], 0)

    def pick(self, value, index, axis):
        return lax.dynamic_index_in_dim(value, index, axis, keepdims=False)

    def cross_sum(self, value, axis):
        kept = self.pick(value, self.x, axis)
        sent = self.pick(value, 1 - self.x, axis)
        return kept.astype(F32) + self.cross(sent.astype(BF)).astype(F32)

    def gather_rows(self, blocks):
        rows, cols = blocks[0].shape
        pieces, where = [], []
        for k, block in enumerate(blocks):
            for r, piece in enumerate(self.side_all(block)):
                pieces += [piece, self.core(piece)]
                where += [(k, r, 0), (k, r, 1)]

        def spots(t, j, c, x):
            return [
                (
                    i, 0, 0, rows, cols,
                    (((slot_place(t, k) * self.side) + (j ^ r)) * 2 + (c ^ s)) * rows, 0,
                )
                for i, (k, r, s) in enumerate(where)
            ]

        return place(pieces, spots, (self.n * rows, cols))

    def sum_rows(self, value):
        rows, cols = value.shape[0] // self.n, value.shape[1]
        parts = value.reshape(LINE, self.side, 2, rows, cols)
        kept = self.pick(parts, self.c, 2).astype(F32)
        parts = kept + self.core(self.pick(parts, 1 - self.c, 2)).astype(F32)
        parts = parts.astype(BF)
        parts = self.side_sum([self.pick(parts, self.j ^ r, 1) for r in range(self.side)])
        return self.line_scatter(
            [self.pick(parts, slot_place(self.t, k), 0).astype(F32) for k in range(LINE)]
        )

    def total(self, value):
        value = value + self.core(value)
        for bit in range(self.side_bits):
            value = value + self.over(value, bit)
        value = value + self.cross(value)
        value = value + self.along(value, ((0, 1), (1, 0), (2, 3), (3, 2)))
        return value + self.turn(value, 2)


def make_body(n):
    def body(
        tokens,
        cotangent,
        lengths,
        attn_gain,
        query_gain,
        key_gain,
        w_query,
        key_weight_matrix,
        value_weight_matrix,
        w_out,
        ffn_gain,
        w_gate,
        w_up,
        w_down,
    ):
        net = Links(n)
        t, j, c, x = net.t, net.j, net.c, net.x
        row_count, width = tokens.shape
        half = row_count // 2
        head_dim = query_gain.shape[0]
        q_cols = w_query.shape[1]
        k_cols = key_weight_matrix.shape[1]
        k_heads = k_cols // head_dim
        dp_index = lax.axis_index("dp")
        slot_length = lengths[dp_index]

        depth = w_gate.shape[0]
        piece = w_down.shape[0]
        side = net.side
        strip = side * piece
        tables = angle_tables(row_count, head_dim, LANES)
        gains = [jnp.tile(gain, LANES // head_dim)[None, :] for gain in (query_gain, key_gain)]
        length = slot_length[None]
        weights = (w_query, key_weight_matrix, value_weight_matrix, w_out, w_gate, w_up, w_down)
        (
            qkv_full, wo_full, units, wd, grad_all, qkv, o_low, log_totals, h_one, hidden_two,
            hidden_state,
        ) = start_layer(
            n, weights, cotangent, length, tokens, attn_gain, tables, gains, ffn_gain
        )

        (
            layer_half, grad_attn_low, g_ffn_part, _, _, _, _,
            g_down, gate_mid, up_mid, gate_kept, gate_got, up_kept, up_got,
        ) = feed_forward(
            side, hidden_two, grad_all, units.reshape(2, width, 2 * strip),
            wd.reshape(2 * strip, width), h_one, ffn_gain,
        )
        layer_out = net.pair_order(layer_half, net.cross(layer_half), x)

        if side != 2:
            gate_sum = (gate_kept.astype(F32) + gate_mid.astype(F32)).astype(BF)
            gate_sum = gate_sum.reshape(LINE, side, 2 * depth, strip)
            gate_kept, gate_got = net.side_start([net.pick(gate_sum, j ^ r, 1) for r in range(side)])
            up_kept, up_got = net.side_end(up_kept, up_mid)
            up_sum = (up_kept.astype(F32) + up_got.astype(F32)).astype(BF)
            up_kept = lax.dynamic_slice_in_dim(up_sum, x * strip, strip, 2)
            up_got = net.cross(lax.dynamic_slice_in_dim(up_sum, (1 - x) * strip, strip, 2))
        g_down = g_down.reshape(2, side, piece, width)
        down_pair = (g_down, g_down)
        if side != 2:
            down_pair = net.side_start([net.pick(g_down, j ^ r, 1) for r in range(side)])

        g_out = mm_tn(o_low, grad_attn_low).astype(BF)
        grad_o_low = mm_nt(grad_attn_low, wo_full).astype(BF)
        g_out_out = net.dp_sum(g_out).astype(F32)
        (
            g_query_w, g_key_w, g_value_w, homes, g_down_out, small, low, low_got,
        ) = end_layer(
            n, piece, (gate_kept, gate_got, up_kept, up_got), down_pair, qkv_full, length,
            hidden_state, qkv, log_totals, grad_o_low, tables, gains, attn_gain,
            g_ffn_part.reshape(-1, LANES),
        )
        g_gate_out, g_up_out, input_grad = finish(
            side, piece, homes, low, low_got, tokens, grad_attn_low, attn_gain
        )
        small = small.reshape(-1)
        return (
            layer_out,
            input_grad,
            small[:width],
            small[2 * width : 2 * width + head_dim],
            small[2 * width + head_dim :],
            g_query_w,
            g_key_w,
            g_value_w,
            g_out_out,
            small[width : 2 * width],
            g_gate_out,
            g_up_out,
            g_down_out,
        )

    return body


def solution(mesh):
    placed = (
        P("dp", None),
        P("dp", None),
        P(),
        P(),
        P(),
        P(),
        P("dp", "tensor"),
        P("dp", "tensor"),
        P("dp", "tensor"),
        P(("tensor", "dp"), None),
        P(),
        P("dp", "tensor"),
        P("dp", "tensor"),
        P(("tensor", "dp"), None),
    )
    return jax.shard_map(
        make_body(mesh.shape["dp"]),
        mesh=mesh,
        in_specs=placed,
        out_specs=(
            P("dp", None),
            P("dp", None),
            P(),
            P(),
            P(),
            P("dp", "tensor"),
            P("dp", "tensor"),
            P("dp", "tensor"),
            P(("tensor", "dp"), None),
            P(),
            P("dp", "tensor"),
            P("dp", "tensor"),
            P(("tensor", "dp"), None),
        ),
        check_vma=False,
    )
```

```python
import functools
import math

import jax
import jax.numpy as jnp
import numpy as np
from jax import lax
from jax.experimental import pallas as pl
from jax.experimental.pallas import tpu as pltpu
from jax.sharding import PartitionSpec as P

EPS = 1e-05
ROPE_BASE = 1000000.0
MASKED = -1e30
LINE = 4
BF = jnp.bfloat16
F32 = jnp.float32


def rms_scale(values, gain):
    return values * lax.rsqrt(jnp.mean(values * values, axis=-1, keepdims=True) + EPS) * gain


def angle_tables(count, head_dim, lanes):
    half_dim = head_dim // 2
    freq = ROPE_BASE ** (np.arange(half_dim) * (-2.0 / head_dim))
    turned = np.arange(count)[:, None] * freq[None, :]
    cosine, sine = np.cos(turned).astype(np.float32), np.sin(turned).astype(np.float32)
    repeats = lanes // head_dim
    return (
        jnp.asarray(np.tile(np.concatenate([cosine, cosine], 1), (1, repeats))),
        jnp.asarray(np.tile(np.concatenate([-sine, sine], 1), (1, repeats))),
    )


LANES = 128
HEAD = LANES // 2


def low_lanes(shape):
    return lax.broadcasted_iota(jnp.int32, shape, 1) < HEAD


def per_head(values):
    low = low_lanes(values.shape)
    first = jnp.sum(jnp.where(low, values, 0.0), axis=1, keepdims=True)
    second = jnp.sum(jnp.where(low, 0.0, values), axis=1, keepdims=True)
    return jnp.where(low, first, second) * (1.0 / HEAD)


def halves_swapped(values):
    lane = lax.broadcasted_iota(jnp.int32, values.shape, 1)
    return jnp.where(
        lane % HEAD < HEAD // 2,
        pltpu.roll(values, LANES - HEAD // 2, 1),
        pltpu.roll(values, HEAD // 2, 1),
    )


def head_norm(values):
    scale = lax.rsqrt(per_head(values * values) + EPS)
    return values * scale, scale


def head_turn(values, cosine, sine):
    return values * cosine + halves_swapped(values) * sine


def head_back(grad, normed, scale, gain, cosine, sine):
    grad = grad * cosine - halves_swapped(grad) * sine
    gain_grad = jnp.sum(grad * normed, axis=0, keepdims=True)
    grad = grad * gain
    return scale * (grad - normed * per_head(grad * normed)), gain_grad


def one_head(pair, second):
    low = low_lanes(pair.shape)
    return jnp.where(low == jnp.logical_not(second), pair, pltpu.roll(pair, HEAD, 1))


def two_rows(slab):
    low = low_lanes(slab.shape)
    return jnp.concatenate([jnp.where(low, slab, 0.0), jnp.where(low, 0.0, slab)], 0).astype(BF)


def allowed_mask(block, first_row, columns, length):
    row = lax.broadcasted_iota(jnp.int32, (2 * block, columns), 0) % block + first_row
    col = lax.broadcasted_iota(jnp.int32, (2 * block, columns), 1)
    return (col <= row) & (col < length)


def attend_kernel(
    block, scale, second, length, q, k, v, cosine, sine, q_gain, k_gain, out, totals
):
    rows = q.shape[0]
    cos, sin = cosine[...], sine[...]
    keys = one_head(head_turn(head_norm(k[...])[0] * k_gain[...], cos, sin), second).astype(BF)
    vals = one_head(v[...], second).astype(BF)
    lane = lax.broadcasted_iota(jnp.int32, (block, LANES), 1)
    for first in range(0, rows, block):
        span = pl.ds(first, block)
        seen = first + block
        allowed = allowed_mask(block, first, seen, length[0])
        kept = jnp.zeros((block, LANES), F32)
        for slab in range(q.shape[1] // LANES):
            cols = pl.ds(slab * LANES, LANES)
            turned = head_turn(
                head_norm(q[span, cols])[0] * q_gain[...], cosine[span, :], sine[span, :]
            )
            scores = mm_nt(two_rows(turned), keys[:seen]) * scale
            scores = jnp.where(allowed, scores, MASKED)
            top = jnp.max(scores, axis=1, keepdims=True)
            probs = jnp.exp(scores - top)
            total = jnp.sum(probs, axis=1, keepdims=True)
            probs = (probs * (1.0 / total)).astype(BF)
            both = mm(probs, vals[:seen])
            out[span, cols] = jnp.where(low_lanes((block, LANES)), both[:block], both[block:]).astype(
                BF
            )
            log_total = top + jnp.log(total)
            kept = jnp.where(lane == 2 * slab, log_total[:block], kept)
            kept = jnp.where(lane == 2 * slab + 1, log_total[block:], kept)
        totals[span, :] = kept


def attend_back_kernel(
    block, scale, second, length, q, k, v, cosine, sine, q_gain, k_gain, totals, grad_out,
    grad_q, grad_k, grad_v, q_gain_grad, k_gain_grad, keys_sum, vals_sum,
):
    rows = q.shape[0]
    cos, sin = cosine[...], sine[...]
    k_normed, k_scale = head_norm(k[...])
    keys = one_head(head_turn(k_normed * k_gain[...], cos, sin), second).astype(BF)
    vals = one_head(v[...], second).astype(BF)
    lane = lax.broadcasted_iota(jnp.int32, (block, LANES), 1)
    keys_sum[...] = jnp.zeros_like(keys_sum)
    vals_sum[...] = jnp.zeros_like(vals_sum)

    for first in range(0, rows, block):
        span = pl.ds(first, block)
        seen = first + block
        allowed = allowed_mask(block, first, seen, length[0])
        kept = totals[span, :]
        for slab in range(q.shape[1] // LANES):
            cols = pl.ds(slab * LANES, LANES)
            q_normed, q_scale = head_norm(q[span, cols])
            turned = two_rows(head_turn(q_normed * q_gain[...], cosine[span, :], sine[span, :]))
            log_total = jnp.concatenate(
                [
                    jnp.sum(jnp.where(lane == 2 * slab + i, kept, 0.0), axis=1, keepdims=True)
                    for i in range(2)
                ],
                0,
            )
            scores = mm_nt(turned, keys[:seen]) * scale
            probs = jnp.exp(jnp.where(allowed, scores, MASKED) - log_total)
            grad_rows = two_rows(grad_out[span, cols].astype(F32))
            grad_probs = mm_nt(grad_rows, vals[:seen])
            drop = jnp.sum(probs * grad_probs, axis=1, keepdims=True)
            grad_scores = (probs * (grad_probs - drop)).astype(BF)
            both = mm(grad_scores, keys[:seen]) * scale
            grad_turned = jnp.where(low_lanes((block, LANES)), both[:block], both[block:])
            grad_proj, gain_part = head_back(
                grad_turned, q_normed, q_scale, q_gain[...], cosine[span, :], sine[span, :]
            )
            grad_q[span, cols] = grad_proj.astype(BF)
            q_gain_grad[...] += gain_part
            keys_sum[:seen] += mm_tn(grad_scores, turned)
            vals_sum[:seen] += mm_tn(probs.astype(BF), grad_rows)

    keys_grad = keys_sum[...] * scale
    keys_grad = keys_grad + pltpu.roll(keys_grad, HEAD, 1)
    vals_grad = vals_sum[...]
    vals_grad = vals_grad + pltpu.roll(vals_grad, HEAD, 1)
    grad_proj, gain_part = head_back(
        keys_grad,
        one_head(k_normed, second),
        one_head(k_scale, second),
        k_gain[...],
        cos,
        sin,
    )
    k_gain_grad[...] += gain_part * 0.5
    keep_low = low_lanes(grad_k.shape)

    @pl.when(jnp.logical_not(second))
    def _():
        grad_k[...] = grad_proj.astype(BF)
        grad_v[...] = vals_grad.astype(BF)

    @pl.when(second)
    def _():
        grad_k[...] = jnp.where(keep_low, grad_k[...].astype(F32), grad_proj).astype(BF)
        grad_v[...] = jnp.where(keep_low, grad_v[...].astype(F32), vals_grad).astype(BF)


def mm(left, right):
    return jnp.dot(left, right, preferred_element_type=F32)


def mm_nt(left, right):
    return lax.dot_general(left, right, (((1,), (1,)), ((), ())), preferred_element_type=F32)


def mm_tn(left, right):
    return lax.dot_general(left, right, (((0,), (0,)), ((), ())), preferred_element_type=F32)


def after(done, *values):
    held, _ = lax.optimization_barrier((values, done))
    return held if len(held) > 1 else held[0]


def slot_place(t, k):
    if k == 0:
        return t
    if k == 1:
        return jnp.where(t == 0, 1, t - 1)
    if k == 2:
        return (t + 2) % LINE
    return jnp.where(t == 3, 0, jnp.where(t == 1, 2, 3))


def coordinates():
    n = lax.axis_size("dp")
    inner = n // LINE
    here = lax.axis_index("dp")
    return here // inner, (here % inner) // 2, here % 2, lax.axis_index("tensor")


def place(blocks, spots, shape):
    listed = spots(0, 0, 0, 0)

    def kernel(*refs):
        sources = refs[: len(blocks)]
        out, held, sem, out_sem = refs[len(blocks) :]
        copies = []
        for k, (b, row, col, rows, cols, to_row, to_col) in enumerate(spots(*coordinates())):
            copies.append(
                pltpu.make_async_copy(
                    sources[b].at[pl.ds(row, rows), pl.ds(col, cols)],
                    held.at[
                        pl.ds(pl.multiple_of(to_row, rows), rows),
                        pl.ds(pl.multiple_of(to_col, cols), cols),
                    ],
                    sem.at[k],
                )
            )
        for copy in copies:
            copy.start()
        for copy in copies:
            copy.wait()
        last = pltpu.make_async_copy(held, out, out_sem)
        last.start()
        last.wait()

    item = blocks[0].dtype.itemsize
    moved = sum(2 * rows * cols * item for _, _, _, rows, cols, _, _ in listed)
    return pl.pallas_call(
        kernel,
        out_shape=jax.ShapeDtypeStruct(shape, blocks[0].dtype),
        in_specs=[pl.BlockSpec(memory_space=pl.ANY)] * len(blocks),
        out_specs=pl.BlockSpec(memory_space=pl.ANY),
        scratch_shapes=[
            pltpu.VMEM(shape, blocks[0].dtype),
            pltpu.SemaphoreType.DMA((len(listed),)),
            pltpu.SemaphoreType.DMA,
        ],
        compiler_params=pltpu.CompilerParams(vmem_limit_bytes=moved // 2 + (4 << 20)),
        cost_estimate=pl.CostEstimate(flops=0, bytes_accessed=moved, transcendentals=0),
    )(*blocks)


class Sends:
    def __init__(self, sems):
        self.sems = sems
        self.made = []

    def start(self, source, target, recv_sem, device, cond=None):
        sem = self.sems.at[len(self.made)]

        def copy():
            return pltpu.make_async_remote_copy(
                src_ref=source,
                dst_ref=target,
                send_sem=sem,
                recv_sem=recv_sem,
                device_id=device,
                device_id_type=pl.DeviceIdType.MESH,
            )

        self.made.append((cond, copy))
        when(cond, lambda: copy().start())

    def wait_sent(self):
        for cond, copy in self.made:
            when(cond, lambda copy=copy: copy().wait_send())


def when(cond, act):
    if cond is None:
        act()
    else:
        pl.when(cond)(act)


def both(first, second):
    if first is None:
        return second
    return first if second is None else jnp.logical_and(first, second)


def arrived(ref, recv_sem, device):
    pltpu.make_async_remote_copy(
        src_ref=ref, dst_ref=ref, send_sem=recv_sem, recv_sem=recv_sem,
        device_id=device, device_id_type=pl.DeviceIdType.MESH,
    ).wait_recv()


def greet(devices):
    barrier = pltpu.get_barrier_semaphore()
    for device in devices:
        pl.semaphore_signal(
            barrier, inc=1, device_id=device, device_id_type=pl.DeviceIdType.MESH
        )
    pl.semaphore_wait(barrier, len(devices))


def start_kernel(side, piece, sliced, scale, *refs):
    w_query, w_key, w_value, w_out, w_gate, w_up, w_down, dm_own = refs[:8]
    length, tokens, attn_gain, cosine, sine, q_gain, k_gain, ffn_gain = refs[8:16]
    outs = refs[16:21]
    proj, attended, totals, h_one, hidden_two, hidden = refs[21:27]
    qkv, out, units, down, dm = bufs = refs[27:32]
    part, cross_sent, cross_got = refs[32:35]
    (
        load_sems, send_sems, qkv_sems, out_sems, unit_sems, pair_sems, down_sems,
        line_sems, core_sems, cross_sem, store_sems,
    ) = refs[35:]
    t, j, c, x = coordinates()
    bits = side.bit_length() - 1
    strip = side * piece

    def at(tt, jj, cc, xx=None):
        return (((tt * side) + jj) * 2 + cc, x if xx is None else xx)

    def block(tt, jj, cc):
        return ((tt * side) + jj) * 2 + cc

    here = at(t, j, c)
    core = at(t, j, 1 - c)
    across = at(t, j, c, 1 - x)
    beside = [at(t, j ^ (1 << bit), c) for bit in range(bits)]
    others = [
        at((t + dt) % LINE, j, c ^ dc) for dt in range(LINE) for dc in range(2) if dt or dc
    ]
    mine = block(t, j, c)
    depth, q_cols = w_query.shape
    k_cols = w_key.shape[1]
    rows, width = tokens.shape
    half = rows // 2

    def rows_of(buf, idx):
        count = depth if buf is qkv else w_out.shape[0]
        return buf.at[pl.ds(pl.multiple_of(idx * count, count), count)]

    own_qkv = pl.ds(pl.multiple_of(mine * depth, depth), depth)
    loads = [
        (w_query, qkv.at[own_qkv, pl.ds(0, q_cols)]),
        (w_key, qkv.at[own_qkv, pl.ds(q_cols, k_cols)]),
        (w_value, qkv.at[own_qkv, pl.ds(q_cols + k_cols, k_cols)]),
        (w_out, rows_of(out, mine)),
        (w_down, down.at[x * side + j]),
        (dm_own.at[pl.ds(pl.multiple_of(x * half, half), half)], dm.at[t, pl.ds(0, half)]),
    ]
    first_unit = len(loads)

    def unit_block(which, tt, jj, cc):
        weight = (w_gate, w_up)[which]
        if sliced:
            col = pl.multiple_of(block(tt, jj, cc) * piece, piece)
            return weight.at[:, pl.ds(col, piece)]
        return weight.at[tt, cc]

    def unit_target(which, tt, jj, cc):
        col = x * strip + (jj * piece if sliced else 0)
        size = piece if sliced else strip
        return units.at[
            which, tt, j, pl.ds(pl.multiple_of(cc * depth, depth), depth),
            pl.ds(pl.multiple_of(col, size), size),
        ]

    def unit_pair(which, tt, jj, xx):
        return units.at[which, tt, jj, :, pl.ds(pl.multiple_of(xx * strip, strip), strip)]

    parts = range(side) if sliced else range(1)
    loads += [
        (unit_block(w, t, jj, c), unit_target(w, t, jj, c)) for w in range(2) for jj in parts
    ]
    loads = [
        pltpu.make_async_copy(a, b, load_sems.at[i]) for i, (a, b) in enumerate(loads)
    ]
    for load in loads:
        load.start()
    greet(others + beside + [across])
    sends = Sends(send_sems)
    for load in loads[:first_unit]:
        load.wait()

    lines = ((qkv, qkv_sems), (out, out_sems))

    def spread(buf, sems, tt, r, cond):
        idx = block(tt, j ^ r, c)
        ref = rows_of(buf, idx)
        for bit in range(bits):
            if (1 << bit) > r:
                sends.start(ref, ref, sems.at[idx], beside[bit], cond)
        sends.start(ref, ref, sems.at[idx], core, cond)

    def pass_on(ref, sem, to_right, to_left):
        if to_right is not False:
            sends.start(ref, ref, sem, at(t + 1, j, c), to_right)
        if to_left is not False:
            sends.start(ref, ref, sem, at(t - 1, j, c), to_left)

    def spread_rest(buf, sems, tt, cond):
        for r in range(1, side):
            idx = block(tt, j ^ r, c)
            when(cond, lambda idx=idx: arrived(rows_of(buf, idx), sems.at[idx], here))
            spread(buf, sems, tt, r, cond)

    def line_places(k):
        return ((t >= k, t - k, True), (t + k < LINE, t + k, False))

    def forward(ref, sem, cond, rightward):
        if rightward:
            pass_on(ref, sem, both(cond, t < LINE - 1), False)
        else:
            pass_on(ref, sem, False, both(cond, t > 0))

    def set_out(buf, sems):
        pass_on(rows_of(buf, mine), sems.at[mine], t < LINE - 1, t > 0)
        spread(buf, sems, t, 0, None)

    def line_step(buf, sems, k):
        for cond, tt, rightward in line_places(k):
            idx = block(tt, j, c)
            when(cond, lambda idx=idx: arrived(rows_of(buf, idx), sems.at[idx], here))
            if k < LINE - 1:
                forward(rows_of(buf, idx), sems.at[idx], cond, rightward)
            spread(buf, sems, tt, 0, cond)
        if k == 1:
            spread_rest(buf, sems, t, None)
        else:
            spread_rest(buf, sems, t - k + 1, t >= k - 1)
            spread_rest(buf, sems, t + k - 1, t + k - 1 < LINE)

    own_down = x * side + j

    def down_set_out():
        for bit in range(bits):
            sends.start(
                down.at[own_down], down.at[own_down], down_sems.at[own_down], beside[bit]
            )

    def down_rest():
        for r in range(1, side):
            idx = x * side + (j ^ r)
            arrived(down.at[idx], down_sems.at[idx], here)
            for bit in range(bits):
                if (1 << bit) > r:
                    sends.start(down.at[idx], down.at[idx], down_sems.at[idx], beside[bit])
            sends.start(down.at[idx], down.at[idx], down_sems.at[idx], across)

    def units_set_out():
        for dt in range(LINE):
            for dc in range(2):
                if dt or dc:
                    tt, cc = (t + dt) % LINE, c ^ dc
                    for w in range(2):
                        for jj in parts:
                            sends.start(
                                unit_block(w, tt, jj, cc),
                                unit_target(w, t, jj, c),
                                unit_sems.at[w, t * 2 + c, jj],
                                at(tt, j, cc),
                            )

    set_out(*lines[0])
    set_out(*lines[1])
    sends.start(down.at[own_down], down.at[own_down], down_sems.at[own_down], across)
    chunk = rows // 16

    @pl.loop(0, 16)
    def _(i):
        span = pl.ds(pl.multiple_of(i * chunk, chunk), chunk)
        hidden[span, :] = rms_scale(tokens[span, :].astype(F32), attn_gain[...]).astype(BF)

    @pl.loop(0, 8)
    def _(i):
        span = pl.ds(pl.multiple_of(i * chunk, chunk), chunk)
        row = lax.broadcasted_iota(jnp.int32, (chunk, width), 0) + i * chunk + x * half
        kept = dm[t, span, :].astype(F32)
        dm[t, span, :] = jnp.where(row < length[0], kept, 0.0).astype(BF)

    for k in range(1, LINE):
        line_step(*lines[0], k)
        line_step(*lines[1], k)
        if k == LINE - 2:
            units_set_out()
    down_set_out()
    stores = []

    def store(source, target):
        copy = pltpu.make_async_copy(source, target, store_sems.at[len(stores)])
        copy.start()
        stores.append(copy)

    def send_pair(w, tt, jj, xx, device):
        ref = unit_pair(w, tt, jj, xx)
        sends.start(ref, ref, pair_sems.at[w, tt, jj, xx], device)

    def pair_came(w, tt, jj, xx):
        arrived(unit_pair(w, tt, jj, xx), pair_sems.at[w, tt, jj, xx], here)

    def unit_first(tt):
        for cc in range(2):
            mine = jnp.logical_and(tt == t, cc == c)
            for w in range(2):
                for jj in parts:
                    when(
                        jnp.logical_not(mine),
                        lambda w=w, cc=cc, jj=jj: arrived(
                            unit_target(w, tt, jj, cc), unit_sems.at[w, tt * 2 + cc, jj], here
                        ),
                    )
        for w in range(2):
            for bit in range(bits):
                send_pair(w, tt, j, x, beside[bit])
            send_pair(w, tt, j, x, across)

    def unit_second(tt, by_side):
        for r in range(1, side):
            for w in range(2):
                pair_came(w, tt, j ^ r, x)
                for bit in range(bits):
                    if (1 << bit) > r:
                        send_pair(w, tt, j ^ r, x, beside[bit])
                if w not in by_side:
                    send_pair(w, tt, j ^ r, x, across)
        for w in by_side:
            pair_came(w, tt, j, 1 - x)
            for bit in range(bits):
                send_pair(w, tt, j, 1 - x, beside[bit])

    def unit_last(tt, by_side):
        for w in range(2):
            for r in range(1 if w in by_side else 0, side):
                pair_came(w, tt, j ^ r, 1 - x)
                for bit in range(bits):
                    if w in by_side and (1 << bit) > r:
                        send_pair(w, tt, j ^ r, 1 - x, beside[bit])

    dm_rows = dm.at[t, pl.ds(0, half)]

    def dm_to_core(tt, cond):
        sends.start(
            dm.at[tt, pl.ds(0, half)], dm.at[tt, pl.ds(half, half)], core_sems.at[tt], core, cond
        )

    def dm_step(k):
        for cond, tt, rightward in line_places(k):
            ref = dm.at[tt, pl.ds(0, half)]
            when(cond, lambda ref=ref, tt=tt: arrived(ref, line_sems.at[tt], here))
            if k < LINE - 1:
                forward(ref, line_sems.at[tt], cond, rightward)
            dm_to_core(tt, cond)

    def finish_line(buf, sems):
        spread_rest(buf, sems, t - LINE + 1, t >= LINE - 1)
        spread_rest(buf, sems, t + LINE - 1, t < 1)
        for tt in range(LINE):
            for jj in range(side):
                idx = block(tt, jj, 1 - c)
                arrived(rows_of(buf, idx), sems.at[idx], here)

    finish_line(*lines[0])
    store(qkv, outs[0])
    for load in loads[first_unit:]:
        load.wait()
    unit_first(t)
    pass_on(dm_rows, line_sems.at[t], t < LINE - 1, t > 0)
    dm_to_core(t, None)

    tile = 256

    @pl.loop(0, proj.shape[1] // tile)
    def _(i):
        cols = pl.ds(pl.multiple_of(i * tile, tile), tile)
        proj[:, cols] = mm(hidden[...], qkv[:, cols])

    group = q_cols // k_cols * HEAD
    key_heads = k_cols // HEAD

    def attend_head(g):
        pair = pl.multiple_of(g // 2 * LANES, LANES)
        wide = pl.ds(pl.multiple_of(g * group, group), group)
        attend_kernel(
            rows // 2, scale, g % 2 == 1, length,
            proj.at[:, wide],
            proj.at[:, pl.ds(q_cols + pair, LANES)],
            proj.at[:, pl.ds(q_cols + k_cols + pair, LANES)],
            cosine, sine, q_gain, k_gain,
            attended.at[:, wide],
            totals.at[:, pl.ds(pl.multiple_of(g * LANES, LANES), LANES)],
        )

    pl.loop(0, key_heads)(attend_head)

    finish_line(*lines[1])
    store(out, outs[1])
    wide = 512
    other_rows = pl.ds(pl.multiple_of((1 - x) * half, half), half)
    own_rows = pl.ds(pl.multiple_of(x * half, half), half)

    @pl.loop(0, width // wide)
    def _(i):
        cols = pl.ds(pl.multiple_of(i * wide, wide), wide)
        cross_sent[:, cols] = mm(attended[other_rows, :], out[:, cols]).astype(BF)

    sends.start(cross_sent, cross_got, cross_sem, across)

    @pl.loop(0, width // wide)
    def _(i):
        cols = pl.ds(pl.multiple_of(i * wide, wide), wide)
        part[:, cols] = mm(attended[own_rows, :], out[:, cols])

    for k in range(1, LINE):
        unit_first(slot_place(t, k))
    down_rest()
    unit_second(t, (0,))
    dm_step(1)
    for k in range(1, LINE):
        unit_second(slot_place(t, k), (0, 1))
    dm_step(2)

    arrived(cross_got, cross_sem, here)
    step = half // 8

    @pl.loop(0, 8)
    def _(i):
        span = pl.ds(pl.multiple_of(i * step, step), step)
        rows_here = pl.ds(pl.multiple_of(x * half + i * step, step), step)
        total = tokens[rows_here, :].astype(F32) + part[span, :] + cross_got[span, :].astype(F32)
        h_one[span, :] = total
        hidden_two[span, :] = rms_scale(total, ffn_gain[...]).astype(BF)

    dm_step(3)
    for k in range(LINE):
        unit_last(slot_place(t, k), (0, 1) if k else (0,))
    store(units, outs[2])
    for jj in range(side):
        idx = (1 - x) * side + jj
        arrived(down.at[idx], down_sems.at[idx], here)
    store(down, outs[3])
    for tt in range(LINE):
        arrived(dm.at[tt, pl.ds(half, half)], core_sems.at[tt], here)
    store(dm, outs[4])
    sends.wait_sent()
    for copy in stores:
        copy.wait()


def start_layer(n, weights, cotangent, length, tokens, attn_gain, tables, gains, ffn_gain):
    w_query, w_key, w_value, w_out, w_gate, w_up, w_down = weights
    side = n // LINE // 2
    depth, piece, width = w_gate.shape[0], w_down.shape[0], w_down.shape[1]
    rows, half = tokens.shape[0], tokens.shape[0] // 2
    q_cols, k_cols = w_query.shape[1], w_key.shape[1]
    cols = q_cols + 2 * k_cols
    strip = side * piece
    sliced = piece % LANES == 0
    if not sliced:
        w_gate, w_up = (
            w.reshape(depth, LINE, side, 2, piece)
            .transpose(1, 3, 0, 2, 4)
            .reshape(LINE, 2, depth, strip)
            for w in (w_gate, w_up)
        )
    shapes = [
        (width, cols),
        (q_cols, width),
        (2, LINE, side, 2 * depth, 2 * strip),
        (2 * side, piece, width),
        (LINE, 2 * half, width),
    ]
    slots = 2 * LINE - 1
    line_sends = 2 * (LINE - 1) + slots * (2 * side - 1)
    sends = 2 * line_sends + 2 * side - 1 + 14 * side + 3 * LINE + 8 + 8 * side * LINE
    any_space = pl.BlockSpec(memory_space=pl.ANY)
    vmem = pl.BlockSpec(memory_space=pltpu.VMEM)
    return pl.pallas_call(
        functools.partial(start_kernel, side, piece, sliced, 1.0 / math.sqrt(HEAD)),
        out_shape=[jax.ShapeDtypeStruct(shape, BF) for shape in shapes]
        + [
            jax.ShapeDtypeStruct((rows, cols), F32),
            jax.ShapeDtypeStruct((rows, q_cols), BF),
            jax.ShapeDtypeStruct((rows, k_cols // HEAD * LANES), F32),
            jax.ShapeDtypeStruct((half, width), F32),
            jax.ShapeDtypeStruct((half, width), BF),
            jax.ShapeDtypeStruct((rows, width), BF),
        ],
        in_specs=[any_space] * 8 + [pl.BlockSpec(memory_space=pltpu.SMEM)] + [vmem] * 7,
        out_specs=[any_space] * 5 + [vmem] * 6,
        scratch_shapes=[pltpu.VMEM(shape, BF) for shape in shapes]
        + [
            pltpu.VMEM((half, width), F32),
            pltpu.VMEM((half, width), BF),
            pltpu.VMEM((half, width), BF),
            pltpu.SemaphoreType.DMA((6 + 2 * side,)),
            pltpu.SemaphoreType.DMA((sends,)),
            pltpu.SemaphoreType.DMA((n,)),
            pltpu.SemaphoreType.DMA((n,)),
            pltpu.SemaphoreType.DMA((2, LINE * 2, side)),
            pltpu.SemaphoreType.DMA((2, LINE, side, 2)),
            pltpu.SemaphoreType.DMA((2 * side,)),
            pltpu.SemaphoreType.DMA((LINE,)),
            pltpu.SemaphoreType.DMA((LINE,)),
            pltpu.SemaphoreType.DMA,
            pltpu.SemaphoreType.DMA((5,)),
        ],
        compiler_params=pltpu.CompilerParams(
            collective_id=0, has_side_effects=True, vmem_limit_bytes=62 << 20
        ),
        cost_estimate=pl.CostEstimate(
            flops=2 * rows * width * cols, bytes_accessed=500 << 20, transcendentals=rows * rows
        ),
    )(
        w_query, w_key, w_value, w_out, w_gate, w_up, w_down, cotangent, length, tokens,
        attn_gain[None, :], *tables, *gains, ffn_gain[None, :],
    )


def feed_kernel(side, *refs):
    h_own, dm_all, units, down, h_one, gain = refs[:6]
    out_half, dab, gain_part, e_own, e_core, e_line, f_out = refs[6:13]
    g_down, gate_mid, up_mid, gate_kept, gate_got, up_kept, up_got = refs[13:20]
    wg, wu, wd, h_all, dm, act, dg, du, e_stage, f_stage, f_send, f_core = refs[20:32]
    load_sems, store_sems, send_sems, line_sems, core_sems, back_sems = refs[32:38]
    done_sems, gate_sems, up_sems, mid_sems, last_sems, e_sems, step_sems, dab_sem, row_sems = refs[38:]
    t, j, c, x = coordinates()
    half, width = h_own.shape
    unit_count = wd.shape[0]
    strip = unit_count // 2
    rows = 2 * half
    bits = side.bit_length() - 1

    def at(tt, cc, jj=None, xx=None):
        jj, xx = j if jj is None else jj, x if xx is None else xx
        return ((tt * side + jj) * 2 + cc, xx)

    here, core, across = at(t, c), at(t, 1 - c), at(t, c, None, 1 - x)
    beside = at(t, c, j ^ (side // 2))
    others = [at((t + dt) % LINE, c) for dt in range(1, LINE)]
    loads = [
        (h_own, h_all.at[t, pl.ds(0, half)]),
        (units.at[0], wg), (units.at[1], wu), (dm_all, dm), (down, wd),
    ]
    loads = [pltpu.make_async_copy(a, b, load_sems.at[i]) for i, (a, b) in enumerate(loads)]
    for load in loads:
        load.start()
    greet(others + [core, across] + ([beside] if bits else []))
    sends, rows_sent = Sends(send_sems), Sends(row_sems)

    def own_rows(tt):
        return h_all.at[tt, pl.ds(0, half)]

    def to_core(tt, cond):
        rows_sent.start(
            own_rows(tt), h_all.at[tt, pl.ds(half, half)], core_sems.at[tt], core, cond
        )

    loads[0].wait()
    rows_sent.start(own_rows(t), own_rows(t), line_sems.at[t], at(t + 1, c), t < LINE - 1)
    rows_sent.start(own_rows(t), own_rows(t), line_sems.at[t], at(t - 1, c), t > 0)
    to_core(t, None)
    for load in loads[1:]:
        load.wait()

    tile = min(512, unit_count)
    wide = min(1024, width)
    e_waits, f_sent, stores = [], [], []

    def store(source, target):
        copy = pltpu.make_async_copy(source, target, store_sems.at[len(stores)])
        copy.start()
        stores.append(copy)
        return copy

    def f_go(k):
        sends.start(
            f_stage.at[k], f_out.at[t], done_sems.at[t], at(slot_place(t, k), c)
        )

    def kept_out(k):
        copy = pltpu.make_async_copy(
            e_stage.at[pl.ds(0, half)], e_own.at[k], mid_sems.at[2, 2 * LINE - 1]
        )
        copy.start()
        return copy.wait

    def later(source, target, sem, device):
        sends.start(source, target, sem, device)
        copy = sends.made.pop()[1]
        sends.made.append((None, None))
        return lambda: copy().wait_send()

    for k in range(LINE):
        tt = slot_place(t, k)
        if k:
            for cond, place_of, forward, target in (
                (t >= k, t - k, t < LINE - 1, t + 1),
                (t + k < LINE, t + k, t > 0, t - 1),
            ):
                when(
                    cond,
                    lambda p=place_of: arrived(own_rows(p), line_sems.at[p], here),
                )
                if k < LINE - 1:
                    rows_sent.start(
                        own_rows(place_of), own_rows(place_of), line_sems.at[place_of],
                        at(target, c), jnp.logical_and(cond, forward),
                    )
                to_core(place_of, cond)
        if k >= 2:
            f_go(k - 1)
        arrived(h_all.at[tt, pl.ds(half, half)], core_sems.at[tt], here)
        if k >= 2:
            f_sent[k - 2]()

        @pl.loop(0, unit_count // tile)
        def _(i):
            cols = pl.ds(pl.multiple_of(i * tile, tile), tile)
            hidden = h_all[tt]
            gate = mm(hidden, wg[:, cols])
            up = mm(hidden, wu[:, cols])
            grad_act = mm_nt(dm[tt], wd[cols, :])
            sigma = lax.logistic(gate)
            silu = gate * sigma
            act[tt, :, cols] = (silu * up).astype(BF)
            dg[tt, :, cols] = (grad_act * up * (sigma * (1.0 + gate * (1.0 - sigma)))).astype(BF)
            du[tt, :, cols] = (grad_act * silu).astype(BF)

        slot = k % 2

        @pl.loop(0, width // wide)
        def _(i):
            span = pl.ds(pl.multiple_of(i * wide, wide), wide)
            grad = mm_nt(dg[tt], wg[span, :]) + mm_nt(du[tt], wu[span, :])
            f_stage[k, :, span] = grad[:half].astype(BF)
            f_send[slot, :, span] = grad[half:].astype(BF)

        f_sent.append(later(f_send.at[slot], f_core.at[k], back_sems.at[k], core))
        for wait in e_waits:
            wait()

        @pl.loop(0, width // wide)
        def _(i):
            span = pl.ds(pl.multiple_of(i * wide, wide), wide)
            e_stage[:, span] = mm(act[tt], wd[:, span]).astype(BF)

        e_waits = [
            kept_out(k),
            later(e_stage.at[pl.ds(half, half)], e_core.at[k], e_sems.at[k], core),
        ]
        arrived(f_core.at[k], back_sems.at[k], here)

        @pl.loop(0, 4)
        def _(i):
            part = pl.ds(pl.multiple_of(i * (half // 4), half // 4), half // 4)
            f_stage[k, part, :] = (
                f_stage[k, part, :].astype(F32) + f_core[k, part, :].astype(F32)
            ).astype(BF)

        if k == LINE - 1:
            f_go(k)

    group = width // LINE
    far = pl.ds(pl.multiple_of((1 - x) * strip, strip), strip)
    near = pl.ds(pl.multiple_of(x * strip, strip), strip)

    def weight_grad(target, grads, tt, send):
        @pl.loop(0, 1)
        def _(i):
            span = pl.ds(tt * group, group)
            hidden = h_all[:, :, span].reshape(LINE * rows, group)
            target[span, :] = mm_tn(hidden, grads[...].reshape(LINE * rows, unit_count)).astype(BF)

        send(tt)

    block = group // side
    whole = side == 2

    def side_rows(tt, jj):
        return pl.ds(pl.multiple_of(tt * group + jj * block, block), block)

    def send_gate(tt):
        span = pl.ds(tt * group, group)
        sends.start(wg.at[span, far], gate_mid.at[span], gate_sems.at[tt], across)
        if not whole:
            store(wg.at[span, near], gate_kept.at[span])

    def send_up(tt):
        for r in range(side):
            span = side_rows(tt, j ^ r)
            if r >= side // 2:
                k = r - side // 2
                sends.start(wu.at[span], up_mid.at[k, tt], up_sems.at[k, tt], beside)
            elif not whole:
                store(wu.at[span], up_kept.at[r, tt])

    for tt in range(LINE):
        weight_grad(wg, dg, tt, send_gate)
        weight_grad(wu, du, tt, send_up)
    tile = min(256, unit_count)

    @pl.loop(0, unit_count // tile)
    def _(i):
        cols = pl.ds(pl.multiple_of(i * tile, tile), tile)
        units_part = act[:, :, cols].reshape(LINE * rows, tile)
        wd[cols, :] = mm_tn(units_part, dm[...].reshape(LINE * rows, width)).astype(BF)

    store(wd, g_down)

    def fetch(pairs):
        copies = [
            pltpu.make_async_copy(a, b, mid_sems.at[2, i]) for i, (a, b) in enumerate(pairs)
        ]
        for copy in copies:
            copy.start()
        for copy in copies:
            copy.wait()

    def add(target, other):
        count = target.shape[0]
        step = min(64, count)

        @pl.loop(0, count // step)
        def _(i):
            part = pl.ds(pl.multiple_of(i * step, step), step)
            target[part, :] = (target[part, :].astype(F32) + other[part, :].astype(F32)).astype(BF)

    upper, lower = pl.ds(0, half), pl.ds(half, half)
    for wait in e_waits:
        wait()
    rows_sent.wait_sent()
    for k in range(LINE):
        arrived(e_core.at[k], e_sems.at[k], here)
    fetch(
        [(e_own.at[k], h_all.at[k, upper]) for k in range(LINE)]
        + [(e_core.at[k], h_all.at[k, lower]) for k in range(LINE)]
    )
    for k in reversed(range(LINE)):
        add(h_all.at[k, upper], h_all.at[k, lower])

    def line_came(i, way, cond, k):
        def act_on():
            arrived(e_line.at[way, i], step_sems.at[way, i], here)
            fetch([(e_line.at[way, i], h_all.at[way, lower])])
            add(h_all.at[k, upper], h_all.at[way, lower])

        when(cond, act_on)

    def line_go(i, way, cond, k):
        sends.start(
            h_all.at[k, upper], e_line.at[way, i], step_sems.at[way, i], at(t + 1 - 2 * way, c),
            cond,
        )

    inner = jnp.logical_and(t >= 1, t <= 2)
    line_go(0, 0, t == 0, 3)
    line_go(0, 1, t == 3, 3)

    for dt in range(1, LINE):
        p = (t + dt) % LINE
        arrived(f_out.at[p], done_sems.at[p], here)
    fetch([(f_out.at[(t + dt) % LINE], f_core.at[dt]) for dt in range(1, LINE)])
    gain_part[...] = jnp.zeros_like(gain_part)
    step = half // 16

    @pl.loop(0, 16)
    def _(i):
        part = pl.ds(pl.multiple_of(i * step, step), step)
        grad = f_stage[0, part, :].astype(F32)
        for dt in range(1, LINE):
            grad = grad + f_core[dt, part, :].astype(F32)
        values = h_one[part, :]
        scale = lax.rsqrt(jnp.mean(values * values, axis=1, keepdims=True) + EPS)
        gain_part[...] += jnp.sum(grad * values * scale, axis=0, keepdims=True)
        grad = grad * gain[...]
        back = jnp.mean(grad * values, axis=1, keepdims=True) * scale * scale
        grad = dm[t, part, :].astype(F32) + scale * (grad - values * back)
        e_stage[part, :] = grad.astype(BF)

    own_rows_out = dab.at[pl.ds(pl.multiple_of(x * half, half), half)]
    store(e_stage.at[upper], own_rows_out)
    sends.start(e_stage.at[upper], own_rows_out, dab_sem, across)
    line_came(0, 0, t == 1, 2)
    line_came(0, 1, t == 2, 2)
    line_go(1, 0, t <= 1, 2)
    line_go(1, 1, t >= 2, 2)
    if whole:
        copies = []
        for tt in range(LINE):
            span = pl.ds(tt * group, group)
            arrived(gate_mid.at[span], gate_sems.at[tt], here)
            arrived(up_mid.at[0, tt], up_sems.at[0, tt], here)
            for i, (source, target) in enumerate(
                (
                    (gate_mid.at[span], dg.at[tt, :, pl.ds(0, strip)]),
                    (up_mid.at[0, tt], du.at[tt, pl.ds(0, block)]),
                )
            ):
                copies.append(pltpu.make_async_copy(source, target, mid_sems.at[i, tt]))
                copies[-1].start()
        for tt in range(LINE):
            mine = side_rows(tt, j)
            copies[2 * tt].wait()
            for jj in range(side):
                span = pl.ds(tt * group + jj * block, block)
                wg[span, near] = (
                    wg[span, near].astype(F32)
                    + dg[tt, pl.ds(jj * block, block), pl.ds(0, strip)].astype(F32)
                ).astype(BF)
            sends.start(
                wg.at[side_rows(tt, 1 - j), near], gate_got.at[tt], last_sems.at[0, tt], beside
            )
            store(wg.at[mine, near], gate_kept.at[tt])
            copies[2 * tt + 1].wait()
            wu[mine, :] = (
                wu[mine, :].astype(F32) + du[tt, pl.ds(0, block), :].astype(F32)
            ).astype(BF)
            sends.start(wu.at[mine, far], up_got.at[tt], last_sems.at[1, tt], across)
            store(wu.at[mine, near], up_kept.at[tt])
    line_came(1, 0, inner, 3)
    line_came(1, 1, inner, 1)
    line_go(2, 0, t == 0, 1)
    line_go(2, 0, inner, 3)
    line_go(2, 1, t >= 1, 1)
    for sent in f_sent[LINE - 2 :]:
        sent()
    sends.made = [item for item in sends.made if item[1] is not None]
    for tt in range(LINE):
        if whole:
            arrived(gate_got.at[tt], last_sems.at[0, tt], here)
            arrived(up_got.at[tt], last_sems.at[1, tt], here)
        else:
            arrived(gate_mid.at[pl.ds(tt * group, group)], gate_sems.at[tt], here)
            for k in range(side // 2):
                arrived(up_mid.at[k, tt], up_sems.at[k, tt], here)
    arrived(dab.at[pl.ds(pl.multiple_of((1 - x) * half, half), half)], dab_sem, here)
    line_came(2, 0, t >= 1, 0)
    line_came(2, 1, t <= 2, 0)

    @pl.loop(0, 16)
    def _(i):
        part = pl.ds(pl.multiple_of(i * step, step), step)
        out_half[part, :] = (h_one[part, :] + h_all[0, part, :].astype(F32)).astype(BF)

    sends.wait_sent()
    for copy in stores:
        copy.wait()


def feed_forward(side, h_own, dm_all, units, down, h_one, ffn_gain):
    half, width = h_own.shape
    unit_count = down.shape[0]
    strip = unit_count // 2
    rows = 2 * half
    group = width // LINE
    block = group // side
    any_space = pl.BlockSpec(memory_space=pl.ANY)
    vmem = pl.BlockSpec(memory_space=pltpu.VMEM)
    mids = [(width, strip), (side // 2, LINE, block, unit_count)]
    last = (LINE, block, strip)
    blocks = (LINE, half, width)
    outs = [blocks, blocks, (2, 3, half, width), blocks, (unit_count, width)] + mids
    outs += [last] * 4 if side == 2 else [mids[0], (1, LANES), mids[1], (1, LANES)]
    held = [
        (width, unit_count), (width, unit_count), (unit_count, width),
        (LINE, rows, width), (LINE, rows, width),
        (LINE, rows, unit_count), (LINE, rows, unit_count), (LINE, rows, unit_count),
        (rows, width), (LINE, half, width), (2, half, width), (LINE, half, width),
    ]
    sends = 3 + 4 * (LINE - 1) + 3 * LINE + 3 * LINE + side // 2 * LINE + 8
    return pl.pallas_call(
        functools.partial(feed_kernel, side),
        out_shape=[
            jax.ShapeDtypeStruct((half, width), BF),
            jax.ShapeDtypeStruct((rows, width), BF),
            jax.ShapeDtypeStruct((1, width), F32),
        ]
        + [jax.ShapeDtypeStruct(shape, BF) for shape in outs],
        in_specs=[any_space] * 4 + [vmem] * 2,
        out_specs=[vmem, any_space, vmem] + [any_space] * len(outs),
        scratch_shapes=[pltpu.VMEM(shape, BF) for shape in held]
        + [
            pltpu.SemaphoreType.DMA((5,)),
            pltpu.SemaphoreType.DMA((3 * LINE + 2 + side // 2 * LINE,)),
            pltpu.SemaphoreType.DMA((sends,)),
            pltpu.SemaphoreType.DMA((LINE,)),
            pltpu.SemaphoreType.DMA((LINE,)),
            pltpu.SemaphoreType.DMA((LINE,)),
            pltpu.SemaphoreType.DMA((LINE,)),
            pltpu.SemaphoreType.DMA((LINE,)),
            pltpu.SemaphoreType.DMA((side // 2, LINE)),
            pltpu.SemaphoreType.DMA((3, 2 * LINE)),
            pltpu.SemaphoreType.DMA((2, LINE)),
            pltpu.SemaphoreType.DMA((LINE,)),
            pltpu.SemaphoreType.DMA((2, 3)),
            pltpu.SemaphoreType.DMA,
            pltpu.SemaphoreType.DMA((3 + 4 * (LINE - 1),)),
        ],
        compiler_params=pltpu.CompilerParams(
            collective_id=1, has_side_effects=True, vmem_limit_bytes=63 << 20
        ),
        cost_estimate=pl.CostEstimate(
            flops=18 * LINE * rows * width * unit_count, bytes_accessed=100 << 20,
            transcendentals=LINE * rows * unit_count,
        ),
    )(h_own, dm_all, units, down, h_one, ffn_gain[None, :])


def end_kernel(side, piece, scale, *refs):
    gate, gate_got, up, up_got, down, down_got, w_qkv, w_out, dab, length = refs[:10]
    hidden, proj, totals, cosine, sine, q_gain, k_gain, attn_gain, ffn_part = refs[10:19]
    q_out, k_out, v_out, homes_out, down_out, small_out, low_out, low_got_out = refs[19:27]
    (
        heads, heads_core, heads_side, line_right, line_left,
        gates, gates_got, ups, ups_got, downs, downs_got, downs_across, homes,
        grads, weights, low, low_got, grad_o, out_held, dab_held,
        keys_sum, vals_sum, q_sum, k_sum, smalls,
    ) = refs[27:52]
    load_sems, send_sems, core_sems, side_sems, line_sems, across_sems = refs[52:58]
    home_sems, small_sems, store_sems = refs[58:]
    t, j, c, x = coordinates()
    bits = side.bit_length() - 1
    depth, q_cols = q_out.shape
    k_cols = k_out.shape[1]
    strip = side * piece

    def at(tt, jj, cc, xx=None):
        return (((tt * side) + jj) * 2 + cc, x if xx is None else xx)

    def block(tt, jj, cc):
        return ((tt * side) + jj) * 2 + cc

    here, core, across = at(t, j, c), at(t, j, 1 - c), at(t, j, c, 1 - x)
    beside = [at(t, j ^ (1 << bit), c) for bit in range(bits)]
    others = [
        at((t + dt) % LINE, j, c ^ dc) for dt in range(LINE) for dc in range(2) if dt or dc
    ]
    loads = [
        (gate, gates), (gate_got, gates_got), (up, ups), (up_got, ups_got),
        (down.at[x], downs) if side == 2 else (down, downs),
        (w_qkv, weights),
    ]
    if side != 2:
        loads.append((down_got, downs_got))
    loads += [(w_out, out_held), (dab, dab_held)]
    loads = [pltpu.make_async_copy(a, b, load_sems.at[i]) for i, (a, b) in enumerate(loads)]
    for load in loads:
        load.start()
    greet(others + beside + [across])
    sends = Sends(send_sems)

    def add(target, first, second):
        count = first.shape[0]
        step = min(64, count)

        @pl.loop(0, count // step)
        def _(i):
            part = pl.ds(pl.multiple_of(i * step, step), step)
            target[part, :] = (first[part, :].astype(F32) + second[part, :].astype(F32)).astype(
                target.dtype
            )

    def go_home(which, rows):
        for tt in range(LINE):
            for cc in range(2):
                mine = jnp.logical_and(t == tt, c == cc)
                source = rows.at[tt, pl.ds(cc * depth, depth)]
                target = homes.at[which, t * 2 + c]
                sends.start(
                    source, target, home_sems.at[which, t * 2 + c], at(tt, j, cc),
                    jnp.logical_not(mine),
                )

                @pl.when(mine)
                def _():
                    homes[which, tt * 2 + cc] = source[...]

    if side == 2:
        sends.start(down.at[1 - x], downs_got, across_sems.at[2], across)
    for which, (mine, got) in enumerate(((gates, gates_got), (ups, ups_got))):
        loads[2 * which].wait()
        loads[2 * which + 1].wait()
        for tt in range(LINE):
            add(mine.at[tt], mine.at[tt], got.at[tt])
        go_home(which, mine)

    def down_second():
        loads[4].wait()
        if side == 2:
            arrived(downs_got, across_sems.at[2], here)
        else:
            loads[6].wait()
        for xx in range(2):
            add(downs.at[xx], downs.at[xx], downs_got.at[xx])
        if side == 2:
            sends.start(downs.at[1 - j], downs_across, across_sems.at[0], beside[0])
        else:
            sends.start(downs.at[1 - x], downs_across, across_sems.at[0], across)

    loads[-2].wait()
    loads[-1].wait()
    tile = min(512, q_cols)

    @pl.loop(0, q_cols // tile)
    def _(i):
        cols = pl.ds(pl.multiple_of(i * tile, tile), tile)
        grad_o[:, cols] = mm_nt(dab_held[...], out_held[cols, :]).astype(BF)

    q_sum[...] = jnp.zeros_like(q_sum)
    k_sum[...] = jnp.zeros_like(k_sum)
    rows = hidden.shape[0]
    group = q_cols // k_cols * HEAD

    @pl.loop(0, k_cols // HEAD)
    def _(g):
        pair = pl.multiple_of(g // 2 * LANES, LANES)
        wide = pl.ds(pl.multiple_of(g * group, group), group)
        k_pair = pl.ds(q_cols + pair, LANES)
        v_pair = pl.ds(q_cols + k_cols + pair, LANES)
        attend_back_kernel(
            rows // 2, scale, g % 2 == 1, length,
            proj.at[:, wide], proj.at[:, k_pair], proj.at[:, v_pair],
            cosine, sine, q_gain, k_gain,
            totals.at[:, pl.ds(pl.multiple_of(g * LANES, LANES), LANES)],
            grad_o.at[:, wide],
            grads.at[:, wide], grads.at[:, k_pair], grads.at[:, v_pair],
            q_sum, k_sum, keys_sum, vals_sum,
        )

    width = hidden.shape[1]
    place_rows = width // LINE
    tile = min(256, place_rows)
    for q in reversed(range(LINE)):
        tt = slot_place(t, q)

        @pl.loop(0, place_rows // tile)
        def _(i):
            span = pl.ds(pl.multiple_of(tt * place_rows + i * tile, tile), tile)
            grad = mm_tn(hidden[:, span], grads[...]).astype(BF)
            first = tt * (2 * side) + i * (tile // depth)
            heads[pl.ds(first, tile // depth)] = grad.reshape(tile // depth, depth, -1)

        for r in range(side):
            sends.start(
                heads.at[block(tt, j ^ r, 1 - c)], heads_core.at[tt, j ^ r],
                core_sems.at[tt, j ^ r], core,
            )

    loads[5].wait()
    wide = min(512, width)
    for i in range(width // wide):
        cols = pl.ds(i * wide, wide)
        grad = mm_nt(grads[...], weights[cols, :])
        low[:, cols] = grad.astype(BF)
        part = jnp.sum(grad * hidden[:, cols].astype(F32), axis=0, keepdims=True)
        part = part / attn_gain[:, cols]
        for k in range(wide // LANES):
            smalls[0, pl.ds(i * (wide // LANES) + k, 1), :] = part[:, k * LANES : (k + 1) * LANES]
    sends.start(low, low_got, across_sems.at[1], across)
    count = width // LANES
    smalls[0, pl.ds(count, count), :] = ffn_part[...]
    q_part, k_part = q_sum[...], k_sum[...]
    q_part = q_part + pltpu.roll(q_part, HEAD, 1)
    k_part = k_part + pltpu.roll(k_part, HEAD, 1)
    smalls[0, pl.ds(2 * count, 1), :] = jnp.where(low_lanes(q_part.shape), q_part, k_part)

    partners = [core] + beside + [across, at(t ^ 1, j, c), at(t ^ 2, j, c)]

    def small_step(i):
        if i:
            arrived(smalls.at[2 * i], small_sems.at[i - 1], here)
            smalls[2 * i - 1] = smalls[max(2 * i - 3, 0)] + smalls[2 * i]
        if i < len(partners):
            source = smalls.at[2 * i - 1] if i else smalls.at[0]
            sends.start(source, smalls.at[2 * i + 2], small_sems.at[i], partners[i])
        return i + 1

    def side_first(q):
        tt = slot_place(t, q)
        for r in reversed(range(side)):
            arrived(heads_core.at[tt, j ^ r], core_sems.at[tt, j ^ r], here)
            mine = heads.at[block(tt, j ^ r, c)]
            add(mine, mine, heads_core.at[tt, j ^ r])
            if bits and r >= side // 2:
                k = side // 2 - 1 + r - side // 2
                sends.start(mine, heads_side.at[tt, k], side_sems.at[tt, k], beside[bits - 1])

    def side_rest(q):
        tt = slot_place(t, q)
        for bit in reversed(range(bits)):
            half = 1 << bit
            for r in range(half):
                arrived(heads_side.at[tt, half - 1 + r], side_sems.at[tt, half - 1 + r], here)
                mine = heads.at[block(tt, j ^ r, c)]
                add(mine, mine, heads_side.at[tt, half - 1 + r])
                if bit and r >= half // 2:
                    k = half // 2 - 1 + r - half // 2
                    sends.start(
                        mine, heads_side.at[tt, k], side_sems.at[tt, k], beside[bit - 1]
                    )
        return heads.at[block(tt, j, c)]

    def line_came(i, way, cond, target):
        line = (line_right, line_left)[way]

        def act():
            arrived(line.at[i], line_sems.at[way, i], here)
            add(target, target, line.at[i])

        when(cond, act)

    def line_go(i, way, cond, source):
        line = (line_right, line_left)[way]
        sends.start(
            source, line.at[i], line_sems.at[way, i], at(t + 1 - 2 * way, j, c), cond
        )

    step = small_step(0)
    side_first(3)
    side_first(2)
    step = small_step(step)
    p3 = side_rest(3)
    line_go(0, 0, t == 0, p3)
    line_go(0, 1, t == 3, p3)
    side_first(1)
    step = small_step(step)
    p2 = side_rest(2)
    line_came(0, 0, t == 1, p2)
    line_came(0, 1, t == 2, p2)
    line_go(1, 0, t <= 1, p2)
    line_go(1, 1, t >= 2, p2)
    side_first(0)
    down_second()

    step = small_step(step)
    p1 = side_rest(1)
    line_came(1, 0, jnp.logical_and(t >= 1, t <= 2), p3)
    line_came(1, 1, jnp.logical_and(t >= 1, t <= 2), p1)
    line_go(2, 0, t == 0, p1)
    line_go(2, 0, jnp.logical_and(t >= 1, t <= 2), p3)
    line_go(2, 1, t >= 1, p1)
    while step <= len(partners):
        step = small_step(step)
    small_out[...] = smalls[2 * len(partners) - 1]
    arrived(downs_across, across_sems.at[0], here)
    add(down_out, downs.at[j if side == 2 else x], downs_across)
    p0 = side_rest(0)
    line_came(2, 0, t >= 1, p0)
    line_came(2, 1, t <= 2, p0)
    q_out[...] = p0[:, pl.ds(0, q_cols)].astype(F32)
    k_out[...] = p0[:, pl.ds(q_cols, k_cols)].astype(F32)
    v_out[...] = p0[:, pl.ds(q_cols + k_cols, k_cols)].astype(F32)
    stores = []

    def store(source, target):
        copy = pltpu.make_async_copy(source, target, store_sems.at[len(stores)])
        copy.start()
        stores.append(copy)

    for which in range(2):
        for tt in range(LINE):
            for cc in range(2):
                when(
                    jnp.logical_not(jnp.logical_and(t == tt, c == cc)),
                    lambda w=which, k=tt * 2 + cc: arrived(
                        homes.at[w, k], home_sems.at[w, k], here
                    ),
                )
    store(homes, homes_out)
    arrived(low_got, across_sems.at[1], here)
    store(low, low_out)
    store(low_got, low_got_out)
    sends.wait_sent()
    for copy in stores:
        copy.wait()


def end_layer(n, piece, pairs, down, w_qkv, w_out, dab, length, hidden, proj, totals, tables,
              gains, attn_gain, ffn_part):
    side = n // LINE // 2
    bits = side.bit_length() - 1
    rows, width = hidden.shape
    cols = w_qkv.shape[1]
    q_cols = w_out.shape[0]
    depth = width // n
    k_cols = (cols - q_cols) // 2
    strip = side * piece
    any_space = pl.BlockSpec(memory_space=pl.ANY)
    vmem = pl.BlockSpec(memory_space=pltpu.VMEM)
    steps = bits + 4
    sides = max(side - 1, 1)
    home = (LINE, 2 * depth, strip)
    held = [
        (n, depth, cols), (LINE, side, depth, cols), (LINE, sides, depth, cols),
        (3, depth, cols), (3, depth, cols),
        home, home, home, home,
        (2, piece, width), (2, piece, width), (piece, width),
        (2, LINE * 2, depth, strip),
        (rows, cols), (width, cols), (rows, width), (rows, width),
        (rows, q_cols), (q_cols, width), (rows, width),
    ]
    small = (2 * (width // LANES) + 1, LANES)
    floats = [
        (rows, LANES), (rows, LANES), (1, LANES), (1, LANES),
        (2 * steps + 1,) + small,
    ]
    sends = LINE * (2 * side - 1) + 3 + steps + 8 + 4 * LINE + 4
    return pl.pallas_call(
        functools.partial(end_kernel, side, piece, 1.0 / math.sqrt(HEAD)),
        out_shape=[
            jax.ShapeDtypeStruct((depth, q_cols), F32),
            jax.ShapeDtypeStruct((depth, k_cols), F32),
            jax.ShapeDtypeStruct((depth, k_cols), F32),
            jax.ShapeDtypeStruct((2, LINE * 2, depth, strip), BF),
            jax.ShapeDtypeStruct((piece, width), F32),
            jax.ShapeDtypeStruct(small, F32),
            jax.ShapeDtypeStruct((rows, width), BF),
            jax.ShapeDtypeStruct((rows, width), BF),
        ],
        in_specs=[any_space] * 9 + [pl.BlockSpec(memory_space=pltpu.SMEM)] + [vmem] * 9,
        out_specs=[vmem] * 3 + [any_space] + [vmem] * 2 + [any_space] * 2,
        scratch_shapes=[pltpu.VMEM(shape, BF) for shape in held]
        + [pltpu.VMEM(shape, F32) for shape in floats]
        + [
            pltpu.SemaphoreType.DMA((9,)),
            pltpu.SemaphoreType.DMA((sends,)),
            pltpu.SemaphoreType.DMA((LINE, side)),
            pltpu.SemaphoreType.DMA((LINE, sides)),
            pltpu.SemaphoreType.DMA((2, 3)),
            pltpu.SemaphoreType.DMA((3,)),
            pltpu.SemaphoreType.DMA((2, LINE * 2)),
            pltpu.SemaphoreType.DMA((steps,)),
            pltpu.SemaphoreType.DMA((4,)),
        ],
        compiler_params=pltpu.CompilerParams(
            collective_id=2, has_side_effects=True, vmem_limit_bytes=62 << 20
        ),
        cost_estimate=pl.CostEstimate(
            flops=8 * rows * width * cols, bytes_accessed=300 << 20, transcendentals=rows * rows
        ),
    )(
        *pairs, *down, w_qkv, w_out, dab, length, hidden, proj, totals, *tables, *gains,
        attn_gain[None, :], ffn_part,
    )


def finish_kernel(side, piece, homes, low, low_got, tokens, dab, gain, gate, up, grad):
    count = gate.shape[0]
    for which, out in enumerate((gate, up)):
        for tt in range(LINE):
            for jj in range(side):
                for cc in range(2):
                    col = ((tt * side + jj) * 2 + cc) * piece
                    out[:, pl.ds(col, piece)] = homes[
                        which, tt * 2 + cc, pl.ds(0, count), pl.ds(jj * piece, piece)
                    ].astype(F32)
    values = tokens[...].astype(F32)
    scale = lax.rsqrt(jnp.mean(values * values, axis=1, keepdims=True) + EPS)
    part = (low[...].astype(F32) + low_got[...].astype(F32)) * gain[...]
    back = jnp.mean(part * values, axis=1, keepdims=True) * scale * scale
    grad[...] = dab[...].astype(F32) + scale * (part - values * back)


def finish(side, piece, homes, low, low_got, tokens, dab, gain):
    rows, width = tokens.shape
    depth, strip = homes.shape[2], homes.shape[3]
    steps = 8 if depth % 128 == 0 else 2
    columns = LINE * 2 * strip
    block = pl.BlockSpec((rows // steps, width), lambda i: (i, 0))
    wide = pl.BlockSpec((depth // steps, columns), lambda i: (i, 0))
    return pl.pallas_call(
        functools.partial(finish_kernel, side, piece),
        grid=(steps,),
        in_specs=[
            pl.BlockSpec((2, LINE * 2, depth // steps, strip), lambda i: (0, 0, i, 0)),
            block, block, block, block,
            pl.BlockSpec((1, width), lambda i: (0, 0)),
        ],
        out_specs=[wide, wide, block],
        out_shape=[
            jax.ShapeDtypeStruct((depth, columns), F32),
            jax.ShapeDtypeStruct((depth, columns), F32),
            jax.ShapeDtypeStruct((rows, width), F32),
        ],
        compiler_params=pltpu.CompilerParams(vmem_limit_bytes=62 << 20),
        cost_estimate=pl.CostEstimate(
            flops=20 * rows * width, bytes_accessed=20 << 20, transcendentals=0
        ),
    )(homes, low, low_got, tokens, dab, gain[None, :])


class Links:
    def __init__(self, n):
        self.n = n
        self.inner = n // LINE
        self.side = self.inner // 2
        self.side_bits = self.side.bit_length() - 1
        self.t, self.j, self.c, self.x = coordinates()

    def core(self, value):
        return lax.ppermute(value, "dp", [(i, i ^ 1) for i in range(self.n)])

    def over(self, value, bit):
        return lax.ppermute(value, "dp", [(i, i ^ (2 << bit)) for i in range(self.n)])

    def cross(self, value):
        return lax.ppermute(value, "tensor", [(0, 1), (1, 0)])

    def along(self, value, moves):
        pairs = [
            (a * self.inner + i, b * self.inner + i) for a, b in moves for i in range(self.inner)
        ]
        return lax.ppermute(value, "dp", pairs)

    def right(self, value, senders):
        return self.along(value, [(a, a + 1) for a in senders])

    def left(self, value, senders):
        return self.along(value, [(a, a - 1) for a in senders])

    def turn(self, value, shift):
        return self.along(value, [(a, (a + shift) % LINE) for a in range(LINE)])

    def line_gather(self, value):
        t = self.t
        r1 = self.right(value, (0, 1, 2))
        l1 = self.left(value, (1, 2, 3))
        r2 = self.right(r1, (1, 2))
        l2 = self.left(l1, (1, 2))
        r3 = self.right(r2, (2,))
        l3 = self.left(l2, (1,))
        return (
            value,
            jnp.where(t == 0, l1, r1),
            jnp.where(t < 2, l2, r2),
            jnp.where(t == 0, l3, jnp.where(t == 3, r3, l1)),
        )

    def lines(self):
        return [[i + k * self.inner for k in range(LINE)] for i in range(self.inner)]

    def line_all(self, value):
        return lax.all_gather(value, "dp", axis_index_groups=self.lines())

    def line_sum(self, value):
        return lax.psum_scatter(
            value, "dp", scatter_dimension=0, axis_index_groups=self.lines()
        )

    def dp_sum(self, value):
        return lax.psum_scatter(value, "dp", scatter_dimension=0, tiled=True)

    def line_scatter(self, parts):
        t = self.t
        p0, p1, p2, p3 = parts
        first = p3.astype(BF)
        r1 = self.right(first, (0,))
        l1 = self.left(first, (3,))
        second = (p2 + r1.astype(F32) + l1.astype(F32)).astype(BF)
        r2 = self.right(second, (0, 1))
        l2 = self.left(second, (2, 3))
        r3 = self.right((jnp.where(t == 0, p1, p3) + r2.astype(F32)).astype(BF), (0, 1, 2))
        l3 = self.left((p1 + l2.astype(F32)).astype(BF), (1, 2, 3))
        return p0 + r3.astype(F32) + l3.astype(F32)

    def line_send(self, parts):
        p0, p1, p2, p3 = parts
        first, second, third = p1.astype(BF), p2.astype(BF), p3.astype(BF)
        got = [
            self.left(first, (1, 2, 3)),
            self.right(first, (0,)),
            self.turn(second, 2),
            self.along(third, ((0, 3), (3, 0))),
            self.right(third, (1, 2)),
        ]
        return p0 + sum(g.astype(F32) for g in got)

    def side_all(self, value):
        blocks = [value]
        for bit in range(self.side_bits):
            blocks += [self.over(block, bit) for block in blocks]
        return blocks

    def side_sum(self, blocks):
        for bit in reversed(range(self.side_bits)):
            width = 1 << bit
            blocks = [
                a.astype(F32) + self.over(b.astype(BF), bit).astype(F32)
                for a, b in zip(blocks[:width], blocks[width:])
            ]
        return blocks[0]

    def side_start(self, blocks):
        for bit in reversed(range(1, len(blocks).bit_length() - 1)):
            half = 1 << bit
            blocks = [
                (a.astype(F32) + self.over(b, bit).astype(F32)).astype(BF)
                for a, b in zip(blocks[:half], blocks[half:])
            ]
        return blocks[0], self.over(blocks[1], 0)

    def side_end(self, kept, got):
        if kept.shape[0] == 1:
            return kept[0], got[0]
        total = (kept.astype(F32) + got.astype(F32)).astype(BF)
        return self.side_start(list(total))

    def pair_order(self, mine, other, where):
        low = jnp.where(where == 0, mine, other)
        high = jnp.where(where == 0, other, mine)
        return jnp.concatenate([low, high], 0)

    def pick(self, value, index, axis):
        return lax.dynamic_index_in_dim(value, index, axis, keepdims=False)

    def cross_sum(self, value, axis):
        kept = self.pick(value, self.x, axis)
        sent = self.pick(value, 1 - self.x, axis)
        return kept.astype(F32) + self.cross(sent.astype(BF)).astype(F32)

    def gather_rows(self, blocks):
        rows, cols = blocks[0].shape
        pieces, where = [], []
        for k, block in enumerate(blocks):
            for r, piece in enumerate(self.side_all(block)):
                pieces += [piece, self.core(piece)]
                where += [(k, r, 0), (k, r, 1)]

        def spots(t, j, c, x):
            return [
                (
                    i, 0, 0, rows, cols,
                    (((slot_place(t, k) * self.side) + (j ^ r)) * 2 + (c ^ s)) * rows, 0,
                )
                for i, (k, r, s) in enumerate(where)
            ]

        return place(pieces, spots, (self.n * rows, cols))

    def sum_rows(self, value):
        rows, cols = value.shape[0] // self.n, value.shape[1]
        parts = value.reshape(LINE, self.side, 2, rows, cols)
        kept = self.pick(parts, self.c, 2).astype(F32)
        parts = kept + self.core(self.pick(parts, 1 - self.c, 2)).astype(F32)
        parts = parts.astype(BF)
        parts = self.side_sum([self.pick(parts, self.j ^ r, 1) for r in range(self.side)])
        return self.line_scatter(
            [self.pick(parts, slot_place(self.t, k), 0).astype(F32) for k in range(LINE)]
        )

    def total(self, value):
        value = value + self.core(value)
        for bit in range(self.side_bits):
            value = value + self.over(value, bit)
        value = value + self.cross(value)
        value = value + self.along(value, ((0, 1), (1, 0), (2, 3), (3, 2)))
        return value + self.turn(value, 2)


def make_body(n):
    def body(
        tokens,
        cotangent,
        lengths,
        attn_gain,
        query_gain,
        key_gain,
        w_query,
        key_weight_matrix,
        value_weight_matrix,
        w_out,
        ffn_gain,
        w_gate,
        w_up,
        w_down,
    ):
        net = Links(n)
        t, j, c, x = net.t, net.j, net.c, net.x
        row_count, width = tokens.shape
        half = row_count // 2
        head_dim = query_gain.shape[0]
        q_cols = w_query.shape[1]
        k_cols = key_weight_matrix.shape[1]
        k_heads = k_cols // head_dim
        dp_index = lax.axis_index("dp")
        slot_length = lengths[dp_index]

        depth = w_gate.shape[0]
        piece = w_down.shape[0]
        side = net.side
        strip = side * piece
        tables = angle_tables(row_count, head_dim, LANES)
        gains = [jnp.tile(gain, LANES // head_dim)[None, :] for gain in (query_gain, key_gain)]
        length = slot_length[None]
        weights = (w_query, key_weight_matrix, value_weight_matrix, w_out, w_gate, w_up, w_down)
        (
            qkv_full, wo_full, units, wd, grad_all, qkv, o_low, log_totals, h_one, hidden_two,
            hidden_state,
        ) = start_layer(
            n, weights, cotangent, length, tokens, attn_gain, tables, gains, ffn_gain
        )

        (
            layer_half, grad_attn_low, g_ffn_part, _, _, _, _,
            g_down, gate_mid, up_mid, gate_kept, gate_got, up_kept, up_got,
        ) = feed_forward(
            side, hidden_two, grad_all, units.reshape(2, width, 2 * strip),
            wd.reshape(2 * strip, width), h_one, ffn_gain,
        )
        layer_out = net.pair_order(layer_half, net.cross(layer_half), x)

        if side != 2:
            gate_sum = (gate_kept.astype(F32) + gate_mid.astype(F32)).astype(BF)
            gate_sum = gate_sum.reshape(LINE, side, 2 * depth, strip)
            gate_kept, gate_got = net.side_start([net.pick(gate_sum, j ^ r, 1) for r in range(side)])
            up_kept, up_got = net.side_end(up_kept, up_mid)
            up_sum = (up_kept.astype(F32) + up_got.astype(F32)).astype(BF)
            up_kept = lax.dynamic_slice_in_dim(up_sum, x * strip, strip, 2)
            up_got = net.cross(lax.dynamic_slice_in_dim(up_sum, (1 - x) * strip, strip, 2))
        g_down = g_down.reshape(2, side, piece, width)
        down_pair = (g_down, g_down)
        if side != 2:
            down_pair = net.side_start([net.pick(g_down, j ^ r, 1) for r in range(side)])

        g_out = mm_tn(o_low, grad_attn_low).astype(BF)
        g_out_out = net.dp_sum(g_out).astype(F32)
        (
            g_query_w, g_key_w, g_value_w, homes, g_down_out, small, low, low_got,
        ) = end_layer(
            n, piece, (gate_kept, gate_got, up_kept, up_got), down_pair, qkv_full, wo_full,
            grad_attn_low, length, hidden_state, qkv, log_totals, tables, gains, attn_gain,
            g_ffn_part.reshape(-1, LANES),
        )
        g_gate_out, g_up_out, input_grad = finish(
            side, piece, homes, low, low_got, tokens, grad_attn_low, attn_gain
        )
        small = small.reshape(-1)
        return (
            layer_out,
            input_grad,
            small[:width],
            small[2 * width : 2 * width + head_dim],
            small[2 * width + head_dim :],
            g_query_w,
            g_key_w,
            g_value_w,
            g_out_out,
            small[width : 2 * width],
            g_gate_out,
            g_up_out,
            g_down_out,
        )

    return body


def solution(mesh):
    placed = (
        P("dp", None),
        P("dp", None),
        P(),
        P(),
        P(),
        P(),
        P("dp", "tensor"),
        P("dp", "tensor"),
        P("dp", "tensor"),
        P(("tensor", "dp"), None),
        P(),
        P("dp", "tensor"),
        P("dp", "tensor"),
        P(("tensor", "dp"), None),
    )
    return jax.shard_map(
        make_body(mesh.shape["dp"]),
        mesh=mesh,
        in_specs=placed,
        out_specs=(
            P("dp", None),
            P("dp", None),
            P(),
            P(),
            P(),
            P("dp", "tensor"),
            P("dp", "tensor"),
            P("dp", "tensor"),
            P(("tensor", "dp"), None),
            P(),
            P("dp", "tensor"),
            P("dp", "tensor"),
            P(("tensor", "dp"), None),
        ),
        check_vma=False,
    )
```

```python
import functools
import math

import jax
import jax.numpy as jnp
import numpy as np
from jax import lax
from jax.experimental import pallas as pl
from jax.experimental.pallas import tpu as pltpu
from jax.sharding import PartitionSpec as P

EPS = 1e-05
ROPE_BASE = 1000000.0
MASKED = -1e30
LINE = 4
BF = jnp.bfloat16
F32 = jnp.float32


def rms_scale(values, gain):
    return values * lax.rsqrt(jnp.mean(values * values, axis=-1, keepdims=True) + EPS) * gain


def angle_tables(count, head_dim, lanes):
    half_dim = head_dim // 2
    freq = ROPE_BASE ** (np.arange(half_dim) * (-2.0 / head_dim))
    turned = np.arange(count)[:, None] * freq[None, :]
    cosine, sine = np.cos(turned).astype(np.float32), np.sin(turned).astype(np.float32)
    repeats = lanes // head_dim
    return (
        jnp.asarray(np.tile(np.concatenate([cosine, cosine], 1), (1, repeats))),
        jnp.asarray(np.tile(np.concatenate([-sine, sine], 1), (1, repeats))),
    )


LANES = 128
HEAD = LANES // 2


def low_lanes(shape):
    return lax.broadcasted_iota(jnp.int32, shape, 1) < HEAD


def per_head(values):
    low = low_lanes(values.shape)
    first = jnp.sum(jnp.where(low, values, 0.0), axis=1, keepdims=True)
    second = jnp.sum(jnp.where(low, 0.0, values), axis=1, keepdims=True)
    return jnp.where(low, first, second) * (1.0 / HEAD)


def halves_swapped(values):
    lane = lax.broadcasted_iota(jnp.int32, values.shape, 1)
    return jnp.where(
        lane % HEAD < HEAD // 2,
        pltpu.roll(values, LANES - HEAD // 2, 1),
        pltpu.roll(values, HEAD // 2, 1),
    )


def head_norm(values):
    scale = lax.rsqrt(per_head(values * values) + EPS)
    return values * scale, scale


def head_turn(values, cosine, sine):
    return values * cosine + halves_swapped(values) * sine


def head_back(grad, normed, scale, gain, cosine, sine):
    grad = grad * cosine - halves_swapped(grad) * sine
    gain_grad = jnp.sum(grad * normed, axis=0, keepdims=True)
    grad = grad * gain
    return scale * (grad - normed * per_head(grad * normed)), gain_grad


def one_head(pair, second):
    low = low_lanes(pair.shape)
    return jnp.where(low == jnp.logical_not(second), pair, pltpu.roll(pair, HEAD, 1))


def two_rows(slab):
    low = low_lanes(slab.shape)
    return jnp.concatenate([jnp.where(low, slab, 0.0), jnp.where(low, 0.0, slab)], 0).astype(BF)


def allowed_mask(block, first_row, columns, length):
    row = lax.broadcasted_iota(jnp.int32, (2 * block, columns), 0) % block + first_row
    col = lax.broadcasted_iota(jnp.int32, (2 * block, columns), 1)
    return (col <= row) & (col < length)


def attend_kernel(
    block, scale, second, length, q, k, v, cosine, sine, q_gain, k_gain, out, totals
):
    rows = q.shape[0]
    cos, sin = cosine[...], sine[...]
    keys = one_head(head_turn(head_norm(k[...])[0] * k_gain[...], cos, sin), second).astype(BF)
    vals = one_head(v[...], second).astype(BF)
    lane = lax.broadcasted_iota(jnp.int32, (block, LANES), 1)
    for first in range(0, rows, block):
        span = pl.ds(first, block)
        seen = first + block
        allowed = allowed_mask(block, first, seen, length[0])
        kept = jnp.zeros((block, LANES), F32)
        for slab in range(q.shape[1] // LANES):
            cols = pl.ds(slab * LANES, LANES)
            turned = head_turn(
                head_norm(q[span, cols])[0] * q_gain[...], cosine[span, :], sine[span, :]
            )
            scores = mm_nt(two_rows(turned), keys[:seen]) * scale
            scores = jnp.where(allowed, scores, MASKED)
            top = jnp.max(scores, axis=1, keepdims=True)
            probs = jnp.exp(scores - top)
            total = jnp.sum(probs, axis=1, keepdims=True)
            probs = (probs * (1.0 / total)).astype(BF)
            both = mm(probs, vals[:seen])
            out[span, cols] = jnp.where(low_lanes((block, LANES)), both[:block], both[block:]).astype(
                BF
            )
            log_total = top + jnp.log(total)
            kept = jnp.where(lane == 2 * slab, log_total[:block], kept)
            kept = jnp.where(lane == 2 * slab + 1, log_total[block:], kept)
        totals[span, :] = kept


def attend_back_kernel(
    block, scale, second, length, q, k, v, cosine, sine, q_gain, k_gain, totals, grad_out,
    grad_q, grad_k, grad_v, q_gain_grad, k_gain_grad, keys_sum, vals_sum,
):
    rows = q.shape[0]
    cos, sin = cosine[...], sine[...]
    k_normed, k_scale = head_norm(k[...])
    keys = one_head(head_turn(k_normed * k_gain[...], cos, sin), second).astype(BF)
    vals = one_head(v[...], second).astype(BF)
    lane = lax.broadcasted_iota(jnp.int32, (block, LANES), 1)
    keys_sum[...] = jnp.zeros_like(keys_sum)
    vals_sum[...] = jnp.zeros_like(vals_sum)

    for first in range(0, rows, block):
        span = pl.ds(first, block)
        seen = first + block
        allowed = allowed_mask(block, first, seen, length[0])
        kept = totals[span, :]
        for slab in range(q.shape[1] // LANES):
            cols = pl.ds(slab * LANES, LANES)
            q_normed, q_scale = head_norm(q[span, cols])
            turned = two_rows(head_turn(q_normed * q_gain[...], cosine[span, :], sine[span, :]))
            log_total = jnp.concatenate(
                [
                    jnp.sum(jnp.where(lane == 2 * slab + i, kept, 0.0), axis=1, keepdims=True)
                    for i in range(2)
                ],
                0,
            )
            scores = mm_nt(turned, keys[:seen]) * scale
            probs = jnp.exp(jnp.where(allowed, scores, MASKED) - log_total)
            grad_rows = two_rows(grad_out[span, cols].astype(F32))
            grad_probs = mm_nt(grad_rows, vals[:seen])
            drop = jnp.sum(probs * grad_probs, axis=1, keepdims=True)
            grad_scores = (probs * (grad_probs - drop)).astype(BF)
            both = mm(grad_scores, keys[:seen]) * scale
            grad_turned = jnp.where(low_lanes((block, LANES)), both[:block], both[block:])
            grad_proj, gain_part = head_back(
                grad_turned, q_normed, q_scale, q_gain[...], cosine[span, :], sine[span, :]
            )
            grad_q[span, cols] = grad_proj.astype(BF)
            q_gain_grad[...] += gain_part
            keys_sum[:seen] += mm_tn(grad_scores, turned)
            vals_sum[:seen] += mm_tn(probs.astype(BF), grad_rows)

    keys_grad = keys_sum[...] * scale
    keys_grad = keys_grad + pltpu.roll(keys_grad, HEAD, 1)
    vals_grad = vals_sum[...]
    vals_grad = vals_grad + pltpu.roll(vals_grad, HEAD, 1)
    grad_proj, gain_part = head_back(
        keys_grad,
        one_head(k_normed, second),
        one_head(k_scale, second),
        k_gain[...],
        cos,
        sin,
    )
    k_gain_grad[...] += gain_part * 0.5
    keep_low = low_lanes(grad_k.shape)

    @pl.when(jnp.logical_not(second))
    def _():
        grad_k[...] = grad_proj.astype(BF)
        grad_v[...] = vals_grad.astype(BF)

    @pl.when(second)
    def _():
        grad_k[...] = jnp.where(keep_low, grad_k[...].astype(F32), grad_proj).astype(BF)
        grad_v[...] = jnp.where(keep_low, grad_v[...].astype(F32), vals_grad).astype(BF)


def mm(left, right):
    return jnp.dot(left, right, preferred_element_type=F32)


def mm_nt(left, right):
    return lax.dot_general(left, right, (((1,), (1,)), ((), ())), preferred_element_type=F32)


def mm_tn(left, right):
    return lax.dot_general(left, right, (((0,), (0,)), ((), ())), preferred_element_type=F32)


def after(done, *values):
    held, _ = lax.optimization_barrier((values, done))
    return held if len(held) > 1 else held[0]


def slot_place(t, k):
    if k == 0:
        return t
    if k == 1:
        return jnp.where(t == 0, 1, t - 1)
    if k == 2:
        return (t + 2) % LINE
    return jnp.where(t == 3, 0, jnp.where(t == 1, 2, 3))


def coordinates():
    n = lax.axis_size("dp")
    inner = n // LINE
    here = lax.axis_index("dp")
    return here // inner, (here % inner) // 2, here % 2, lax.axis_index("tensor")


def place(blocks, spots, shape):
    listed = spots(0, 0, 0, 0)

    def kernel(*refs):
        sources = refs[: len(blocks)]
        out, held, sem, out_sem = refs[len(blocks) :]
        copies = []
        for k, (b, row, col, rows, cols, to_row, to_col) in enumerate(spots(*coordinates())):
            copies.append(
                pltpu.make_async_copy(
                    sources[b].at[pl.ds(row, rows), pl.ds(col, cols)],
                    held.at[
                        pl.ds(pl.multiple_of(to_row, rows), rows),
                        pl.ds(pl.multiple_of(to_col, cols), cols),
                    ],
                    sem.at[k],
                )
            )
        for copy in copies:
            copy.start()
        for copy in copies:
            copy.wait()
        last = pltpu.make_async_copy(held, out, out_sem)
        last.start()
        last.wait()

    item = blocks[0].dtype.itemsize
    moved = sum(2 * rows * cols * item for _, _, _, rows, cols, _, _ in listed)
    return pl.pallas_call(
        kernel,
        out_shape=jax.ShapeDtypeStruct(shape, blocks[0].dtype),
        in_specs=[pl.BlockSpec(memory_space=pl.ANY)] * len(blocks),
        out_specs=pl.BlockSpec(memory_space=pl.ANY),
        scratch_shapes=[
            pltpu.VMEM(shape, blocks[0].dtype),
            pltpu.SemaphoreType.DMA((len(listed),)),
            pltpu.SemaphoreType.DMA,
        ],
        compiler_params=pltpu.CompilerParams(vmem_limit_bytes=moved // 2 + (4 << 20)),
        cost_estimate=pl.CostEstimate(flops=0, bytes_accessed=moved, transcendentals=0),
    )(*blocks)


class Sends:
    def __init__(self, sems):
        self.sems = sems
        self.made = []

    def start(self, source, target, recv_sem, device, cond=None):
        sem = self.sems.at[len(self.made)]

        def copy():
            return pltpu.make_async_remote_copy(
                src_ref=source,
                dst_ref=target,
                send_sem=sem,
                recv_sem=recv_sem,
                device_id=device,
                device_id_type=pl.DeviceIdType.MESH,
            )

        self.made.append((cond, copy))
        when(cond, lambda: copy().start())

    def wait_sent(self):
        for cond, copy in self.made:
            when(cond, lambda copy=copy: copy().wait_send())


def when(cond, act):
    if cond is None:
        act()
    else:
        pl.when(cond)(act)


def both(first, second):
    if first is None:
        return second
    return first if second is None else jnp.logical_and(first, second)


def arrived(ref, recv_sem, device):
    pltpu.make_async_remote_copy(
        src_ref=ref, dst_ref=ref, send_sem=recv_sem, recv_sem=recv_sem,
        device_id=device, device_id_type=pl.DeviceIdType.MESH,
    ).wait_recv()


def greet(devices):
    barrier = pltpu.get_barrier_semaphore()
    for device in devices:
        pl.semaphore_signal(
            barrier, inc=1, device_id=device, device_id_type=pl.DeviceIdType.MESH
        )
    pl.semaphore_wait(barrier, len(devices))


def start_kernel(side, piece, sliced, scale, *refs):
    w_query, w_key, w_value, w_out, w_gate, w_up, w_down, dm_own = refs[:8]
    length, tokens, attn_gain, cosine, sine, q_gain, k_gain, ffn_gain = refs[8:16]
    outs = refs[16:21]
    proj, attended, totals, h_one, hidden_two, hidden = refs[21:27]
    qkv, out, units, down, dm = bufs = refs[27:32]
    part, cross_sent, cross_got = refs[32:35]
    (
        load_sems, send_sems, qkv_sems, out_sems, unit_sems, pair_sems, down_sems,
        line_sems, core_sems, cross_sem, store_sems,
    ) = refs[35:]
    t, j, c, x = coordinates()
    bits = side.bit_length() - 1
    strip = side * piece

    def at(tt, jj, cc, xx=None):
        return (((tt * side) + jj) * 2 + cc, x if xx is None else xx)

    def block(tt, jj, cc):
        return ((tt * side) + jj) * 2 + cc

    here = at(t, j, c)
    core = at(t, j, 1 - c)
    across = at(t, j, c, 1 - x)
    beside = [at(t, j ^ (1 << bit), c) for bit in range(bits)]
    others = [
        at((t + dt) % LINE, j, c ^ dc) for dt in range(LINE) for dc in range(2) if dt or dc
    ]
    mine = block(t, j, c)
    depth, q_cols = w_query.shape
    k_cols = w_key.shape[1]
    rows, width = tokens.shape
    half = rows // 2

    def rows_of(buf, idx):
        count = depth if buf is qkv else w_out.shape[0]
        return buf.at[pl.ds(pl.multiple_of(idx * count, count), count)]

    own_qkv = pl.ds(pl.multiple_of(mine * depth, depth), depth)
    loads = [
        (w_query, qkv.at[own_qkv, pl.ds(0, q_cols)]),
        (w_key, qkv.at[own_qkv, pl.ds(q_cols, k_cols)]),
        (w_value, qkv.at[own_qkv, pl.ds(q_cols + k_cols, k_cols)]),
        (w_out, rows_of(out, mine)),
        (w_down, down.at[x * side + j]),
        (dm_own.at[pl.ds(pl.multiple_of(x * half, half), half)], dm.at[t, pl.ds(0, half)]),
    ]
    first_unit = len(loads)

    def unit_block(which, tt, jj, cc):
        weight = (w_gate, w_up)[which]
        if sliced:
            col = pl.multiple_of(block(tt, jj, cc) * piece, piece)
            return weight.at[:, pl.ds(col, piece)]
        return weight.at[tt, cc]

    def unit_target(which, tt, jj, cc):
        col = x * strip + (jj * piece if sliced else 0)
        size = piece if sliced else strip
        return units.at[
            which, tt, j, pl.ds(pl.multiple_of(cc * depth, depth), depth),
            pl.ds(pl.multiple_of(col, size), size),
        ]

    def unit_pair(which, tt, jj, xx):
        return units.at[which, tt, jj, :, pl.ds(pl.multiple_of(xx * strip, strip), strip)]

    parts = range(side) if sliced else range(1)
    loads += [
        (unit_block(w, t, jj, c), unit_target(w, t, jj, c)) for w in range(2) for jj in parts
    ]
    loads = [
        pltpu.make_async_copy(a, b, load_sems.at[i]) for i, (a, b) in enumerate(loads)
    ]
    for load in loads:
        load.start()
    greet(others + beside + [across])
    sends = Sends(send_sems)
    for load in loads[:first_unit]:
        load.wait()

    lines = ((qkv, qkv_sems), (out, out_sems))

    def spread(buf, sems, tt, r, cond):
        idx = block(tt, j ^ r, c)
        ref = rows_of(buf, idx)
        for bit in range(bits):
            if (1 << bit) > r:
                sends.start(ref, ref, sems.at[idx], beside[bit], cond)
        sends.start(ref, ref, sems.at[idx], core, cond)

    def pass_on(ref, sem, to_right, to_left):
        if to_right is not False:
            sends.start(ref, ref, sem, at(t + 1, j, c), to_right)
        if to_left is not False:
            sends.start(ref, ref, sem, at(t - 1, j, c), to_left)

    def spread_rest(buf, sems, tt, cond):
        for r in range(1, side):
            idx = block(tt, j ^ r, c)
            when(cond, lambda idx=idx: arrived(rows_of(buf, idx), sems.at[idx], here))
            spread(buf, sems, tt, r, cond)

    def line_places(k):
        return ((t >= k, t - k, True), (t + k < LINE, t + k, False))

    def forward(ref, sem, cond, rightward):
        if rightward:
            pass_on(ref, sem, both(cond, t < LINE - 1), False)
        else:
            pass_on(ref, sem, False, both(cond, t > 0))

    def set_out(buf, sems):
        pass_on(rows_of(buf, mine), sems.at[mine], t < LINE - 1, t > 0)
        spread(buf, sems, t, 0, None)

    def line_step(buf, sems, k):
        for cond, tt, rightward in line_places(k):
            idx = block(tt, j, c)
            when(cond, lambda idx=idx: arrived(rows_of(buf, idx), sems.at[idx], here))
            if k < LINE - 1:
                forward(rows_of(buf, idx), sems.at[idx], cond, rightward)
            spread(buf, sems, tt, 0, cond)
        if k == 1:
            spread_rest(buf, sems, t, None)
        else:
            spread_rest(buf, sems, t - k + 1, t >= k - 1)
            spread_rest(buf, sems, t + k - 1, t + k - 1 < LINE)

    own_down = x * side + j

    def down_set_out():
        for bit in range(bits):
            sends.start(
                down.at[own_down], down.at[own_down], down_sems.at[own_down], beside[bit]
            )

    def down_rest():
        for r in range(1, side):
            idx = x * side + (j ^ r)
            arrived(down.at[idx], down_sems.at[idx], here)
            for bit in range(bits):
                if (1 << bit) > r:
                    sends.start(down.at[idx], down.at[idx], down_sems.at[idx], beside[bit])
            sends.start(down.at[idx], down.at[idx], down_sems.at[idx], across)

    def units_set_out():
        for dt in range(LINE):
            for dc in range(2):
                if dt or dc:
                    tt, cc = (t + dt) % LINE, c ^ dc
                    for w in range(2):
                        for jj in parts:
                            sends.start(
                                unit_block(w, tt, jj, cc),
                                unit_target(w, t, jj, c),
                                unit_sems.at[w, t * 2 + c, jj],
                                at(tt, j, cc),
                            )

    set_out(*lines[0])
    set_out(*lines[1])
    sends.start(down.at[own_down], down.at[own_down], down_sems.at[own_down], across)
    chunk = rows // 16

    @pl.loop(0, 16)
    def _(i):
        span = pl.ds(pl.multiple_of(i * chunk, chunk), chunk)
        hidden[span, :] = rms_scale(tokens[span, :].astype(F32), attn_gain[...]).astype(BF)

    @pl.loop(0, 8)
    def _(i):
        span = pl.ds(pl.multiple_of(i * chunk, chunk), chunk)
        row = lax.broadcasted_iota(jnp.int32, (chunk, width), 0) + i * chunk + x * half
        kept = dm[t, span, :].astype(F32)
        dm[t, span, :] = jnp.where(row < length[0], kept, 0.0).astype(BF)

    for k in range(1, LINE):
        line_step(*lines[0], k)
        line_step(*lines[1], k)
        if k == LINE - 2:
            units_set_out()
    down_set_out()
    stores = []

    def store(source, target):
        copy = pltpu.make_async_copy(source, target, store_sems.at[len(stores)])
        copy.start()
        stores.append(copy)

    def send_pair(w, tt, jj, xx, device):
        ref = unit_pair(w, tt, jj, xx)
        sends.start(ref, ref, pair_sems.at[w, tt, jj, xx], device)

    def pair_came(w, tt, jj, xx):
        arrived(unit_pair(w, tt, jj, xx), pair_sems.at[w, tt, jj, xx], here)

    def unit_first(tt):
        for cc in range(2):
            mine = jnp.logical_and(tt == t, cc == c)
            for w in range(2):
                for jj in parts:
                    when(
                        jnp.logical_not(mine),
                        lambda w=w, cc=cc, jj=jj: arrived(
                            unit_target(w, tt, jj, cc), unit_sems.at[w, tt * 2 + cc, jj], here
                        ),
                    )
        for w in range(2):
            for bit in range(bits):
                send_pair(w, tt, j, x, beside[bit])
            send_pair(w, tt, j, x, across)

    def unit_second(tt, by_side):
        for r in range(1, side):
            for w in range(2):
                pair_came(w, tt, j ^ r, x)
                for bit in range(bits):
                    if (1 << bit) > r:
                        send_pair(w, tt, j ^ r, x, beside[bit])
                if w not in by_side:
                    send_pair(w, tt, j ^ r, x, across)
        for w in by_side:
            pair_came(w, tt, j, 1 - x)
            for bit in range(bits):
                send_pair(w, tt, j, 1 - x, beside[bit])

    def unit_last(tt, by_side):
        for w in range(2):
            for r in range(1 if w in by_side else 0, side):
                pair_came(w, tt, j ^ r, 1 - x)
                for bit in range(bits):
                    if w in by_side and (1 << bit) > r:
                        send_pair(w, tt, j ^ r, 1 - x, beside[bit])

    dm_rows = dm.at[t, pl.ds(0, half)]

    def dm_to_core(tt, cond):
        sends.start(
            dm.at[tt, pl.ds(0, half)], dm.at[tt, pl.ds(half, half)], core_sems.at[tt], core, cond
        )

    def dm_step(k):
        for cond, tt, rightward in line_places(k):
            ref = dm.at[tt, pl.ds(0, half)]
            when(cond, lambda ref=ref, tt=tt: arrived(ref, line_sems.at[tt], here))
            if k < LINE - 1:
                forward(ref, line_sems.at[tt], cond, rightward)
            dm_to_core(tt, cond)

    def finish_line(buf, sems):
        spread_rest(buf, sems, t - LINE + 1, t >= LINE - 1)
        spread_rest(buf, sems, t + LINE - 1, t < 1)
        for tt in range(LINE):
            for jj in range(side):
                idx = block(tt, jj, 1 - c)
                arrived(rows_of(buf, idx), sems.at[idx], here)

    finish_line(*lines[0])
    store(qkv, outs[0])
    for load in loads[first_unit:]:
        load.wait()
    unit_first(t)
    pass_on(dm_rows, line_sems.at[t], t < LINE - 1, t > 0)
    dm_to_core(t, None)

    tile = 256

    @pl.loop(0, proj.shape[1] // tile)
    def _(i):
        cols = pl.ds(pl.multiple_of(i * tile, tile), tile)
        proj[:, cols] = mm(hidden[...], qkv[:, cols])

    group = q_cols // k_cols * HEAD
    key_heads = k_cols // HEAD

    def attend_head(g):
        pair = pl.multiple_of(g // 2 * LANES, LANES)
        wide = pl.ds(pl.multiple_of(g * group, group), group)
        attend_kernel(
            rows // 2, scale, g % 2 == 1, length,
            proj.at[:, wide],
            proj.at[:, pl.ds(q_cols + pair, LANES)],
            proj.at[:, pl.ds(q_cols + k_cols + pair, LANES)],
            cosine, sine, q_gain, k_gain,
            attended.at[:, wide],
            totals.at[:, pl.ds(pl.multiple_of(g * LANES, LANES), LANES)],
        )

    pl.loop(0, key_heads)(attend_head)

    finish_line(*lines[1])
    store(out, outs[1])
    wide = 512
    other_rows = pl.ds(pl.multiple_of((1 - x) * half, half), half)
    own_rows = pl.ds(pl.multiple_of(x * half, half), half)

    @pl.loop(0, width // wide)
    def _(i):
        cols = pl.ds(pl.multiple_of(i * wide, wide), wide)
        cross_sent[:, cols] = mm(attended[other_rows, :], out[:, cols]).astype(BF)

    sends.start(cross_sent, cross_got, cross_sem, across)

    @pl.loop(0, width // wide)
    def _(i):
        cols = pl.ds(pl.multiple_of(i * wide, wide), wide)
        part[:, cols] = mm(attended[own_rows, :], out[:, cols])

    for k in range(1, LINE):
        unit_first(slot_place(t, k))
    down_rest()
    unit_second(t, (0,))
    dm_step(1)
    for k in range(1, LINE):
        unit_second(slot_place(t, k), (0, 1))
    dm_step(2)

    arrived(cross_got, cross_sem, here)
    step = half // 8

    @pl.loop(0, 8)
    def _(i):
        span = pl.ds(pl.multiple_of(i * step, step), step)
        rows_here = pl.ds(pl.multiple_of(x * half + i * step, step), step)
        total = tokens[rows_here, :].astype(F32) + part[span, :] + cross_got[span, :].astype(F32)
        h_one[span, :] = total
        hidden_two[span, :] = rms_scale(total, ffn_gain[...]).astype(BF)

    dm_step(3)
    for jj in range(side):
        idx = (1 - x) * side + jj
        arrived(down.at[idx], down_sems.at[idx], here)
    store(down, outs[3])
    for tt in range(LINE):
        arrived(dm.at[tt, pl.ds(half, half)], core_sems.at[tt], here)
    store(dm, outs[4])
    for k in range(LINE):
        place_of = slot_place(t, k)
        unit_last(place_of, (0, 1) if k else (0,))
        store(units.at[:, place_of], outs[2].at[:, place_of])
    sends.wait_sent()
    for copy in stores:
        copy.wait()


def start_layer(n, weights, cotangent, length, tokens, attn_gain, tables, gains, ffn_gain):
    w_query, w_key, w_value, w_out, w_gate, w_up, w_down = weights
    side = n // LINE // 2
    depth, piece, width = w_gate.shape[0], w_down.shape[0], w_down.shape[1]
    rows, half = tokens.shape[0], tokens.shape[0] // 2
    q_cols, k_cols = w_query.shape[1], w_key.shape[1]
    cols = q_cols + 2 * k_cols
    strip = side * piece
    sliced = piece % LANES == 0
    if not sliced:
        w_gate, w_up = (
            w.reshape(depth, LINE, side, 2, piece)
            .transpose(1, 3, 0, 2, 4)
            .reshape(LINE, 2, depth, strip)
            for w in (w_gate, w_up)
        )
    shapes = [
        (width, cols),
        (q_cols, width),
        (2, LINE, side, 2 * depth, 2 * strip),
        (2 * side, piece, width),
        (LINE, 2 * half, width),
    ]
    slots = 2 * LINE - 1
    line_sends = 2 * (LINE - 1) + slots * (2 * side - 1)
    sends = 2 * line_sends + 2 * side - 1 + 14 * side + 3 * LINE + 8 + 8 * side * LINE
    any_space = pl.BlockSpec(memory_space=pl.ANY)
    vmem = pl.BlockSpec(memory_space=pltpu.VMEM)
    return pl.pallas_call(
        functools.partial(start_kernel, side, piece, sliced, 1.0 / math.sqrt(HEAD)),
        out_shape=[jax.ShapeDtypeStruct(shape, BF) for shape in shapes]
        + [
            jax.ShapeDtypeStruct((rows, cols), F32),
            jax.ShapeDtypeStruct((rows, q_cols), BF),
            jax.ShapeDtypeStruct((rows, k_cols // HEAD * LANES), F32),
            jax.ShapeDtypeStruct((half, width), F32),
            jax.ShapeDtypeStruct((half, width), BF),
            jax.ShapeDtypeStruct((rows, width), BF),
        ],
        in_specs=[any_space] * 8 + [pl.BlockSpec(memory_space=pltpu.SMEM)] + [vmem] * 7,
        out_specs=[any_space] * 5 + [vmem] * 6,
        scratch_shapes=[pltpu.VMEM(shape, BF) for shape in shapes]
        + [
            pltpu.VMEM((half, width), F32),
            pltpu.VMEM((half, width), BF),
            pltpu.VMEM((half, width), BF),
            pltpu.SemaphoreType.DMA((6 + 2 * side,)),
            pltpu.SemaphoreType.DMA((sends,)),
            pltpu.SemaphoreType.DMA((n,)),
            pltpu.SemaphoreType.DMA((n,)),
            pltpu.SemaphoreType.DMA((2, LINE * 2, side)),
            pltpu.SemaphoreType.DMA((2, LINE, side, 2)),
            pltpu.SemaphoreType.DMA((2 * side,)),
            pltpu.SemaphoreType.DMA((LINE,)),
            pltpu.SemaphoreType.DMA((LINE,)),
            pltpu.SemaphoreType.DMA,
            pltpu.SemaphoreType.DMA((8,)),
        ],
        compiler_params=pltpu.CompilerParams(
            collective_id=0, has_side_effects=True, vmem_limit_bytes=62 << 20
        ),
        cost_estimate=pl.CostEstimate(
            flops=2 * rows * width * cols, bytes_accessed=500 << 20, transcendentals=rows * rows
        ),
    )(
        w_query, w_key, w_value, w_out, w_gate, w_up, w_down, cotangent, length, tokens,
        attn_gain[None, :], *tables, *gains, ffn_gain[None, :],
    )


def feed_kernel(side, *refs):
    h_own, dm_all, units, down, h_one, gain = refs[:6]
    out_half, dab, gain_part, e_own, e_core, e_line, f_out = refs[6:13]
    g_down, gate_mid, up_mid, gate_kept, gate_got, up_kept, up_got = refs[13:20]
    wg, wu, wd, h_all, dm, act, dg, du, e_stage, f_stage, f_send, f_core = refs[20:32]
    load_sems, store_sems, send_sems, line_sems, core_sems, back_sems = refs[32:38]
    done_sems, gate_sems, up_sems, mid_sems, last_sems, e_sems, step_sems, dab_sem, row_sems = refs[38:]
    t, j, c, x = coordinates()
    half, width = h_own.shape
    unit_count = wd.shape[0]
    strip = unit_count // 2
    rows = 2 * half
    bits = side.bit_length() - 1

    def at(tt, cc, jj=None, xx=None):
        jj, xx = j if jj is None else jj, x if xx is None else xx
        return ((tt * side + jj) * 2 + cc, xx)

    here, core, across = at(t, c), at(t, 1 - c), at(t, c, None, 1 - x)
    beside = at(t, c, j ^ (side // 2))
    others = [at((t + dt) % LINE, c) for dt in range(1, LINE)]
    loads = [
        (h_own, h_all.at[t, pl.ds(0, half)]),
        (units.at[0], wg), (units.at[1], wu), (dm_all, dm), (down, wd),
    ]
    loads = [pltpu.make_async_copy(a, b, load_sems.at[i]) for i, (a, b) in enumerate(loads)]
    for load in loads:
        load.start()
    greet(others + [core, across] + ([beside] if bits else []))
    sends, rows_sent = Sends(send_sems), Sends(row_sems)

    def own_rows(tt):
        return h_all.at[tt, pl.ds(0, half)]

    def to_core(tt, cond):
        rows_sent.start(
            own_rows(tt), h_all.at[tt, pl.ds(half, half)], core_sems.at[tt], core, cond
        )

    loads[0].wait()
    rows_sent.start(own_rows(t), own_rows(t), line_sems.at[t], at(t + 1, c), t < LINE - 1)
    rows_sent.start(own_rows(t), own_rows(t), line_sems.at[t], at(t - 1, c), t > 0)
    to_core(t, None)
    for load in loads[1:]:
        load.wait()

    tile = min(512, unit_count)
    wide = min(1024, width)
    e_waits, f_sent, stores = [], [], []

    def store(source, target):
        copy = pltpu.make_async_copy(source, target, store_sems.at[len(stores)])
        copy.start()
        stores.append(copy)
        return copy

    def f_go(k):
        sends.start(
            f_stage.at[k], f_out.at[t], done_sems.at[t], at(slot_place(t, k), c)
        )

    def kept_out(k):
        copy = pltpu.make_async_copy(
            e_stage.at[pl.ds(0, half)], e_own.at[k], mid_sems.at[2, 2 * LINE - 1]
        )
        copy.start()
        return copy.wait

    def later(source, target, sem, device):
        sends.start(source, target, sem, device)
        copy = sends.made.pop()[1]
        sends.made.append((None, None))
        return lambda: copy().wait_send()

    for k in range(LINE):
        tt = slot_place(t, k)
        if k:
            for cond, place_of, forward, target in (
                (t >= k, t - k, t < LINE - 1, t + 1),
                (t + k < LINE, t + k, t > 0, t - 1),
            ):
                when(
                    cond,
                    lambda p=place_of: arrived(own_rows(p), line_sems.at[p], here),
                )
                if k < LINE - 1:
                    rows_sent.start(
                        own_rows(place_of), own_rows(place_of), line_sems.at[place_of],
                        at(target, c), jnp.logical_and(cond, forward),
                    )
                to_core(place_of, cond)
        if k >= 2:
            f_go(k - 1)
        arrived(h_all.at[tt, pl.ds(half, half)], core_sems.at[tt], here)
        if k >= 2:
            f_sent[k - 2]()

        @pl.loop(0, unit_count // tile)
        def _(i):
            cols = pl.ds(pl.multiple_of(i * tile, tile), tile)
            hidden = h_all[tt]
            gate = mm(hidden, wg[:, cols])
            up = mm(hidden, wu[:, cols])
            grad_act = mm_nt(dm[tt], wd[cols, :])
            sigma = lax.logistic(gate)
            silu = gate * sigma
            act[tt, :, cols] = (silu * up).astype(BF)
            dg[tt, :, cols] = (grad_act * up * (sigma * (1.0 + gate * (1.0 - sigma)))).astype(BF)
            du[tt, :, cols] = (grad_act * silu).astype(BF)

        slot = k % 2

        @pl.loop(0, width // wide)
        def _(i):
            span = pl.ds(pl.multiple_of(i * wide, wide), wide)
            grad = mm_nt(dg[tt], wg[span, :]) + mm_nt(du[tt], wu[span, :])
            f_stage[k, :, span] = grad[:half].astype(BF)
            f_send[slot, :, span] = grad[half:].astype(BF)

        f_sent.append(later(f_send.at[slot], f_core.at[k], back_sems.at[k], core))
        for wait in e_waits:
            wait()

        @pl.loop(0, width // wide)
        def _(i):
            span = pl.ds(pl.multiple_of(i * wide, wide), wide)
            e_stage[:, span] = mm(act[tt], wd[:, span]).astype(BF)

        e_waits = [
            kept_out(k),
            later(e_stage.at[pl.ds(half, half)], e_core.at[k], e_sems.at[k], core),
        ]
        arrived(f_core.at[k], back_sems.at[k], here)

        @pl.loop(0, 4)
        def _(i):
            part = pl.ds(pl.multiple_of(i * (half // 4), half // 4), half // 4)
            f_stage[k, part, :] = (
                f_stage[k, part, :].astype(F32) + f_core[k, part, :].astype(F32)
            ).astype(BF)

        if k == LINE - 1:
            f_go(k)

    group = width // LINE
    far = pl.ds(pl.multiple_of((1 - x) * strip, strip), strip)
    near = pl.ds(pl.multiple_of(x * strip, strip), strip)

    def weight_grad(target, grads, tt, send):
        @pl.loop(0, 1)
        def _(i):
            span = pl.ds(tt * group, group)
            hidden = h_all[:, :, span].reshape(LINE * rows, group)
            target[span, :] = mm_tn(hidden, grads[...].reshape(LINE * rows, unit_count)).astype(BF)

        send(tt)

    block = group // side
    whole = side == 2

    def side_rows(tt, jj):
        return pl.ds(pl.multiple_of(tt * group + jj * block, block), block)

    def send_gate(tt):
        span = pl.ds(tt * group, group)
        sends.start(wg.at[span, far], gate_mid.at[span], gate_sems.at[tt], across)
        if not whole:
            store(wg.at[span, near], gate_kept.at[span])

    def send_up(tt):
        for r in range(side):
            span = side_rows(tt, j ^ r)
            if r >= side // 2:
                k = r - side // 2
                sends.start(wu.at[span], up_mid.at[k, tt], up_sems.at[k, tt], beside)
            elif not whole:
                store(wu.at[span], up_kept.at[r, tt])

    for tt in range(LINE):
        weight_grad(wg, dg, tt, send_gate)
        weight_grad(wu, du, tt, send_up)
    tile = min(256, unit_count)

    @pl.loop(0, unit_count // tile)
    def _(i):
        cols = pl.ds(pl.multiple_of(i * tile, tile), tile)
        units_part = act[:, :, cols].reshape(LINE * rows, tile)
        wd[cols, :] = mm_tn(units_part, dm[...].reshape(LINE * rows, width)).astype(BF)

    store(wd, g_down)

    def fetch(pairs):
        copies = [
            pltpu.make_async_copy(a, b, mid_sems.at[2, i]) for i, (a, b) in enumerate(pairs)
        ]
        for copy in copies:
            copy.start()
        for copy in copies:
            copy.wait()

    def add(target, other):
        count = target.shape[0]
        step = min(64, count)

        @pl.loop(0, count // step)
        def _(i):
            part = pl.ds(pl.multiple_of(i * step, step), step)
            target[part, :] = (target[part, :].astype(F32) + other[part, :].astype(F32)).astype(BF)

    upper, lower = pl.ds(0, half), pl.ds(half, half)
    for wait in e_waits:
        wait()
    rows_sent.wait_sent()
    for k in range(LINE):
        arrived(e_core.at[k], e_sems.at[k], here)
    fetch(
        [(e_own.at[k], h_all.at[k, upper]) for k in range(LINE)]
        + [(e_core.at[k], h_all.at[k, lower]) for k in range(LINE)]
    )
    for k in reversed(range(LINE)):
        add(h_all.at[k, upper], h_all.at[k, lower])

    def line_came(i, way, cond, k):
        def act_on():
            arrived(e_line.at[way, i], step_sems.at[way, i], here)
            fetch([(e_line.at[way, i], h_all.at[way, lower])])
            add(h_all.at[k, upper], h_all.at[way, lower])

        when(cond, act_on)

    def line_go(i, way, cond, k):
        sends.start(
            h_all.at[k, upper], e_line.at[way, i], step_sems.at[way, i], at(t + 1 - 2 * way, c),
            cond,
        )

    inner = jnp.logical_and(t >= 1, t <= 2)
    line_go(0, 0, t == 0, 3)
    line_go(0, 1, t == 3, 3)

    for dt in range(1, LINE):
        p = (t + dt) % LINE
        arrived(f_out.at[p], done_sems.at[p], here)
    fetch([(f_out.at[(t + dt) % LINE], f_core.at[dt]) for dt in range(1, LINE)])
    gain_part[...] = jnp.zeros_like(gain_part)
    step = half // 16

    @pl.loop(0, 16)
    def _(i):
        part = pl.ds(pl.multiple_of(i * step, step), step)
        grad = f_stage[0, part, :].astype(F32)
        for dt in range(1, LINE):
            grad = grad + f_core[dt, part, :].astype(F32)
        values = h_one[part, :]
        scale = lax.rsqrt(jnp.mean(values * values, axis=1, keepdims=True) + EPS)
        gain_part[...] += jnp.sum(grad * values * scale, axis=0, keepdims=True)
        grad = grad * gain[...]
        back = jnp.mean(grad * values, axis=1, keepdims=True) * scale * scale
        grad = dm[t, part, :].astype(F32) + scale * (grad - values * back)
        e_stage[part, :] = grad.astype(BF)

    own_rows_out = dab.at[pl.ds(pl.multiple_of(x * half, half), half)]
    store(e_stage.at[upper], own_rows_out)
    sends.start(e_stage.at[upper], own_rows_out, dab_sem, across)
    line_came(0, 0, t == 1, 2)
    line_came(0, 1, t == 2, 2)
    line_go(1, 0, t <= 1, 2)
    line_go(1, 1, t >= 2, 2)
    if whole:
        copies = []
        for tt in range(LINE):
            span = pl.ds(tt * group, group)
            arrived(gate_mid.at[span], gate_sems.at[tt], here)
            arrived(up_mid.at[0, tt], up_sems.at[0, tt], here)
            for i, (source, target) in enumerate(
                (
                    (gate_mid.at[span], dg.at[tt, :, pl.ds(0, strip)]),
                    (up_mid.at[0, tt], du.at[tt, pl.ds(0, block)]),
                )
            ):
                copies.append(pltpu.make_async_copy(source, target, mid_sems.at[i, tt]))
                copies[-1].start()
        for tt in range(LINE):
            mine = side_rows(tt, j)
            copies[2 * tt].wait()
            for jj in range(side):
                span = pl.ds(tt * group + jj * block, block)
                wg[span, near] = (
                    wg[span, near].astype(F32)
                    + dg[tt, pl.ds(jj * block, block), pl.ds(0, strip)].astype(F32)
                ).astype(BF)
            sends.start(
                wg.at[side_rows(tt, 1 - j), near], gate_got.at[tt], last_sems.at[0, tt], beside
            )
            store(wg.at[mine, near], gate_kept.at[tt])
            copies[2 * tt + 1].wait()
            wu[mine, :] = (
                wu[mine, :].astype(F32) + du[tt, pl.ds(0, block), :].astype(F32)
            ).astype(BF)
            sends.start(wu.at[mine, far], up_got.at[tt], last_sems.at[1, tt], across)
            store(wu.at[mine, near], up_kept.at[tt])
    line_came(1, 0, inner, 3)
    line_came(1, 1, inner, 1)
    line_go(2, 0, t == 0, 1)
    line_go(2, 0, inner, 3)
    line_go(2, 1, t >= 1, 1)
    for sent in f_sent[LINE - 2 :]:
        sent()
    sends.made = [item for item in sends.made if item[1] is not None]
    for tt in range(LINE):
        if whole:
            arrived(gate_got.at[tt], last_sems.at[0, tt], here)
            arrived(up_got.at[tt], last_sems.at[1, tt], here)
        else:
            arrived(gate_mid.at[pl.ds(tt * group, group)], gate_sems.at[tt], here)
            for k in range(side // 2):
                arrived(up_mid.at[k, tt], up_sems.at[k, tt], here)
    arrived(dab.at[pl.ds(pl.multiple_of((1 - x) * half, half), half)], dab_sem, here)
    line_came(2, 0, t >= 1, 0)
    line_came(2, 1, t <= 2, 0)

    @pl.loop(0, 16)
    def _(i):
        part = pl.ds(pl.multiple_of(i * step, step), step)
        out_half[part, :] = (h_one[part, :] + h_all[0, part, :].astype(F32)).astype(BF)

    sends.wait_sent()
    for copy in stores:
        copy.wait()


def feed_forward(side, h_own, dm_all, units, down, h_one, ffn_gain):
    half, width = h_own.shape
    unit_count = down.shape[0]
    strip = unit_count // 2
    rows = 2 * half
    group = width // LINE
    block = group // side
    any_space = pl.BlockSpec(memory_space=pl.ANY)
    vmem = pl.BlockSpec(memory_space=pltpu.VMEM)
    mids = [(width, strip), (side // 2, LINE, block, unit_count)]
    last = (LINE, block, strip)
    blocks = (LINE, half, width)
    outs = [blocks, blocks, (2, 3, half, width), blocks, (unit_count, width)] + mids
    outs += [last] * 4 if side == 2 else [mids[0], (1, LANES), mids[1], (1, LANES)]
    held = [
        (width, unit_count), (width, unit_count), (unit_count, width),
        (LINE, rows, width), (LINE, rows, width),
        (LINE, rows, unit_count), (LINE, rows, unit_count), (LINE, rows, unit_count),
        (rows, width), (LINE, half, width), (2, half, width), (LINE, half, width),
    ]
    sends = 3 + 4 * (LINE - 1) + 3 * LINE + 3 * LINE + side // 2 * LINE + 8
    return pl.pallas_call(
        functools.partial(feed_kernel, side),
        out_shape=[
            jax.ShapeDtypeStruct((half, width), BF),
            jax.ShapeDtypeStruct((rows, width), BF),
            jax.ShapeDtypeStruct((1, width), F32),
        ]
        + [jax.ShapeDtypeStruct(shape, BF) for shape in outs],
        in_specs=[any_space] * 4 + [vmem] * 2,
        out_specs=[vmem, any_space, vmem] + [any_space] * len(outs),
        scratch_shapes=[pltpu.VMEM(shape, BF) for shape in held]
        + [
            pltpu.SemaphoreType.DMA((5,)),
            pltpu.SemaphoreType.DMA((3 * LINE + 2 + side // 2 * LINE,)),
            pltpu.SemaphoreType.DMA((sends,)),
            pltpu.SemaphoreType.DMA((LINE,)),
            pltpu.SemaphoreType.DMA((LINE,)),
            pltpu.SemaphoreType.DMA((LINE,)),
            pltpu.SemaphoreType.DMA((LINE,)),
            pltpu.SemaphoreType.DMA((LINE,)),
            pltpu.SemaphoreType.DMA((side // 2, LINE)),
            pltpu.SemaphoreType.DMA((3, 2 * LINE)),
            pltpu.SemaphoreType.DMA((2, LINE)),
            pltpu.SemaphoreType.DMA((LINE,)),
            pltpu.SemaphoreType.DMA((2, 3)),
            pltpu.SemaphoreType.DMA,
            pltpu.SemaphoreType.DMA((3 + 4 * (LINE - 1),)),
        ],
        compiler_params=pltpu.CompilerParams(
            collective_id=1, has_side_effects=True, vmem_limit_bytes=63 << 20
        ),
        cost_estimate=pl.CostEstimate(
            flops=18 * LINE * rows * width * unit_count, bytes_accessed=100 << 20,
            transcendentals=LINE * rows * unit_count,
        ),
    )(h_own, dm_all, units, down, h_one, ffn_gain[None, :])


def end_kernel(side, piece, scale, *refs):
    gate, gate_got, up, up_got, down, down_got, w_qkv, w_out, dab, length = refs[:10]
    hidden, proj, totals, cosine, sine, q_gain, k_gain, attn_gain, ffn_part = refs[10:19]
    q_out, k_out, v_out, homes_out, down_out, small_out, low_out, low_got_out = refs[19:27]
    (
        heads, heads_core, heads_side, line_right, line_left,
        gates, gates_got, ups, ups_got, downs, downs_got, downs_across, homes,
        grads, weights, low, low_got, grad_o, out_held, dab_held,
        keys_sum, vals_sum, q_sum, k_sum, smalls,
    ) = refs[27:52]
    load_sems, send_sems, core_sems, side_sems, line_sems, across_sems = refs[52:58]
    home_sems, small_sems, store_sems = refs[58:]
    t, j, c, x = coordinates()
    bits = side.bit_length() - 1
    depth, q_cols = q_out.shape
    k_cols = k_out.shape[1]
    strip = side * piece

    def at(tt, jj, cc, xx=None):
        return (((tt * side) + jj) * 2 + cc, x if xx is None else xx)

    def block(tt, jj, cc):
        return ((tt * side) + jj) * 2 + cc

    here, core, across = at(t, j, c), at(t, j, 1 - c), at(t, j, c, 1 - x)
    beside = [at(t, j ^ (1 << bit), c) for bit in range(bits)]
    others = [
        at((t + dt) % LINE, j, c ^ dc) for dt in range(LINE) for dc in range(2) if dt or dc
    ]
    loads = [
        (gate, gates), (gate_got, gates_got), (up, ups), (up_got, ups_got),
        (down.at[x], downs) if side == 2 else (down, downs),
        (w_qkv, weights),
    ]
    if side != 2:
        loads.append((down_got, downs_got))
    loads += [(w_out, out_held), (dab, dab_held)]
    loads = [pltpu.make_async_copy(a, b, load_sems.at[i]) for i, (a, b) in enumerate(loads)]
    for load in loads:
        load.start()
    greet(others + beside + [across])
    sends = Sends(send_sems)

    def add(target, first, second):
        count = first.shape[0]
        step = min(64, count)

        @pl.loop(0, count // step)
        def _(i):
            part = pl.ds(pl.multiple_of(i * step, step), step)
            target[part, :] = (first[part, :].astype(F32) + second[part, :].astype(F32)).astype(
                target.dtype
            )

    def go_home(which, rows):
        for tt in range(LINE):
            for cc in range(2):
                mine = jnp.logical_and(t == tt, c == cc)
                source = rows.at[tt, pl.ds(cc * depth, depth)]
                target = homes.at[which, t * 2 + c]
                sends.start(
                    source, target, home_sems.at[which, t * 2 + c], at(tt, j, cc),
                    jnp.logical_not(mine),
                )

                @pl.when(mine)
                def _():
                    homes[which, tt * 2 + cc] = source[...]

    if side == 2:
        sends.start(down.at[1 - x], downs_got, across_sems.at[2], across)
    for which, (mine, got) in enumerate(((gates, gates_got), (ups, ups_got))):
        loads[2 * which].wait()
        loads[2 * which + 1].wait()
        for tt in range(LINE):
            add(mine.at[tt], mine.at[tt], got.at[tt])
        go_home(which, mine)

    def down_second():
        loads[4].wait()
        if side == 2:
            arrived(downs_got, across_sems.at[2], here)
        else:
            loads[6].wait()
        for xx in range(2):
            add(downs.at[xx], downs.at[xx], downs_got.at[xx])
        if side == 2:
            sends.start(downs.at[1 - j], downs_across, across_sems.at[0], beside[0])
        else:
            sends.start(downs.at[1 - x], downs_across, across_sems.at[0], across)

    loads[-2].wait()
    loads[-1].wait()
    tile = min(512, q_cols)

    @pl.loop(0, q_cols // tile)
    def _(i):
        cols = pl.ds(pl.multiple_of(i * tile, tile), tile)
        grad_o[:, cols] = mm_nt(dab_held[...], out_held[cols, :]).astype(BF)

    q_sum[...] = jnp.zeros_like(q_sum)
    k_sum[...] = jnp.zeros_like(k_sum)
    rows = hidden.shape[0]
    group = q_cols // k_cols * HEAD

    @pl.loop(0, k_cols // HEAD)
    def _(g):
        pair = pl.multiple_of(g // 2 * LANES, LANES)
        wide = pl.ds(pl.multiple_of(g * group, group), group)
        k_pair = pl.ds(q_cols + pair, LANES)
        v_pair = pl.ds(q_cols + k_cols + pair, LANES)
        attend_back_kernel(
            rows // 2, scale, g % 2 == 1, length,
            proj.at[:, wide], proj.at[:, k_pair], proj.at[:, v_pair],
            cosine, sine, q_gain, k_gain,
            totals.at[:, pl.ds(pl.multiple_of(g * LANES, LANES), LANES)],
            grad_o.at[:, wide],
            grads.at[:, wide], grads.at[:, k_pair], grads.at[:, v_pair],
            q_sum, k_sum, keys_sum, vals_sum,
        )

    width = hidden.shape[1]
    place_rows = width // LINE
    tile = min(256, place_rows)
    for q in reversed(range(LINE)):
        tt = slot_place(t, q)

        @pl.loop(0, place_rows // tile)
        def _(i):
            span = pl.ds(pl.multiple_of(tt * place_rows + i * tile, tile), tile)
            grad = mm_tn(hidden[:, span], grads[...]).astype(BF)
            first = tt * (2 * side) + i * (tile // depth)
            heads[pl.ds(first, tile // depth)] = grad.reshape(tile // depth, depth, -1)

        for r in range(side):
            sends.start(
                heads.at[block(tt, j ^ r, 1 - c)], heads_core.at[tt, j ^ r],
                core_sems.at[tt, j ^ r], core,
            )

    loads[5].wait()
    wide = min(512, width)
    for i in range(width // wide):
        cols = pl.ds(i * wide, wide)
        grad = mm_nt(grads[...], weights[cols, :])
        low[:, cols] = grad.astype(BF)
        part = jnp.sum(grad * hidden[:, cols].astype(F32), axis=0, keepdims=True)
        part = part / attn_gain[:, cols]
        for k in range(wide // LANES):
            smalls[0, pl.ds(i * (wide // LANES) + k, 1), :] = part[:, k * LANES : (k + 1) * LANES]
    sends.start(low, low_got, across_sems.at[1], across)
    count = width // LANES
    smalls[0, pl.ds(count, count), :] = ffn_part[...]
    q_part, k_part = q_sum[...], k_sum[...]
    q_part = q_part + pltpu.roll(q_part, HEAD, 1)
    k_part = k_part + pltpu.roll(k_part, HEAD, 1)
    smalls[0, pl.ds(2 * count, 1), :] = jnp.where(low_lanes(q_part.shape), q_part, k_part)

    partners = [core] + beside + [across, at(t ^ 1, j, c), at(t ^ 2, j, c)]

    def small_step(i):
        if i:
            arrived(smalls.at[2 * i], small_sems.at[i - 1], here)
            smalls[2 * i - 1] = smalls[max(2 * i - 3, 0)] + smalls[2 * i]
        if i < len(partners):
            source = smalls.at[2 * i - 1] if i else smalls.at[0]
            sends.start(source, smalls.at[2 * i + 2], small_sems.at[i], partners[i])
        return i + 1

    def side_first(q):
        tt = slot_place(t, q)
        for r in reversed(range(side)):
            arrived(heads_core.at[tt, j ^ r], core_sems.at[tt, j ^ r], here)
            mine = heads.at[block(tt, j ^ r, c)]
            add(mine, mine, heads_core.at[tt, j ^ r])
            if bits and r >= side // 2:
                k = side // 2 - 1 + r - side // 2
                sends.start(mine, heads_side.at[tt, k], side_sems.at[tt, k], beside[bits - 1])

    def side_rest(q):
        tt = slot_place(t, q)
        for bit in reversed(range(bits)):
            half = 1 << bit
            for r in range(half):
                arrived(heads_side.at[tt, half - 1 + r], side_sems.at[tt, half - 1 + r], here)
                mine = heads.at[block(tt, j ^ r, c)]
                add(mine, mine, heads_side.at[tt, half - 1 + r])
                if bit and r >= half // 2:
                    k = half // 2 - 1 + r - half // 2
                    sends.start(
                        mine, heads_side.at[tt, k], side_sems.at[tt, k], beside[bit - 1]
                    )
        return heads.at[block(tt, j, c)]

    def line_came(i, way, cond, target):
        line = (line_right, line_left)[way]

        def act():
            arrived(line.at[i], line_sems.at[way, i], here)
            add(target, target, line.at[i])

        when(cond, act)

    def line_go(i, way, cond, source):
        line = (line_right, line_left)[way]
        sends.start(
            source, line.at[i], line_sems.at[way, i], at(t + 1 - 2 * way, j, c), cond
        )

    step = small_step(0)
    side_first(3)
    side_first(2)
    step = small_step(step)
    p3 = side_rest(3)
    line_go(0, 0, t == 0, p3)
    line_go(0, 1, t == 3, p3)
    side_first(1)
    step = small_step(step)
    p2 = side_rest(2)
    line_came(0, 0, t == 1, p2)
    line_came(0, 1, t == 2, p2)
    line_go(1, 0, t <= 1, p2)
    line_go(1, 1, t >= 2, p2)
    side_first(0)
    down_second()

    step = small_step(step)
    p1 = side_rest(1)
    line_came(1, 0, jnp.logical_and(t >= 1, t <= 2), p3)
    line_came(1, 1, jnp.logical_and(t >= 1, t <= 2), p1)
    line_go(2, 0, t == 0, p1)
    line_go(2, 0, jnp.logical_and(t >= 1, t <= 2), p3)
    line_go(2, 1, t >= 1, p1)
    while step <= len(partners):
        step = small_step(step)
    small_out[...] = smalls[2 * len(partners) - 1]
    arrived(downs_across, across_sems.at[0], here)
    add(down_out, downs.at[j if side == 2 else x], downs_across)
    p0 = side_rest(0)
    line_came(2, 0, t >= 1, p0)
    line_came(2, 1, t <= 2, p0)
    q_out[...] = p0[:, pl.ds(0, q_cols)].astype(F32)
    k_out[...] = p0[:, pl.ds(q_cols, k_cols)].astype(F32)
    v_out[...] = p0[:, pl.ds(q_cols + k_cols, k_cols)].astype(F32)
    stores = []

    def store(source, target):
        copy = pltpu.make_async_copy(source, target, store_sems.at[len(stores)])
        copy.start()
        stores.append(copy)

    for which in range(2):
        for tt in range(LINE):
            for cc in range(2):
                when(
                    jnp.logical_not(jnp.logical_and(t == tt, c == cc)),
                    lambda w=which, k=tt * 2 + cc: arrived(
                        homes.at[w, k], home_sems.at[w, k], here
                    ),
                )
    store(homes, homes_out)
    arrived(low_got, across_sems.at[1], here)
    store(low, low_out)
    store(low_got, low_got_out)
    sends.wait_sent()
    for copy in stores:
        copy.wait()


def end_layer(n, piece, pairs, down, w_qkv, w_out, dab, length, hidden, proj, totals, tables,
              gains, attn_gain, ffn_part):
    side = n // LINE // 2
    bits = side.bit_length() - 1
    rows, width = hidden.shape
    cols = w_qkv.shape[1]
    q_cols = w_out.shape[0]
    depth = width // n
    k_cols = (cols - q_cols) // 2
    strip = side * piece
    any_space = pl.BlockSpec(memory_space=pl.ANY)
    vmem = pl.BlockSpec(memory_space=pltpu.VMEM)
    steps = bits + 4
    sides = max(side - 1, 1)
    home = (LINE, 2 * depth, strip)
    held = [
        (n, depth, cols), (LINE, side, depth, cols), (LINE, sides, depth, cols),
        (3, depth, cols), (3, depth, cols),
        home, home, home, home,
        (2, piece, width), (2, piece, width), (piece, width),
        (2, LINE * 2, depth, strip),
        (rows, cols), (width, cols), (rows, width), (rows, width),
        (rows, q_cols), (q_cols, width), (rows, width),
    ]
    small = (2 * (width // LANES) + 1, LANES)
    floats = [
        (rows, LANES), (rows, LANES), (1, LANES), (1, LANES),
        (2 * steps + 1,) + small,
    ]
    sends = LINE * (2 * side - 1) + 3 + steps + 8 + 4 * LINE + 4
    return pl.pallas_call(
        functools.partial(end_kernel, side, piece, 1.0 / math.sqrt(HEAD)),
        out_shape=[
            jax.ShapeDtypeStruct((depth, q_cols), F32),
            jax.ShapeDtypeStruct((depth, k_cols), F32),
            jax.ShapeDtypeStruct((depth, k_cols), F32),
            jax.ShapeDtypeStruct((2, LINE * 2, depth, strip), BF),
            jax.ShapeDtypeStruct((piece, width), F32),
            jax.ShapeDtypeStruct(small, F32),
            jax.ShapeDtypeStruct((rows, width), BF),
            jax.ShapeDtypeStruct((rows, width), BF),
        ],
        in_specs=[any_space] * 9 + [pl.BlockSpec(memory_space=pltpu.SMEM)] + [vmem] * 9,
        out_specs=[vmem] * 3 + [any_space] + [vmem] * 2 + [any_space] * 2,
        scratch_shapes=[pltpu.VMEM(shape, BF) for shape in held]
        + [pltpu.VMEM(shape, F32) for shape in floats]
        + [
            pltpu.SemaphoreType.DMA((9,)),
            pltpu.SemaphoreType.DMA((sends,)),
            pltpu.SemaphoreType.DMA((LINE, side)),
            pltpu.SemaphoreType.DMA((LINE, sides)),
            pltpu.SemaphoreType.DMA((2, 3)),
            pltpu.SemaphoreType.DMA((3,)),
            pltpu.SemaphoreType.DMA((2, LINE * 2)),
            pltpu.SemaphoreType.DMA((steps,)),
            pltpu.SemaphoreType.DMA((4,)),
        ],
        compiler_params=pltpu.CompilerParams(
            collective_id=2, has_side_effects=True, vmem_limit_bytes=62 << 20
        ),
        cost_estimate=pl.CostEstimate(
            flops=8 * rows * width * cols, bytes_accessed=300 << 20, transcendentals=rows * rows
        ),
    )(
        *pairs, *down, w_qkv, w_out, dab, length, hidden, proj, totals, *tables, *gains,
        attn_gain[None, :], ffn_part,
    )


def finish_kernel(side, piece, homes, low, low_got, tokens, dab, gain, gate, up, grad):
    count = gate.shape[0]
    for which, out in enumerate((gate, up)):
        for tt in range(LINE):
            for jj in range(side):
                for cc in range(2):
                    col = ((tt * side + jj) * 2 + cc) * piece
                    out[:, pl.ds(col, piece)] = homes[
                        which, tt * 2 + cc, pl.ds(0, count), pl.ds(jj * piece, piece)
                    ].astype(F32)
    values = tokens[...].astype(F32)
    scale = lax.rsqrt(jnp.mean(values * values, axis=1, keepdims=True) + EPS)
    part = (low[...].astype(F32) + low_got[...].astype(F32)) * gain[...]
    back = jnp.mean(part * values, axis=1, keepdims=True) * scale * scale
    grad[...] = dab[...].astype(F32) + scale * (part - values * back)


def finish(side, piece, homes, low, low_got, tokens, dab, gain):
    rows, width = tokens.shape
    depth, strip = homes.shape[2], homes.shape[3]
    steps = 8 if depth % 128 == 0 else 2
    columns = LINE * 2 * strip
    block = pl.BlockSpec((rows // steps, width), lambda i: (i, 0))
    wide = pl.BlockSpec((depth // steps, columns), lambda i: (i, 0))
    return pl.pallas_call(
        functools.partial(finish_kernel, side, piece),
        grid=(steps,),
        in_specs=[
            pl.BlockSpec((2, LINE * 2, depth // steps, strip), lambda i: (0, 0, i, 0)),
            block, block, block, block,
            pl.BlockSpec((1, width), lambda i: (0, 0)),
        ],
        out_specs=[wide, wide, block],
        out_shape=[
            jax.ShapeDtypeStruct((depth, columns), F32),
            jax.ShapeDtypeStruct((depth, columns), F32),
            jax.ShapeDtypeStruct((rows, width), F32),
        ],
        compiler_params=pltpu.CompilerParams(vmem_limit_bytes=62 << 20),
        cost_estimate=pl.CostEstimate(
            flops=20 * rows * width, bytes_accessed=20 << 20, transcendentals=0
        ),
    )(homes, low, low_got, tokens, dab, gain[None, :])


class Links:
    def __init__(self, n):
        self.n = n
        self.inner = n // LINE
        self.side = self.inner // 2
        self.side_bits = self.side.bit_length() - 1
        self.t, self.j, self.c, self.x = coordinates()

    def core(self, value):
        return lax.ppermute(value, "dp", [(i, i ^ 1) for i in range(self.n)])

    def over(self, value, bit):
        return lax.ppermute(value, "dp", [(i, i ^ (2 << bit)) for i in range(self.n)])

    def cross(self, value):
        return lax.ppermute(value, "tensor", [(0, 1), (1, 0)])

    def along(self, value, moves):
        pairs = [
            (a * self.inner + i, b * self.inner + i) for a, b in moves for i in range(self.inner)
        ]
        return lax.ppermute(value, "dp", pairs)

    def right(self, value, senders):
        return self.along(value, [(a, a + 1) for a in senders])

    def left(self, value, senders):
        return self.along(value, [(a, a - 1) for a in senders])

    def turn(self, value, shift):
        return self.along(value, [(a, (a + shift) % LINE) for a in range(LINE)])

    def line_gather(self, value):
        t = self.t
        r1 = self.right(value, (0, 1, 2))
        l1 = self.left(value, (1, 2, 3))
        r2 = self.right(r1, (1, 2))
        l2 = self.left(l1, (1, 2))
        r3 = self.right(r2, (2,))
        l3 = self.left(l2, (1,))
        return (
            value,
            jnp.where(t == 0, l1, r1),
            jnp.where(t < 2, l2, r2),
            jnp.where(t == 0, l3, jnp.where(t == 3, r3, l1)),
        )

    def lines(self):
        return [[i + k * self.inner for k in range(LINE)] for i in range(self.inner)]

    def line_all(self, value):
        return lax.all_gather(value, "dp", axis_index_groups=self.lines())

    def line_sum(self, value):
        return lax.psum_scatter(
            value, "dp", scatter_dimension=0, axis_index_groups=self.lines()
        )

    def dp_sum(self, value):
        return lax.psum_scatter(value, "dp", scatter_dimension=0, tiled=True)

    def line_scatter(self, parts):
        t = self.t
        p0, p1, p2, p3 = parts
        first = p3.astype(BF)
        r1 = self.right(first, (0,))
        l1 = self.left(first, (3,))
        second = (p2 + r1.astype(F32) + l1.astype(F32)).astype(BF)
        r2 = self.right(second, (0, 1))
        l2 = self.left(second, (2, 3))
        r3 = self.right((jnp.where(t == 0, p1, p3) + r2.astype(F32)).astype(BF), (0, 1, 2))
        l3 = self.left((p1 + l2.astype(F32)).astype(BF), (1, 2, 3))
        return p0 + r3.astype(F32) + l3.astype(F32)

    def line_send(self, parts):
        p0, p1, p2, p3 = parts
        first, second, third = p1.astype(BF), p2.astype(BF), p3.astype(BF)
        got = [
            self.left(first, (1, 2, 3)),
            self.right(first, (0,)),
            self.turn(second, 2),
            self.along(third, ((0, 3), (3, 0))),
            self.right(third, (1, 2)),
        ]
        return p0 + sum(g.astype(F32) for g in got)

    def side_all(self, value):
        blocks = [value]
        for bit in range(self.side_bits):
            blocks += [self.over(block, bit) for block in blocks]
        return blocks

    def side_sum(self, blocks):
        for bit in reversed(range(self.side_bits)):
            width = 1 << bit
            blocks = [
                a.astype(F32) + self.over(b.astype(BF), bit).astype(F32)
                for a, b in zip(blocks[:width], blocks[width:])
            ]
        return blocks[0]

    def side_start(self, blocks):
        for bit in reversed(range(1, len(blocks).bit_length() - 1)):
            half = 1 << bit
            blocks = [
                (a.astype(F32) + self.over(b, bit).astype(F32)).astype(BF)
                for a, b in zip(blocks[:half], blocks[half:])
            ]
        return blocks[0], self.over(blocks[1], 0)

    def side_end(self, kept, got):
        if kept.shape[0] == 1:
            return kept[0], got[0]
        total = (kept.astype(F32) + got.astype(F32)).astype(BF)
        return self.side_start(list(total))

    def pair_order(self, mine, other, where):
        low = jnp.where(where == 0, mine, other)
        high = jnp.where(where == 0, other, mine)
        return jnp.concatenate([low, high], 0)

    def pick(self, value, index, axis):
        return lax.dynamic_index_in_dim(value, index, axis, keepdims=False)

    def cross_sum(self, value, axis):
        kept = self.pick(value, self.x, axis)
        sent = self.pick(value, 1 - self.x, axis)
        return kept.astype(F32) + self.cross(sent.astype(BF)).astype(F32)

    def gather_rows(self, blocks):
        rows, cols = blocks[0].shape
        pieces, where = [], []
        for k, block in enumerate(blocks):
            for r, piece in enumerate(self.side_all(block)):
                pieces += [piece, self.core(piece)]
                where += [(k, r, 0), (k, r, 1)]

        def spots(t, j, c, x):
            return [
                (
                    i, 0, 0, rows, cols,
                    (((slot_place(t, k) * self.side) + (j ^ r)) * 2 + (c ^ s)) * rows, 0,
                )
                for i, (k, r, s) in enumerate(where)
            ]

        return place(pieces, spots, (self.n * rows, cols))

    def sum_rows(self, value):
        rows, cols = value.shape[0] // self.n, value.shape[1]
        parts = value.reshape(LINE, self.side, 2, rows, cols)
        kept = self.pick(parts, self.c, 2).astype(F32)
        parts = kept + self.core(self.pick(parts, 1 - self.c, 2)).astype(F32)
        parts = parts.astype(BF)
        parts = self.side_sum([self.pick(parts, self.j ^ r, 1) for r in range(self.side)])
        return self.line_scatter(
            [self.pick(parts, slot_place(self.t, k), 0).astype(F32) for k in range(LINE)]
        )

    def total(self, value):
        value = value + self.core(value)
        for bit in range(self.side_bits):
            value = value + self.over(value, bit)
        value = value + self.cross(value)
        value = value + self.along(value, ((0, 1), (1, 0), (2, 3), (3, 2)))
        return value + self.turn(value, 2)


def make_body(n):
    def body(
        tokens,
        cotangent,
        lengths,
        attn_gain,
        query_gain,
        key_gain,
        w_query,
        key_weight_matrix,
        value_weight_matrix,
        w_out,
        ffn_gain,
        w_gate,
        w_up,
        w_down,
    ):
        net = Links(n)
        t, j, c, x = net.t, net.j, net.c, net.x
        row_count, width = tokens.shape
        half = row_count // 2
        head_dim = query_gain.shape[0]
        q_cols = w_query.shape[1]
        k_cols = key_weight_matrix.shape[1]
        k_heads = k_cols // head_dim
        dp_index = lax.axis_index("dp")
        slot_length = lengths[dp_index]

        depth = w_gate.shape[0]
        piece = w_down.shape[0]
        side = net.side
        strip = side * piece
        tables = angle_tables(row_count, head_dim, LANES)
        gains = [jnp.tile(gain, LANES // head_dim)[None, :] for gain in (query_gain, key_gain)]
        length = slot_length[None]
        weights = (w_query, key_weight_matrix, value_weight_matrix, w_out, w_gate, w_up, w_down)
        (
            qkv_full, wo_full, units, wd, grad_all, qkv, o_low, log_totals, h_one, hidden_two,
            hidden_state,
        ) = start_layer(
            n, weights, cotangent, length, tokens, attn_gain, tables, gains, ffn_gain
        )

        (
            layer_half, grad_attn_low, g_ffn_part, _, _, _, _,
            g_down, gate_mid, up_mid, gate_kept, gate_got, up_kept, up_got,
        ) = feed_forward(
            side, hidden_two, grad_all, units.reshape(2, width, 2 * strip),
            wd.reshape(2 * strip, width), h_one, ffn_gain,
        )
        layer_out = net.pair_order(layer_half, net.cross(layer_half), x)

        if side != 2:
            gate_sum = (gate_kept.astype(F32) + gate_mid.astype(F32)).astype(BF)
            gate_sum = gate_sum.reshape(LINE, side, 2 * depth, strip)
            gate_kept, gate_got = net.side_start([net.pick(gate_sum, j ^ r, 1) for r in range(side)])
            up_kept, up_got = net.side_end(up_kept, up_mid)
            up_sum = (up_kept.astype(F32) + up_got.astype(F32)).astype(BF)
            up_kept = lax.dynamic_slice_in_dim(up_sum, x * strip, strip, 2)
            up_got = net.cross(lax.dynamic_slice_in_dim(up_sum, (1 - x) * strip, strip, 2))
        g_down = g_down.reshape(2, side, piece, width)
        down_pair = (g_down, g_down)
        if side != 2:
            down_pair = net.side_start([net.pick(g_down, j ^ r, 1) for r in range(side)])

        g_out = mm_tn(o_low, grad_attn_low).astype(BF)
        g_out_out = net.dp_sum(g_out).astype(F32)
        (
            g_query_w, g_key_w, g_value_w, homes, g_down_out, small, low, low_got,
        ) = end_layer(
            n, piece, (gate_kept, gate_got, up_kept, up_got), down_pair, qkv_full, wo_full,
            grad_attn_low, length, hidden_state, qkv, log_totals, tables, gains, attn_gain,
            g_ffn_part.reshape(-1, LANES),
        )
        g_gate_out, g_up_out, input_grad = finish(
            side, piece, homes, low, low_got, tokens, grad_attn_low, attn_gain
        )
        small = small.reshape(-1)
        return (
            layer_out,
            input_grad,
            small[:width],
            small[2 * width : 2 * width + head_dim],
            small[2 * width + head_dim :],
            g_query_w,
            g_key_w,
            g_value_w,
            g_out_out,
            small[width : 2 * width],
            g_gate_out,
            g_up_out,
            g_down_out,
        )

    return body


def solution(mesh):
    placed = (
        P("dp", None),
        P("dp", None),
        P(),
        P(),
        P(),
        P(),
        P("dp", "tensor"),
        P("dp", "tensor"),
        P("dp", "tensor"),
        P(("tensor", "dp"), None),
        P(),
        P("dp", "tensor"),
        P("dp", "tensor"),
        P(("tensor", "dp"), None),
    )
    return jax.shard_map(
        make_body(mesh.shape["dp"]),
        mesh=mesh,
        in_specs=placed,
        out_specs=(
            P("dp", None),
            P("dp", None),
            P(),
            P(),
            P(),
            P("dp", "tensor"),
            P("dp", "tensor"),
            P("dp", "tensor"),
            P(("tensor", "dp"), None),
            P(),
            P("dp", "tensor"),
            P("dp", "tensor"),
            P(("tensor", "dp"), None),
        ),
        check_vma=False,
    )
```
